32 devices in a mesh: rows: 4 (over x, core), pts: 8 (over z, y).
Axes of the slice: x: 2, y: 2, z: 4, core: 2. Of those that a mesh axis runs over, the one named last changes fastest.
Arguments:
- features: bfloat16 [8192, 128], P('pts'), may hold values from -6 to 6
- targets: bfloat16 [8192, 256], P('pts'), may hold values from -6 to 6
- coefficients: float32 [8192, 256], P('pts'), may hold values from -6 to 6
- momentum: float32 [8192, 256], P('pts'), may hold values from -6 to 6
- block_index: int32 [2, 2048], replicated, may hold values from 0 to 8191, as said below
- pivot_index: int32 [2, 512], replicated, may hold values from 0 to 2047, as said below
- nystrom_core: bfloat16 [2, 512, 512], replicated, may hold values from -0.5 to 3
Outputs:
- new_coefficients: float32 [8192, 256], P('pts')
- new_momentum: float32 [8192, 256], P('pts')
The draws below stay inside these ranges and needn't reach their ends.
Inputs may be any that keep to these rules, and one draw needn't show every extreme that they name: `block_index`: each row lists 2048 distinct points; a point p belongs to index p // 1024 of pts; in each row one index of pts, drawn from the seed, owns exactly 192 of the points in every aligned group of 512 positions, and no index owns more than 192 points of any such group. `pivot_index`: each row lists 512 distinct positions.
All inputs are finite; a program needn't handle non-finite values.
Results may differ from the reference program's by a relative error of at most 0.0041.
The reference program's roundings to bfloat16 on the way count: a program that leaves them out, or rounds other values in their place, can miss the bound.
Values may be sent and summed in bfloat16 or wider, within the bound.
No kernel may reach another device: no remote copies, remote signals or barrier semaphores. Data moves between devices by JAX's collectives and lax.ppermute only.
A program may use at most 64 MiB of HBM per device.

```python
import math
import jax
import jax.numpy as jnp
from jax import lax

DF = 128
NOUT = 256
BLK = 2048
RANK = 512
UPDATES = 2
PTS_DEV = 1024
NPTS = 8192
GROUP = 512
CAP = 192
N_PTS = 8


def shuffle_points(one_key):
    return jax.random.permutation(one_key, PTS_DEV).astype(jnp.int32)


def pick_block(key):
    owner_count = NPTS // PTS_DEV
    group_count = BLK // GROUP
    busy_key, group_key, place_key = jax.random.split(key, 3)
    busiest = jax.random.randint(busy_key, (), 0, owner_count).astype(jnp.int32)
    group_keys = jax.random.split(group_key, group_count)

    def fill_group(group_one):
        ticket_key, order_key = jax.random.split(group_one)
        tickets = jax.random.permutation(ticket_key, (owner_count - 1) * CAP)[:GROUP - CAP].astype(jnp.int32)
        others = (busiest + 1 + tickets // CAP) % owner_count
        sequence = jnp.concatenate([jnp.full((CAP,), busiest, jnp.int32), others.astype(jnp.int32)])
        return jax.random.permutation(order_key, sequence).astype(jnp.int32)
    owner = jax.vmap(fill_group)(group_keys).reshape(BLK).astype(jnp.int32)
    marks = (owner[:, None] == jnp.arange(owner_count, dtype=jnp.int32)[None, :]).astype(jnp.int32)
    before = jnp.cumsum(marks, axis=0) - marks
    rank_within = jnp.sum(before * marks, axis=1).astype(jnp.int32)
    shuffles = jax.vmap(shuffle_points)(jax.random.split(place_key, owner_count))
    return (owner * PTS_DEV + shuffles[owner, rank_within]).astype(jnp.int32)


def draw_block_index(key, part):
    keys = jax.random.split(key, UPDATES)
    return jax.vmap(pick_block)(keys).astype(jnp.int32)


def pick_pivots(key):
    scores = jax.random.randint(key, (BLK,), 0, 32768) * BLK + jnp.arange(BLK, dtype=jnp.int32)
    return lax.top_k(scores.astype(jnp.int32), RANK)[1].astype(jnp.int32)


def draw_pivot_index(key, part):
    keys = jax.random.split(key, UPDATES)
    return jax.vmap(pick_pivots)(keys).astype(jnp.int32)


def draw_nystrom_core(key, part):
    diag_key, off_key = jax.random.split(key, 2)
    diagonal = jax.random.uniform(diag_key, (UPDATES, RANK), jnp.float32, 1.2, 2.8)
    spread = 0.45 / math.sqrt(RANK)
    raw_part = jax.random.normal(off_key, (UPDATES, RANK, RANK), jnp.float32) * spread
    off_part = (raw_part + jnp.swapaxes(raw_part, 1, 2)) * (1.0 / math.sqrt(2.0))
    centred = jnp.eye(RANK, dtype=jnp.float32)[None, :, :] * diagonal[:, :, None]
    centred = centred - (diagonal[:, :, None] + diagonal[:, None, :]) / RANK
    centred = centred + jnp.sum(diagonal, axis=1)[:, None, None] / (RANK * RANK)
    return jnp.clip(centred + off_part, -0.5, 3.0).astype(jnp.bfloat16)


def steps_of(rng, shape, cuts, least, top_value):
    factor_of, own = 1.0, jax.random.fold_in(rng, 6)
    for axis_at, shards_of in cuts:
        heights = jnp.exp(jax.random.uniform(jax.random.fold_in(own, axis_at), (shards_of,), jnp.float32, least / len(cuts), top_value / len(cuts)))
        factor_of = factor_of * jnp.repeat(heights, shape[axis_at] // shards_of).reshape([-1 if axis == axis_at else 1 for axis in range(len(shape))])
    return factor_of


def normal_values(key, extent, deviation, most, shards=(), held_as=jnp.bfloat16):
    entries = deviation * jax.random.normal(key, extent, jnp.float32)
    if shards:
        entries = entries * steps_of(key, extent, shards, -0.22, 0.18)
    return jnp.clip(entries, -most, most).astype(held_as)


def setup_inputs(seed: int = 0) -> dict:
    arg_keys = jax.random.split(jax.random.key(seed), 8)
    return {
        "features": normal_values(arg_keys[0], (NPTS, DF), 1.0, 6.0, ((0, 8),)),
        "targets": normal_values(arg_keys[1], (NPTS, NOUT), 1.0, 6.0, ((0, 8),)),
        "coefficients": normal_values(arg_keys[2], (NPTS, NOUT), 1.0, 6.0, ((0, 8),), jnp.float32),
        "momentum": normal_values(arg_keys[3], (NPTS, NOUT), 1.0, 6.0, ((0, 8),), jnp.float32),
        "block_index": draw_block_index(jax.random.fold_in(arg_keys[7], 71), 0),
        "pivot_index": draw_pivot_index(jax.random.fold_in(arg_keys[7], 71), 0),
        "nystrom_core": draw_nystrom_core(jax.random.fold_in(arg_keys[7], 71), 0),
    }


alpha_mix = 0.6
beta_keep = 0.9
step_size = 0.2
momentum_gain = 1.5
ridge_term = 1.0


def kernel_tile(left_rows, right_rows):
    inner_prod = lax.dot_general(left_rows, right_rows, (((1,), (1,)), ((), ())), preferred_element_type=jnp.float32)
    left_sq = jnp.sum(jnp.square(left_rows.astype(jnp.float32)), axis=1)
    right_sq = jnp.sum(jnp.square(right_rows.astype(jnp.float32)), axis=1)
    squared = left_sq[:, None] + right_sq[None, :] - 2.0 * inner_prod
    return jnp.exp(squared * (-3.5 / left_rows.shape[1])).astype(jnp.bfloat16)


def reference(features, targets, coefficients, momentum, block_index, pivot_index, nystrom_core):
    current = coefficients
    momentum_now = momentum
    feat_blocks = features.reshape(N_PTS, PTS_DEV, DF)
    for update in range(UPDATES):
        mixed = alpha_mix * momentum_now + (1.0 - alpha_mix) * current
        mixed_bf = mixed.astype(jnp.bfloat16)
        block_points = block_index[update]
        block_feats = features[block_points]
        offset = ridge_term * mixed[block_points] - targets[block_points].astype(jnp.float32)

        def accumulate(running, pieces):
            feat_piece, coef_piece = pieces
            return running + jnp.dot(kernel_tile(block_feats, feat_piece), coef_piece, preferred_element_type=jnp.float32), None

        running, unused = lax.scan(accumulate, jnp.zeros((BLK, NOUT), jnp.float32), (feat_blocks, mixed_bf.reshape(N_PTS, PTS_DEV, NOUT)))
        resid = running + offset
        resid_bf = resid.astype(jnp.bfloat16)
        pivot_feats = block_feats[pivot_index[update]]
        factor = kernel_tile(block_feats, pivot_feats)
        proj = lax.dot_general(factor, resid_bf, (((0,), (0,)), ((), ())), preferred_element_type=jnp.float32)
        lifted = jnp.dot(nystrom_core[update], proj.astype(jnp.bfloat16), preferred_element_type=jnp.float32).astype(jnp.bfloat16)
        step_bf = (resid - jnp.dot(factor, lifted, preferred_element_type=jnp.float32)).astype(jnp.bfloat16)
        step_bf = lax.optimization_barrier(step_bf)
        change = step_bf.astype(jnp.float32)
        current = mixed.at[block_points].add(-step_size * change)
        momentum_now = (beta_keep * momentum_now + (1.0 - beta_keep) * mixed).at[block_points].add(-step_size * momentum_gain * change)
    return current, momentum_now
```

```python
import jax
import jax.numpy as jnp
from jax import lax
from jax.sharding import PartitionSpec as P

UPDATES = 2


alpha_mix = 0.6
beta_keep = 0.9
step_size = 0.2
momentum_gain = 1.5
ridge_term = 1.0

f32 = jnp.float32
bf16 = jnp.bfloat16


def mm(a, b, ca, cb):
    return lax.dot_general(a, b, (((ca,), (cb,)), ((), ())), preferred_element_type=f32)


def kernel_tile(left_rows, right_rows):
    inner_prod = mm(left_rows, right_rows, 1, 1)
    left_sq = jnp.sum(jnp.square(left_rows.astype(f32)), axis=1)
    right_sq = jnp.sum(jnp.square(right_rows.astype(f32)), axis=1)
    squared = left_sq[:, None] + right_sq[None, :] - 2.0 * inner_prod
    return jnp.exp(squared * (-3.5 / left_rows.shape[1])).astype(bf16)


def split_two(value):
    high = value.astype(bf16)
    return high, (value - high.astype(f32)).astype(bf16)


def shards(features, targets, coefficients, momentum, block_index, pivot_index, nystrom_core):
    row_count = lax.axis_size("rows")
    pts_count = lax.axis_size("pts")
    row_id = lax.axis_index("rows")
    pts_id = lax.axis_index("pts")
    local_points = features.shape[0]
    block = block_index.shape[1]
    rank = pivot_index.shape[1]
    outputs = coefficients.shape[1]
    per_row = block // row_count
    per_device = per_row // pts_count
    row_cols = outputs // row_count
    own_cols = row_cols // pts_count
    first_point = pts_id * local_points
    points = lax.broadcasted_iota(jnp.int32, (local_points, 1), 0) + first_point

    place = [(points == block_index[u][None, :]).astype(bf16) for u in range(UPDATES)]

    own_rows = []
    for u in range(UPDATES):
        mine = lax.dynamic_slice_in_dim(place[u], row_id * per_row, per_row, axis=1)
        own_rows.append(mm(mine, features, 0, 0).astype(bf16).reshape(pts_count, per_device, -1))
    sent = jnp.concatenate(own_rows, axis=1)
    came = lax.all_to_all(sent, "pts", 0, 0, tiled=False)
    chunk = jnp.sum(came.astype(f32), axis=0).astype(bf16)
    over_pts = lax.all_gather(chunk, "pts", axis=0, tiled=False)
    over_rows = lax.all_gather(over_pts, "rows", axis=0, tiled=False)
    over_rows = over_rows.reshape(row_count, pts_count, UPDATES, per_device, features.shape[1])
    block_feats = [over_rows[:, :, u].reshape(block, features.shape[1]) for u in range(UPDATES)]

    first_col = row_id * row_cols
    current = lax.dynamic_slice_in_dim(coefficients, first_col, row_cols, axis=1).T
    moving = lax.dynamic_slice_in_dim(momentum, first_col, row_cols, axis=1).T
    goal = lax.dynamic_slice_in_dim(targets, first_col, row_cols, axis=1).T.astype(f32)

    all_steps = []
    for u in range(UPDATES):
        mixed = alpha_mix * moving + (1.0 - alpha_mix) * current
        high, low = split_two(ridge_term * mixed - goal)
        tile = kernel_tile(features, block_feats[u])
        partial_value = (
            mm(mixed.astype(bf16), tile, 1, 0) + mm(high, place[u], 1, 0) + mm(low, place[u], 1, 0)
        )
        pieces = partial_value.astype(bf16).reshape(pts_count, own_cols, block)
        summed = lax.all_to_all(pieces, "pts", 0, 0, tiled=False)
        resid = jnp.sum(summed.astype(f32), axis=0)
        at_pivot = (
            lax.broadcasted_iota(jnp.int32, (block, 1), 0) == pivot_index[u][None, :]
        ).astype(bf16)
        pivot_feats = mm(at_pivot, block_feats[u], 0, 0).astype(bf16)
        factor = kernel_tile(block_feats[u], pivot_feats)
        proj = mm(resid.astype(bf16), factor, 1, 0)
        lifted = mm(proj.astype(bf16), nystrom_core[u], 1, 1).astype(bf16)
        step_bf = (resid - mm(lifted, factor, 1, 1)).astype(bf16)
        steps = lax.all_gather(step_bf, "pts", axis=0, tiled=True)
        change = mm(steps, place[u], 1, 1)
        all_steps.append(change.astype(bf16))
        current = mixed - step_size * change
        moving = beta_keep * moving + (1.0 - beta_keep) * mixed - step_size * momentum_gain * change

    gathered = lax.all_gather(jnp.stack(all_steps), "rows", axis=1, tiled=True)
    current = coefficients
    moving = momentum
    for u in range(UPDATES):
        change = gathered[u].T.astype(f32)
        mixed = alpha_mix * moving + (1.0 - alpha_mix) * current
        current = mixed - step_size * change
        moving = beta_keep * moving + (1.0 - beta_keep) * mixed - step_size * momentum_gain * change
    return (current, moving)


def solution(mesh):
    in_specs = (P("pts", None), P("pts", None), P("pts", None), P("pts", None), P(), P(), P())
    out_specs = (P("pts", None), P("pts", None))
    return jax.shard_map(shards, mesh=mesh, in_specs=in_specs, out_specs=out_specs, check_vma=False)
```

```python
import jax
import jax.numpy as jnp
from jax import lax
from jax.sharding import PartitionSpec as P

UPDATES = 2


alpha_mix = 0.6
beta_keep = 0.9
step_size = 0.2
momentum_gain = 1.5
ridge_term = 1.0

f32 = jnp.float32
bf16 = jnp.bfloat16


def mm(a, b, ca, cb):
    return lax.dot_general(a, b, (((ca,), (cb,)), ((), ())), preferred_element_type=f32)


def kernel_tile(left_rows, right_rows):
    inner_prod = mm(left_rows, right_rows, 1, 1)
    left_sq = jnp.sum(jnp.square(left_rows.astype(f32)), axis=1)
    right_sq = jnp.sum(jnp.square(right_rows.astype(f32)), axis=1)
    squared = left_sq[:, None] + right_sq[None, :] - 2.0 * inner_prod
    return jnp.exp(squared * (-3.5 / left_rows.shape[1])).astype(bf16)


def split_two(value):
    high = value.astype(bf16)
    return high, (value - high.astype(f32)).astype(bf16)


def gather_direct(value, axis):
    count = lax.axis_size(axis)
    me = lax.axis_index(axis)
    held = [value]
    for away in range(1, count):
        held.append(lax.ppermute(value, axis, [(i, (i - away) % count) for i in range(count)]))
    twice = jnp.stack(held + held)
    return lax.dynamic_slice_in_dim(twice, (count - me) % count, count, axis=0)


def shards(features, targets, coefficients, momentum, block_index, pivot_index, nystrom_core):
    row_count = lax.axis_size("rows")
    pts_count = lax.axis_size("pts")
    row_id = lax.axis_index("rows")
    pts_id = lax.axis_index("pts")
    local_points = features.shape[0]
    block = block_index.shape[1]
    rank = pivot_index.shape[1]
    outputs = coefficients.shape[1]
    per_row = block // row_count
    per_device = per_row // pts_count
    row_cols = outputs // row_count
    own_cols = row_cols // pts_count
    first_point = pts_id * local_points
    points = lax.broadcasted_iota(jnp.int32, (local_points, 1), 0) + first_point

    place = [(points == block_index[u][None, :]).astype(bf16) for u in range(UPDATES)]

    own_rows = []
    for u in range(UPDATES):
        mine = lax.dynamic_slice_in_dim(place[u], row_id * per_row, per_row, axis=1)
        own_rows.append(mm(mine, features, 0, 0).astype(bf16).reshape(pts_count, per_device, -1))
    sent = jnp.concatenate(own_rows, axis=1)
    came = lax.all_to_all(sent, "pts", 0, 0, tiled=False)
    chunk = jnp.sum(came.astype(f32), axis=0).astype(bf16)
    over_pts = gather_direct(chunk, "pts")
    over_rows = gather_direct(over_pts, "rows")
    over_rows = over_rows.reshape(row_count, pts_count, UPDATES, per_device, features.shape[1])
    block_feats = [over_rows[:, :, u].reshape(block, features.shape[1]) for u in range(UPDATES)]

    first_col = row_id * row_cols
    current = lax.dynamic_slice_in_dim(coefficients, first_col, row_cols, axis=1).T
    moving = lax.dynamic_slice_in_dim(momentum, first_col, row_cols, axis=1).T
    goal = lax.dynamic_slice_in_dim(targets, first_col, row_cols, axis=1).T.astype(f32)

    all_steps = []
    for u in range(UPDATES):
        mixed = alpha_mix * moving + (1.0 - alpha_mix) * current
        high, low = split_two(ridge_term * mixed - goal)
        tile = kernel_tile(features, block_feats[u])
        partial_value = (
            mm(mixed.astype(bf16), tile, 1, 0) + mm(high, place[u], 1, 0) + mm(low, place[u], 1, 0)
        )
        pieces = partial_value.astype(bf16).reshape(pts_count, own_cols, block)
        summed = lax.all_to_all(pieces, "pts", 0, 0, tiled=False)
        resid = jnp.sum(summed.astype(f32), axis=0)
        at_pivot = (
            lax.broadcasted_iota(jnp.int32, (block, 1), 0) == pivot_index[u][None, :]
        ).astype(bf16)
        pivot_feats = mm(at_pivot, block_feats[u], 0, 0).astype(bf16)
        factor = kernel_tile(block_feats[u], pivot_feats)
        proj = mm(resid.astype(bf16), factor, 1, 0)
        lifted = mm(proj.astype(bf16), nystrom_core[u], 1, 1).astype(bf16)
        step_bf = (resid - mm(lifted, factor, 1, 1)).astype(bf16)
        steps = gather_direct(step_bf, "pts").reshape(row_cols, block)
        change = mm(steps, place[u], 1, 1)
        all_steps.append(change.astype(bf16))
        current = mixed - step_size * change
        moving = beta_keep * moving + (1.0 - beta_keep) * mixed - step_size * momentum_gain * change

    gathered = gather_direct(jnp.stack(all_steps), "rows")
    gathered = gathered.transpose(1, 0, 2, 3).reshape(UPDATES, outputs, local_points)
    current = coefficients
    moving = momentum
    for u in range(UPDATES):
        change = gathered[u].T.astype(f32)
        mixed = alpha_mix * moving + (1.0 - alpha_mix) * current
        current = mixed - step_size * change
        moving = beta_keep * moving + (1.0 - beta_keep) * mixed - step_size * momentum_gain * change
    return (current, moving)


def solution(mesh):
    in_specs = (P("pts", None), P("pts", None), P("pts", None), P("pts", None), P(), P(), P())
    out_specs = (P("pts", None), P("pts", None))
    return jax.shard_map(shards, mesh=mesh, in_specs=in_specs, out_specs=out_specs, check_vma=False)
```

```python
import functools
import math

import jax
import jax.numpy as jnp
from jax import lax
from jax.experimental import pallas as pl
from jax.experimental.pallas import tpu as pltpu
from jax.sharding import PartitionSpec as P

UPDATES = 2


alpha_mix = 0.6
beta_keep = 0.9
step_size = 0.2
momentum_gain = 1.5
ridge_term = 1.0

f32 = jnp.float32
bf16 = jnp.bfloat16
i32 = jnp.int32


def mm(a, b, ca, cb):
    return lax.dot_general(a, b, (((ca,), (cb,)), ((), ())), preferred_element_type=f32)


def split_two(value):
    high = value.astype(bf16)
    return high, (value - high.astype(f32)).astype(bf16)


def mixed_of(current, moving):
    return alpha_mix * moving + (1.0 - alpha_mix) * current


def stepped(current, moving, change):
    mixed = mixed_of(current, moving)
    return (
        mixed - step_size * change,
        beta_keep * moving + (1.0 - beta_keep) * mixed - step_size * momentum_gain * change,
    )


def iota(shape, axis):
    return lax.broadcasted_iota(i32, shape, axis)


def before_matrix(n):
    return jnp.where(iota((n, n), 0) < iota((n, n), 1), 1.0, 0.0).astype(bf16)


def slots_of(indices, before, points, owners, cap):
    owner = lax.div(indices, jnp.full_like(indices, points))
    marks = iota((owners, indices.shape[1]), 0) == owner
    counts = jnp.where(marks, 1.0, 0.0)
    earlier = mm(counts.astype(bf16), before, 1, 0)
    rank = jnp.sum(counts * earlier, axis=0, keepdims=True)
    return owner * cap + rank.astype(i32)


def point_rows(indices, slots, me, points, cap):
    held = iota((cap, indices.shape[1]), 0) + me * cap == slots
    local = (indices - me * points + 1).astype(f32)
    point = jnp.sum(jnp.where(held, local, 0.0), axis=1, keepdims=True).astype(i32) - 1
    return jnp.where(iota((cap, points), 1) == point, 1.0, 0.0).astype(bf16)


def pack_kernel(cap, owners, where_ref, blocks_ref, feats_ref, *outs):
    row, me = where_ref[0], where_ref[1]
    points = feats_ref.shape[0]
    before = before_matrix(blocks_ref.shape[3])
    for u, out in enumerate(outs):
        indices = blocks_ref[u, row]
        slots = slots_of(indices, before, points, owners, cap)
        rows = point_rows(indices, slots, me, points, cap)
        packed = mm(rows, feats_ref[...], 1, 0).astype(bf16)
        for o in range(owners):
            out[o] = packed


def index_kernel(cap, owners, points, where_ref, blocks_ref, slots_ref, *rows_refs):
    me = where_ref[1]
    before = before_matrix(blocks_ref.shape[3])
    for u, rows_ref in enumerate(rows_refs):
        for g in range(blocks_ref.shape[1]):
            indices = blocks_ref[u, g]
            slots = slots_of(indices, before, points, owners, cap)
            slots_ref[u, g] = slots
            rows_ref[g * cap : (g + 1) * cap, :] = point_rows(indices, slots, me, points, cap)


def compact_kernel(u, where_ref, slots_ref, got_ref, out_ref):
    owners, cap, width = got_ref.shape
    slots = slots_ref[u, where_ref[0]]
    place = jnp.where(iota((owners * cap, slots.shape[1]), 0) == slots, 1.0, 0.0).astype(bf16)
    out_ref[...] = mm(got_ref[...].reshape(owners * cap, width), place, 0, 0).astype(bf16)


def tile_of(left, left_norm, right_t, right_norm):
    scale = 7.0 / left.shape[1] * math.log2(math.e)
    return jnp.exp2(mm(left, right_t, 1, 0) * scale - left_norm - right_norm).astype(bf16)


def scaled_norm(rows, axis):
    width = rows.shape[axis]
    return jnp.sum(jnp.square(rows.astype(f32)), axis=axis, keepdims=True) * (
        3.5 / width * math.log2(math.e)
    )


def partial_kernel(u, where_ref, blocks_ref, feats_ref, b0, b1, b2, b3, w_ref, z_ref, t_ref, *rest):
    *done, out_ref, part_ref, coef_ref = rest
    row, me = where_ref[0], where_ref[1]
    points = feats_ref.shape[0]
    groups, count = blocks_ref.shape[1], blocks_ref.shape[3]
    current, moving = w_ref[...], z_ref[...]
    if done:
        current, moving = stepped(current, moving, dense_steps(done[0][...], done[1][...]))
    mixed = mixed_of(current, moving)
    high, low = split_two(ridge_term * mixed - t_ref[...])
    cols = mixed.shape[0]
    coef_ref[0:cols] = mixed.astype(bf16)
    coef_ref[cols : 2 * cols] = high
    coef_ref[2 * cols : 3 * cols] = low
    chunk = 256
    for k, b_ref in enumerate((b0, b1, b2, b3)):
        group = lax.bitwise_xor(row, k)
        right = b_ref[...]
        right_norm = scaled_norm(right, 0)
        local = blocks_ref[u, group] - me * points
        total = jnp.zeros((cols, count), f32)
        for c in range(0, points, chunk):
            left = feats_ref[c : c + chunk, :]
            tile = tile_of(left, scaled_norm(left, 1), right, right_norm)
            place = jnp.where(iota((chunk, count), 0) + c == local, 1.0, 0.0).astype(bf16)
            total += mm(coef_ref[0:cols, c : c + chunk], tile, 1, 0)
            offset = mm(coef_ref[cols : 3 * cols, c : c + chunk], place, 1, 0)
            total += offset[:cols] + offset[cols:]
        half = groups // 2
        start = pl.multiple_of(lax.rem(group, half) * count, count)
        part_ref[lax.div(group, half), :, pl.ds(start, count)] = total
    own = cols // out_ref.shape[0]
    for o in range(out_ref.shape[0]):
        both = jnp.concatenate([part_ref[h, o * own : (o + 1) * own, :] for h in range(2)], axis=0)
        out_ref[o] = both.astype(bf16)


def dense_steps(got, rows):
    sources, double, lanes = got.shape
    own = double // 2
    wide = got.astype(f32)
    total = None
    for h in range(2):
        packed = wide[:, h * own : (h + 1) * own, :].reshape(sources * own, lanes).astype(bf16)
        part = mm(packed, rows[h * lanes : (h + 1) * lanes, :], 1, 0)
        total = part if total is None else total + part
    return total


def factor_kernel(where_ref, pivots_ref, b0, b1, b2, b3, out_ref):
    row = where_ref[0]
    count = b0.shape[1]
    pivots = pivots_ref[...]
    feats = jnp.zeros((b0.shape[0], pivots.shape[1]), f32)
    blocks = (b0, b1, b2, b3)
    for k, b_ref in enumerate(blocks):
        first = lax.bitwise_xor(row, k) * count
        chosen = iota((count, pivots.shape[1]), 0) + first == pivots
        feats += mm(b_ref[...], jnp.where(chosen, 1.0, 0.0).astype(bf16), 1, 0)
    left = feats.T
    left_norm = scaled_norm(left, 1)
    left = left.astype(bf16)
    for k, b_ref in enumerate(blocks):
        right = b_ref[...]
        start = pl.multiple_of(lax.bitwise_xor(row, k) * count, count)
        out_ref[:, pl.ds(start, count)] = tile_of(left, left_norm, right, scaled_norm(right, 0))


def chain_kernel(u, cap, got_ref, factor_ref, core_ref, slots_ref, out_ref):
    owners = got_ref.shape[0]
    groups, count = slots_ref.shape[1], slots_ref.shape[3]
    summed = got_ref[0].astype(f32)
    for o in range(1, owners):
        summed += got_ref[o].astype(f32)
    own = summed.shape[0] // 2
    resid = jnp.concatenate([summed[:own], summed[own:]], axis=1)
    factor = factor_ref[...]
    proj = mm(resid.astype(bf16), factor, 1, 1)
    lifted = mm(proj.astype(bf16), core_ref[...], 1, 1).astype(bf16)
    step = (resid - mm(lifted, factor, 1, 0)).astype(bf16)
    packed = []
    for g in range(groups):
        place = iota((owners * cap, count), 0) == slots_ref[u, g]
        packed.append(
            mm(step[:, g * count : (g + 1) * count], jnp.where(place, 1.0, 0.0).astype(bf16), 1, 1)
        )
    half = groups // 2
    for o in range(owners):
        lanes = [x[:, o * cap : (o + 1) * cap] for x in packed]
        both = jnp.concatenate(
            [jnp.concatenate(lanes[h * half : (h + 1) * half], axis=1) for h in range(2)], axis=0
        ).astype(bf16)
        for copy in range(out_ref.shape[0] // owners):
            out_ref[copy * owners + o] = both


def finish_kernel(
    where_ref, w_ref, z_ref, s0, s1, s2, s3, last_ref, rows0_ref, rows1_ref, wo_ref, zo_ref, dense_ref
):
    row = where_ref[0]
    cols = s0.shape[0] * s0.shape[1] // 2
    for k, s_ref in enumerate((s0, s1, s2, s3)):
        start = pl.multiple_of(lax.bitwise_xor(row, k) * cols, cols)
        dense_ref[pl.ds(start, cols), :] = dense_steps(s_ref[...], rows0_ref[...])
    current, moving = stepped(w_ref[...], z_ref[...], dense_ref[...].T)
    current, moving = stepped(current, moving, dense_steps(last_ref[...], rows1_ref[...]).T)
    wo_ref[...] = current
    zo_ref[...] = moving


VMEM = pl.BlockSpec(memory_space=pltpu.VMEM)
SMEM = pl.BlockSpec(memory_space=pltpu.SMEM)


def call(body, outs, *args, scratch=(), flops=0):
    out_bytes = sum(math.prod(o.shape) * o.dtype.itemsize for o in outs)
    in_bytes = sum(math.prod(a.shape) * a.dtype.itemsize for a in args)
    return pl.pallas_call(
        body,
        out_shape=outs,
        in_specs=[SMEM if a.ndim == 1 else VMEM for a in args],
        out_specs=[VMEM] * len(outs),
        scratch_shapes=list(scratch),
        compiler_params=pltpu.CompilerParams(vmem_limit_bytes=40 * 2**20),
        cost_estimate=pl.CostEstimate(
            flops=int(flops), bytes_accessed=in_bytes + out_bytes, transcendentals=0
        ),
    )(*args)


def like(shape, dtype=bf16):
    return jax.ShapeDtypeStruct(shape, dtype)


def swap_rows(value, k):
    count = lax.axis_size("rows")
    return lax.ppermute(value, "rows", [(i, i ^ k) for i in range(count)])


def with_kernels(features, current, moving, goal, coefficients, momentum, block_index, pivot_index, core):
    rows, owners = lax.axis_size("rows"), lax.axis_size("pts")
    points, width = features.shape
    block = block_index.shape[1]
    rank = pivot_index.shape[1]
    outputs = coefficients.shape[1]
    count = block // rows
    cap = 3 * count // owners
    cols = outputs // rows
    own = cols // owners
    where = jnp.stack([lax.axis_index("rows"), lax.axis_index("pts")]).astype(i32)
    blocks = block_index.reshape(UPDATES, rows, 1, count)
    flops = 2.0 * points * block * (width + 3 * cols)

    packed = call(
        functools.partial(pack_kernel, cap, owners),
        [like((owners, cap, width))] * UPDATES,
        where,
        blocks,
        features,
    )
    came = [lax.all_to_all(packed[u], "pts", 0, 0, tiled=True) for u in range(UPDATES)]
    slots, *place = call(
        functools.partial(index_kernel, cap, owners, points),
        [like((UPDATES, rows, 1, count), i32)] + [like((rows * cap, points))] * UPDATES,
        where,
        blocks,
    )
    feats = []
    for u in range(UPDATES):
        (mine,) = call(
            functools.partial(compact_kernel, u), [like((width, count))], where, slots, came[u]
        )
        feats.append([mine] + [swap_rows(mine, k) for k in range(1, rows)])

    half = rows // 2
    done = []
    for u in range(UPDATES):
        (pieces,) = call(
            functools.partial(partial_kernel, u),
            [like((owners, 2 * own, half * count))],
            where,
            blocks,
            features,
            *feats[u],
            current,
            moving,
            goal,
            *done,
            scratch=[pltpu.VMEM((2, cols, half * count), f32), pltpu.VMEM((3 * cols, points), bf16)],
            flops=flops,
        )
        summed = lax.all_to_all(pieces, "pts", 0, 0, tiled=True)
        (factor,) = call(
            factor_kernel,
            [like((rank, block))],
            where,
            pivot_index[u][None, :],
            *feats[u],
            flops=2.0 * rank * block * (2 * width),
        )
        last = u == UPDATES - 1
        copies = owners * (rows if last else 1)
        (steps,) = call(
            functools.partial(chain_kernel, u, cap),
            [like((copies, 2 * own, half * cap))],
            summed,
            factor,
            core[u],
            slots,
        )
        if last:
            final = lax.all_to_all(steps, ("rows", "pts"), 0, 0, tiled=True)
        else:
            got = lax.all_to_all(steps, "pts", 0, 0, tiled=True)
            done = [got, place[u]]
            first = [got] + [swap_rows(got, k) for k in range(1, rows)]

    return call(
        finish_kernel,
        [like(coefficients.shape, f32)] * 2,
        where,
        coefficients,
        momentum,
        *first,
        final,
        *place,
        scratch=[pltpu.VMEM((outputs, points), f32)],
    )


def kernel_tile(left_rows, right_rows):
    inner_prod = mm(left_rows, right_rows, 1, 1)
    left_sq = jnp.sum(jnp.square(left_rows.astype(f32)), axis=1)
    right_sq = jnp.sum(jnp.square(right_rows.astype(f32)), axis=1)
    squared = left_sq[:, None] + right_sq[None, :] - 2.0 * inner_prod
    return jnp.exp(squared * (-3.5 / left_rows.shape[1])).astype(bf16)


def with_operations(features, current, moving, goal, coefficients, momentum, block_index, pivot_index, core):
    row_count, pts_count = lax.axis_size("rows"), lax.axis_size("pts")
    row_id, pts_id = lax.axis_index("rows"), lax.axis_index("pts")
    points = features.shape[0]
    block = block_index.shape[1]
    outputs = coefficients.shape[1]
    per_row = block // row_count
    per_device = per_row // pts_count
    row_cols = outputs // row_count
    own_cols = row_cols // pts_count
    ids = iota((points, 1), 0) + pts_id * points
    place = [(ids == block_index[u][None, :]).astype(bf16) for u in range(UPDATES)]
    own_rows = []
    for u in range(UPDATES):
        mine = lax.dynamic_slice_in_dim(place[u], row_id * per_row, per_row, axis=1)
        own_rows.append(mm(mine, features, 0, 0).astype(bf16).reshape(pts_count, per_device, -1))
    came = lax.all_to_all(jnp.concatenate(own_rows, axis=1), "pts", 0, 0, tiled=False)
    chunk = jnp.sum(came.astype(f32), axis=0).astype(bf16)
    spread = lax.all_gather(lax.all_gather(chunk, "pts", axis=0), "rows", axis=0)
    spread = spread.reshape(row_count, pts_count, UPDATES, per_device, features.shape[1])
    all_steps = []
    for u in range(UPDATES):
        block_feats = spread[:, :, u].reshape(block, features.shape[1])
        mixed = mixed_of(current, moving)
        high, low = split_two(ridge_term * mixed - goal)
        tile = kernel_tile(features, block_feats)
        partial_value = (
            mm(mixed.astype(bf16), tile, 1, 0) + mm(high, place[u], 1, 0) + mm(low, place[u], 1, 0)
        )
        pieces = partial_value.astype(bf16).reshape(pts_count, own_cols, block)
        summed = lax.all_to_all(pieces, "pts", 0, 0, tiled=False)
        resid = jnp.sum(summed.astype(f32), axis=0)
        at_pivot = (iota((block, 1), 0) == pivot_index[u][None, :]).astype(bf16)
        factor = kernel_tile(block_feats, mm(at_pivot, block_feats, 0, 0).astype(bf16))
        proj = mm(resid.astype(bf16), factor, 1, 0)
        lifted = mm(proj.astype(bf16), core[u], 1, 1).astype(bf16)
        step_bf = (resid - mm(lifted, factor, 1, 1)).astype(bf16)
        steps = lax.all_gather(step_bf, "pts", axis=0, tiled=True)
        change = mm(steps, place[u], 1, 1)
        all_steps.append(change.astype(bf16))
        current, moving = stepped(current, moving, change)
    gathered = lax.all_gather(jnp.stack(all_steps), "rows", axis=1, tiled=True)
    current, moving = coefficients, momentum
    for u in range(UPDATES):
        current, moving = stepped(current, moving, gathered[u].T.astype(f32))
    return (current, moving)


def shards(features, targets, coefficients, momentum, block_index, pivot_index, nystrom_core):
    rows, owners = lax.axis_size("rows"), lax.axis_size("pts")
    outputs = coefficients.shape[1]
    cols = outputs // rows
    count = block_index.shape[1] // rows
    first = lax.axis_index("rows") * cols

    def own_columns(value):
        return lax.dynamic_slice_in_dim(value, first, cols, axis=1).T.astype(f32)

    fits = rows == 4 and cols == 8 * owners and count % 128 == 0 and (3 * count // owners) % 64 == 0
    plan = with_kernels if fits else with_operations
    current, moving = plan(
        features,
        own_columns(coefficients),
        own_columns(momentum),
        own_columns(targets),
        coefficients,
        momentum,
        block_index,
        pivot_index,
        nystrom_core,
    )
    return (current, moving)


def solution(mesh):
    in_specs = (P("pts", None), P("pts", None), P("pts", None), P("pts", None), P(), P(), P())
    out_specs = (P("pts", None), P("pts", None))
    return jax.shard_map(shards, mesh=mesh, in_specs=in_specs, out_specs=out_specs, check_vma=False)
```

```python
import functools
import math

import jax
import jax.numpy as jnp
from jax import lax
from jax.experimental import pallas as pl
from jax.experimental.pallas import tpu as pltpu
from jax.sharding import PartitionSpec as P

UPDATES = 2


alpha_mix = 0.6
beta_keep = 0.9
step_size = 0.2
momentum_gain = 1.5
ridge_term = 1.0

f32 = jnp.float32
bf16 = jnp.bfloat16
i32 = jnp.int32


def mm(a, b, ca, cb):
    return lax.dot_general(a, b, (((ca,), (cb,)), ((), ())), preferred_element_type=f32)


def split_two(value):
    high = value.astype(bf16)
    return high, (value - high.astype(f32)).astype(bf16)


def mixed_of(current, moving):
    return alpha_mix * moving + (1.0 - alpha_mix) * current


mix_per_step = alpha_mix * step_size * momentum_gain + (1.0 - alpha_mix) * step_size


def stepped(current, moving, change):
    mixed = mixed_of(current, moving)
    if change is None:
        return mixed, beta_keep * moving + (1.0 - beta_keep) * mixed
    return (
        mixed - step_size * change,
        beta_keep * moving + (1.0 - beta_keep) * mixed - step_size * momentum_gain * change,
    )


def iota(shape, axis):
    return lax.broadcasted_iota(i32, shape, axis)


def before_matrix(n):
    return jnp.where(iota((n, n), 0) < iota((n, n), 1), 1.0, 0.0).astype(bf16)


def slots_of(indices, before, points, owners, cap):
    owner = lax.div(indices, jnp.full_like(indices, points))
    marks = iota((owners, indices.shape[1]), 0) == owner
    counts = jnp.where(marks, 1.0, 0.0)
    earlier = mm(counts.astype(bf16), before, 1, 0)
    rank = jnp.sum(counts * earlier, axis=0, keepdims=True)
    return owner * cap + rank.astype(i32)


def point_rows(indices, slots, me, points, cap):
    held = iota((cap, indices.shape[1]), 0) + me * cap == slots
    local = (indices - me * points + 1).astype(f32)
    point = jnp.sum(jnp.where(held, local, 0.0), axis=1, keepdims=True).astype(i32) - 1
    return jnp.where(iota((cap, points), 1) == point, 1.0, 0.0).astype(bf16)


def pack_kernel(cap, owners, where_ref, blocks_ref, feats_ref, *outs):
    row, me = where_ref[0], where_ref[1]
    points = feats_ref.shape[0]
    before = before_matrix(blocks_ref.shape[3])
    for u, out in enumerate(outs):
        indices = blocks_ref[u, row]
        slots = slots_of(indices, before, points, owners, cap)
        rows = point_rows(indices, slots, me, points, cap)
        packed = mm(rows, feats_ref[...], 1, 0).astype(bf16)
        for o in range(owners):
            out[o] = packed


def index_kernel(cap, owners, points, where_ref, blocks_ref, slots_ref, *rows_refs):
    me = where_ref[1]
    before = before_matrix(blocks_ref.shape[3])
    for u, rows_ref in enumerate(rows_refs):
        for g in range(blocks_ref.shape[1]):
            indices = blocks_ref[u, g]
            slots = slots_of(indices, before, points, owners, cap)
            slots_ref[u, g] = slots
            rows_ref[g * cap : (g + 1) * cap, :] = point_rows(indices, slots, me, points, cap)


def prepare_kernel(w_ref, z_ref, t_ref, coef_ref, base_ref, goal_ref):
    current, moving = w_ref[...], z_ref[...]
    mixed = mixed_of(current, moving)
    goal = t_ref[...].astype(f32)
    base_ref[...] = mixed_of(*stepped(current, moving, None)).T
    goal_ref[...] = goal.T
    put_coefficients(coef_ref, mixed.T, goal.T)


def put_coefficients(coef_ref, mixed, goal):
    cols = mixed.shape[0]
    high, low = split_two(ridge_term * mixed - goal)
    coef_ref[0:cols] = mixed.astype(bf16)
    coef_ref[cols : 2 * cols] = high
    coef_ref[2 * cols : 3 * cols] = low


def scaled_norm(rows, axis):
    scale = 3.5 / rows.shape[axis] * math.log2(math.e)
    return jnp.sum(jnp.square(rows.astype(f32)), axis=axis, keepdims=True) * scale


def tile_of(left, left_norm, right_t, right_norm):
    scale = 7.0 / left.shape[1] * math.log2(math.e)
    return jnp.exp2(mm(left, right_t, 1, 0) * scale - left_norm - right_norm).astype(bf16)


def tile_kernel(u, where_ref, slots_ref, got_ref, feats_ref, block_ref, tile_ref):
    owners, cap, width = got_ref.shape
    slots = slots_ref[u, where_ref[0]]
    place = jnp.where(iota((owners * cap, slots.shape[1]), 0) == slots, 1.0, 0.0).astype(bf16)
    block = mm(got_ref[...].reshape(owners * cap, width), place, 0, 0)
    block_norm = scaled_norm(block, 0)
    block = block.astype(bf16)
    block_ref[...] = block
    chunk = 256
    for c in range(0, feats_ref.shape[0], chunk):
        left = feats_ref[c : c + chunk, :]
        tile_ref[c : c + chunk, :] = tile_of(left, scaled_norm(left, 1), block, block_norm)


def product_kernel(u, where_ref, blocks_ref, tile_ref, *rest):
    *given, out_ref, coef_ref = rest
    row, me = where_ref[0], where_ref[1]
    points, count = tile_ref.shape
    if len(given) == 1:
        coef_ref = given[0]
    else:
        base_ref, goal_ref, got_ref, rows_ref = given
        change = dense_steps(got_ref[...], rows_ref[...])
        put_coefficients(coef_ref, base_ref[...] - mix_per_step * change, goal_ref[...])
    cols = coef_ref.shape[0] // 3
    local = blocks_ref[u, row] - me * points
    place = jnp.where(iota((points, count), 0) == local, 1.0, 0.0).astype(bf16)
    total = mm(coef_ref[0:cols], tile_ref[...], 1, 0)
    total += mm(coef_ref[cols : 2 * cols], place, 1, 0) + mm(coef_ref[2 * cols :], place, 1, 0)
    pieces, double, lanes = out_ref.shape
    own = double // 2
    for d in range(pieces):
        part = total[d * own : (d + 1) * own]
        out_ref[d] = jnp.concatenate([part[:, :lanes], part[:, lanes:]], axis=0).astype(bf16)


def dense_steps(got, rows):
    sources, double, lanes = got.shape
    own = double // 2
    wide = got.astype(f32)
    total = None
    for h in range(2):
        packed = wide[:, h * own : (h + 1) * own, :].reshape(sources * own, lanes).astype(bf16)
        part = mm(packed, rows[h * lanes : (h + 1) * lanes, :], 1, 0)
        total = part if total is None else total + part
    return total


def factor_kernel(u, where_ref, pivots_ref, b0, b1, b2, b3, out_ref):
    row = where_ref[0]
    count = b0.shape[1]
    pivots = pivots_ref[u]
    feats = jnp.zeros((b0.shape[0], pivots.shape[1]), f32)
    blocks = (b0, b1, b2, b3)
    for k, b_ref in enumerate(blocks):
        first = lax.bitwise_xor(row, k) * count
        chosen = iota((count, pivots.shape[1]), 0) + first == pivots
        feats += mm(b_ref[...], jnp.where(chosen, 1.0, 0.0).astype(bf16), 1, 0)
    left = feats.T
    left_norm = scaled_norm(left, 1)
    left = left.astype(bf16)
    for k, b_ref in enumerate(blocks):
        right = b_ref[...]
        start = pl.multiple_of(lax.bitwise_xor(row, k) * count, count)
        out_ref[:, pl.ds(start, count)] = tile_of(left, left_norm, right, scaled_norm(right, 0))


def chain_kernel(u, cap, owners, got_ref, factor_ref, core_ref, slots_ref, out_ref):
    groups, count = slots_ref.shape[1], slots_ref.shape[3]
    own = got_ref.shape[1] // 2
    sums = []
    for g in range(groups):
        summed = got_ref[g * owners].astype(f32)
        for o in range(1, owners):
            summed += got_ref[g * owners + o].astype(f32)
        sums += [summed[:own], summed[own:]]
    resid = jnp.concatenate(sums, axis=1)
    factor = factor_ref[...]
    proj = mm(resid.astype(bf16), factor, 1, 1)
    lifted = mm(proj.astype(bf16), core_ref[u], 1, 1).astype(bf16)
    step = (resid - mm(lifted, factor, 1, 0)).astype(bf16)
    packed = []
    for g in range(groups):
        place = iota((owners * cap, count), 0) == slots_ref[u, g]
        packed.append(
            mm(step[:, g * count : (g + 1) * count], jnp.where(place, 1.0, 0.0).astype(bf16), 1, 1)
        )
    half = groups // 2
    for o in range(owners):
        lanes = [x[:, o * cap : (o + 1) * cap] for x in packed]
        both = jnp.concatenate(
            [jnp.concatenate(lanes[h * half : (h + 1) * half], axis=1) for h in range(2)], axis=0
        ).astype(bf16)
        for copy in range(out_ref.shape[0] // owners):
            out_ref[copy * owners + o] = both


def middle_kernel(w_ref, z_ref, got_ref, rows_ref, mixed_ref, kept_ref):
    change = dense_steps(got_ref[...], rows_ref[...]).T
    state = stepped(w_ref[...], z_ref[...], change)
    mixed_ref[...], kept_ref[...] = stepped(*state, None)


def finish_kernel(mixed_ref, kept_ref, got_ref, rows_ref, w_ref, z_ref):
    change = dense_steps(got_ref[...], rows_ref[...]).T
    w_ref[...] = mixed_ref[...] - step_size * change
    z_ref[...] = kept_ref[...] - step_size * momentum_gain * change


VMEM = pl.BlockSpec(memory_space=pltpu.VMEM)
SMEM = pl.BlockSpec(memory_space=pltpu.SMEM)


def call(body, outs, *args, scratch=(), flops=0):
    out_bytes = sum(math.prod(o.shape) * o.dtype.itemsize for o in outs)
    in_bytes = sum(math.prod(a.shape) * a.dtype.itemsize for a in args)
    return pl.pallas_call(
        body,
        out_shape=outs,
        in_specs=[SMEM if a.ndim == 1 else VMEM for a in args],
        out_specs=[VMEM] * len(outs),
        scratch_shapes=list(scratch),
        compiler_params=pltpu.CompilerParams(vmem_limit_bytes=40 * 2**20),
        cost_estimate=pl.CostEstimate(
            flops=int(flops), bytes_accessed=in_bytes + out_bytes, transcendentals=0
        ),
    )(*args)


def like(shape, dtype=bf16):
    return jax.ShapeDtypeStruct(shape, dtype)


def swap_rows(value, k):
    count = lax.axis_size("rows")
    return lax.ppermute(value, "rows", [(i, i ^ k) for i in range(count)])


def with_kernels(features, targets, coefficients, momentum, block_index, pivot_index, core):
    rows, owners = lax.axis_size("rows"), lax.axis_size("pts")
    points, width = features.shape
    block = block_index.shape[1]
    rank = pivot_index.shape[1]
    outputs = coefficients.shape[1]
    count = block // rows
    cap = 3 * count // owners
    own = outputs // rows // owners
    half = rows // 2
    where = jnp.stack([lax.axis_index("rows"), lax.axis_index("pts")]).astype(i32)
    blocks = block_index.reshape(UPDATES, rows, 1, count)
    pivots = pivot_index.reshape(UPDATES, 1, rank)

    packed = call(
        functools.partial(pack_kernel, cap, owners),
        [like((owners, cap, width))] * UPDATES,
        where,
        blocks,
        features,
    )
    came = [lax.all_to_all(packed[u], "pts", 0, 0, tiled=True) for u in range(UPDATES)]
    slots, *place = call(
        functools.partial(index_kernel, cap, owners, points),
        [like((UPDATES, rows, 1, count), i32)] + [like((rows * cap, points))] * UPDATES,
        where,
        blocks,
    )
    coef, base, goal = call(
        prepare_kernel,
        [like((3 * outputs, points)), like((outputs, points), f32), like((outputs, points), f32)],
        coefficients,
        momentum,
        targets,
    )
    tiles, feats = [], []
    for u in range(UPDATES):
        mine, tile = call(
            functools.partial(tile_kernel, u),
            [like((width, count)), like((points, count))],
            where,
            slots,
            came[u],
            features,
            flops=2.0 * points * count * width,
        )
        tiles.append(tile)
        feats.append([mine] + [swap_rows(mine, k) for k in range(1, rows)])

    given = [coef]
    for u in range(UPDATES):
        (pieces,) = call(
            functools.partial(product_kernel, u),
            [like((rows * owners, 2 * own, count // 2))],
            where,
            blocks,
            tiles[u],
            *given,
            scratch=[pltpu.VMEM(coef.shape, bf16)],
            flops=2.0 * points * count * 3 * outputs,
        )
        summed = lax.all_to_all(pieces, ("rows", "pts"), 0, 0, tiled=True)
        (factor,) = call(
            functools.partial(factor_kernel, u),
            [like((rank, block))],
            where,
            pivots,
            *feats[u],
            flops=2.0 * rank * block * (2 * width),
        )
        (steps,) = call(
            functools.partial(chain_kernel, u, cap, owners),
            [like((rows * owners, 2 * own, half * cap))],
            summed,
            factor,
            core,
            slots,
        )
        got = lax.all_to_all(steps, ("rows", "pts"), 0, 0, tiled=True)
        if u + 1 < UPDATES:
            given = [base, goal, got, place[u]]
            mixed, kept = call(
                middle_kernel,
                [like(coefficients.shape, f32)] * 2,
                coefficients,
                momentum,
                got,
                place[u],
            )
    return call(
        finish_kernel, [like(coefficients.shape, f32)] * 2, mixed, kept, got, place[UPDATES - 1]
    )


def kernel_tile(left_rows, right_rows):
    inner_prod = mm(left_rows, right_rows, 1, 1)
    left_sq = jnp.sum(jnp.square(left_rows.astype(f32)), axis=1)
    right_sq = jnp.sum(jnp.square(right_rows.astype(f32)), axis=1)
    squared = left_sq[:, None] + right_sq[None, :] - 2.0 * inner_prod
    return jnp.exp(squared * (-3.5 / left_rows.shape[1])).astype(bf16)


def with_operations(features, targets, coefficients, momentum, block_index, pivot_index, core):
    row_count, pts_count = lax.axis_size("rows"), lax.axis_size("pts")
    row_id, pts_id = lax.axis_index("rows"), lax.axis_index("pts")
    points = features.shape[0]
    block = block_index.shape[1]
    outputs = coefficients.shape[1]
    per_row = block // row_count
    per_device = per_row // pts_count
    row_cols = outputs // row_count
    own_cols = row_cols // pts_count
    first = row_id * row_cols
    current, moving, goal = (
        lax.dynamic_slice_in_dim(value, first, row_cols, axis=1).T.astype(f32)
        for value in (coefficients, momentum, targets)
    )
    ids = iota((points, 1), 0) + pts_id * points
    place = [(ids == block_index[u][None, :]).astype(bf16) for u in range(UPDATES)]
    own_rows = []
    for u in range(UPDATES):
        mine = lax.dynamic_slice_in_dim(place[u], row_id * per_row, per_row, axis=1)
        own_rows.append(mm(mine, features, 0, 0).astype(bf16).reshape(pts_count, per_device, -1))
    came = lax.all_to_all(jnp.concatenate(own_rows, axis=1), "pts", 0, 0, tiled=False)
    chunk = jnp.sum(came.astype(f32), axis=0).astype(bf16)
    spread = lax.all_gather(lax.all_gather(chunk, "pts", axis=0), "rows", axis=0)
    spread = spread.reshape(row_count, pts_count, UPDATES, per_device, features.shape[1])
    all_steps = []
    for u in range(UPDATES):
        block_feats = spread[:, :, u].reshape(block, features.shape[1])
        mixed = mixed_of(current, moving)
        high, low = split_two(ridge_term * mixed - goal)
        tile = kernel_tile(features, block_feats)
        partial_value = (
            mm(mixed.astype(bf16), tile, 1, 0) + mm(high, place[u], 1, 0) + mm(low, place[u], 1, 0)
        )
        pieces = partial_value.astype(bf16).reshape(pts_count, own_cols, block)
        summed = lax.all_to_all(pieces, "pts", 0, 0, tiled=False)
        resid = jnp.sum(summed.astype(f32), axis=0)
        at_pivot = (iota((block, 1), 0) == pivot_index[u][None, :]).astype(bf16)
        factor = kernel_tile(block_feats, mm(at_pivot, block_feats, 0, 0).astype(bf16))
        proj = mm(resid.astype(bf16), factor, 1, 0)
        lifted = mm(proj.astype(bf16), core[u], 1, 1).astype(bf16)
        step_bf = (resid - mm(lifted, factor, 1, 1)).astype(bf16)
        steps = lax.all_gather(step_bf, "pts", axis=0, tiled=True)
        change = mm(steps, place[u], 1, 1)
        all_steps.append(change.astype(bf16))
        current, moving = stepped(current, moving, change)
    gathered = lax.all_gather(jnp.stack(all_steps), "rows", axis=1, tiled=True)
    current, moving = coefficients, momentum
    for u in range(UPDATES):
        current, moving = stepped(current, moving, gathered[u].T.astype(f32))
    return (current, moving)


def shards(features, targets, coefficients, momentum, block_index, pivot_index, nystrom_core):
    rows, owners = lax.axis_size("rows"), lax.axis_size("pts")
    count = block_index.shape[1] // rows
    fits = rows == 4 and coefficients.shape[1] == 8 * rows * owners
    fits = fits and count % 256 == 0 and (3 * count // owners) % 64 == 0 and UPDATES == 2
    plan = with_kernels if fits else with_operations
    return plan(
        features, targets, coefficients, momentum, block_index, pivot_index, nystrom_core
    )


def solution(mesh):
    in_specs = (P("pts", None), P("pts", None), P("pts", None), P("pts", None), P(), P(), P())
    out_specs = (P("pts", None), P("pts", None))
    return jax.shard_map(shards, mesh=mesh, in_specs=in_specs, out_specs=out_specs, check_vma=False)
```

```python
import functools
import math

import jax
import jax.numpy as jnp
from jax import lax
from jax.experimental import pallas as pl
from jax.experimental.pallas import tpu as pltpu
from jax.sharding import PartitionSpec as P

UPDATES = 2


alpha_mix = 0.6
beta_keep = 0.9
step_size = 0.2
momentum_gain = 1.5
ridge_term = 1.0

f32 = jnp.float32
bf16 = jnp.bfloat16
i32 = jnp.int32


def mm(a, b, ca, cb):
    return lax.dot_general(a, b, (((ca,), (cb,)), ((), ())), preferred_element_type=f32)


def split_two(value):
    high = value.astype(bf16)
    return high, (value - high.astype(f32)).astype(bf16)


def mixed_of(current, moving):
    return alpha_mix * moving + (1.0 - alpha_mix) * current


mix_per_step = alpha_mix * step_size * momentum_gain + (1.0 - alpha_mix) * step_size


def stepped(current, moving, change):
    mixed = mixed_of(current, moving)
    if change is None:
        return mixed, beta_keep * moving + (1.0 - beta_keep) * mixed
    return (
        mixed - step_size * change,
        beta_keep * moving + (1.0 - beta_keep) * mixed - step_size * momentum_gain * change,
    )


def iota(shape, axis):
    return lax.broadcasted_iota(i32, shape, axis)


def one_hot(chosen):
    return jnp.where(chosen, 1.0, 0.0).astype(bf16)


def before_matrix(n):
    return one_hot(iota((n, n), 0) < iota((n, n), 1))


def slots_of(indices, before, points, owners, cap):
    owner = lax.div(indices, jnp.full_like(indices, points))
    marks = iota((owners, indices.shape[1]), 0) == owner
    counts = jnp.where(marks, 1.0, 0.0)
    earlier = mm(counts.astype(bf16), before, 1, 0)
    rank = jnp.sum(counts * earlier, axis=0, keepdims=True)
    return owner * cap + rank.astype(i32)


def point_rows(indices, slots, me, points, cap):
    held = iota((cap, indices.shape[1]), 0) + me * cap == slots
    local = (indices - me * points + 1).astype(f32)
    point = jnp.sum(jnp.where(held, local, 0.0), axis=1, keepdims=True).astype(i32) - 1
    return one_hot(iota((cap, points), 1) == point)


def start_all(pairs, sems):
    copies = [pltpu.make_async_copy(a, b, sems.at[n]) for n, (a, b) in enumerate(pairs)]
    for copy in copies:
        copy.start()
    return copies


def wait_all(copies):
    for copy in copies:
        copy.wait()


def group_row(blocks, u, group, count):
    return blocks[u : u + 1, pl.ds(pl.multiple_of(group * count, count), count)]


def pack_kernel(count, cap, blocks_hbm, feats_hbm, out_hbm, blocks, feats, packed, sems):
    row, me = lax.axis_index("rows"), lax.axis_index("pts")
    points, owners = feats.shape[0], out_hbm.shape[0]
    reads = start_all([(blocks_hbm, blocks), (feats_hbm, feats)], sems)
    before = before_matrix(count)
    reads[0].wait()
    rows = []
    for u in range(UPDATES):
        indices = group_row(blocks, u, row, count)
        slots = slots_of(indices, before, points, owners, cap)
        rows.append(point_rows(indices, slots, me, points, cap))
    reads[1].wait()
    for u in range(UPDATES):
        packed[u * cap : (u + 1) * cap, :] = mm(rows[u], feats[...], 1, 0).astype(bf16)
    wait_all(start_all([(packed, out_hbm.at[o]) for o in range(owners)], sems))


def coefficients_of(mixed, goal):
    high, low = split_two(ridge_term * mixed - goal)
    return mixed.astype(bf16), high, low


def prepare_kernel(
    count, cap, owners,
    blocks_hbm, w_hbm, z_hbm, t_hbm, coef_hbm, rows_hbm, slots_hbm,
    blocks, w, z, t, coef, rows, slots, sems,
):
    me = lax.axis_index("pts")
    points, outputs = w.shape
    reads = start_all([(blocks_hbm, blocks), (w_hbm, w), (z_hbm, z), (t_hbm, t)], sems)
    before = before_matrix(count)
    reads[0].wait()
    groups = blocks.shape[1] // count
    for u in range(UPDATES):
        for g in range(groups):
            indices = blocks[u : u + 1, g * count : (g + 1) * count]
            held = slots_of(indices, before, points, owners, cap)
            n = u * groups + g
            slots[n : n + 1, :] = held
            rows[u, g * cap : (g + 1) * cap, :] = point_rows(indices, held, me, points, cap)
    wait_all(reads[1:])
    current, moving = w[...], z[...]
    goal = t[...].astype(f32).T
    for u in range(UPDATES):
        mixed = mixed_of(current, moving).T
        for n, part in enumerate(coefficients_of(mixed, goal)):
            coef[u, n * outputs : (n + 1) * outputs, :] = part
        current, moving = stepped(current, moving, None)
    wait_all(start_all([(coef, coef_hbm), (rows, rows_hbm), (slots, slots_hbm)], sems))


def scaled_norm(rows, axis):
    scale = 3.5 / rows.shape[axis] * math.log2(math.e)
    return jnp.sum(jnp.square(rows.astype(f32)), axis=axis, keepdims=True) * scale


def tile_of(left, left_norm, right_t, right_norm):
    scale = 7.0 / left.shape[1] * math.log2(math.e)
    return jnp.exp2(mm(left, right_t, 1, 0) * scale - left_norm - right_norm)


CHUNK = 256


def sums_kernel(
    cap,
    came, blocks_hbm, feats_hbm, coef_hbm, block_hbm, pieces_hbm,
    blocks, feats, coef, block, tile, place, pieces, sems,
):
    row, me = lax.axis_index("rows"), lax.axis_index("pts")
    owners, _, width = came.shape
    points, count = tile.shape
    outputs = coef.shape[1] // 3
    reads = start_all([(blocks_hbm, blocks), (feats_hbm, feats), (coef_hbm, coef)], sems)
    before = before_matrix(count)
    reads[0].wait()
    for u in range(UPDATES):
        indices = group_row(blocks, u, row, count)
        slots = slots_of(indices, before, points, owners, cap)
        chosen = one_hot(iota((owners * cap, count), 0) == slots)
        packed = came[:, u * cap : (u + 1) * cap, :].reshape(owners * cap, width)
        block[u] = mm(packed, chosen, 0, 0).astype(bf16)
    reads[1].wait()
    writes = [pltpu.make_async_copy(block, block_hbm, sems.at[0])]
    writes[0].start()
    for u in range(UPDATES):
        right = block[u]
        right_norm = scaled_norm(right, 0)
        local = group_row(blocks, u, row, count) - me * points
        for c in range(0, points, CHUNK):
            left = feats[c : c + CHUNK, :]
            tile[c : c + CHUNK, :] = tile_of(left, scaled_norm(left, 1), right, right_norm).astype(bf16)
            place[c : c + CHUNK, :] = one_hot(iota((CHUNK, count), 0) + c == local)
        if u == 0:
            reads[2].wait()
        total = mm(coef[u, 0:outputs], tile[...], 1, 0)
        total += mm(coef[u, outputs : 2 * outputs], place[...], 1, 0)
        total += mm(coef[u, 2 * outputs :], place[...], 1, 0)
        devices, _, lanes = pieces.shape
        own = outputs // devices
        for d in range(devices):
            part = total[d * own : (d + 1) * own]
            pieces[d, 2 * own * u : 2 * own * (u + 1), :] = jnp.concatenate(
                [part[:, :lanes], part[:, lanes:]], axis=0
            ).astype(bf16)
    writes.append(pltpu.make_async_copy(pieces, pieces_hbm, sems.at[1]))
    writes[1].start()
    wait_all(writes)


def factors_kernel(
    b0_hbm, b1_hbm, b2_hbm, b3_hbm, blocks_hbm, pivots_hbm, factor_hbm, cross_hbm,
    feats, blocks, pivots, factor, cross, sems,
):
    row = lax.axis_index("rows")
    groups, _, width, count = feats.shape
    pairs = [(b_hbm, feats.at[k]) for k, b_hbm in enumerate((b0_hbm, b1_hbm, b2_hbm, b3_hbm))]
    wait_all(start_all(pairs + [(blocks_hbm, blocks), (pivots_hbm, pivots)], sems))
    places = [lax.bitwise_xor(row, k) for k in range(groups)]
    for u in range(UPDATES):
        chosen_feats = jnp.zeros((width, pivots.shape[1]), f32)
        for k in range(groups):
            chosen = iota((count, pivots.shape[1]), 0) + places[k] * count == pivots[u : u + 1, :]
            chosen_feats += mm(feats[k, u], one_hot(chosen), 1, 0)
        left = chosen_feats.T
        left_norm = scaled_norm(left, 1)
        left = left.astype(bf16)
        for k in range(groups):
            right = feats[k, u]
            start = pl.multiple_of(places[k] * count, count)
            factor[u, :, pl.ds(start, count)] = tile_of(
                left, left_norm, right, scaled_norm(right, 0)
            ).astype(bf16)
    writes = start_all([(factor, factor_hbm)], sems)
    sent = 1
    for k in range(groups):
        left = feats[k, 0].astype(f32).T
        left_norm = scaled_norm(left, 1)
        left = left.astype(bf16)
        left_points = group_row(blocks, 0, places[k], count).astype(f32)
        left_points = jnp.broadcast_to(left_points, (8, count)).T[:, 0:1]
        for m in range(groups):
            right = feats[m, 1]
            right_norm = scaled_norm(right, 0)
            right_points = group_row(blocks, 1, places[m], count).astype(f32)
            for c in range(0, count, CHUNK):
                rows = slice(c, c + CHUNK)
                value = tile_of(left[rows], left_norm[rows], right, right_norm)
                same = jnp.where(left_points[rows] == right_points, ridge_term, 0.0)
                cross[m, k, rows, :] = (value.astype(bf16).astype(f32) + same).astype(bf16)
            start = pl.multiple_of(places[k] * count, count)
            copy = pltpu.make_async_copy(
                cross.at[m, k], cross_hbm.at[places[m], pl.ds(start, count), :], sems.at[sent]
            )
            copy.start()
            writes.append(copy)
            sent += 1
    wait_all(writes)


def chain_kernel(
    cap, owners,
    summed, factor_hbm, core_hbm, cross_hbm, slots_hbm, out_hbm,
    factor, core, cross, slots, packed, sems,
):
    groups, _, count = cross.shape
    own = summed.shape[1] // (2 * UPDATES)
    pairs = []
    for u in range(UPDATES):
        pairs += [(factor_hbm.at[u], factor.at[u]), (core_hbm.at[u], core.at[u])]
        if u == 0:
            pairs += [(slots_hbm, slots)]
            pairs += [(cross_hbm.at[g], cross.at[g]) for g in range(groups)]
    reads = start_all(pairs, sems)
    step = None
    for u in range(UPDATES):
        sums = []
        for g in range(groups):
            part = summed[g * owners, 2 * own * u : 2 * own * (u + 1), :].astype(f32)
            for o in range(1, owners):
                part += summed[g * owners + o, 2 * own * u : 2 * own * (u + 1), :].astype(f32)
            part = jnp.concatenate([part[:own], part[own:]], axis=1)
            if u:
                reads[3 + g].wait()
                part -= mix_per_step * mm(step, cross[g], 1, 0)
            sums.append(part)
        resid = jnp.concatenate(sums, axis=1)
        wait_all(reads[0:3] if u == 0 else reads[3 + groups :])
        proj = mm(resid.astype(bf16), factor[u], 1, 1)
        lifted = mm(proj.astype(bf16), core[u], 1, 1).astype(bf16)
        step = (resid - mm(lifted, factor[u], 1, 0)).astype(bf16)
        parts = []
        for g in range(groups):
            n = u * groups + g
            place = one_hot(iota((owners * cap, count), 0) == slots[n : n + 1, :])
            parts.append(mm(step[:, g * count : (g + 1) * count], place, 1, 1))
        half = groups // 2
        for o in range(owners):
            lanes = [x[:, o * cap : (o + 1) * cap] for x in parts]
            packed[o, 2 * own * u : 2 * own * (u + 1), :] = jnp.concatenate(
                [jnp.concatenate(lanes[h * half : (h + 1) * half], axis=1) for h in range(2)], axis=0
            ).astype(bf16)
    copies = out_hbm.shape[0] // owners
    wait_all(
        start_all([(packed, out_hbm.at[pl.ds(n * owners, owners)]) for n in range(copies)], sems)
    )


def finish_kernel(
    got, w_hbm, z_hbm, rows_hbm, w_out, z_out, w, z, rows, steps, w_new, z_new, sems, out_sems
):
    points = w.shape[0]
    sources, deep, lanes = got.shape
    own = deep // (2 * UPDATES)
    chunks = range(0, points, CHUNK)
    pairs = []
    for c in chunks:
        part = slice(c, c + CHUNK)
        pairs += [(rows_hbm.at[:, :, part], rows.at[:, :, part])]
        pairs += [(w_hbm.at[part], w.at[part]), (z_hbm.at[part], z.at[part])]
    reads = start_all(pairs, sems)
    wide = got[...].astype(f32)
    for u in range(UPDATES):
        for h in range(2):
            first = own * (2 * u + h)
            part = wide[:, first : first + own, :].reshape(sources * own, lanes)
            steps[u, :, h * lanes : (h + 1) * lanes] = part.astype(bf16)
    writes = []
    for n, c in enumerate(chunks):
        part = slice(c, c + CHUNK)
        wait_all(reads[3 * n : 3 * n + 3])
        current, moving = w[part, :], z[part, :]
        for u in range(UPDATES):
            change = mm(steps[u], rows[u, :, part], 1, 0).T
            current, moving = stepped(current, moving, change)
        w_new[part, :] = current
        z_new[part, :] = moving
        for m, (a, b) in enumerate(((w_new, w_out), (z_new, z_out))):
            copy = pltpu.make_async_copy(a.at[part], b.at[part], out_sems.at[2 * n + m])
            copy.start()
            writes.append(copy)
    wait_all(writes)


VMEM = pl.BlockSpec(memory_space=pltpu.VMEM)
HBM = pl.BlockSpec(memory_space=pltpu.HBM)


def like(shape, dtype=bf16):
    return jax.ShapeDtypeStruct(shape, dtype)


def call(body, outs, inside, *args, near=0, sems=(), flops=0):
    moved = sum(math.prod(o.shape) * o.dtype.itemsize for o in [*outs, *args])
    return pl.pallas_call(
        body,
        out_shape=outs,
        in_specs=[VMEM] * near + [HBM] * (len(args) - near),
        out_specs=[HBM] * len(outs),
        scratch_shapes=[pltpu.VMEM(x.shape, x.dtype) for x in inside]
        + [pltpu.SemaphoreType.DMA((n,)) for n in sems],
        compiler_params=pltpu.CompilerParams(vmem_limit_bytes=48 * 2**20),
        cost_estimate=pl.CostEstimate(flops=int(flops), bytes_accessed=moved, transcendentals=0),
    )(*args)


def swap_rows(value, k):
    count = lax.axis_size("rows")
    return lax.ppermute(value, "rows", [(i, i ^ k) for i in range(count)])


def with_kernels(features, targets, coefficients, momentum, block_index, pivot_index, core):
    rows, owners = lax.axis_size("rows"), lax.axis_size("pts")
    points, width = features.shape
    block = block_index.shape[1]
    rank = pivot_index.shape[1]
    outputs = coefficients.shape[1]
    count = block // rows
    cap = 3 * count // owners
    devices = rows * owners
    own = outputs // devices
    deep = 2 * own * UPDATES
    half = rows // 2
    wide = like(coefficients.shape, f32)

    (packed,) = call(
        functools.partial(pack_kernel, count, cap),
        [like((owners, UPDATES * cap, width))],
        [block_index, features, like((UPDATES * cap, width))],
        block_index,
        features,
        sems=(owners,),
    )
    came = lax.all_to_all(packed, "pts", 0, 0, tiled=True)
    kept = [
        like((UPDATES, 3 * outputs, points)),
        like((UPDATES, rows * cap, points)),
        like((UPDATES * rows, count), i32),
    ]
    coef, place, slots = call(
        functools.partial(prepare_kernel, count, cap, owners),
        kept,
        [block_index, coefficients, momentum, targets, *kept],
        block_index,
        coefficients,
        momentum,
        targets,
        sems=(4,),
    )
    feats = like((UPDATES, width, count))
    pieces = like((devices, deep, count // 2))
    tile = like((points, count))
    mine, pieces = call(
        functools.partial(sums_kernel, cap),
        [feats, pieces],
        [block_index, features, coef, feats, tile, tile, pieces],
        came,
        block_index,
        features,
        coef,
        near=1,
        sems=(3,),
        flops=2.0 * UPDATES * points * count * (width + 3 * outputs),
    )
    summed = lax.all_to_all(pieces, ("rows", "pts"), 0, 0, tiled=True)
    beside, across = swap_rows(mine, 1), swap_rows(mine, 2)
    kept = [like((UPDATES, rank, block)), like((rows, block, count))]
    factor, cross = call(
        factors_kernel,
        kept,
        [
            like((rows, *feats.shape)),
            block_index,
            pivot_index,
            kept[0],
            like((rows, rows, count, count)),
        ],
        mine,
        beside,
        across,
        swap_rows(across, 1),
        block_index,
        pivot_index,
        sems=(rows * rows + 1,),
        flops=2.0 * width * block * (UPDATES * rank + block),
    )
    (steps,) = call(
        functools.partial(chain_kernel, cap, owners),
        [like((devices, deep, half * cap))],
        [factor, core, cross, slots, like((owners, deep, half * cap))],
        summed,
        factor,
        core,
        cross,
        slots,
        near=1,
        sems=(2 * UPDATES + 1 + rows,),
    )
    got = lax.all_to_all(steps, ("rows", "pts"), 0, 0, tiled=True)
    parts = points // CHUNK
    return call(
        finish_kernel,
        [wide] * 2,
        [wide, wide, place, like((UPDATES, outputs, rows * cap)), wide, wide],
        got,
        coefficients,
        momentum,
        place,
        near=1,
        sems=(3 * parts, 2 * parts),
    )


def kernel_tile(left_rows, right_rows):
    inner_prod = mm(left_rows, right_rows, 1, 1)
    left_sq = jnp.sum(jnp.square(left_rows.astype(f32)), axis=1)
    right_sq = jnp.sum(jnp.square(right_rows.astype(f32)), axis=1)
    squared = left_sq[:, None] + right_sq[None, :] - 2.0 * inner_prod
    return jnp.exp(squared * (-3.5 / left_rows.shape[1])).astype(bf16)


def with_operations(features, targets, coefficients, momentum, block_index, pivot_index, core):
    row_count, pts_count = lax.axis_size("rows"), lax.axis_size("pts")
    row_id, pts_id = lax.axis_index("rows"), lax.axis_index("pts")
    points = features.shape[0]
    block = block_index.shape[1]
    outputs = coefficients.shape[1]
    per_row = block // row_count
    per_device = per_row // pts_count
    row_cols = outputs // row_count
    own_cols = row_cols // pts_count
    first = row_id * row_cols
    current, moving, goal = (
        lax.dynamic_slice_in_dim(value, first, row_cols, axis=1).T.astype(f32)
        for value in (coefficients, momentum, targets)
    )
    ids = iota((points, 1), 0) + pts_id * points
    place = [(ids == block_index[u][None, :]).astype(bf16) for u in range(UPDATES)]
    own_rows = []
    for u in range(UPDATES):
        mine = lax.dynamic_slice_in_dim(place[u], row_id * per_row, per_row, axis=1)
        own_rows.append(mm(mine, features, 0, 0).astype(bf16).reshape(pts_count, per_device, -1))
    came = lax.all_to_all(jnp.concatenate(own_rows, axis=1), "pts", 0, 0, tiled=False)
    chunk = jnp.sum(came.astype(f32), axis=0).astype(bf16)
    spread = lax.all_gather(lax.all_gather(chunk, "pts", axis=0), "rows", axis=0)
    spread = spread.reshape(row_count, pts_count, UPDATES, per_device, features.shape[1])
    all_steps = []
    for u in range(UPDATES):
        block_feats = spread[:, :, u].reshape(block, features.shape[1])
        mixed = mixed_of(current, moving)
        high, low = split_two(ridge_term * mixed - goal)
        tile = kernel_tile(features, block_feats)
        partial_value = (
            mm(mixed.astype(bf16), tile, 1, 0) + mm(high, place[u], 1, 0) + mm(low, place[u], 1, 0)
        )
        pieces = partial_value.astype(bf16).reshape(pts_count, own_cols, block)
        summed = lax.all_to_all(pieces, "pts", 0, 0, tiled=False)
        resid = jnp.sum(summed.astype(f32), axis=0)
        at_pivot = (iota((block, 1), 0) == pivot_index[u][None, :]).astype(bf16)
        factor = kernel_tile(block_feats, mm(at_pivot, block_feats, 0, 0).astype(bf16))
        proj = mm(resid.astype(bf16), factor, 1, 0)
        lifted = mm(proj.astype(bf16), core[u], 1, 1).astype(bf16)
        step_bf = (resid - mm(lifted, factor, 1, 1)).astype(bf16)
        steps = lax.all_gather(step_bf, "pts", axis=0, tiled=True)
        change = mm(steps, place[u], 1, 1)
        all_steps.append(change.astype(bf16))
        current, moving = stepped(current, moving, change)
    gathered = lax.all_gather(jnp.stack(all_steps), "rows", axis=1, tiled=True)
    current, moving = coefficients, momentum
    for u in range(UPDATES):
        current, moving = stepped(current, moving, gathered[u].T.astype(f32))
    return (current, moving)


def shards(features, targets, coefficients, momentum, block_index, pivot_index, nystrom_core):
    rows, owners = lax.axis_size("rows"), lax.axis_size("pts")
    count = block_index.shape[1] // rows
    fits = rows == 4 and coefficients.shape[1] == 8 * rows * owners
    fits = fits and coefficients.shape[0] % CHUNK == 0 and count % CHUNK == 0 and (3 * count // owners) % 64 == 0
    plan = with_kernels if fits else with_operations
    return plan(
        features, targets, coefficients, momentum, block_index, pivot_index, nystrom_core
    )


def solution(mesh):
    in_specs = (P("pts", None), P("pts", None), P("pts", None), P("pts", None), P(), P(), P())
    out_specs = (P("pts", None), P("pts", None))
    return jax.shard_map(shards, mesh=mesh, in_specs=in_specs, out_specs=out_specs, check_vma=False)
```

```python
import functools
import math

import jax
import jax.numpy as jnp
from jax import lax
from jax.experimental import pallas as pl
from jax.experimental.pallas import tpu as pltpu
from jax.sharding import PartitionSpec as P

UPDATES = 2


alpha_mix = 0.6
beta_keep = 0.9
step_size = 0.2
momentum_gain = 1.5
ridge_term = 1.0

f32 = jnp.float32
bf16 = jnp.bfloat16
i32 = jnp.int32


def mm(a, b, ca, cb):
    return lax.dot_general(a, b, (((ca,), (cb,)), ((), ())), preferred_element_type=f32)


def split_two(value):
    high = value.astype(bf16)
    return high, (value - high.astype(f32)).astype(bf16)


def mixed_of(current, moving):
    return alpha_mix * moving + (1.0 - alpha_mix) * current


mix_per_step = alpha_mix * step_size * momentum_gain + (1.0 - alpha_mix) * step_size


def stepped(current, moving, change):
    mixed = mixed_of(current, moving)
    if change is None:
        return mixed, beta_keep * moving + (1.0 - beta_keep) * mixed
    return (
        mixed - step_size * change,
        beta_keep * moving + (1.0 - beta_keep) * mixed - step_size * momentum_gain * change,
    )


def iota(shape, axis):
    return lax.broadcasted_iota(i32, shape, axis)


def one_hot(chosen):
    return jnp.where(chosen, 1.0, 0.0).astype(bf16)


def before_matrix(n):
    return one_hot(iota((n, n), 0) < iota((n, n), 1))


def slots_of(indices, before, points, owners, cap):
    owner = lax.div(indices, jnp.full_like(indices, points))
    marks = iota((owners, indices.shape[1]), 0) == owner
    counts = jnp.where(marks, 1.0, 0.0)
    earlier = mm(counts.astype(bf16), before, 1, 0)
    rank = jnp.sum(counts * earlier, axis=0, keepdims=True)
    return owner * cap + rank.astype(i32)


def point_rows(indices, slots, me, points, cap):
    held = iota((cap, indices.shape[1]), 0) + me * cap == slots
    local = (indices - me * points + 1).astype(f32)
    point = jnp.sum(jnp.where(held, local, 0.0), axis=1, keepdims=True).astype(i32) - 1
    return one_hot(iota((cap, points), 1) == point)


def start_all(pairs, sems):
    copies = [pltpu.make_async_copy(a, b, sems.at[n]) for n, (a, b) in enumerate(pairs)]
    for copy in copies:
        copy.start()
    return copies


def wait_all(copies):
    for copy in copies:
        copy.wait()


def group_row(blocks, u, group, count):
    return blocks[u : u + 1, pl.ds(pl.multiple_of(group * count, count), count)]


def pack_kernel(count, cap, blocks_hbm, feats_hbm, out_hbm, blocks, feats, packed, sems):
    row, me = lax.axis_index("rows"), lax.axis_index("pts")
    points, owners = feats.shape[0], out_hbm.shape[0]
    reads = start_all([(blocks_hbm, blocks), (feats_hbm, feats)], sems)
    before = before_matrix(count)
    reads[0].wait()
    rows = []
    for u in range(UPDATES):
        indices = group_row(blocks, u, row, count)
        slots = slots_of(indices, before, points, owners, cap)
        rows.append(point_rows(indices, slots, me, points, cap))
    reads[1].wait()
    for u in range(UPDATES):
        packed[u * cap : (u + 1) * cap, :] = mm(rows[u], feats[...], 1, 0).astype(bf16)
    wait_all(start_all([(packed, out_hbm.at[o]) for o in range(owners)], sems))


def coefficients_of(mixed, goal):
    high, low = split_two(ridge_term * mixed - goal)
    return mixed.astype(bf16), high, low


def prepare_kernel(
    count, cap, owners,
    blocks_hbm, w_hbm, z_hbm, t_hbm, coef_hbm, rows_hbm, slots_hbm,
    blocks, w, z, t, coef, rows, slots, sems,
):
    me = lax.axis_index("pts")
    points, outputs = w.shape
    reads = start_all([(blocks_hbm, blocks), (w_hbm, w), (z_hbm, z), (t_hbm, t)], sems)
    before = before_matrix(count)
    reads[0].wait()
    groups = blocks.shape[1] // count
    for u in range(UPDATES):
        for g in range(groups):
            indices = blocks[u : u + 1, g * count : (g + 1) * count]
            held = slots_of(indices, before, points, owners, cap)
            n = u * groups + g
            slots[n : n + 1, :] = held
            rows[u, g * cap : (g + 1) * cap, :] = point_rows(indices, held, me, points, cap)
    wait_all(reads[1:])
    current, moving = w[...], z[...]
    goal = t[...].astype(f32).T
    for u in range(UPDATES):
        mixed = mixed_of(current, moving).T
        for n, part in enumerate(coefficients_of(mixed, goal)):
            coef[u, n * outputs : (n + 1) * outputs, :] = part
        current, moving = stepped(current, moving, None)
    wait_all(start_all([(coef, coef_hbm), (rows, rows_hbm), (slots, slots_hbm)], sems))


def extended(rows, axis, first):
    rest = -0.5 * jnp.sum(jnp.square(rows.astype(f32)), axis=axis, keepdims=True)
    parts = []
    for _ in range(3):
        parts.append(rest.astype(bf16).astype(f32))
        rest = rest - parts[-1]
    parts = parts + [1.0] * 3 if first else [1.0] * 3 + parts
    at = iota(rows.shape, axis)
    extra = jnp.zeros(rows.shape, f32)
    for n, part in enumerate(parts):
        extra = jnp.where(at == n, part, extra)
    return jnp.concatenate([rows.astype(bf16), extra.astype(bf16)], axis=axis)


def exponent(left, right):
    return mm(left, right, 1, 0) * (7.0 / (left.shape[1] // 2) * math.log2(math.e))


CHUNK = 256


def compact_kernel(cap, points, came, blocks_hbm, block_hbm, blocks, block, sems):
    row = lax.axis_index("rows")
    owners, _, width = came.shape
    count = block.shape[2]
    wait_all(start_all([(blocks_hbm, blocks)], sems))
    before = before_matrix(count)
    for u in range(UPDATES):
        slots = slots_of(group_row(blocks, u, row, count), before, points, owners, cap)
        chosen = one_hot(iota((owners * cap, count), 0) == slots)
        packed = came[:, u * cap : (u + 1) * cap, :].reshape(owners * cap, width)
        block[u] = mm(packed, chosen, 0, 0).astype(bf16)
    wait_all(start_all([(block, block_hbm)], sems))


def sums_kernel(
    blocks_hbm, block_hbm, feats_hbm, coef_hbm, pieces_hbm,
    blocks, block, feats, coef, tile, place, pieces, sems,
):
    row, me = lax.axis_index("rows"), lax.axis_index("pts")
    points, count = tile.shape
    outputs = coef.shape[1] // 3
    pairs = [(blocks_hbm, blocks), (block_hbm, block), (feats_hbm, feats), (coef_hbm, coef)]
    reads = start_all(pairs, sems)
    wait_all(reads[:3])
    left = extended(feats[...], 1, True)
    for u in range(UPDATES):
        right = extended(block[u], 0, False)
        local = group_row(blocks, u, row, count) - me * points
        for c in range(0, points, CHUNK):
            tile[c : c + CHUNK, :] = jnp.exp2(exponent(left[c : c + CHUNK], right)).astype(bf16)
            place[c : c + CHUNK, :] = one_hot(iota((CHUNK, count), 0) + c == local)
        if u == 0:
            reads[3].wait()
        total = mm(coef[u, 0:outputs], tile[...], 1, 0)
        total += mm(coef[u, outputs : 2 * outputs], place[...], 1, 0)
        total += mm(coef[u, 2 * outputs :], place[...], 1, 0)
        devices, _, lanes = pieces.shape
        own = outputs // devices
        for d in range(devices):
            part = total[d * own : (d + 1) * own]
            pieces[d, 2 * own * u : 2 * own * (u + 1), :] = jnp.concatenate(
                [part[:, :lanes], part[:, lanes:]], axis=0
            ).astype(bf16)
    wait_all(start_all([(pieces, pieces_hbm)], sems))


def factors_kernel(
    b0_hbm, b1_hbm, b2_hbm, b3_hbm, blocks_hbm, pivots_hbm, factor_hbm, cross_hbm,
    feats, blocks, pivots, factor, cross, sems,
):
    row = lax.axis_index("rows")
    groups, _, width, count = feats.shape
    pairs = [(b_hbm, feats.at[k]) for k, b_hbm in enumerate((b0_hbm, b1_hbm, b2_hbm, b3_hbm))]
    wait_all(start_all(pairs + [(blocks_hbm, blocks), (pivots_hbm, pivots)], sems))
    places = [lax.bitwise_xor(row, k) for k in range(groups)]
    rights = [[extended(feats[k, u], 0, False) for k in range(groups)] for u in range(UPDATES)]
    for u in range(UPDATES):
        chosen_feats = jnp.zeros((width, pivots.shape[1]), f32)
        for k in range(groups):
            chosen = iota((count, pivots.shape[1]), 0) + places[k] * count == pivots[u : u + 1, :]
            chosen_feats += mm(feats[k, u], one_hot(chosen), 1, 0)
        left = extended(chosen_feats.T, 1, True)
        for k in range(groups):
            start = pl.multiple_of(places[k] * count, count)
            value = jnp.exp2(exponent(left, rights[u][k]))
            factor[u, :, pl.ds(start, count)] = value.astype(bf16)
    writes = start_all([(factor, factor_hbm)], sems)
    sent = 1
    for k in range(groups):
        left = extended(feats[k, 0].astype(f32).T, 1, True)
        left_points = group_row(blocks, 0, places[k], count).astype(f32)
        left_points = jnp.broadcast_to(left_points, (8, count)).T[:, 0:1]
        for m in range(groups):
            right_points = group_row(blocks, 1, places[m], count).astype(f32)
            for c in range(0, count, CHUNK):
                rows = slice(c, c + CHUNK)
                power = exponent(left[rows], rights[1][m])
                power = jnp.where(left_points[rows] == right_points, math.log2(1.0 + ridge_term), power)
                cross[m, k, rows, :] = jnp.exp2(power).astype(bf16)
            start = pl.multiple_of(places[k] * count, count)
            copy = pltpu.make_async_copy(
                cross.at[m, k], cross_hbm.at[places[m], pl.ds(start, count), :], sems.at[sent]
            )
            copy.start()
            writes.append(copy)
            sent += 1
    wait_all(writes)


def chain_kernel(
    cap, owners,
    summed, factor_hbm, core_hbm, cross_hbm, slots_hbm, out_hbm,
    factor, core, cross, slots, packed, sems,
):
    groups, _, count = cross.shape
    own = summed.shape[1] // (2 * UPDATES)
    pairs = []
    for u in range(UPDATES):
        pairs += [(factor_hbm.at[u], factor.at[u]), (core_hbm.at[u], core.at[u])]
        if u == 0:
            pairs += [(slots_hbm, slots)]
            pairs += [(cross_hbm.at[g], cross.at[g]) for g in range(groups)]
    reads = start_all(pairs, sems)
    step = None
    for u in range(UPDATES):
        sums = []
        for g in range(groups):
            part = summed[g * owners, 2 * own * u : 2 * own * (u + 1), :].astype(f32)
            for o in range(1, owners):
                part += summed[g * owners + o, 2 * own * u : 2 * own * (u + 1), :].astype(f32)
            part = jnp.concatenate([part[:own], part[own:]], axis=1)
            if u:
                reads[3 + g].wait()
                part -= mix_per_step * mm(step, cross[g], 1, 0)
            sums.append(part)
        resid = jnp.concatenate(sums, axis=1)
        wait_all(reads[0:3] if u == 0 else reads[3 + groups :])
        proj = mm(resid.astype(bf16), factor[u], 1, 1)
        lifted = mm(proj.astype(bf16), core[u], 1, 1).astype(bf16)
        step = (resid - mm(lifted, factor[u], 1, 0)).astype(bf16)
        parts = []
        for g in range(groups):
            n = u * groups + g
            place = one_hot(iota((owners * cap, count), 0) == slots[n : n + 1, :])
            parts.append(mm(step[:, g * count : (g + 1) * count], place, 1, 1))
        half = groups // 2
        for o in range(owners):
            lanes = [x[:, o * cap : (o + 1) * cap] for x in parts]
            packed[o, 2 * own * u : 2 * own * (u + 1), :] = jnp.concatenate(
                [jnp.concatenate(lanes[h * half : (h + 1) * half], axis=1) for h in range(2)], axis=0
            ).astype(bf16)
    copies = out_hbm.shape[0] // owners
    wait_all(
        start_all([(packed, out_hbm.at[pl.ds(n * owners, owners)]) for n in range(copies)], sems)
    )


def finish_kernel(
    got, w_hbm, z_hbm, rows_hbm, w_out, z_out, w, z, rows, steps, w_new, z_new, sems, out_sems
):
    points = w.shape[0]
    sources, deep, lanes = got.shape
    own = deep // (2 * UPDATES)
    chunks = range(0, points, CHUNK)
    pairs = []
    for c in chunks:
        part = slice(c, c + CHUNK)
        pairs += [(rows_hbm.at[:, :, part], rows.at[:, :, part])]
        pairs += [(w_hbm.at[part], w.at[part]), (z_hbm.at[part], z.at[part])]
    reads = start_all(pairs, sems)
    wide = got[...].astype(f32)
    for u in range(UPDATES):
        for h in range(2):
            first = own * (2 * u + h)
            part = wide[:, first : first + own, :].reshape(sources * own, lanes)
            steps[u, :, h * lanes : (h + 1) * lanes] = part.astype(bf16)
    writes = []
    for n, c in enumerate(chunks):
        part = slice(c, c + CHUNK)
        wait_all(reads[3 * n : 3 * n + 3])
        current, moving = w[part, :], z[part, :]
        for u in range(UPDATES):
            change = mm(steps[u], rows[u, :, part], 1, 0).T
            current, moving = stepped(current, moving, change)
        w_new[part, :] = current
        z_new[part, :] = moving
        for m, (a, b) in enumerate(((w_new, w_out), (z_new, z_out))):
            copy = pltpu.make_async_copy(a.at[part], b.at[part], out_sems.at[2 * n + m])
            copy.start()
            writes.append(copy)
    wait_all(writes)


VMEM = pl.BlockSpec(memory_space=pltpu.VMEM)
HBM = pl.BlockSpec(memory_space=pltpu.HBM)


def like(shape, dtype=bf16):
    return jax.ShapeDtypeStruct(shape, dtype)


def call(body, outs, inside, *args, near=0, sems=(), flops=0):
    moved = sum(math.prod(o.shape) * o.dtype.itemsize for o in [*outs, *args])
    return pl.pallas_call(
        body,
        out_shape=outs,
        in_specs=[VMEM] * near + [HBM] * (len(args) - near),
        out_specs=[HBM] * len(outs),
        scratch_shapes=[pltpu.VMEM(x.shape, x.dtype) for x in inside]
        + [pltpu.SemaphoreType.DMA((n,)) for n in sems],
        compiler_params=pltpu.CompilerParams(vmem_limit_bytes=62 * 2**20),
        cost_estimate=pl.CostEstimate(flops=int(flops), bytes_accessed=moved, transcendentals=0),
    )(*args)


def swap_rows(value, k):
    count = lax.axis_size("rows")
    return lax.ppermute(value, "rows", [(i, i ^ k) for i in range(count)])


def with_kernels(features, targets, coefficients, momentum, block_index, pivot_index, core):
    rows, owners = lax.axis_size("rows"), lax.axis_size("pts")
    points, width = features.shape
    block = block_index.shape[1]
    rank = pivot_index.shape[1]
    outputs = coefficients.shape[1]
    count = block // rows
    cap = 3 * count // owners
    devices = rows * owners
    own = outputs // devices
    deep = 2 * own * UPDATES
    half = rows // 2
    wide = like(coefficients.shape, f32)

    (packed,) = call(
        functools.partial(pack_kernel, count, cap),
        [like((owners, UPDATES * cap, width))],
        [block_index, features, like((UPDATES * cap, width))],
        block_index,
        features,
        sems=(owners,),
    )
    came = lax.all_to_all(packed, "pts", 0, 0, tiled=True)
    kept = [
        like((UPDATES, 3 * outputs, points)),
        like((UPDATES, rows * cap, points)),
        like((UPDATES * rows, count), i32),
    ]
    coef, place, slots = call(
        functools.partial(prepare_kernel, count, cap, owners),
        kept,
        [block_index, coefficients, momentum, targets, *kept],
        block_index,
        coefficients,
        momentum,
        targets,
        sems=(4,),
    )
    feats = like((UPDATES, width, count))
    pieces = like((devices, deep, count // 2))
    tile = like((points, count))
    (mine,) = call(
        functools.partial(compact_kernel, cap, points),
        [feats],
        [block_index, feats],
        came,
        block_index,
        near=1,
        sems=(1,),
    )
    beside, across = swap_rows(mine, 1), swap_rows(mine, 2)
    (pieces,) = call(
        sums_kernel,
        [pieces],
        [block_index, feats, features, coef, tile, tile, pieces],
        block_index,
        mine,
        features,
        coef,
        sems=(4,),
        flops=2.0 * UPDATES * points * count * (width + 3 * outputs),
    )
    summed = lax.all_to_all(pieces, ("rows", "pts"), 0, 0, tiled=True)
    kept = [like((UPDATES, rank, block)), like((rows, block, count))]
    factor, cross = call(
        factors_kernel,
        kept,
        [
            like((rows, *feats.shape)),
            block_index,
            pivot_index,
            kept[0],
            like((rows, rows, count, count)),
        ],
        mine,
        beside,
        across,
        swap_rows(across, 1),
        block_index,
        pivot_index,
        sems=(rows * rows + 1,),
        flops=2.0 * width * block * (UPDATES * rank + block),
    )
    (steps,) = call(
        functools.partial(chain_kernel, cap, owners),
        [like((devices, deep, half * cap))],
        [factor, core, cross, slots, like((owners, deep, half * cap))],
        summed,
        factor,
        core,
        cross,
        slots,
        near=1,
        sems=(2 * UPDATES + 1 + rows,),
    )
    got = lax.all_to_all(steps, ("rows", "pts"), 0, 0, tiled=True)
    parts = points // CHUNK
    return call(
        finish_kernel,
        [wide] * 2,
        [wide, wide, place, like((UPDATES, outputs, rows * cap)), wide, wide],
        got,
        coefficients,
        momentum,
        place,
        near=1,
        sems=(3 * parts, 2 * parts),
    )


def kernel_tile(left_rows, right_rows):
    inner_prod = mm(left_rows, right_rows, 1, 1)
    left_sq = jnp.sum(jnp.square(left_rows.astype(f32)), axis=1)
    right_sq = jnp.sum(jnp.square(right_rows.astype(f32)), axis=1)
    squared = left_sq[:, None] + right_sq[None, :] - 2.0 * inner_prod
    return jnp.exp(squared * (-3.5 / left_rows.shape[1])).astype(bf16)


def with_operations(features, targets, coefficients, momentum, block_index, pivot_index, core):
    row_count, pts_count = lax.axis_size("rows"), lax.axis_size("pts")
    row_id, pts_id = lax.axis_index("rows"), lax.axis_index("pts")
    points = features.shape[0]
    block = block_index.shape[1]
    outputs = coefficients.shape[1]
    per_row = block // row_count
    per_device = per_row // pts_count
    row_cols = outputs // row_count
    own_cols = row_cols // pts_count
    first = row_id * row_cols
    current, moving, goal = (
        lax.dynamic_slice_in_dim(value, first, row_cols, axis=1).T.astype(f32)
        for value in (coefficients, momentum, targets)
    )
    ids = iota((points, 1), 0) + pts_id * points
    place = [(ids == block_index[u][None, :]).astype(bf16) for u in range(UPDATES)]
    own_rows = []
    for u in range(UPDATES):
        mine = lax.dynamic_slice_in_dim(place[u], row_id * per_row, per_row, axis=1)
        own_rows.append(mm(mine, features, 0, 0).astype(bf16).reshape(pts_count, per_device, -1))
    came = lax.all_to_all(jnp.concatenate(own_rows, axis=1), "pts", 0, 0, tiled=False)
    chunk = jnp.sum(came.astype(f32), axis=0).astype(bf16)
    spread = lax.all_gather(lax.all_gather(chunk, "pts", axis=0), "rows", axis=0)
    spread = spread.reshape(row_count, pts_count, UPDATES, per_device, features.shape[1])
    all_steps = []
    for u in range(UPDATES):
        block_feats = spread[:, :, u].reshape(block, features.shape[1])
        mixed = mixed_of(current, moving)
        high, low = split_two(ridge_term * mixed - goal)
        tile = kernel_tile(features, block_feats)
        partial_value = (
            mm(mixed.astype(bf16), tile, 1, 0) + mm(high, place[u], 1, 0) + mm(low, place[u], 1, 0)
        )
        pieces = partial_value.astype(bf16).reshape(pts_count, own_cols, block)
        summed = lax.all_to_all(pieces, "pts", 0, 0, tiled=False)
        resid = jnp.sum(summed.astype(f32), axis=0)
        at_pivot = (iota((block, 1), 0) == pivot_index[u][None, :]).astype(bf16)
        factor = kernel_tile(block_feats, mm(at_pivot, block_feats, 0, 0).astype(bf16))
        proj = mm(resid.astype(bf16), factor, 1, 0)
        lifted = mm(proj.astype(bf16), core[u], 1, 1).astype(bf16)
        step_bf = (resid - mm(lifted, factor, 1, 1)).astype(bf16)
        steps = lax.all_gather(step_bf, "pts", axis=0, tiled=True)
        change = mm(steps, place[u], 1, 1)
        all_steps.append(change.astype(bf16))
        current, moving = stepped(current, moving, change)
    gathered = lax.all_gather(jnp.stack(all_steps), "rows", axis=1, tiled=True)
    current, moving = coefficients, momentum
    for u in range(UPDATES):
        current, moving = stepped(current, moving, gathered[u].T.astype(f32))
    return (current, moving)


def shards(features, targets, coefficients, momentum, block_index, pivot_index, nystrom_core):
    rows, owners = lax.axis_size("rows"), lax.axis_size("pts")
    count = block_index.shape[1] // rows
    fits = rows == 4 and coefficients.shape[1] == 8 * rows * owners
    fits = fits and coefficients.shape[0] % CHUNK == 0 and count % CHUNK == 0 and (3 * count // owners) % 64 == 0
    plan = with_kernels if fits else with_operations
    return plan(
        features, targets, coefficients, momentum, block_index, pivot_index, nystrom_core
    )


def solution(mesh):
    in_specs = (P("pts", None), P("pts", None), P("pts", None), P("pts", None), P(), P(), P())
    out_specs = (P("pts", None), P("pts", None))
    return jax.shard_map(shards, mesh=mesh, in_specs=in_specs, out_specs=out_specs, check_vma=False)
```

```python
import functools
import math

import jax
import jax.numpy as jnp
from jax import lax
from jax.experimental import pallas as pl
from jax.experimental.pallas import tpu as pltpu
from jax.sharding import PartitionSpec as P

UPDATES = 2


alpha_mix = 0.6
beta_keep = 0.9
step_size = 0.2
momentum_gain = 1.5
ridge_term = 1.0

f32 = jnp.float32
bf16 = jnp.bfloat16
i32 = jnp.int32


def mm(a, b, ca, cb):
    return lax.dot_general(a, b, (((ca,), (cb,)), ((), ())), preferred_element_type=f32)


def split_two(value):
    high = value.astype(bf16)
    return high, (value - high.astype(f32)).astype(bf16)


def mixed_of(current, moving):
    return alpha_mix * moving + (1.0 - alpha_mix) * current


mix_per_step = alpha_mix * step_size * momentum_gain + (1.0 - alpha_mix) * step_size


def stepped(current, moving, change):
    mixed = mixed_of(current, moving)
    if change is None:
        return mixed, beta_keep * moving + (1.0 - beta_keep) * mixed
    return (
        mixed - step_size * change,
        beta_keep * moving + (1.0 - beta_keep) * mixed - step_size * momentum_gain * change,
    )


def iota(shape, axis):
    return lax.broadcasted_iota(i32, shape, axis)


def one_hot(chosen):
    return jnp.where(chosen, 1.0, 0.0).astype(bf16)


def before_matrix(n):
    return one_hot(iota((n, n), 0) < iota((n, n), 1))


def slots_of(indices, before, points, owners, cap):
    owner = lax.div(indices, jnp.full_like(indices, points))
    marks = iota((owners, indices.shape[1]), 0) == owner
    counts = jnp.where(marks, 1.0, 0.0)
    earlier = mm(counts.astype(bf16), before, 1, 0)
    rank = jnp.sum(counts * earlier, axis=0, keepdims=True)
    return owner * cap + rank.astype(i32)


def point_rows(indices, slots, me, points, cap):
    held = iota((cap, indices.shape[1]), 0) + me * cap == slots
    local = (indices - me * points + 1).astype(f32)
    point = jnp.sum(jnp.where(held, local, 0.0), axis=1, keepdims=True).astype(i32) - 1
    return one_hot(iota((cap, points), 1) == point)


def start_all(pairs, sems):
    copies = [pltpu.make_async_copy(a, b, sems.at[n]) for n, (a, b) in enumerate(pairs)]
    for copy in copies:
        copy.start()
    return copies


def wait_all(copies):
    for copy in copies:
        copy.wait()


def group_row(blocks, u, group, count):
    return blocks[u : u + 1, pl.ds(pl.multiple_of(group * count, count), count)]


def pack_kernel(count, cap, blocks_hbm, feats_hbm, out_hbm, blocks, feats, packed, sems):
    row, me = lax.axis_index("rows"), lax.axis_index("pts")
    points, owners = feats.shape[0], out_hbm.shape[0]
    reads = start_all([(blocks_hbm, blocks), (feats_hbm, feats)], sems)
    before = before_matrix(count)
    reads[0].wait()
    rows = []
    for u in range(UPDATES):
        indices = group_row(blocks, u, row, count)
        slots = slots_of(indices, before, points, owners, cap)
        rows.append(point_rows(indices, slots, me, points, cap))
    reads[1].wait()
    for u in range(UPDATES):
        packed[u * cap : (u + 1) * cap, :] = mm(rows[u], feats[...], 1, 0).astype(bf16)
    wait_all(start_all([(packed, out_hbm.at[o]) for o in range(owners)], sems))


def two_digits(row):
    high = lax.shift_right_logical(row, jnp.full_like(row, 7))
    shape = (8, row.shape[1])
    value = jnp.where(iota(shape, 0) == 0, high, lax.bitwise_and(row, jnp.full_like(row, 127)))
    return value.astype(f32).astype(bf16)


def from_digits(digits):
    return (digits[0:1] * 128.0 + digits[1:2]).astype(i32)


def prepare_kernel(
    count, cap, owners,
    blocks_hbm, pivots_hbm, w_hbm, z_hbm, t_hbm,
    coef_hbm, offset_hbm, rows_hbm, ids_hbm, starts_hbm, chosen_hbm,
    blocks, pivots, w, z, t, coef, offset, rows, ids, starts, chosen, sems,
):
    row, me = lax.axis_index("rows"), lax.axis_index("pts")
    points, outputs = w.shape
    pairs = [(blocks_hbm, blocks), (pivots_hbm, pivots), (w_hbm, w), (z_hbm, z), (t_hbm, t)]
    reads = start_all(pairs, sems)
    before = before_matrix(count)
    wait_all(reads[:2])
    groups = blocks.shape[1] // count
    for u in range(UPDATES):
        pivot = pivots[u : u + 1, :]
        found = jnp.zeros((8, pivot.shape[1]), f32)
        for g in range(groups):
            n = u * groups + g
            indices = blocks[u : u + 1, g * count : (g + 1) * count]
            owner = lax.div(indices, jnp.full_like(indices, points))
            owner_ids = iota((owners, count), 0)
            marks = jnp.where(owner_ids == owner, 1.0, 0.0)
            earlier = mm(marks.astype(bf16), before, 1, 0)
            start = jnp.sum(jnp.where(owner < owner_ids, 1.0, 0.0), axis=1, keepdims=True)
            rank = jnp.sum(marks * earlier, axis=0, keepdims=True)
            place = (rank + jnp.sum(marks * start, axis=0, keepdims=True)).astype(i32)
            held = owner * cap + rank.astype(i32)
            rows[u, g * cap : (g + 1) * cap, :] = point_rows(indices, held, me, points, cap)
            ordered = one_hot(iota((count, count), 0) == place)
            ids[n : n + 1, :] = from_digits(mm(two_digits(indices), ordered, 1, 1))
            diagonal = iota((owners, 128), 0) == iota((owners, 128), 1)
            starts[n : n + 1, :] = jnp.sum(
                jnp.where(diagonal, start, 0.0), axis=0, keepdims=True
            ).astype(i32)
            at_pivot = one_hot(iota((count, pivot.shape[1]), 0) + g * count == pivot)
            found += mm(two_digits(place + g * count), at_pivot, 1, 0)
        chosen[u : u + 1, :] = from_digits(found)
    wait_all(reads[2:])
    current, moving = w[...], z[...]
    goal = t[...].astype(f32).T
    for u in range(UPDATES):
        mixed = mixed_of(current, moving).T
        high, low = split_two(ridge_term * mixed - goal)
        coef[u] = mixed.astype(bf16)
        local = ids[pl.ds(u * groups + row, 1), :] - me * points
        place = one_hot(iota((points, count), 0) == local)
        offset[u] = mm(high, place, 1, 0) + mm(low, place, 1, 0)
        current, moving = stepped(current, moving, None)
    pairs = [(coef, coef_hbm), (offset, offset_hbm), (rows, rows_hbm), (ids, ids_hbm)]
    wait_all(start_all([*pairs, (starts, starts_hbm), (chosen, chosen_hbm)], sems))


def extended(rows, axis, first):
    rest = -0.5 * jnp.sum(jnp.square(rows.astype(f32)), axis=axis, keepdims=True)
    parts = []
    for _ in range(3):
        parts.append(rest.astype(bf16).astype(f32))
        rest = rest - parts[-1]
    parts = parts + [1.0] * 3 if first else [1.0] * 3 + parts
    at = iota(rows.shape, axis)
    extra = jnp.zeros(rows.shape, f32)
    for n, part in enumerate(parts):
        extra = jnp.where(at == n, part, extra)
    return jnp.concatenate([rows.astype(bf16), extra.astype(bf16)], axis=axis)


def exponent(left, right):
    return mm(left, right, 1, 0) * (7.0 / (left.shape[1] // 2) * math.log2(math.e))


CHUNK = 256


def compact_kernel(came, starts_hbm, block_hbm, starts, wide, block, sems):
    row = lax.axis_index("rows")
    owners, deep, _ = came.shape
    cap = deep // UPDATES
    groups = starts.shape[0] // UPDATES
    count = block.shape[2]
    wait_all(start_all([(starts_hbm, starts)], sems))
    for u in range(UPDATES):
        for o in range(owners):
            start = starts[u * groups + row, o]
            wide[u, pl.ds(start, cap), :] = came[o, u * cap : (u + 1) * cap, :].astype(f32)
        block[u] = wide[u, 0:count, :].T.astype(bf16)
    wait_all(start_all([(block, block_hbm)], sems))


def sums_kernel(
    block_hbm, feats_hbm, coef_hbm, offset_hbm, pieces_hbm,
    block, feats, coef, offset, tile, pieces, sems,
):
    points, count = tile.shape
    outputs = coef.shape[1]
    pairs = [(block_hbm, block), (feats_hbm, feats), (coef_hbm, coef), (offset_hbm, offset)]
    reads = start_all(pairs, sems)
    wait_all(reads[:2])
    left = extended(feats[...], 1, True)
    for u in range(UPDATES):
        right = extended(block[u], 0, False)
        for c in range(0, points, CHUNK):
            tile[c : c + CHUNK, :] = jnp.exp2(exponent(left[c : c + CHUNK], right)).astype(bf16)
        if u == 0:
            wait_all(reads[2:])
        total = offset[u] + mm(coef[u], tile[...], 1, 0)
        devices, _, lanes = pieces.shape
        own = outputs // devices
        for d in range(devices):
            part = total[d * own : (d + 1) * own]
            pieces[d, 2 * own * u : 2 * own * (u + 1), :] = jnp.concatenate(
                [part[:, :lanes], part[:, lanes:]], axis=0
            ).astype(bf16)
    wait_all(start_all([(pieces, pieces_hbm)], sems))


def factors_kernel(
    b0_hbm, b1_hbm, b2_hbm, b3_hbm, ids_hbm, pivots_hbm, factor_hbm, cross_hbm,
    feats, ids, pivots, factor, cross, sems,
):
    row = lax.axis_index("rows")
    groups, _, width, count = feats.shape
    pairs = [(b_hbm, feats.at[k]) for k, b_hbm in enumerate((b0_hbm, b1_hbm, b2_hbm, b3_hbm))]
    wait_all(start_all(pairs + [(ids_hbm, ids), (pivots_hbm, pivots)], sems))
    places = [lax.bitwise_xor(row, k) for k in range(groups)]
    rights = [[extended(feats[k, u], 0, False) for k in range(groups)] for u in range(UPDATES)]
    for u in range(UPDATES):
        chosen_feats = jnp.zeros((width, pivots.shape[1]), f32)
        for k in range(groups):
            chosen = iota((count, pivots.shape[1]), 0) + places[k] * count == pivots[u : u + 1, :]
            chosen_feats += mm(feats[k, u], one_hot(chosen), 1, 0)
        left = extended(chosen_feats.T, 1, True)
        for k in range(groups):
            start = pl.multiple_of(places[k] * count, count)
            value = jnp.exp2(exponent(left, rights[u][k]))
            factor[u, :, pl.ds(start, count)] = value.astype(bf16)
    writes = start_all([(factor, factor_hbm)], sems)
    sent = 1
    for k in range(groups):
        left = extended(feats[k, 0].astype(f32).T, 1, True)
        left_points = ids[pl.ds(places[k], 1), :].astype(f32)
        left_points = jnp.broadcast_to(left_points, (8, count)).T[:, 0:1]
        for m in range(groups):
            right_points = ids[pl.ds(groups + places[m], 1), :].astype(f32)
            for c in range(0, count, CHUNK):
                rows = slice(c, c + CHUNK)
                power = exponent(left[rows], rights[1][m])
                power = jnp.where(left_points[rows] == right_points, math.log2(1.0 + ridge_term), power)
                cross[m, k, rows, :] = jnp.exp2(power).astype(bf16)
            start = pl.multiple_of(places[k] * count, count)
            copy = pltpu.make_async_copy(
                cross.at[m, k], cross_hbm.at[places[m], pl.ds(start, count), :], sems.at[sent]
            )
            copy.start()
            writes.append(copy)
            sent += 1
    wait_all(writes)


def chain_kernel(
    cap, owners,
    summed, factor_hbm, core_hbm, cross_hbm, starts_hbm, out_hbm,
    factor, core, cross, starts, packed, sems,
):
    groups, _, count = cross.shape
    own = summed.shape[1] // (2 * UPDATES)
    pairs = []
    for u in range(UPDATES):
        pairs += [(factor_hbm.at[u], factor.at[u]), (core_hbm.at[u], core.at[u])]
        if u == 0:
            pairs += [(starts_hbm, starts)]
            pairs += [(cross_hbm.at[g], cross.at[g]) for g in range(groups)]
    reads = start_all(pairs, sems)
    step = None
    for u in range(UPDATES):
        sums = []
        for g in range(groups):
            part = summed[g * owners, 2 * own * u : 2 * own * (u + 1), :].astype(f32)
            for o in range(1, owners):
                part += summed[g * owners + o, 2 * own * u : 2 * own * (u + 1), :].astype(f32)
            part = jnp.concatenate([part[:own], part[own:]], axis=1)
            if u:
                reads[3 + g].wait()
                part -= mix_per_step * mm(step, cross[g], 1, 0)
            sums.append(part)
        resid = jnp.concatenate(sums, axis=1)
        wait_all(reads[0:3] if u == 0 else reads[3 + groups :])
        proj = mm(resid.astype(bf16), factor[u], 1, 1)
        lifted = mm(proj.astype(bf16), core[u], 1, 1).astype(bf16)
        step = (resid - mm(lifted, factor[u], 1, 0)).astype(bf16)
        half = groups // 2
        for o in range(owners):
            lanes = []
            for g in range(groups):
                part = step[:, g * count : (g + 1) * count].astype(f32)
                back = lax.rem(count - starts[u * groups + g, o], count)
                lanes.append(pltpu.roll(part, back, 1)[:, :cap])
            packed[o, 2 * own * u : 2 * own * (u + 1), :] = jnp.concatenate(
                [jnp.concatenate(lanes[h * half : (h + 1) * half], axis=1) for h in range(2)], axis=0
            ).astype(bf16)
    copies = out_hbm.shape[0] // owners
    wait_all(
        start_all([(packed, out_hbm.at[pl.ds(n * owners, owners)]) for n in range(copies)], sems)
    )


def finish_kernel(
    got, w_hbm, z_hbm, rows_hbm, w_out, z_out, w, z, rows, steps, w_new, z_new, sems, out_sems
):
    points = w.shape[0]
    sources, deep, lanes = got.shape
    own = deep // (2 * UPDATES)
    chunks = range(0, points, CHUNK)
    pairs = []
    for c in chunks:
        part = slice(c, c + CHUNK)
        pairs += [(rows_hbm.at[:, :, part], rows.at[:, :, part])]
        pairs += [(w_hbm.at[part], w.at[part]), (z_hbm.at[part], z.at[part])]
    reads = start_all(pairs, sems)
    wide = got[...].astype(f32)
    for u in range(UPDATES):
        for h in range(2):
            first = own * (2 * u + h)
            part = wide[:, first : first + own, :].reshape(sources * own, lanes)
            steps[u, :, h * lanes : (h + 1) * lanes] = part.astype(bf16)
    writes = []
    for n, c in enumerate(chunks):
        part = slice(c, c + CHUNK)
        wait_all(reads[3 * n : 3 * n + 3])
        current, moving = w[part, :], z[part, :]
        for u in range(UPDATES):
            change = mm(steps[u], rows[u, :, part], 1, 0).T
            current, moving = stepped(current, moving, change)
        w_new[part, :] = current
        z_new[part, :] = moving
        for m, (a, b) in enumerate(((w_new, w_out), (z_new, z_out))):
            copy = pltpu.make_async_copy(a.at[part], b.at[part], out_sems.at[2 * n + m])
            copy.start()
            writes.append(copy)
    wait_all(writes)


VMEM = pl.BlockSpec(memory_space=pltpu.VMEM)
HBM = pl.BlockSpec(memory_space=pltpu.HBM)
in_smem = type(pltpu.SMEM((1,), i32))


def like(shape, dtype=bf16):
    return jax.ShapeDtypeStruct(shape, dtype)


def call(body, outs, inside, *args, near=0, sems=(), flops=0, grant=62):
    moved = sum(math.prod(o.shape) * o.dtype.itemsize for o in [*outs, *args])
    return pl.pallas_call(
        body,
        out_shape=outs,
        in_specs=[VMEM] * near + [HBM] * (len(args) - near),
        out_specs=[HBM] * len(outs),
        scratch_shapes=[
            x if isinstance(x, in_smem) else pltpu.VMEM(x.shape, x.dtype) for x in inside
        ]
        + [pltpu.SemaphoreType.DMA((n,)) for n in sems],
        compiler_params=pltpu.CompilerParams(vmem_limit_bytes=grant * 2**20),
        cost_estimate=pl.CostEstimate(flops=int(flops), bytes_accessed=moved, transcendentals=0),
    )(*args)


def swap_rows(value, k):
    count = lax.axis_size("rows")
    return lax.ppermute(value, "rows", [(i, i ^ k) for i in range(count)])


def with_kernels(features, targets, coefficients, momentum, block_index, pivot_index, core):
    rows, owners = lax.axis_size("rows"), lax.axis_size("pts")
    points, width = features.shape
    block = block_index.shape[1]
    rank = pivot_index.shape[1]
    outputs = coefficients.shape[1]
    count = block // rows
    cap = 3 * count // owners
    devices = rows * owners
    own = outputs // devices
    deep = 2 * own * UPDATES
    half = rows // 2
    wide = like(coefficients.shape, f32)

    (packed,) = call(
        functools.partial(pack_kernel, count, cap),
        [like((owners, UPDATES * cap, width))],
        [block_index, features, like((UPDATES * cap, width))],
        block_index,
        features,
        sems=(owners,),
    )
    came = lax.all_to_all(packed, "pts", 0, 0, tiled=True)
    kept = [
        like((UPDATES, outputs, points)),
        like((UPDATES, outputs, count), f32),
        like((UPDATES, rows * cap, points)),
        like((UPDATES * rows, count), i32),
        like((UPDATES * rows, 128), i32),
        like((UPDATES, rank), i32),
    ]
    given = [block_index, pivot_index, coefficients, momentum, targets]
    coef, offset, place, ids, starts, chosen = call(
        functools.partial(prepare_kernel, count, cap, owners),
        kept,
        given + kept,
        *given,
        sems=(6,),
    )
    feats = like((UPDATES, width, count))
    inside_starts = pltpu.SMEM(starts.shape, i32)
    (mine,) = call(
        compact_kernel,
        [feats],
        [inside_starts, like((UPDATES, count + cap, width), f32), feats],
        came,
        starts,
        near=1,
        sems=(1,),
    )
    beside, across = swap_rows(mine, 1), swap_rows(mine, 2)
    pieces = like((devices, deep, count // 2))
    (pieces,) = call(
        sums_kernel,
        [pieces],
        [feats, features, coef, offset, like((points, count)), pieces],
        mine,
        features,
        coef,
        offset,
        sems=(4,),
        flops=2.0 * UPDATES * points * count * (2 * width + outputs),
    )
    pieces, across = lax.optimization_barrier((pieces, across))
    summed = lax.all_to_all(pieces, ("rows", "pts"), 0, 0, tiled=True)
    kept = [like((UPDATES, rank, block)), like((rows, block, count))]
    factor, cross = call(
        factors_kernel,
        kept,
        [
            like((rows, *feats.shape)),
            ids,
            chosen,
            kept[0],
            like((rows, rows, count, count)),
        ],
        mine,
        beside,
        across,
        swap_rows(across, 1),
        ids,
        chosen,
        sems=(rows * rows + 1,),
        flops=2.0 * width * block * (UPDATES * rank + block),
    )
    (steps,) = call(
        functools.partial(chain_kernel, cap, owners),
        [like((devices, deep, half * cap))],
        [factor, core, cross, inside_starts, like((owners, deep, half * cap))],
        summed,
        factor,
        core,
        cross,
        starts,
        near=1,
        sems=(2 * UPDATES + 1 + rows,),
    )
    got = lax.all_to_all(steps, ("rows", "pts"), 0, 0, tiled=True)
    parts = points // CHUNK
    return call(
        finish_kernel,
        [wide] * 2,
        [wide, wide, place, like((UPDATES, outputs, rows * cap)), wide, wide],
        got,
        coefficients,
        momentum,
        place,
        near=1,
        sems=(3 * parts, 2 * parts),
        grant=40,
    )


def kernel_tile(left_rows, right_rows):
    inner_prod = mm(left_rows, right_rows, 1, 1)
    left_sq = jnp.sum(jnp.square(left_rows.astype(f32)), axis=1)
    right_sq = jnp.sum(jnp.square(right_rows.astype(f32)), axis=1)
    squared = left_sq[:, None] + right_sq[None, :] - 2.0 * inner_prod
    return jnp.exp(squared * (-3.5 / left_rows.shape[1])).astype(bf16)


def with_operations(features, targets, coefficients, momentum, block_index, pivot_index, core):
    row_count, pts_count = lax.axis_size("rows"), lax.axis_size("pts")
    row_id, pts_id = lax.axis_index("rows"), lax.axis_index("pts")
    points = features.shape[0]
    block = block_index.shape[1]
    outputs = coefficients.shape[1]
    per_row = block // row_count
    per_device = per_row // pts_count
    row_cols = outputs // row_count
    own_cols = row_cols // pts_count
    first = row_id * row_cols
    current, moving, goal = (
        lax.dynamic_slice_in_dim(value, first, row_cols, axis=1).T.astype(f32)
        for value in (coefficients, momentum, targets)
    )
    ids = iota((points, 1), 0) + pts_id * points
    place = [(ids == block_index[u][None, :]).astype(bf16) for u in range(UPDATES)]
    own_rows = []
    for u in range(UPDATES):
        mine = lax.dynamic_slice_in_dim(place[u], row_id * per_row, per_row, axis=1)
        own_rows.append(mm(mine, features, 0, 0).astype(bf16).reshape(pts_count, per_device, -1))
    came = lax.all_to_all(jnp.concatenate(own_rows, axis=1), "pts", 0, 0, tiled=False)
    chunk = jnp.sum(came.astype(f32), axis=0).astype(bf16)
    spread = lax.all_gather(lax.all_gather(chunk, "pts", axis=0), "rows", axis=0)
    spread = spread.reshape(row_count, pts_count, UPDATES, per_device, features.shape[1])
    all_steps = []
    for u in range(UPDATES):
        block_feats = spread[:, :, u].reshape(block, features.shape[1])
        mixed = mixed_of(current, moving)
        high, low = split_two(ridge_term * mixed - goal)
        tile = kernel_tile(features, block_feats)
        partial_value = (
            mm(mixed.astype(bf16), tile, 1, 0) + mm(high, place[u], 1, 0) + mm(low, place[u], 1, 0)
        )
        pieces = partial_value.astype(bf16).reshape(pts_count, own_cols, block)
        summed = lax.all_to_all(pieces, "pts", 0, 0, tiled=False)
        resid = jnp.sum(summed.astype(f32), axis=0)
        at_pivot = (iota((block, 1), 0) == pivot_index[u][None, :]).astype(bf16)
        factor = kernel_tile(block_feats, mm(at_pivot, block_feats, 0, 0).astype(bf16))
        proj = mm(resid.astype(bf16), factor, 1, 0)
        lifted = mm(proj.astype(bf16), core[u], 1, 1).astype(bf16)
        step_bf = (resid - mm(lifted, factor, 1, 1)).astype(bf16)
        steps = lax.all_gather(step_bf, "pts", axis=0, tiled=True)
        change = mm(steps, place[u], 1, 1)
        all_steps.append(change.astype(bf16))
        current, moving = stepped(current, moving, change)
    gathered = lax.all_gather(jnp.stack(all_steps), "rows", axis=1, tiled=True)
    current, moving = coefficients, momentum
    for u in range(UPDATES):
        current, moving = stepped(current, moving, gathered[u].T.astype(f32))
    return (current, moving)


def shards(features, targets, coefficients, momentum, block_index, pivot_index, nystrom_core):
    rows, owners = lax.axis_size("rows"), lax.axis_size("pts")
    count = block_index.shape[1] // rows
    fits = rows == 4 and coefficients.shape[1] == 8 * rows * owners
    fits = fits and coefficients.shape[0] % CHUNK == 0 and count % CHUNK == 0 and (3 * count // owners) % 64 == 0
    plan = with_kernels if fits else with_operations
    return plan(
        features, targets, coefficients, momentum, block_index, pivot_index, nystrom_core
    )


def solution(mesh):
    in_specs = (P("pts", None), P("pts", None), P("pts", None), P("pts", None), P(), P(), P())
    out_specs = (P("pts", None), P("pts", None))
    return jax.shard_map(shards, mesh=mesh, in_specs=in_specs, out_specs=out_specs, check_vma=False)
```

```python
import functools
import math

import jax
import jax.numpy as jnp
from jax import lax
from jax.experimental import pallas as pl
from jax.experimental.pallas import tpu as pltpu
from jax.sharding import PartitionSpec as P

UPDATES = 2


alpha_mix = 0.6
beta_keep = 0.9
step_size = 0.2
momentum_gain = 1.5
ridge_term = 1.0

f32 = jnp.float32
bf16 = jnp.bfloat16
i32 = jnp.int32


def mm(a, b, ca, cb):
    return lax.dot_general(a, b, (((ca,), (cb,)), ((), ())), preferred_element_type=f32)


def split_two(value):
    high = value.astype(bf16)
    return high, (value - high.astype(f32)).astype(bf16)


def mixed_of(current, moving):
    return alpha_mix * moving + (1.0 - alpha_mix) * current


mix_per_step = alpha_mix * step_size * momentum_gain + (1.0 - alpha_mix) * step_size


def stepped(current, moving, change):
    mixed = mixed_of(current, moving)
    if change is None:
        return mixed, beta_keep * moving + (1.0 - beta_keep) * mixed
    return (
        mixed - step_size * change,
        beta_keep * moving + (1.0 - beta_keep) * mixed - step_size * momentum_gain * change,
    )


def iota(shape, axis):
    return lax.broadcasted_iota(i32, shape, axis)


def one_hot(chosen):
    return jnp.where(chosen, 1.0, 0.0).astype(bf16)


def before_matrix(n):
    return one_hot(iota((n, n), 0) < iota((n, n), 1))


def slots_of(indices, before, points, owners, cap):
    owner = lax.div(indices, jnp.full_like(indices, points))
    marks = iota((owners, indices.shape[1]), 0) == owner
    counts = jnp.where(marks, 1.0, 0.0)
    earlier = mm(counts.astype(bf16), before, 1, 0)
    rank = jnp.sum(counts * earlier, axis=0, keepdims=True)
    return owner * cap + rank.astype(i32)


def point_rows(indices, slots, me, points, cap):
    held = iota((cap, indices.shape[1]), 0) + me * cap == slots
    local = (indices - me * points + 1).astype(f32)
    point = jnp.sum(jnp.where(held, local, 0.0), axis=1, keepdims=True).astype(i32) - 1
    return one_hot(iota((cap, points), 1) == point)


def start_all(pairs, sems):
    copies = [pltpu.make_async_copy(a, b, sems.at[n]) for n, (a, b) in enumerate(pairs)]
    for copy in copies:
        copy.start()
    return copies


def wait_all(copies):
    for copy in copies:
        copy.wait()


def group_row(blocks, u, group, count):
    return blocks[u : u + 1, pl.ds(pl.multiple_of(group * count, count), count)]


def pack_kernel(count, cap, owners, blocks_hbm, feats_hbm, out_hbm, blocks, feats, packed, sems):
    row, me = lax.axis_index("rows"), lax.axis_index("pts")
    points = feats.shape[0]
    reads = start_all([(blocks_hbm, blocks), (feats_hbm, feats)], sems)
    before = before_matrix(count)
    reads[0].wait()
    rows = []
    for u in range(UPDATES):
        indices = group_row(blocks, u, row, count)
        slots = slots_of(indices, before, points, owners, cap)
        rows.append(point_rows(indices, slots, me, points, cap))
    reads[1].wait()
    for u in range(UPDATES):
        packed[u * cap : (u + 1) * cap, :] = mm(rows[u], feats[...], 1, 0).astype(bf16)
    wait_all(start_all([(packed, out_hbm)], sems))


def two_digits(row):
    high = lax.shift_right_logical(row, jnp.full_like(row, 7))
    shape = (8, row.shape[1])
    value = jnp.where(iota(shape, 0) == 0, high, lax.bitwise_and(row, jnp.full_like(row, 127)))
    return value.astype(f32).astype(bf16)


def from_digits(digits):
    return (digits[0:1] * 128.0 + digits[1:2]).astype(i32)


def prepare_kernel(
    count, cap, owners,
    blocks_hbm, pivots_hbm, w_hbm, z_hbm, t_hbm,
    coef_hbm, offset_hbm, rows_hbm, ids_hbm, starts_hbm, chosen_hbm,
    blocks, pivots, w, z, t, coef, offset, rows, ids, starts, chosen, sems,
):
    row, me = lax.axis_index("rows"), lax.axis_index("pts")
    points, outputs = w.shape
    pairs = [(blocks_hbm, blocks), (pivots_hbm, pivots), (w_hbm, w), (z_hbm, z), (t_hbm, t)]
    reads = start_all(pairs, sems)
    before = before_matrix(count)
    wait_all(reads[:2])
    groups = blocks.shape[1] // count
    for u in range(UPDATES):
        pivot = pivots[u : u + 1, :]
        found = jnp.zeros((8, pivot.shape[1]), f32)
        for g in range(groups):
            n = u * groups + g
            indices = blocks[u : u + 1, g * count : (g + 1) * count]
            owner = lax.div(indices, jnp.full_like(indices, points))
            owner_ids = iota((owners, count), 0)
            marks = jnp.where(owner_ids == owner, 1.0, 0.0)
            earlier = mm(marks.astype(bf16), before, 1, 0)
            start = jnp.sum(jnp.where(owner < owner_ids, 1.0, 0.0), axis=1, keepdims=True)
            rank = jnp.sum(marks * earlier, axis=0, keepdims=True)
            place = (rank + jnp.sum(marks * start, axis=0, keepdims=True)).astype(i32)
            held = owner * cap + rank.astype(i32)
            rows[u, g * cap : (g + 1) * cap, :] = point_rows(indices, held, me, points, cap)
            ordered = one_hot(iota((count, count), 0) == place)
            ids[n : n + 1, :] = from_digits(mm(two_digits(indices), ordered, 1, 1))
            diagonal = iota((owners, 128), 0) == iota((owners, 128), 1)
            starts[n : n + 1, :] = jnp.sum(
                jnp.where(diagonal, start, 0.0), axis=0, keepdims=True
            ).astype(i32)
            at_pivot = one_hot(iota((count, pivot.shape[1]), 0) + g * count == pivot)
            found += mm(two_digits(place + g * count), at_pivot, 1, 0)
        chosen[u : u + 1, :] = from_digits(found)
    wait_all(reads[2:])
    current, moving = w[...], z[...]
    goal = t[...].astype(f32).T
    for u in range(UPDATES):
        mixed = mixed_of(current, moving).T
        high, low = split_two(ridge_term * mixed - goal)
        coef[u] = mixed.astype(bf16)
        local = ids[pl.ds(u * groups + row, 1), :] - me * points
        place = one_hot(iota((points, count), 0) == local)
        offset[u] = mm(high, place, 1, 0) + mm(low, place, 1, 0)
        current, moving = stepped(current, moving, None)
    pairs = [(coef, coef_hbm), (offset, offset_hbm), (rows, rows_hbm), (ids, ids_hbm)]
    wait_all(start_all([*pairs, (starts, starts_hbm), (chosen, chosen_hbm)], sems))


def extended(rows, axis, first):
    rest = -0.5 * jnp.sum(jnp.square(rows.astype(f32)), axis=axis, keepdims=True)
    parts = []
    for _ in range(3):
        parts.append(rest.astype(bf16).astype(f32))
        rest = rest - parts[-1]
    parts = parts + [1.0] * 3 if first else [1.0] * 3 + parts
    at = iota(rows.shape, axis)
    extra = jnp.zeros(rows.shape, f32)
    for n, part in enumerate(parts):
        extra = jnp.where(at == n, part, extra)
    return jnp.concatenate([rows.astype(bf16), extra.astype(bf16)], axis=axis)


def exponent(left, right):
    return mm(left, right, 1, 0) * (7.0 / (left.shape[1] // 2) * math.log2(math.e))


CHUNK = 256


def compact_kernel(*refs):
    *came_hbm, starts_hbm, block_hbm, came, starts, wide, block, sems = refs
    row, me = lax.axis_index("rows"), lax.axis_index("pts")
    owners, deep, _ = came.shape
    cap = deep // UPDATES
    groups = starts.shape[0] // UPDATES
    count = block.shape[2]
    pairs = [(a, came.at[k]) for k, a in enumerate(came_hbm)]
    wait_all(start_all([*pairs, (starts_hbm, starts)], sems))
    for u in range(UPDATES):
        for o in range(owners):
            start = starts[u * groups + row, o]
            rows = came[lax.bitwise_xor(me, o), u * cap : (u + 1) * cap, :]
            wide[u, pl.ds(start, cap), :] = rows.astype(f32)
        block[u] = wide[u, 0:count, :].T.astype(bf16)
    wait_all(start_all([(block, block_hbm)], sems))


def sums_kernel(
    block_hbm, feats_hbm, coef_hbm, offset_hbm, pieces_hbm,
    block, feats, coef, offset, tile, pieces, sems,
):
    points, count = tile.shape
    outputs = coef.shape[1]
    pairs = [(block_hbm, block), (feats_hbm, feats), (coef_hbm, coef), (offset_hbm, offset)]
    reads = start_all(pairs, sems)
    wait_all(reads[:2])
    left = extended(feats[...], 1, True)
    for u in range(UPDATES):
        right = extended(block[u], 0, False)
        for c in range(0, points, CHUNK):
            tile[c : c + CHUNK, :] = jnp.exp2(exponent(left[c : c + CHUNK], right)).astype(bf16)
        if u == 0:
            wait_all(reads[2:])
        total = offset[u] + mm(coef[u], tile[...], 1, 0)
        devices, _, lanes = pieces.shape
        own = outputs // devices
        for d in range(devices):
            part = total[d * own : (d + 1) * own]
            pieces[d, 2 * own * u : 2 * own * (u + 1), :] = jnp.concatenate(
                [part[:, :lanes], part[:, lanes:]], axis=0
            ).astype(bf16)
    wait_all(start_all([(pieces, pieces_hbm)], sems))


def factors_kernel(
    b0_hbm, b1_hbm, b2_hbm, b3_hbm, ids_hbm, pivots_hbm, factor_hbm, cross_hbm,
    feats, ids, pivots, factor, cross, sems,
):
    row = lax.axis_index("rows")
    groups, _, width, count = feats.shape
    pairs = [(b_hbm, feats.at[k]) for k, b_hbm in enumerate((b0_hbm, b1_hbm, b2_hbm, b3_hbm))]
    wait_all(start_all(pairs + [(ids_hbm, ids), (pivots_hbm, pivots)], sems))
    places = [lax.bitwise_xor(row, k) for k in range(groups)]
    rights = [[extended(feats[k, u], 0, False) for k in range(groups)] for u in range(UPDATES)]
    for u in range(UPDATES):
        chosen_feats = jnp.zeros((width, pivots.shape[1]), f32)
        for k in range(groups):
            chosen = iota((count, pivots.shape[1]), 0) + places[k] * count == pivots[u : u + 1, :]
            chosen_feats += mm(feats[k, u], one_hot(chosen), 1, 0)
        left = extended(chosen_feats.T, 1, True)
        for k in range(groups):
            start = pl.multiple_of(places[k] * count, count)
            value = jnp.exp2(exponent(left, rights[u][k]))
            factor[u, :, pl.ds(start, count)] = value.astype(bf16)
    writes = start_all([(factor, factor_hbm)], sems)
    sent = 1
    for k in range(groups):
        left = extended(feats[k, 0].astype(f32).T, 1, True)
        left_points = ids[pl.ds(places[k], 1), :].astype(f32)
        left_points = jnp.broadcast_to(left_points, (8, count)).T[:, 0:1]
        for m in range(groups):
            right_points = ids[pl.ds(groups + places[m], 1), :].astype(f32)
            for c in range(0, count, CHUNK):
                rows = slice(c, c + CHUNK)
                power = exponent(left[rows], rights[1][m])
                power = jnp.where(left_points[rows] == right_points, math.log2(1.0 + ridge_term), power)
                cross[m, k, rows, :] = jnp.exp2(power).astype(bf16)
            start = pl.multiple_of(places[k] * count, count)
            copy = pltpu.make_async_copy(
                cross.at[m, k], cross_hbm.at[places[m], pl.ds(start, count), :], sems.at[sent]
            )
            copy.start()
            writes.append(copy)
            sent += 1
    wait_all(writes)


def chain_kernel(
    cap, owners,
    summed, factor_hbm, core_hbm, cross_hbm, starts_hbm, out_hbm,
    factor, core, cross, starts, packed, sems,
):
    groups, _, count = cross.shape
    own = summed.shape[1] // (2 * UPDATES)
    pairs = []
    for u in range(UPDATES):
        pairs += [(factor_hbm.at[u], factor.at[u]), (core_hbm.at[u], core.at[u])]
        if u == 0:
            pairs += [(starts_hbm, starts)]
            pairs += [(cross_hbm.at[g], cross.at[g]) for g in range(groups)]
    reads = start_all(pairs, sems)
    step = None
    for u in range(UPDATES):
        sums = []
        for g in range(groups):
            part = summed[g * owners, 2 * own * u : 2 * own * (u + 1), :].astype(f32)
            for o in range(1, owners):
                part += summed[g * owners + o, 2 * own * u : 2 * own * (u + 1), :].astype(f32)
            part = jnp.concatenate([part[:own], part[own:]], axis=1)
            if u:
                reads[3 + g].wait()
                part -= mix_per_step * mm(step, cross[g], 1, 0)
            sums.append(part)
        resid = jnp.concatenate(sums, axis=1)
        wait_all(reads[0:3] if u == 0 else reads[3 + groups :])
        proj = mm(resid.astype(bf16), factor[u], 1, 1)
        lifted = mm(proj.astype(bf16), core[u], 1, 1).astype(bf16)
        step = (resid - mm(lifted, factor[u], 1, 0)).astype(bf16)
        half = groups // 2
        for o in range(owners):
            lanes = []
            for g in range(groups):
                part = step[:, g * count : (g + 1) * count].astype(f32)
                back = lax.rem(count - starts[u * groups + g, o], count)
                lanes.append(pltpu.roll(part, back, 1)[:, :cap])
            packed[o, 2 * own * u : 2 * own * (u + 1), :] = jnp.concatenate(
                [jnp.concatenate(lanes[h * half : (h + 1) * half], axis=1) for h in range(2)], axis=0
            ).astype(bf16)
    copies = out_hbm.shape[0] // owners
    wait_all(
        start_all([(packed, out_hbm.at[pl.ds(n * owners, owners)]) for n in range(copies)], sems)
    )


def finish_kernel(
    got, w_hbm, z_hbm, rows_hbm, w_out, z_out, w, z, rows, steps, w_new, z_new, sems, out_sems
):
    points = w.shape[0]
    sources, deep, lanes = got.shape
    own = deep // (2 * UPDATES)
    chunks = range(0, points, CHUNK)
    pairs = []
    for c in chunks:
        part = slice(c, c + CHUNK)
        pairs += [(rows_hbm.at[:, :, part], rows.at[:, :, part])]
        pairs += [(w_hbm.at[part], w.at[part]), (z_hbm.at[part], z.at[part])]
    reads = start_all(pairs, sems)
    wide = got[...].astype(f32)
    for u in range(UPDATES):
        for h in range(2):
            first = own * (2 * u + h)
            part = wide[:, first : first + own, :].reshape(sources * own, lanes)
            steps[u, :, h * lanes : (h + 1) * lanes] = part.astype(bf16)
    writes = []
    for n, c in enumerate(chunks):
        part = slice(c, c + CHUNK)
        wait_all(reads[3 * n : 3 * n + 3])
        current, moving = w[part, :], z[part, :]
        for u in range(UPDATES):
            change = mm(steps[u], rows[u, :, part], 1, 0).T
            current, moving = stepped(current, moving, change)
        w_new[part, :] = current
        z_new[part, :] = moving
        for m, (a, b) in enumerate(((w_new, w_out), (z_new, z_out))):
            copy = pltpu.make_async_copy(a.at[part], b.at[part], out_sems.at[2 * n + m])
            copy.start()
            writes.append(copy)
    wait_all(writes)


VMEM = pl.BlockSpec(memory_space=pltpu.VMEM)
HBM = pl.BlockSpec(memory_space=pltpu.HBM)
in_smem = type(pltpu.SMEM((1,), i32))


def like(shape, dtype=bf16):
    return jax.ShapeDtypeStruct(shape, dtype)


def call(body, outs, inside, *args, near=0, sems=(), flops=0, grant=62):
    moved = sum(math.prod(o.shape) * o.dtype.itemsize for o in [*outs, *args])
    return pl.pallas_call(
        body,
        out_shape=outs,
        in_specs=[VMEM] * near + [HBM] * (len(args) - near),
        out_specs=[HBM] * len(outs),
        scratch_shapes=[
            x if isinstance(x, in_smem) else pltpu.VMEM(x.shape, x.dtype) for x in inside
        ]
        + [pltpu.SemaphoreType.DMA((n,)) for n in sems],
        compiler_params=pltpu.CompilerParams(vmem_limit_bytes=grant * 2**20),
        cost_estimate=pl.CostEstimate(flops=int(flops), bytes_accessed=moved, transcendentals=0),
    )(*args)


def swap(value, axis, k):
    return lax.ppermute(value, axis, [(i, i ^ k) for i in range(lax.axis_size(axis))])


def with_kernels(features, targets, coefficients, momentum, block_index, pivot_index, core):
    rows, owners = lax.axis_size("rows"), lax.axis_size("pts")
    points, width = features.shape
    block = block_index.shape[1]
    rank = pivot_index.shape[1]
    outputs = coefficients.shape[1]
    count = block // rows
    cap = 3 * count // owners
    devices = rows * owners
    own = outputs // devices
    deep = 2 * own * UPDATES
    half = rows // 2
    wide = like(coefficients.shape, f32)

    (packed,) = call(
        functools.partial(pack_kernel, count, cap, owners),
        [like((UPDATES * cap, width))],
        [block_index, features, like((UPDATES * cap, width))],
        block_index,
        features,
        sems=(2,),
    )
    came = {k: swap(packed, "pts", k) for k in reversed(range(1, owners))}
    kept = [
        like((UPDATES, outputs, points)),
        like((UPDATES, outputs, count), f32),
        like((UPDATES, rows * cap, points)),
        like((UPDATES * rows, count), i32),
        like((UPDATES * rows, 128), i32),
        like((UPDATES, rank), i32),
    ]
    given = [block_index, pivot_index, coefficients, momentum, targets]
    coef, offset, place, ids, starts, chosen = call(
        functools.partial(prepare_kernel, count, cap, owners),
        kept,
        given + kept,
        *given,
        sems=(6,),
    )
    feats = like((UPDATES, width, count))
    inside_starts = pltpu.SMEM(starts.shape, i32)
    (mine,) = call(
        compact_kernel,
        [feats],
        [
            like((owners, *packed.shape)),
            inside_starts,
            like((UPDATES, count + cap, width), f32),
            feats,
        ],
        packed,
        *[came[k] for k in range(1, owners)],
        starts,
        sems=(owners + 1,),
        grant=40,
    )
    beside, across = swap(mine, "rows", 1), swap(mine, "rows", 2)
    pieces = like((devices, deep, count // 2))
    (pieces,) = call(
        sums_kernel,
        [pieces],
        [feats, features, coef, offset, like((points, count)), pieces],
        mine,
        features,
        coef,
        offset,
        sems=(4,),
        flops=2.0 * UPDATES * points * count * (2 * width + outputs),
    )
    pieces, across = lax.optimization_barrier((pieces, across))
    summed = lax.all_to_all(pieces, ("rows", "pts"), 0, 0, tiled=True)
    kept = [like((UPDATES, rank, block)), like((rows, block, count))]
    factor, cross = call(
        factors_kernel,
        kept,
        [
            like((rows, *feats.shape)),
            ids,
            chosen,
            kept[0],
            like((rows, rows, count, count)),
        ],
        mine,
        beside,
        across,
        swap(across, "rows", 1),
        ids,
        chosen,
        sems=(rows * rows + 1,),
        flops=2.0 * width * block * (UPDATES * rank + block),
    )
    (steps,) = call(
        functools.partial(chain_kernel, cap, owners),
        [like((devices, deep, half * cap))],
        [factor, core, cross, inside_starts, like((owners, deep, half * cap))],
        summed,
        factor,
        core,
        cross,
        starts,
        near=1,
        sems=(2 * UPDATES + 1 + rows,),
    )
    got = lax.all_to_all(steps, ("rows", "pts"), 0, 0, tiled=True)
    parts = points // CHUNK
    return call(
        finish_kernel,
        [wide] * 2,
        [wide, wide, place, like((UPDATES, outputs, rows * cap)), wide, wide],
        got,
        coefficients,
        momentum,
        place,
        near=1,
        sems=(3 * parts, 2 * parts),
        grant=48,
    )


def kernel_tile(left_rows, right_rows):
    inner_prod = mm(left_rows, right_rows, 1, 1)
    left_sq = jnp.sum(jnp.square(left_rows.astype(f32)), axis=1)
    right_sq = jnp.sum(jnp.square(right_rows.astype(f32)), axis=1)
    squared = left_sq[:, None] + right_sq[None, :] - 2.0 * inner_prod
    return jnp.exp(squared * (-3.5 / left_rows.shape[1])).astype(bf16)


def with_operations(features, targets, coefficients, momentum, block_index, pivot_index, core):
    row_count, pts_count = lax.axis_size("rows"), lax.axis_size("pts")
    row_id, pts_id = lax.axis_index("rows"), lax.axis_index("pts")
    points = features.shape[0]
    block = block_index.shape[1]
    outputs = coefficients.shape[1]
    per_row = block // row_count
    per_device = per_row // pts_count
    row_cols = outputs // row_count
    own_cols = row_cols // pts_count
    first = row_id * row_cols
    current, moving, goal = (
        lax.dynamic_slice_in_dim(value, first, row_cols, axis=1).T.astype(f32)
        for value in (coefficients, momentum, targets)
    )
    ids = iota((points, 1), 0) + pts_id * points
    place = [(ids == block_index[u][None, :]).astype(bf16) for u in range(UPDATES)]
    own_rows = []
    for u in range(UPDATES):
        mine = lax.dynamic_slice_in_dim(place[u], row_id * per_row, per_row, axis=1)
        own_rows.append(mm(mine, features, 0, 0).astype(bf16).reshape(pts_count, per_device, -1))
    came = lax.all_to_all(jnp.concatenate(own_rows, axis=1), "pts", 0, 0, tiled=False)
    chunk = jnp.sum(came.astype(f32), axis=0).astype(bf16)
    spread = lax.all_gather(lax.all_gather(chunk, "pts", axis=0), "rows", axis=0)
    spread = spread.reshape(row_count, pts_count, UPDATES, per_device, features.shape[1])
    all_steps = []
    for u in range(UPDATES):
        block_feats = spread[:, :, u].reshape(block, features.shape[1])
        mixed = mixed_of(current, moving)
        high, low = split_two(ridge_term * mixed - goal)
        tile = kernel_tile(features, block_feats)
        partial_value = (
            mm(mixed.astype(bf16), tile, 1, 0) + mm(high, place[u], 1, 0) + mm(low, place[u], 1, 0)
        )
        pieces = partial_value.astype(bf16).reshape(pts_count, own_cols, block)
        summed = lax.all_to_all(pieces, "pts", 0, 0, tiled=False)
        resid = jnp.sum(summed.astype(f32), axis=0)
        at_pivot = (iota((block, 1), 0) == pivot_index[u][None, :]).astype(bf16)
        factor = kernel_tile(block_feats, mm(at_pivot, block_feats, 0, 0).astype(bf16))
        proj = mm(resid.astype(bf16), factor, 1, 0)
        lifted = mm(proj.astype(bf16), core[u], 1, 1).astype(bf16)
        step_bf = (resid - mm(lifted, factor, 1, 1)).astype(bf16)
        steps = lax.all_gather(step_bf, "pts", axis=0, tiled=True)
        change = mm(steps, place[u], 1, 1)
        all_steps.append(change.astype(bf16))
        current, moving = stepped(current, moving, change)
    gathered = lax.all_gather(jnp.stack(all_steps), "rows", axis=1, tiled=True)
    current, moving = coefficients, momentum
    for u in range(UPDATES):
        current, moving = stepped(current, moving, gathered[u].T.astype(f32))
    return (current, moving)


def shards(features, targets, coefficients, momentum, block_index, pivot_index, nystrom_core):
    rows, owners = lax.axis_size("rows"), lax.axis_size("pts")
    count = block_index.shape[1] // rows
    fits = rows == 4 and owners == 8 and coefficients.shape[1] == 8 * rows * owners
    fits = fits and coefficients.shape[0] % CHUNK == 0 and count % CHUNK == 0 and (3 * count // owners) % 64 == 0
    plan = with_kernels if fits else with_operations
    return plan(
        features, targets, coefficients, momentum, block_index, pivot_index, nystrom_core
    )


def solution(mesh):
    in_specs = (P("pts", None), P("pts", None), P("pts", None), P("pts", None), P(), P(), P())
    out_specs = (P("pts", None), P("pts", None))
    return jax.shard_map(shards, mesh=mesh, in_specs=in_specs, out_specs=out_specs, check_vma=False)
```

```python
import functools
import math

import jax
import jax.numpy as jnp
from jax import lax
from jax.experimental import pallas as pl
from jax.experimental.pallas import tpu as pltpu
from jax.sharding import PartitionSpec as P

UPDATES = 2


alpha_mix = 0.6
beta_keep = 0.9
step_size = 0.2
momentum_gain = 1.5
ridge_term = 1.0

f32 = jnp.float32
bf16 = jnp.bfloat16
i32 = jnp.int32


def mm(a, b, ca, cb):
    return lax.dot_general(a, b, (((ca,), (cb,)), ((), ())), preferred_element_type=f32)


def split_two(value):
    high = value.astype(bf16)
    return high, (value - high.astype(f32)).astype(bf16)


def mixed_of(current, moving):
    return alpha_mix * moving + (1.0 - alpha_mix) * current


mix_per_step = alpha_mix * step_size * momentum_gain + (1.0 - alpha_mix) * step_size


def stepped(current, moving, change):
    mixed = mixed_of(current, moving)
    if change is None:
        return mixed, beta_keep * moving + (1.0 - beta_keep) * mixed
    return (
        mixed - step_size * change,
        beta_keep * moving + (1.0 - beta_keep) * mixed - step_size * momentum_gain * change,
    )


def iota(shape, axis):
    return lax.broadcasted_iota(i32, shape, axis)


def one_hot(chosen):
    return jnp.where(chosen, 1.0, 0.0).astype(bf16)


def before_matrix(n):
    return one_hot(iota((n, n), 0) < iota((n, n), 1))


def slots_of(indices, before, points, owners, cap):
    owner = lax.div(indices, jnp.full_like(indices, points))
    marks = iota((owners, indices.shape[1]), 0) == owner
    counts = jnp.where(marks, 1.0, 0.0)
    earlier = mm(counts.astype(bf16), before, 1, 0)
    rank = jnp.sum(counts * earlier, axis=0, keepdims=True)
    return owner * cap + rank.astype(i32)


def point_rows(indices, slots, me, points, cap):
    held = iota((cap, indices.shape[1]), 0) + me * cap == slots
    local = (indices - me * points + 1).astype(f32)
    point = jnp.sum(jnp.where(held, local, 0.0), axis=1, keepdims=True).astype(i32) - 1
    return one_hot(iota((cap, points), 1) == point)


def start_all(pairs, sems):
    copies = [pltpu.make_async_copy(a, b, sems.at[n]) for n, (a, b) in enumerate(pairs)]
    for copy in copies:
        copy.start()
    return copies


def wait_all(copies):
    for copy in copies:
        copy.wait()


def group_row(blocks, u, group, count):
    return blocks[u : u + 1, pl.ds(pl.multiple_of(group * count, count), count)]


def pack_kernel(count, cap, owners, blocks_hbm, feats_hbm, out_hbm, blocks, feats, packed, sems):
    row, me = lax.axis_index("rows"), lax.axis_index("pts")
    points = feats.shape[0]
    reads = start_all([(blocks_hbm, blocks), (feats_hbm, feats)], sems)
    before = before_matrix(count)
    reads[0].wait()
    rows = []
    for u in range(UPDATES):
        indices = group_row(blocks, u, row, count)
        slots = slots_of(indices, before, points, owners, cap)
        rows.append(point_rows(indices, slots, me, points, cap))
    reads[1].wait()
    for u in range(UPDATES):
        packed[u * cap : (u + 1) * cap, :] = mm(rows[u], feats[...], 1, 0).astype(bf16)
    wait_all(start_all([(packed, out_hbm)], sems))


def two_digits(row):
    high = lax.shift_right_logical(row, jnp.full_like(row, 7))
    shape = (8, row.shape[1])
    value = jnp.where(iota(shape, 0) == 0, high, lax.bitwise_and(row, jnp.full_like(row, 127)))
    return value.astype(f32).astype(bf16)


def from_digits(digits):
    return (digits[0:1] * 128.0 + digits[1:2]).astype(i32)


def prepare_kernel(
    count, cap, owners,
    blocks_hbm, pivots_hbm, w_hbm, z_hbm, t_hbm,
    coef_hbm, offset_hbm, rows_hbm, ids_hbm, starts_hbm, chosen_hbm,
    blocks, pivots, w, z, t, coef, offset, rows, ids, starts, chosen, sems, out_sems,
):
    row, me = lax.axis_index("rows"), lax.axis_index("pts")
    points, outputs = w.shape
    pairs = [(blocks_hbm, blocks), (pivots_hbm, pivots), (w_hbm, w), (z_hbm, z), (t_hbm, t)]
    reads = start_all(pairs, sems)
    before = before_matrix(count)
    wait_all(reads[:2])
    groups = blocks.shape[1] // count
    for u in range(UPDATES):
        pivot = pivots[u : u + 1, :]
        found = jnp.zeros((8, pivot.shape[1]), f32)
        for g in range(groups):
            n = u * groups + g
            indices = blocks[u : u + 1, g * count : (g + 1) * count]
            owner = lax.div(indices, jnp.full_like(indices, points))
            owner_ids = iota((owners, count), 0)
            marks = jnp.where(owner_ids == owner, 1.0, 0.0)
            earlier = mm(marks.astype(bf16), before, 1, 0)
            start = jnp.sum(jnp.where(owner < owner_ids, 1.0, 0.0), axis=1, keepdims=True)
            rank = jnp.sum(marks * earlier, axis=0, keepdims=True)
            place = (rank + jnp.sum(marks * start, axis=0, keepdims=True)).astype(i32)
            held = owner * cap + rank.astype(i32)
            rows[u, g * cap : (g + 1) * cap, :] = point_rows(indices, held, me, points, cap)
            ordered = one_hot(iota((count, count), 0) == place)
            ids[n : n + 1, :] = from_digits(mm(two_digits(indices), ordered, 1, 1))
            diagonal = iota((owners, 128), 0) == iota((owners, 128), 1)
            starts[n : n + 1, :] = jnp.sum(
                jnp.where(diagonal, start, 0.0), axis=0, keepdims=True
            ).astype(i32)
            at_pivot = one_hot(iota((count, pivot.shape[1]), 0) + g * count == pivot)
            found += mm(two_digits(place + g * count), at_pivot, 1, 0)
        chosen[u : u + 1, :] = from_digits(found)
    pairs = [(starts, starts_hbm), (ids, ids_hbm), (chosen, chosen_hbm), (rows, rows_hbm)]
    writes = start_all(pairs, out_sems)
    wait_all(reads[2:])
    current, moving = w[...], z[...]
    goal = t[...].astype(f32).T
    for u in range(UPDATES):
        mixed = mixed_of(current, moving).T
        high, low = split_two(ridge_term * mixed - goal)
        coef[u] = mixed.astype(bf16)
        local = ids[pl.ds(u * groups + row, 1), :] - me * points
        place = one_hot(iota((points, count), 0) == local)
        offset[u] = mm(high, place, 1, 0) + mm(low, place, 1, 0)
        current, moving = stepped(current, moving, None)
        for a, b in ((coef, coef_hbm), (offset, offset_hbm)):
            writes.append(pltpu.make_async_copy(a.at[u], b.at[u], out_sems.at[len(writes)]))
            writes[-1].start()
    wait_all(writes)


def extended(rows, axis, first):
    rest = -0.5 * jnp.sum(jnp.square(rows.astype(f32)), axis=axis, keepdims=True)
    parts = []
    for _ in range(3):
        parts.append(rest.astype(bf16).astype(f32))
        rest = rest - parts[-1]
    parts = parts + [1.0] * 3 if first else [1.0] * 3 + parts
    at = iota(rows.shape, axis)
    extra = jnp.zeros(rows.shape, f32)
    for n, part in enumerate(parts):
        extra = jnp.where(at == n, part, extra)
    return jnp.concatenate([rows.astype(bf16), extra.astype(bf16)], axis=axis)


def exponent(left, right):
    return mm(left, right, 1, 0) * (7.0 / (left.shape[1] // 2) * math.log2(math.e))


CHUNK = 256


def compact_kernel(*refs):
    *came_hbm, starts_hbm, block_hbm, came, starts, wide, block, sems = refs
    row, me = lax.axis_index("rows"), lax.axis_index("pts")
    owners, deep, _ = came.shape
    cap = deep // UPDATES
    groups = starts.shape[0] // UPDATES
    count = block.shape[2]
    pairs = [(a, came.at[k]) for k, a in enumerate(came_hbm)]
    wait_all(start_all([*pairs, (starts_hbm, starts)], sems))
    for u in range(UPDATES):
        for o in range(owners):
            start = starts[u * groups + row, o]
            rows = came[lax.bitwise_xor(me, o), u * cap : (u + 1) * cap, :]
            wide[u, pl.ds(start, cap), :] = rows.astype(f32)
        block[u] = wide[u, 0:count, :].T.astype(bf16)
    wait_all(start_all([(block, block_hbm)], sems))


def sums_kernel(
    block_hbm, feats_hbm, coef_hbm, offset_hbm, pieces_hbm,
    block, feats, coef, offset, tile, pieces, sems,
):
    points, count = tile.shape
    outputs = coef.shape[1]
    pairs = [(block_hbm, block), (feats_hbm, feats), (coef_hbm, coef), (offset_hbm, offset)]
    reads = start_all(pairs, sems)
    wait_all(reads[:2])
    left = extended(feats[...], 1, True)
    for u in range(UPDATES):
        right = extended(block[u], 0, False)
        for c in range(0, points, CHUNK):
            tile[c : c + CHUNK, :] = jnp.exp2(exponent(left[c : c + CHUNK], right)).astype(bf16)
        if u == 0:
            wait_all(reads[2:])
        total = offset[u] + mm(coef[u], tile[...], 1, 0)
        devices, _, lanes = pieces.shape
        own = outputs // devices
        for d in range(devices):
            part = total[d * own : (d + 1) * own]
            pieces[d, 2 * own * u : 2 * own * (u + 1), :] = jnp.concatenate(
                [part[:, :lanes], part[:, lanes:]], axis=0
            ).astype(bf16)
    wait_all(start_all([(pieces, pieces_hbm)], sems))


def factors_kernel(
    b0_hbm, b1_hbm, b2_hbm, b3_hbm, ids_hbm, pivots_hbm, factor_hbm, cross_hbm,
    feats, ids, pivots, factor, cross, sems,
):
    row = lax.axis_index("rows")
    groups, _, width, count = feats.shape
    pairs = [(b_hbm, feats.at[k]) for k, b_hbm in enumerate((b0_hbm, b1_hbm, b2_hbm, b3_hbm))]
    wait_all(start_all(pairs + [(ids_hbm, ids), (pivots_hbm, pivots)], sems))
    places = [lax.bitwise_xor(row, k) for k in range(groups)]
    rights = [[extended(feats[k, u], 0, False) for k in range(groups)] for u in range(UPDATES)]
    for u in range(UPDATES):
        chosen_feats = jnp.zeros((width, pivots.shape[1]), f32)
        for k in range(groups):
            chosen = iota((count, pivots.shape[1]), 0) + places[k] * count == pivots[u : u + 1, :]
            chosen_feats += mm(feats[k, u], one_hot(chosen), 1, 0)
        left = extended(chosen_feats.T, 1, True)
        for k in range(groups):
            start = pl.multiple_of(places[k] * count, count)
            value = jnp.exp2(exponent(left, rights[u][k]))
            factor[u, :, pl.ds(start, count)] = value.astype(bf16)
    writes = start_all([(factor, factor_hbm)], sems)
    sent = 1
    for k in range(groups):
        left = extended(feats[k, 0].astype(f32).T, 1, True)
        left_points = ids[pl.ds(places[k], 1), :].astype(f32)
        left_points = jnp.broadcast_to(left_points, (8, count)).T[:, 0:1]
        for m in range(groups):
            right_points = ids[pl.ds(groups + places[m], 1), :].astype(f32)
            for c in range(0, count, CHUNK):
                rows = slice(c, c + CHUNK)
                power = exponent(left[rows], rights[1][m])
                power = jnp.where(left_points[rows] == right_points, math.log2(1.0 + ridge_term), power)
                cross[m, k, rows, :] = jnp.exp2(power).astype(bf16)
            start = pl.multiple_of(places[k] * count, count)
            copy = pltpu.make_async_copy(
                cross.at[m, k], cross_hbm.at[places[m], pl.ds(start, count), :], sems.at[sent]
            )
            copy.start()
            writes.append(copy)
            sent += 1
    wait_all(writes)


def chain_kernel(
    cap, owners,
    summed_hbm, factor_hbm, core_hbm, cross_hbm, starts_hbm, out_hbm,
    summed, factor, core, cross, starts, packed, sems,
):
    groups, _, count = cross.shape
    own = summed.shape[1] // (2 * UPDATES)
    pairs = [(summed_hbm, summed)]
    for u in range(UPDATES):
        pairs += [(factor_hbm.at[u], factor.at[u]), (core_hbm.at[u], core.at[u])]
        if u == 0:
            pairs += [(starts_hbm, starts)]
            pairs += [(cross_hbm.at[g], cross.at[g]) for g in range(groups)]
    reads = start_all(pairs, sems)
    first, *reads = reads
    first.wait()
    step = None
    for u in range(UPDATES):
        sums = []
        for g in range(groups):
            part = summed[g * owners, 2 * own * u : 2 * own * (u + 1), :].astype(f32)
            for o in range(1, owners):
                part += summed[g * owners + o, 2 * own * u : 2 * own * (u + 1), :].astype(f32)
            part = jnp.concatenate([part[:own], part[own:]], axis=1)
            if u:
                reads[3 + g].wait()
                part -= mix_per_step * mm(step, cross[g], 1, 0)
            sums.append(part)
        resid = jnp.concatenate(sums, axis=1)
        wait_all(reads[0:3] if u == 0 else reads[3 + groups :])
        proj = mm(resid.astype(bf16), factor[u], 1, 1)
        lifted = mm(proj.astype(bf16), core[u], 1, 1).astype(bf16)
        step = (resid - mm(lifted, factor[u], 1, 0)).astype(bf16)
        half = groups // 2
        for o in range(owners):
            lanes = []
            for g in range(groups):
                part = step[:, g * count : (g + 1) * count].astype(f32)
                back = lax.rem(count - starts[u * groups + g, o], count)
                lanes.append(pltpu.roll(part, back, 1)[:, :cap])
            packed[o, 2 * own * u : 2 * own * (u + 1), :] = jnp.concatenate(
                [jnp.concatenate(lanes[h * half : (h + 1) * half], axis=1) for h in range(2)], axis=0
            ).astype(bf16)
    wait_all(start_all([(packed, out_hbm)], sems))


def finish_kernel(
    g0_hbm, g1_hbm, g2_hbm, g3_hbm, w_hbm, z_hbm, rows_hbm, w_out, z_out,
    got, w, z, rows, steps, w_new, z_new, sems, out_sems,
):
    row = lax.axis_index("rows")
    points = w.shape[0]
    sources, deep, lanes = got.shape
    own = deep // (2 * UPDATES)
    chunks = range(0, points, CHUNK)
    pairs = []
    for k, g_hbm in enumerate((g0_hbm, g1_hbm, g2_hbm, g3_hbm)):
        size = g_hbm.shape[0]
        first = pl.multiple_of(lax.bitwise_xor(row, k) * size, size)
        pairs.append((g_hbm, got.at[pl.ds(first, size)]))
    for c in chunks:
        part = slice(c, c + CHUNK)
        pairs += [(rows_hbm.at[:, :, part], rows.at[:, :, part])]
        pairs += [(w_hbm.at[part], w.at[part]), (z_hbm.at[part], z.at[part])]
    reads = start_all(pairs, sems)
    wait_all(reads[:4])
    reads = reads[4:]
    wide = got[...].astype(f32)
    for u in range(UPDATES):
        for h in range(2):
            first = own * (2 * u + h)
            part = wide[:, first : first + own, :].reshape(sources * own, lanes)
            steps[u, :, h * lanes : (h + 1) * lanes] = part.astype(bf16)
    writes = []
    for n, c in enumerate(chunks):
        part = slice(c, c + CHUNK)
        wait_all(reads[3 * n : 3 * n + 3])
        current, moving = w[part, :], z[part, :]
        for u in range(UPDATES):
            change = mm(steps[u], rows[u, :, part], 1, 0).T
            current, moving = stepped(current, moving, change)
        w_new[part, :] = current
        z_new[part, :] = moving
        for m, (a, b) in enumerate(((w_new, w_out), (z_new, z_out))):
            copy = pltpu.make_async_copy(a.at[part], b.at[part], out_sems.at[2 * n + m])
            copy.start()
            writes.append(copy)
    wait_all(writes)


VMEM = pl.BlockSpec(memory_space=pltpu.VMEM)
HBM = pl.BlockSpec(memory_space=pltpu.HBM)
in_smem = type(pltpu.SMEM((1,), i32))


def like(shape, dtype=bf16):
    return jax.ShapeDtypeStruct(shape, dtype)


def call(body, outs, inside, *args, near=0, sems=(), flops=0, grant=62):
    moved = sum(math.prod(o.shape) * o.dtype.itemsize for o in [*outs, *args])
    return pl.pallas_call(
        body,
        out_shape=outs,
        in_specs=[VMEM] * near + [HBM] * (len(args) - near),
        out_specs=[HBM] * len(outs),
        scratch_shapes=[
            x if isinstance(x, in_smem) else pltpu.VMEM(x.shape, x.dtype) for x in inside
        ]
        + [pltpu.SemaphoreType.DMA((n,)) for n in sems],
        compiler_params=pltpu.CompilerParams(vmem_limit_bytes=grant * 2**20),
        cost_estimate=pl.CostEstimate(flops=int(flops), bytes_accessed=moved, transcendentals=0),
    )(*args)


def swap(value, axis, k):
    return lax.ppermute(value, axis, [(i, i ^ k) for i in range(lax.axis_size(axis))])


def with_kernels(features, targets, coefficients, momentum, block_index, pivot_index, core):
    rows, owners = lax.axis_size("rows"), lax.axis_size("pts")
    points, width = features.shape
    block = block_index.shape[1]
    rank = pivot_index.shape[1]
    outputs = coefficients.shape[1]
    count = block // rows
    cap = 3 * count // owners
    devices = rows * owners
    own = outputs // devices
    deep = 2 * own * UPDATES
    half = rows // 2
    wide = like(coefficients.shape, f32)

    (packed,) = call(
        functools.partial(pack_kernel, count, cap, owners),
        [like((UPDATES * cap, width))],
        [block_index, features, like((UPDATES * cap, width))],
        block_index,
        features,
        sems=(2,),
    )
    came = {k: swap(packed, "pts", k) for k in reversed(range(owners // 2, owners))}
    kept = [
        like((UPDATES, outputs, points)),
        like((UPDATES, outputs, count), f32),
        like((UPDATES, rows * cap, points)),
        like((UPDATES * rows, count), i32),
        like((UPDATES * rows, 128), i32),
        like((UPDATES, rank), i32),
    ]
    given = [block_index, pivot_index, coefficients, momentum, targets]
    coef, offset, place, ids, starts, chosen = call(
        functools.partial(prepare_kernel, count, cap, owners),
        kept,
        given + kept,
        *given,
        sems=(5, 4 + 2 * UPDATES),
    )
    again, starts = lax.optimization_barrier((packed, starts))
    came.update({k: swap(again, "pts", k) for k in reversed(range(1, owners // 2))})
    feats = like((UPDATES, width, count))
    inside_starts = pltpu.SMEM(starts.shape, i32)
    (mine,) = call(
        compact_kernel,
        [feats],
        [
            like((owners, *packed.shape)),
            inside_starts,
            like((UPDATES, count + cap, width), f32),
            feats,
        ],
        packed,
        *[came[k] for k in range(1, owners)],
        starts,
        sems=(owners + 1,),
    )
    beside, across = swap(mine, "rows", 1), swap(mine, "rows", 2)
    pieces = like((devices, deep, count // 2))
    (pieces,) = call(
        sums_kernel,
        [pieces],
        [feats, features, coef, offset, like((points, count)), pieces],
        mine,
        features,
        coef,
        offset,
        sems=(4,),
        flops=2.0 * UPDATES * points * count * (2 * width + outputs),
    )
    pieces, across = lax.optimization_barrier((pieces, across))
    summed = lax.all_to_all(pieces, ("rows", "pts"), 0, 0, tiled=True)
    kept = [like((UPDATES, rank, block)), like((rows, block, count))]
    factor, cross = call(
        factors_kernel,
        kept,
        [
            like((rows, *feats.shape)),
            ids,
            chosen,
            kept[0],
            like((rows, rows, count, count)),
        ],
        mine,
        beside,
        across,
        swap(across, "rows", 1),
        ids,
        chosen,
        sems=(rows * rows + 1,),
        flops=2.0 * width * block * (UPDATES * rank + block),
    )
    pieces = like((owners, deep, half * cap))
    (steps,) = call(
        functools.partial(chain_kernel, cap, owners),
        [pieces],
        [summed, factor, core, cross, inside_starts, pieces],
        summed,
        factor,
        core,
        cross,
        starts,
        sems=(2 * UPDATES + 2 + rows,),
    )
    got = lax.all_to_all(steps, "pts", 0, 0, tiled=True)
    beside, across = swap(got, "rows", 1), swap(got, "rows", 2)
    parts = points // CHUNK
    return call(
        finish_kernel,
        [wide] * 2,
        [
            like((devices, deep, half * cap)),
            wide,
            wide,
            place,
            like((UPDATES, outputs, rows * cap)),
            wide,
            wide,
        ],
        got,
        beside,
        across,
        swap(across, "rows", 1),
        coefficients,
        momentum,
        place,
        sems=(rows + 3 * parts, 2 * parts),
    )


def kernel_tile(left_rows, right_rows):
    inner_prod = mm(left_rows, right_rows, 1, 1)
    left_sq = jnp.sum(jnp.square(left_rows.astype(f32)), axis=1)
    right_sq = jnp.sum(jnp.square(right_rows.astype(f32)), axis=1)
    squared = left_sq[:, None] + right_sq[None, :] - 2.0 * inner_prod
    return jnp.exp(squared * (-3.5 / left_rows.shape[1])).astype(bf16)


def with_operations(features, targets, coefficients, momentum, block_index, pivot_index, core):
    row_count, pts_count = lax.axis_size("rows"), lax.axis_size("pts")
    row_id, pts_id = lax.axis_index("rows"), lax.axis_index("pts")
    points = features.shape[0]
    block = block_index.shape[1]
    outputs = coefficients.shape[1]
    per_row = block // row_count
    per_device = per_row // pts_count
    row_cols = outputs // row_count
    own_cols = row_cols // pts_count
    first = row_id * row_cols
    current, moving, goal = (
        lax.dynamic_slice_in_dim(value, first, row_cols, axis=1).T.astype(f32)
        for value in (coefficients, momentum, targets)
    )
    ids = iota((points, 1), 0) + pts_id * points
    place = [(ids == block_index[u][None, :]).astype(bf16) for u in range(UPDATES)]
    own_rows = []
    for u in range(UPDATES):
        mine = lax.dynamic_slice_in_dim(place[u], row_id * per_row, per_row, axis=1)
        own_rows.append(mm(mine, features, 0, 0).astype(bf16).reshape(pts_count, per_device, -1))
    came = lax.all_to_all(jnp.concatenate(own_rows, axis=1), "pts", 0, 0, tiled=False)
    chunk = jnp.sum(came.astype(f32), axis=0).astype(bf16)
    spread = lax.all_gather(lax.all_gather(chunk, "pts", axis=0), "rows", axis=0)
    spread = spread.reshape(row_count, pts_count, UPDATES, per_device, features.shape[1])
    all_steps = []
    for u in range(UPDATES):
        block_feats = spread[:, :, u].reshape(block, features.shape[1])
        mixed = mixed_of(current, moving)
        high, low = split_two(ridge_term * mixed - goal)
        tile = kernel_tile(features, block_feats)
        partial_value = (
            mm(mixed.astype(bf16), tile, 1, 0) + mm(high, place[u], 1, 0) + mm(low, place[u], 1, 0)
        )
        pieces = partial_value.astype(bf16).reshape(pts_count, own_cols, block)
        summed = lax.all_to_all(pieces, "pts", 0, 0, tiled=False)
        resid = jnp.sum(summed.astype(f32), axis=0)
        at_pivot = (iota((block, 1), 0) == pivot_index[u][None, :]).astype(bf16)
        factor = kernel_tile(block_feats, mm(at_pivot, block_feats, 0, 0).astype(bf16))
        proj = mm(resid.astype(bf16), factor, 1, 0)
        lifted = mm(proj.astype(bf16), core[u], 1, 1).astype(bf16)
        step_bf = (resid - mm(lifted, factor, 1, 1)).astype(bf16)
        steps = lax.all_gather(step_bf, "pts", axis=0, tiled=True)
        change = mm(steps, place[u], 1, 1)
        all_steps.append(change.astype(bf16))
        current, moving = stepped(current, moving, change)
    gathered = lax.all_gather(jnp.stack(all_steps), "rows", axis=1, tiled=True)
    current, moving = coefficients, momentum
    for u in range(UPDATES):
        current, moving = stepped(current, moving, gathered[u].T.astype(f32))
    return (current, moving)


def shards(features, targets, coefficients, momentum, block_index, pivot_index, nystrom_core):
    rows, owners = lax.axis_size("rows"), lax.axis_size("pts")
    count = block_index.shape[1] // rows
    fits = rows == 4 and owners == 8 and coefficients.shape[1] == 8 * rows * owners
    fits = fits and coefficients.shape[0] % CHUNK == 0 and count % CHUNK == 0 and (3 * count // owners) % 64 == 0
    plan = with_kernels if fits else with_operations
    return plan(
        features, targets, coefficients, momentum, block_index, pivot_index, nystrom_core
    )


def solution(mesh):
    in_specs = (P("pts", None), P("pts", None), P("pts", None), P("pts", None), P(), P(), P())
    out_specs = (P("pts", None), P("pts", None))
    return jax.shard_map(shards, mesh=mesh, in_specs=in_specs, out_specs=out_specs, check_vma=False)
```

```python
import functools
import math

import jax
import jax.numpy as jnp
from jax import lax
from jax.experimental import pallas as pl
from jax.experimental.pallas import tpu as pltpu
from jax.sharding import PartitionSpec as P

UPDATES = 2


alpha_mix = 0.6
beta_keep = 0.9
step_size = 0.2
momentum_gain = 1.5
ridge_term = 1.0

f32 = jnp.float32
bf16 = jnp.bfloat16
i32 = jnp.int32


def mm(a, b, ca, cb):
    return lax.dot_general(a, b, (((ca,), (cb,)), ((), ())), preferred_element_type=f32)


def split_two(value):
    high = value.astype(bf16)
    return high, (value - high.astype(f32)).astype(bf16)


def mixed_of(current, moving):
    return alpha_mix * moving + (1.0 - alpha_mix) * current


mix_per_step = alpha_mix * step_size * momentum_gain + (1.0 - alpha_mix) * step_size


def stepped(current, moving, change):
    mixed = mixed_of(current, moving)
    if change is None:
        return mixed, beta_keep * moving + (1.0 - beta_keep) * mixed
    return (
        mixed - step_size * change,
        beta_keep * moving + (1.0 - beta_keep) * mixed - step_size * momentum_gain * change,
    )


def iota(shape, axis):
    return lax.broadcasted_iota(i32, shape, axis)


def one_hot(chosen):
    return jnp.where(chosen, 1.0, 0.0).astype(bf16)


def before_matrix(n):
    return one_hot(iota((n, n), 0) < iota((n, n), 1))


def owners_of(indices, before, points, owners):
    owner = lax.div(indices, jnp.full_like(indices, points))
    owner_ids = iota((owners, indices.shape[1]), 0)
    marks = jnp.where(owner_ids == owner, 1.0, 0.0)
    earlier = mm(marks.astype(bf16), before, 1, 0)
    rank = jnp.sum(marks * earlier, axis=0, keepdims=True)
    start = jnp.sum(jnp.where(owner < owner_ids, 1.0, 0.0), axis=1, keepdims=True)
    return marks, rank, start


def sorted_places(marks, rank, start):
    return (rank + jnp.sum(marks * start, axis=0, keepdims=True)).astype(i32)


def lane_row(column):
    n = column.shape[0]
    diagonal = iota((n, 128), 0) == iota((n, 128), 1)
    return jnp.sum(jnp.where(diagonal, column, 0.0), axis=0, keepdims=True).astype(i32)


def sorted_points(indices, place):
    count = indices.shape[1]
    return from_digits(mm(two_digits(indices), one_hot(iota((count, count), 0) == place), 1, 1))


def two_digits(row):
    high = lax.shift_right_logical(row, jnp.full_like(row, 7))
    shape = (8, row.shape[1])
    value = jnp.where(iota(shape, 0) == 0, high, lax.bitwise_and(row, jnp.full_like(row, 127)))
    return value.astype(f32).astype(bf16)


def from_digits(digits):
    return (digits[0:1] * 128.0 + digits[1:2]).astype(i32)


def start_all(pairs, sems):
    copies = [pltpu.make_async_copy(a, b, sems.at[n]) for n, (a, b) in enumerate(pairs)]
    for copy in copies:
        copy.start()
    return copies


def wait_all(copies):
    for copy in copies:
        copy.wait()


def group_row(blocks, u, group, count):
    return blocks[u : u + 1, pl.ds(pl.multiple_of(group * count, count), count)]


def pack_kernel(count, cap, owners, blocks_hbm, feats_hbm, out_hbm, blocks, feats, packed, sems):
    row, me = lax.axis_index("rows"), lax.axis_index("pts")
    points = feats.shape[0]
    reads = start_all([(blocks_hbm, blocks), (feats_hbm, feats)], sems)
    before = before_matrix(count)
    reads[0].wait()
    rows = []
    for u in range(UPDATES):
        indices = group_row(blocks, u, row, count)
        local = indices - me * points
        mine = jnp.where((local >= 0) & (local < points), 1.0, 0.0)
        rank = mm(jnp.broadcast_to(mine, (8, count)).astype(bf16), before, 1, 0)[0:1]
        held = (iota((cap, count), 0) == rank.astype(i32)) & (mine > 0.0)
        point = jnp.sum(jnp.where(held, (local + 1).astype(f32), 0.0), axis=1, keepdims=True)
        rows.append(one_hot(iota((cap, points), 1) == point.astype(i32) - 1))
    reads[1].wait()
    for u in range(UPDATES):
        packed[u * cap : (u + 1) * cap, :] = mm(rows[u], feats[...], 1, 0).astype(bf16)
    wait_all(start_all([(packed, out_hbm)], sems))


def prepare_kernel(
    count, owners,
    blocks_hbm, w_hbm, z_hbm, t_hbm, coef_hbm, offset_hbm, starts_hbm,
    blocks, w, z, t, coef, offset, starts, sems, out_sems,
):
    row, me = lax.axis_index("rows"), lax.axis_index("pts")
    points, outputs = w.shape
    reads = start_all([(blocks_hbm, blocks), (w_hbm, w), (z_hbm, z), (t_hbm, t)], sems)
    before = before_matrix(count)
    reads[0].wait()
    locals_of = []
    for u in range(UPDATES):
        indices = group_row(blocks, u, row, count)
        marks, rank, start = owners_of(indices, before, points, owners)
        starts[u : u + 1, :] = lane_row(start)
        locals_of.append(sorted_points(indices, sorted_places(marks, rank, start)) - me * points)
    writes = start_all([(starts, starts_hbm)], out_sems)
    wait_all(reads[1:])
    current, moving = w[...], z[...]
    goal = t[...].astype(f32).T
    for u in range(UPDATES):
        mixed = mixed_of(current, moving).T
        high, low = split_two(ridge_term * mixed - goal)
        coef[u] = mixed.astype(bf16)
        place = one_hot(iota((points, count), 0) == locals_of[u])
        offset[u] = mm(high, place, 1, 0) + mm(low, place, 1, 0)
        current, moving = stepped(current, moving, None)
        for a, b in ((coef, coef_hbm), (offset, offset_hbm)):
            writes.append(pltpu.make_async_copy(a.at[u], b.at[u], out_sems.at[len(writes)]))
            writes[-1].start()
    wait_all(writes)


def order_kernel(
    count, points, owners,
    blocks_hbm, pivots_hbm, ids_hbm, starts_hbm, chosen_hbm,
    blocks, pivots, ids, starts, chosen, sems,
):
    wait_all(start_all([(blocks_hbm, blocks), (pivots_hbm, pivots)], sems))
    before = before_matrix(count)
    groups = blocks.shape[1] // count
    for u in range(UPDATES):
        pivot = pivots[u : u + 1, :]
        found = jnp.zeros((8, pivot.shape[1]), f32)
        for g in range(groups):
            n = u * groups + g
            indices = blocks[u : u + 1, g * count : (g + 1) * count]
            marks, rank, start = owners_of(indices, before, points, owners)
            place = sorted_places(marks, rank, start)
            ids[n : n + 1, :] = sorted_points(indices, place)
            starts[n : n + 1, :] = lane_row(start)
            at_pivot = one_hot(iota((count, pivot.shape[1]), 0) + g * count == pivot)
            found += mm(two_digits(place + g * count), at_pivot, 1, 0)
        chosen[u : u + 1, :] = from_digits(found)
    wait_all(start_all([(ids, ids_hbm), (starts, starts_hbm), (chosen, chosen_hbm)], sems))


def slots_kernel(count, points, cap, blocks_hbm, slots_hbm, blocks, slots, sems):
    me = lax.axis_index("pts")
    wait_all(start_all([(blocks_hbm, blocks)], sems))
    before = before_matrix(count)
    groups = blocks.shape[1] // count
    for u in range(UPDATES):
        found = jnp.zeros((8, groups * cap), f32)
        for g in range(groups):
            local = blocks[u : u + 1, g * count : (g + 1) * count] - me * points
            mine = (local >= 0) & (local < points)
            counts = jnp.where(mine, 1.0, 0.0)
            rank = mm(jnp.broadcast_to(counts, (8, count)).astype(bf16), before, 1, 0)[0:1]
            held = jnp.where(mine, rank.astype(i32) + g * cap, -1)
            chosen = one_hot(iota((groups * cap, count), 0) == held)
            found += mm(two_digits(jnp.where(mine, local + 1, 0)), chosen, 1, 1)
        slots[u : u + 1, :] = from_digits(found) - 1
    wait_all(start_all([(slots, slots_hbm)], sems))


def extended(rows, axis, first):
    rest = -0.5 * jnp.sum(jnp.square(rows.astype(f32)), axis=axis, keepdims=True)
    parts = []
    for _ in range(3):
        parts.append(rest.astype(bf16).astype(f32))
        rest = rest - parts[-1]
    parts = parts + [1.0] * 3 if first else [1.0] * 3 + parts
    at = iota(rows.shape, axis)
    extra = jnp.zeros(rows.shape, f32)
    for n, part in enumerate(parts):
        extra = jnp.where(at == n, part, extra)
    return jnp.concatenate([rows.astype(bf16), extra.astype(bf16)], axis=axis)


def exponent(left, right):
    return mm(left, right, 1, 0) * (7.0 / (left.shape[1] // 2) * math.log2(math.e))


CHUNK = 256


def compact_kernel(*refs):
    *came_hbm, starts_hbm, block_hbm, came, starts, wide, block, sems = refs
    me = lax.axis_index("pts")
    owners, deep, _ = came.shape
    cap = deep // UPDATES
    count = block.shape[2]
    pairs = [(a, came.at[k]) for k, a in enumerate(came_hbm)]
    wait_all(start_all([*pairs, (starts_hbm, starts)], sems))
    for u in range(UPDATES):
        for o in range(owners):
            start = starts[u, o]
            rows = came[lax.bitwise_xor(me, o), u * cap : (u + 1) * cap, :]
            wide[u, pl.ds(start, cap), :] = rows.astype(f32)
        block[u] = wide[u, 0:count, :].T.astype(bf16)
    wait_all(start_all([(block, block_hbm)], sems))


def sums_kernel(
    block_hbm, feats_hbm, coef_hbm, offset_hbm, pieces_hbm,
    block, feats, coef, offset, tile, pieces, sems,
):
    points, count = tile.shape
    outputs = coef.shape[1]
    pairs = [(block_hbm, block), (feats_hbm, feats), (coef_hbm, coef), (offset_hbm, offset)]
    reads = start_all(pairs, sems)
    wait_all(reads[:2])
    left = extended(feats[...], 1, True)
    for u in range(UPDATES):
        right = extended(block[u], 0, False)
        for c in range(0, points, CHUNK):
            tile[c : c + CHUNK, :] = jnp.exp2(exponent(left[c : c + CHUNK], right)).astype(bf16)
        if u == 0:
            wait_all(reads[2:])
        total = offset[u] + mm(coef[u], tile[...], 1, 0)
        devices, _, lanes = pieces.shape
        own = outputs // devices
        for d in range(devices):
            part = total[d * own : (d + 1) * own]
            pieces[d, 2 * own * u : 2 * own * (u + 1), :] = jnp.concatenate(
                [part[:, :lanes], part[:, lanes:]], axis=0
            ).astype(bf16)
    wait_all(start_all([(pieces, pieces_hbm)], sems))


def factors_kernel(
    b0_hbm, b1_hbm, b2_hbm, b3_hbm, ids_hbm, pivots_hbm, factor_hbm, cross_hbm,
    feats, ids, pivots, factor, cross, sems,
):
    row = lax.axis_index("rows")
    groups, _, width, count = feats.shape
    pairs = [(b_hbm, feats.at[k]) for k, b_hbm in enumerate((b0_hbm, b1_hbm, b2_hbm, b3_hbm))]
    wait_all(start_all(pairs + [(ids_hbm, ids), (pivots_hbm, pivots)], sems))
    places = [lax.bitwise_xor(row, k) for k in range(groups)]
    rights = [[extended(feats[k, u], 0, False) for k in range(groups)] for u in range(UPDATES)]
    for u in range(UPDATES):
        chosen_feats = jnp.zeros((width, pivots.shape[1]), f32)
        for k in range(groups):
            chosen = iota((count, pivots.shape[1]), 0) + places[k] * count == pivots[u : u + 1, :]
            chosen_feats += mm(feats[k, u], one_hot(chosen), 1, 0)
        left = extended(chosen_feats.T, 1, True)
        for k in range(groups):
            start = pl.multiple_of(places[k] * count, count)
            value = jnp.exp2(exponent(left, rights[u][k]))
            factor[u, :, pl.ds(start, count)] = value.astype(bf16)
    writes = start_all([(factor, factor_hbm)], sems)
    sent = 1
    for k in range(groups):
        left = extended(feats[k, 0].astype(f32).T, 1, True)
        left_points = ids[pl.ds(places[k], 1), :].astype(f32)
        left_points = jnp.broadcast_to(left_points, (8, count)).T[:, 0:1]
        for m in range(groups):
            right_points = ids[pl.ds(groups + places[m], 1), :].astype(f32)
            for c in range(0, count, CHUNK):
                rows = slice(c, c + CHUNK)
                power = exponent(left[rows], rights[1][m])
                power = jnp.where(left_points[rows] == right_points, math.log2(1.0 + ridge_term), power)
                cross[m, k, rows, :] = jnp.exp2(power).astype(bf16)
            start = pl.multiple_of(places[k] * count, count)
            copy = pltpu.make_async_copy(
                cross.at[m, k], cross_hbm.at[places[m], pl.ds(start, count), :], sems.at[sent]
            )
            copy.start()
            writes.append(copy)
            sent += 1
    wait_all(writes)


def chain_kernel(
    cap, owners,
    summed_hbm, factor_hbm, core_hbm, cross_hbm, starts_hbm, out_hbm,
    summed, factor, core, cross, starts, packed, sems,
):
    groups, _, count = cross.shape
    own = summed.shape[1] // (2 * UPDATES)
    pairs = [(summed_hbm, summed)]
    for u in range(UPDATES):
        pairs += [(factor_hbm.at[u], factor.at[u]), (core_hbm.at[u], core.at[u])]
        if u == 0:
            pairs += [(starts_hbm, starts)]
            pairs += [(cross_hbm.at[g], cross.at[g]) for g in range(groups)]
    reads = start_all(pairs, sems)
    first, *reads = reads
    first.wait()
    step = None
    for u in range(UPDATES):
        sums = []
        for g in range(groups):
            part = summed[g * owners, 2 * own * u : 2 * own * (u + 1), :].astype(f32)
            for o in range(1, owners):
                part += summed[g * owners + o, 2 * own * u : 2 * own * (u + 1), :].astype(f32)
            part = jnp.concatenate([part[:own], part[own:]], axis=1)
            if u:
                reads[3 + g].wait()
                part -= mix_per_step * mm(step, cross[g], 1, 0)
            sums.append(part)
        resid = jnp.concatenate(sums, axis=1)
        wait_all(reads[0:3] if u == 0 else reads[3 + groups :])
        proj = mm(resid.astype(bf16), factor[u], 1, 1)
        lifted = mm(proj.astype(bf16), core[u], 1, 1).astype(bf16)
        step = (resid - mm(lifted, factor[u], 1, 0)).astype(bf16)
        half = groups // 2
        for o in range(owners):
            lanes = []
            for g in range(groups):
                part = step[:, g * count : (g + 1) * count].astype(f32)
                back = lax.rem(count - starts[u * groups + g, o], count)
                lanes.append(pltpu.roll(part, back, 1)[:, :cap])
            packed[o, 2 * own * u : 2 * own * (u + 1), :] = jnp.concatenate(
                [jnp.concatenate(lanes[h * half : (h + 1) * half], axis=1) for h in range(2)], axis=0
            ).astype(bf16)
    wait_all(start_all([(packed, out_hbm)], sems))


def finish_kernel(
    g0_hbm, g1_hbm, g2_hbm, g3_hbm, slots_hbm, w_hbm, z_hbm, w_out, z_out,
    got, slots, w, z, steps, w_new, z_new, sems, out_sems,
):
    row = lax.axis_index("rows")
    points = w.shape[0]
    sources, deep, lanes = got.shape
    own = deep // (2 * UPDATES)
    chunks = range(0, points, CHUNK)
    pairs = [(slots_hbm, slots)]
    for k, g_hbm in enumerate((g0_hbm, g1_hbm, g2_hbm, g3_hbm)):
        size = g_hbm.shape[0]
        first = pl.multiple_of(lax.bitwise_xor(row, k) * size, size)
        pairs.append((g_hbm, got.at[pl.ds(first, size)]))
    for c in chunks:
        part = slice(c, c + CHUNK)
        pairs += [(w_hbm.at[part], w.at[part]), (z_hbm.at[part], z.at[part])]
    reads = start_all(pairs, sems)
    wait_all(reads[:5])
    reads = reads[5:]
    wide = got[...].astype(f32)
    for u in range(UPDATES):
        for h in range(2):
            first = own * (2 * u + h)
            part = wide[:, first : first + own, :].reshape(sources * own, lanes)
            steps[u, h * lanes : (h + 1) * lanes, :] = part.T.astype(bf16)
    writes = []
    for n, c in enumerate(chunks):
        part = slice(c, c + CHUNK)
        changes = []
        for u in range(UPDATES):
            rows = one_hot(iota((CHUNK, slots.shape[1]), 0) + c == slots[u : u + 1, :])
            changes.append(mm(rows, steps[u], 1, 0))
        wait_all(reads[2 * n : 2 * n + 2])
        current, moving = w[part, :], z[part, :]
        for change in changes:
            current, moving = stepped(current, moving, change)
        w_new[part, :] = current
        z_new[part, :] = moving
        for m, (a, b) in enumerate(((w_new, w_out), (z_new, z_out))):
            copy = pltpu.make_async_copy(a.at[part], b.at[part], out_sems.at[2 * n + m])
            copy.start()
            writes.append(copy)
    wait_all(writes)


VMEM = pl.BlockSpec(memory_space=pltpu.VMEM)
HBM = pl.BlockSpec(memory_space=pltpu.HBM)
in_smem = type(pltpu.SMEM((1,), i32))


def like(shape, dtype=bf16):
    return jax.ShapeDtypeStruct(shape, dtype)


def call(body, outs, inside, *args, near=0, sems=(), flops=0, grant=62):
    moved = sum(math.prod(o.shape) * o.dtype.itemsize for o in [*outs, *args])
    return pl.pallas_call(
        body,
        out_shape=outs,
        in_specs=[VMEM] * near + [HBM] * (len(args) - near),
        out_specs=[HBM] * len(outs),
        scratch_shapes=[
            x if isinstance(x, in_smem) else pltpu.VMEM(x.shape, x.dtype) for x in inside
        ]
        + [pltpu.SemaphoreType.DMA((n,)) for n in sems],
        compiler_params=pltpu.CompilerParams(vmem_limit_bytes=grant * 2**20),
        cost_estimate=pl.CostEstimate(flops=int(flops), bytes_accessed=moved, transcendentals=0),
    )(*args)


def swap(value, axis, k):
    return lax.ppermute(value, axis, [(i, i ^ k) for i in range(lax.axis_size(axis))])


def with_kernels(features, targets, coefficients, momentum, block_index, pivot_index, core):
    rows, owners = lax.axis_size("rows"), lax.axis_size("pts")
    points, width = features.shape
    block = block_index.shape[1]
    rank = pivot_index.shape[1]
    outputs = coefficients.shape[1]
    count = block // rows
    cap = 3 * count // owners
    devices = rows * owners
    own = outputs // devices
    deep = 2 * own * UPDATES
    half = rows // 2
    wide = like(coefficients.shape, f32)

    (packed,) = call(
        functools.partial(pack_kernel, count, cap, owners),
        [like((UPDATES * cap, width))],
        [block_index, features, like((UPDATES * cap, width))],
        block_index,
        features,
        sems=(2,),
    )
    came = {k: swap(packed, "pts", k) for k in reversed(range(owners // 2, owners))}
    kept = [
        like((UPDATES, outputs, points)),
        like((UPDATES, outputs, count), f32),
        like((8, 128), i32),
    ]
    given = [block_index, coefficients, momentum, targets]
    coef, offset, row_starts = call(
        functools.partial(prepare_kernel, count, owners),
        kept,
        given + kept,
        *given,
        sems=(4, 1 + 2 * UPDATES),
    )
    again, row_starts = lax.optimization_barrier((packed, row_starts))
    came.update({k: swap(again, "pts", k) for k in reversed(range(1, owners // 2))})
    feats = like((UPDATES, width, count))
    inside_starts = pltpu.SMEM(row_starts.shape, i32)
    (mine,) = call(
        compact_kernel,
        [feats],
        [
            like((owners, *packed.shape)),
            inside_starts,
            like((UPDATES, count + cap, width), f32),
            feats,
        ],
        packed,
        *[came[k] for k in range(1, owners)],
        row_starts,
        sems=(owners + 1,),
        grant=61,
    )
    beside, across = swap(mine, "rows", 1), swap(mine, "rows", 2)
    pieces = like((devices, deep, count // 2))
    (pieces,) = call(
        sums_kernel,
        [pieces],
        [feats, features, coef, offset, like((points, count)), pieces],
        mine,
        features,
        coef,
        offset,
        sems=(4,),
        flops=2.0 * UPDATES * points * count * (2 * width + outputs),
    )
    pieces, later_index = lax.optimization_barrier((pieces, block_index))
    kept = [like((UPDATES * rows, count), i32), like((8, 128), i32), like((UPDATES, rank), i32)]
    ids, starts, chosen = call(
        functools.partial(order_kernel, count, points, owners),
        kept,
        [block_index, pivot_index, *kept],
        later_index,
        pivot_index,
        sems=(3,),
    )
    pieces, across, ids = lax.optimization_barrier((pieces, across, ids))
    summed = lax.all_to_all(pieces, ("rows", "pts"), 0, 0, tiled=True)
    kept = [like((UPDATES, rank, block)), like((rows, block, count))]
    factor, cross = call(
        factors_kernel,
        kept,
        [
            like((rows, *feats.shape)),
            ids,
            chosen,
            kept[0],
            like((rows, rows, count, count)),
        ],
        mine,
        beside,
        across,
        swap(across, "rows", 1),
        ids,
        chosen,
        sems=(rows * rows + 2,),
        grant=61,
        flops=2.0 * width * block * (UPDATES * rank + block),
    )
    pieces = like((owners, deep, half * cap))
    (steps,) = call(
        functools.partial(chain_kernel, cap, owners),
        [pieces],
        [summed, factor, core, cross, inside_starts, pieces],
        summed,
        factor,
        core,
        cross,
        starts,
        sems=(2 * UPDATES + 2 + rows,),
        grant=61,
    )
    steps, later_index = lax.optimization_barrier((steps, block_index))
    (slots,) = call(
        functools.partial(slots_kernel, count, points, cap),
        [like((UPDATES, rows * cap), i32)],
        [block_index, like((UPDATES, rows * cap), i32)],
        later_index,
        sems=(1,),
    )
    got = lax.all_to_all(steps, "pts", 0, 0, tiled=True)
    beside, across = swap(got, "rows", 1), swap(got, "rows", 2)
    parts = points // CHUNK
    return call(
        finish_kernel,
        [wide] * 2,
        [
            like((devices, deep, half * cap)),
            slots,
            wide,
            wide,
            like((UPDATES, rows * cap, outputs)),
            wide,
            wide,
        ],
        got,
        beside,
        across,
        swap(across, "rows", 1),
        slots,
        coefficients,
        momentum,
        sems=(1 + rows + 2 * parts, 2 * parts),
        grant=61,
    )


def kernel_tile(left_rows, right_rows):
    inner_prod = mm(left_rows, right_rows, 1, 1)
    left_sq = jnp.sum(jnp.square(left_rows.astype(f32)), axis=1)
    right_sq = jnp.sum(jnp.square(right_rows.astype(f32)), axis=1)
    squared = left_sq[:, None] + right_sq[None, :] - 2.0 * inner_prod
    return jnp.exp(squared * (-3.5 / left_rows.shape[1])).astype(bf16)


def with_operations(features, targets, coefficients, momentum, block_index, pivot_index, core):
    row_count, pts_count = lax.axis_size("rows"), lax.axis_size("pts")
    row_id, pts_id = lax.axis_index("rows"), lax.axis_index("pts")
    points = features.shape[0]
    block = block_index.shape[1]
    outputs = coefficients.shape[1]
    per_row = block // row_count
    per_device = per_row // pts_count
    row_cols = outputs // row_count
    own_cols = row_cols // pts_count
    first = row_id * row_cols
    current, moving, goal = (
        lax.dynamic_slice_in_dim(value, first, row_cols, axis=1).T.astype(f32)
        for value in (coefficients, momentum, targets)
    )
    ids = iota((points, 1), 0) + pts_id * points
    place = [(ids == block_index[u][None, :]).astype(bf16) for u in range(UPDATES)]
    own_rows = []
    for u in range(UPDATES):
        mine = lax.dynamic_slice_in_dim(place[u], row_id * per_row, per_row, axis=1)
        own_rows.append(mm(mine, features, 0, 0).astype(bf16).reshape(pts_count, per_device, -1))
    came = lax.all_to_all(jnp.concatenate(own_rows, axis=1), "pts", 0, 0, tiled=False)
    chunk = jnp.sum(came.astype(f32), axis=0).astype(bf16)
    spread = lax.all_gather(lax.all_gather(chunk, "pts", axis=0), "rows", axis=0)
    spread = spread.reshape(row_count, pts_count, UPDATES, per_device, features.shape[1])
    all_steps = []
    for u in range(UPDATES):
        block_feats = spread[:, :, u].reshape(block, features.shape[1])
        mixed = mixed_of(current, moving)
        high, low = split_two(ridge_term * mixed - goal)
        tile = kernel_tile(features, block_feats)
        partial_value = (
            mm(mixed.astype(bf16), tile, 1, 0) + mm(high, place[u], 1, 0) + mm(low, place[u], 1, 0)
        )
        pieces = partial_value.astype(bf16).reshape(pts_count, own_cols, block)
        summed = lax.all_to_all(pieces, "pts", 0, 0, tiled=False)
        resid = jnp.sum(summed.astype(f32), axis=0)
        at_pivot = (iota((block, 1), 0) == pivot_index[u][None, :]).astype(bf16)
        factor = kernel_tile(block_feats, mm(at_pivot, block_feats, 0, 0).astype(bf16))
        proj = mm(resid.astype(bf16), factor, 1, 0)
        lifted = mm(proj.astype(bf16), core[u], 1, 1).astype(bf16)
        step_bf = (resid - mm(lifted, factor, 1, 1)).astype(bf16)
        steps = lax.all_gather(step_bf, "pts", axis=0, tiled=True)
        change = mm(steps, place[u], 1, 1)
        all_steps.append(change.astype(bf16))
        current, moving = stepped(current, moving, change)
    gathered = lax.all_gather(jnp.stack(all_steps), "rows", axis=1, tiled=True)
    current, moving = coefficients, momentum
    for u in range(UPDATES):
        current, moving = stepped(current, moving, gathered[u].T.astype(f32))
    return (current, moving)


def shards(features, targets, coefficients, momentum, block_index, pivot_index, nystrom_core):
    rows, owners = lax.axis_size("rows"), lax.axis_size("pts")
    count = block_index.shape[1] // rows
    fits = rows == 4 and owners == 8 and coefficients.shape[1] == 8 * rows * owners
    fits = fits and coefficients.shape[0] % CHUNK == 0 and count % CHUNK == 0 and (3 * count // owners) % 64 == 0 and UPDATES * rows == 8
    plan = with_kernels if fits else with_operations
    return plan(
        features, targets, coefficients, momentum, block_index, pivot_index, nystrom_core
    )


def solution(mesh):
    in_specs = (P("pts", None), P("pts", None), P("pts", None), P("pts", None), P(), P(), P())
    out_specs = (P("pts", None), P("pts", None))
    return jax.shard_map(shards, mesh=mesh, in_specs=in_specs, out_specs=out_specs, check_vma=False)
```

```python
import functools
import math

import jax
import jax.numpy as jnp
from jax import lax
from jax.experimental import pallas as pl
from jax.experimental.pallas import tpu as pltpu
from jax.sharding import PartitionSpec as P

UPDATES = 2


alpha_mix = 0.6
beta_keep = 0.9
step_size = 0.2
momentum_gain = 1.5
ridge_term = 1.0

f32 = jnp.float32
bf16 = jnp.bfloat16
i32 = jnp.int32


def mm(a, b, ca, cb):
    return lax.dot_general(a, b, (((ca,), (cb,)), ((), ())), preferred_element_type=f32)


def split_two(value):
    high = value.astype(bf16)
    return high, (value - high.astype(f32)).astype(bf16)


def mixed_of(current, moving):
    return alpha_mix * moving + (1.0 - alpha_mix) * current


mix_per_step = alpha_mix * step_size * momentum_gain + (1.0 - alpha_mix) * step_size


def stepped(current, moving, change):
    mixed = mixed_of(current, moving)
    if change is None:
        return mixed, beta_keep * moving + (1.0 - beta_keep) * mixed
    return (
        mixed - step_size * change,
        beta_keep * moving + (1.0 - beta_keep) * mixed - step_size * momentum_gain * change,
    )


def iota(shape, axis):
    return lax.broadcasted_iota(i32, shape, axis)


def one_hot(chosen):
    return jnp.where(chosen, 1.0, 0.0).astype(bf16)


def before_matrix(n):
    return one_hot(iota((n, n), 0) < iota((n, n), 1))


def owners_of(indices, before, points, owners):
    owner = lax.div(indices, jnp.full_like(indices, points))
    owner_ids = iota((owners, indices.shape[1]), 0)
    marks = jnp.where(owner_ids == owner, 1.0, 0.0)
    earlier = mm(marks.astype(bf16), before, 1, 0)
    rank = jnp.sum(marks * earlier, axis=0, keepdims=True)
    start = jnp.sum(jnp.where(owner < owner_ids, 1.0, 0.0), axis=1, keepdims=True)
    return marks, rank, start


def sorted_places(marks, rank, start):
    return (rank + jnp.sum(marks * start, axis=0, keepdims=True)).astype(i32)


def lane_row(column):
    n = column.shape[0]
    diagonal = iota((n, 128), 0) == iota((n, 128), 1)
    return jnp.sum(jnp.where(diagonal, column, 0.0), axis=0, keepdims=True).astype(i32)


def sorted_points(indices, place):
    count = indices.shape[1]
    return from_digits(mm(two_digits(indices), one_hot(iota((count, count), 0) == place), 1, 1))


def two_digits(row):
    high = lax.shift_right_logical(row, jnp.full_like(row, 7))
    shape = (8, row.shape[1])
    value = jnp.where(iota(shape, 0) == 0, high, lax.bitwise_and(row, jnp.full_like(row, 127)))
    return value.astype(f32).astype(bf16)


def from_digits(digits):
    return (digits[0:1] * 128.0 + digits[1:2]).astype(i32)


def start_all(pairs, sems):
    copies = [pltpu.make_async_copy(a, b, sems.at[n]) for n, (a, b) in enumerate(pairs)]
    for copy in copies:
        copy.start()
    return copies


def wait_all(copies):
    for copy in copies:
        copy.wait()


def group_row(blocks, u, group, count):
    return blocks[u : u + 1, pl.ds(pl.multiple_of(group * count, count), count)]


def pack_kernel(count, cap, owners, blocks_hbm, feats_hbm, out_hbm, blocks, feats, packed, sems):
    row, me = lax.axis_index("rows"), lax.axis_index("pts")
    points = feats.shape[0]
    reads = start_all([(blocks_hbm, blocks), (feats_hbm, feats)], sems)
    before = before_matrix(count)
    reads[0].wait()
    rows = []
    for u in range(UPDATES):
        indices = group_row(blocks, u, row, count)
        local = indices - me * points
        mine = jnp.where((local >= 0) & (local < points), 1.0, 0.0)
        rank = mm(jnp.broadcast_to(mine, (8, count)).astype(bf16), before, 1, 0)[0:1]
        held = (iota((cap, count), 0) == rank.astype(i32)) & (mine > 0.0)
        point = jnp.sum(jnp.where(held, (local + 1).astype(f32), 0.0), axis=1, keepdims=True)
        rows.append(one_hot(iota((cap, points), 1) == point.astype(i32) - 1))
    reads[1].wait()
    for u in range(UPDATES):
        packed[u * cap : (u + 1) * cap, :] = mm(rows[u], feats[...], 1, 0).astype(bf16)
    wait_all(start_all([(packed, out_hbm)], sems))


def prepare_kernel(
    count, owners,
    blocks_hbm, w_hbm, z_hbm, t_hbm, coef_hbm, offset_hbm, starts_hbm,
    blocks, w, z, t, coef, offset, starts, sems, out_sems,
):
    row, me = lax.axis_index("rows"), lax.axis_index("pts")
    points, outputs = w.shape
    reads = start_all([(blocks_hbm, blocks), (w_hbm, w), (z_hbm, z), (t_hbm, t)], sems)
    before = before_matrix(count)
    reads[0].wait()
    locals_of = []
    for u in range(UPDATES):
        indices = group_row(blocks, u, row, count)
        marks, rank, start = owners_of(indices, before, points, owners)
        starts[u : u + 1, :] = lane_row(start)
        locals_of.append(sorted_points(indices, sorted_places(marks, rank, start)) - me * points)
    writes = start_all([(starts, starts_hbm)], out_sems)
    wait_all(reads[1:])
    current, moving = w[...], z[...]
    goal = t[...].astype(f32).T
    for u in range(UPDATES):
        mixed = mixed_of(current, moving).T
        high, low = split_two(ridge_term * mixed - goal)
        coef[u] = mixed.astype(bf16)
        place = one_hot(iota((points, count), 0) == locals_of[u])
        offset[u] = mm(high, place, 1, 0) + mm(low, place, 1, 0)
        current, moving = stepped(current, moving, None)
        for a, b in ((coef, coef_hbm), (offset, offset_hbm)):
            writes.append(pltpu.make_async_copy(a.at[u], b.at[u], out_sems.at[len(writes)]))
            writes[-1].start()
    wait_all(writes)


def order_kernel(
    count, points, owners,
    blocks_hbm, pivots_hbm, ids_hbm, starts_hbm, chosen_hbm,
    blocks, pivots, ids, starts, chosen, sems,
):
    wait_all(start_all([(blocks_hbm, blocks), (pivots_hbm, pivots)], sems))
    before = before_matrix(count)
    groups = blocks.shape[1] // count
    for u in range(UPDATES):
        pivot = pivots[u : u + 1, :]
        found = jnp.zeros((8, pivot.shape[1]), f32)
        for g in range(groups):
            n = u * groups + g
            indices = blocks[u : u + 1, g * count : (g + 1) * count]
            marks, rank, start = owners_of(indices, before, points, owners)
            place = sorted_places(marks, rank, start)
            ids[n : n + 1, :] = sorted_points(indices, place)
            starts[n : n + 1, :] = lane_row(start)
            at_pivot = one_hot(iota((count, pivot.shape[1]), 0) + g * count == pivot)
            found += mm(two_digits(place + g * count), at_pivot, 1, 0)
        chosen[u : u + 1, :] = from_digits(found)
    wait_all(start_all([(ids, ids_hbm), (starts, starts_hbm), (chosen, chosen_hbm)], sems))


def slots_kernel(count, points, cap, blocks_hbm, slots_hbm, blocks, slots, sems):
    me = lax.axis_index("pts")
    wait_all(start_all([(blocks_hbm, blocks)], sems))
    before = before_matrix(count)
    groups = blocks.shape[1] // count
    for u in range(UPDATES):
        found = jnp.zeros((8, groups * cap), f32)
        for g in range(groups):
            local = blocks[u : u + 1, g * count : (g + 1) * count] - me * points
            mine = (local >= 0) & (local < points)
            counts = jnp.where(mine, 1.0, 0.0)
            rank = mm(jnp.broadcast_to(counts, (8, count)).astype(bf16), before, 1, 0)[0:1]
            held = jnp.where(mine, rank.astype(i32) + g * cap, -1)
            chosen = one_hot(iota((groups * cap, count), 0) == held)
            found += mm(two_digits(jnp.where(mine, local + 1, 0)), chosen, 1, 1)
        slots[u : u + 1, :] = from_digits(found) - 1
    wait_all(start_all([(slots, slots_hbm)], sems))


def extended(rows, axis, first):
    rest = -0.5 * jnp.sum(jnp.square(rows.astype(f32)), axis=axis, keepdims=True)
    parts = []
    for _ in range(3):
        parts.append(rest.astype(bf16).astype(f32))
        rest = rest - parts[-1]
    parts = parts + [1.0] * 3 if first else [1.0] * 3 + parts
    at = iota(rows.shape, axis)
    extra = jnp.zeros(rows.shape, f32)
    for n, part in enumerate(parts):
        extra = jnp.where(at == n, part, extra)
    return jnp.concatenate([rows.astype(bf16), extra.astype(bf16)], axis=axis)


def exponent(left, right):
    return mm(left, right, 1, 0) * (7.0 / (left.shape[1] // 2) * math.log2(math.e))


CHUNK = 256


def compact_kernel(*refs):
    *came_hbm, starts_hbm, block_hbm, came, starts, wide, block, sems = refs
    me = lax.axis_index("pts")
    owners, deep, _ = came.shape
    cap = deep // UPDATES
    count = block.shape[2]
    pairs = [(a, came.at[k]) for k, a in enumerate(came_hbm)]
    wait_all(start_all([*pairs, (starts_hbm, starts)], sems))
    for u in range(UPDATES):
        for o in range(owners):
            start = starts[u, o]
            rows = came[lax.bitwise_xor(me, o), u * cap : (u + 1) * cap, :]
            wide[u, pl.ds(start, cap), :] = rows.astype(f32)
        block[u] = wide[u, 0:count, :].T.astype(bf16)
    wait_all(start_all([(block, block_hbm)], sems))


def sums_kernel(
    block_hbm, feats_hbm, coef_hbm, offset_hbm, pieces_hbm,
    block, feats, coef, offset, tile, pieces, sems,
):
    outputs = coef.shape[1]
    pairs = [(block_hbm, block), (feats_hbm, feats), (coef_hbm, coef), (offset_hbm, offset)]
    reads = start_all(pairs, sems)
    wait_all(reads[:2])
    left = extended(feats[...], 1, True)
    for u in range(UPDATES):
        right = extended(block[u], 0, False)
        tile[...] = jnp.exp2(exponent(left, right)).astype(bf16)
        if u == 0:
            wait_all(reads[2:])
        total = offset[u] + mm(coef[u], tile[...], 1, 0)
        devices, _, lanes = pieces.shape
        own = outputs // devices
        for d in range(devices):
            part = total[d * own : (d + 1) * own]
            pieces[d, 2 * own * u : 2 * own * (u + 1), :] = jnp.concatenate(
                [part[:, :lanes], part[:, lanes:]], axis=0
            ).astype(bf16)
    wait_all(start_all([(pieces, pieces_hbm)], sems))


def factors_kernel(
    b0_hbm, b1_hbm, b2_hbm, b3_hbm, ids_hbm, pivots_hbm, factor_hbm, cross_hbm,
    feats, ids, pivots, factor, cross, sems,
):
    row = lax.axis_index("rows")
    groups, _, width, count = feats.shape
    pairs = [(b_hbm, feats.at[k]) for k, b_hbm in enumerate((b0_hbm, b1_hbm, b2_hbm, b3_hbm))]
    wait_all(start_all(pairs + [(ids_hbm, ids), (pivots_hbm, pivots)], sems))
    places = [lax.bitwise_xor(row, k) for k in range(groups)]
    rights = [[extended(feats[k, u], 0, False) for k in range(groups)] for u in range(UPDATES)]
    for u in range(UPDATES):
        chosen_feats = jnp.zeros((width, pivots.shape[1]), f32)
        for k in range(groups):
            chosen = iota((count, pivots.shape[1]), 0) + places[k] * count == pivots[u : u + 1, :]
            chosen_feats += mm(feats[k, u], one_hot(chosen), 1, 0)
        left = extended(chosen_feats.T, 1, True)
        for k in range(groups):
            start = pl.multiple_of(places[k] * count, count)
            value = jnp.exp2(exponent(left, rights[u][k]))
            factor[u, :, pl.ds(start, count)] = value.astype(bf16)
    writes = start_all([(factor, factor_hbm)], sems)
    lefts, left_points = [], []
    for k in range(groups):
        lefts.append(extended(feats[k, 0].astype(f32).T, 1, True))
        points = ids[pl.ds(places[k], 1), :].astype(f32)
        left_points.append(jnp.broadcast_to(points, (8, count)).T[:, 0:1])
    left, left_points = jnp.concatenate(lefts, axis=0), jnp.concatenate(left_points, axis=0)
    sent = 1
    for m in range(groups):
        right_points = ids[pl.ds(groups + places[m], 1), :].astype(f32)
        power = exponent(left, rights[1][m])
        power = jnp.where(left_points == right_points, math.log2(1.0 + ridge_term), power)
        cross[m] = jnp.exp2(power).astype(bf16).reshape(groups, count, count)
        for k in range(groups):
            start = pl.multiple_of(places[k] * count, count)
            copy = pltpu.make_async_copy(
                cross.at[m, k], cross_hbm.at[places[m], pl.ds(start, count), :], sems.at[sent]
            )
            copy.start()
            writes.append(copy)
            sent += 1
    wait_all(writes)


def chain_kernel(
    cap, owners,
    summed_hbm, factor_hbm, core_hbm, cross_hbm, starts_hbm, out_hbm,
    summed, factor, core, cross, starts, packed, sems,
):
    groups, _, count = cross.shape
    own = summed.shape[1] // (2 * UPDATES)
    pairs = [(summed_hbm, summed)]
    for u in range(UPDATES):
        pairs += [(factor_hbm.at[u], factor.at[u]), (core_hbm.at[u], core.at[u])]
        if u == 0:
            pairs += [(starts_hbm, starts)]
            pairs += [(cross_hbm.at[g], cross.at[g]) for g in range(groups)]
    reads = start_all(pairs, sems)
    first, *reads = reads
    first.wait()
    step = None
    for u in range(UPDATES):
        sums = []
        for g in range(groups):
            part = summed[g * owners, 2 * own * u : 2 * own * (u + 1), :].astype(f32)
            for o in range(1, owners):
                part += summed[g * owners + o, 2 * own * u : 2 * own * (u + 1), :].astype(f32)
            part = jnp.concatenate([part[:own], part[own:]], axis=1)
            if u:
                reads[3 + g].wait()
                part -= mix_per_step * mm(step, cross[g], 1, 0)
            sums.append(part)
        resid = jnp.concatenate(sums, axis=1)
        wait_all(reads[0:3] if u == 0 else reads[3 + groups :])
        proj = mm(resid.astype(bf16), factor[u], 1, 1)
        lifted = mm(proj.astype(bf16), core[u], 1, 1).astype(bf16)
        step = (resid - mm(lifted, factor[u], 1, 0)).astype(bf16)
        half = groups // 2
        for o in range(owners):
            lanes = []
            for g in range(groups):
                part = step[:, g * count : (g + 1) * count].astype(f32)
                back = lax.rem(count - starts[u * groups + g, o], count)
                lanes.append(pltpu.roll(part, back, 1)[:, :cap])
            packed[o, 2 * own * u : 2 * own * (u + 1), :] = jnp.concatenate(
                [jnp.concatenate(lanes[h * half : (h + 1) * half], axis=1) for h in range(2)], axis=0
            ).astype(bf16)
    wait_all(start_all([(packed, out_hbm)], sems))


def finish_kernel(
    g0_hbm, g1_hbm, g2_hbm, g3_hbm, slots_hbm, w_hbm, z_hbm, w_out, z_out,
    got, slots, w, z, steps, w_new, z_new, sems, out_sems,
):
    row = lax.axis_index("rows")
    points = w.shape[0]
    sources, deep, lanes = got.shape
    own = deep // (2 * UPDATES)
    chunks = range(0, points, CHUNK)
    pairs = [(slots_hbm, slots)]
    for k, g_hbm in enumerate((g0_hbm, g1_hbm, g2_hbm, g3_hbm)):
        size = g_hbm.shape[0]
        first = pl.multiple_of(lax.bitwise_xor(row, k) * size, size)
        pairs.append((g_hbm, got.at[pl.ds(first, size)]))
    for c in chunks:
        part = slice(c, c + CHUNK)
        pairs += [(w_hbm.at[part], w.at[part]), (z_hbm.at[part], z.at[part])]
    reads = start_all(pairs, sems)
    wait_all(reads[:5])
    reads = reads[5:]
    wide = got[...].astype(f32)
    for u in range(UPDATES):
        for h in range(2):
            first = own * (2 * u + h)
            part = wide[:, first : first + own, :].reshape(sources * own, lanes)
            steps[u, h * lanes : (h + 1) * lanes, :] = part.T.astype(bf16)
    changes = []
    for u in range(UPDATES):
        rows = one_hot(iota((points, slots.shape[1]), 0) == slots[u : u + 1, :])
        changes.append(mm(rows, steps[u], 1, 0))
    writes = []
    for n, c in enumerate(chunks):
        part = slice(c, c + CHUNK)
        wait_all(reads[2 * n : 2 * n + 2])
        current, moving = w[part, :], z[part, :]
        for change in changes:
            current, moving = stepped(current, moving, change[part])
        w_new[part, :] = current
        z_new[part, :] = moving
        for m, (a, b) in enumerate(((w_new, w_out), (z_new, z_out))):
            copy = pltpu.make_async_copy(a.at[part], b.at[part], out_sems.at[2 * n + m])
            copy.start()
            writes.append(copy)
    wait_all(writes)


VMEM = pl.BlockSpec(memory_space=pltpu.VMEM)
HBM = pl.BlockSpec(memory_space=pltpu.HBM)
in_smem = type(pltpu.SMEM((1,), i32))


def like(shape, dtype=bf16):
    return jax.ShapeDtypeStruct(shape, dtype)


def call(body, outs, inside, *args, near=0, sems=(), flops=0, grant=62):
    moved = sum(math.prod(o.shape) * o.dtype.itemsize for o in [*outs, *args])
    return pl.pallas_call(
        body,
        out_shape=outs,
        in_specs=[VMEM] * near + [HBM] * (len(args) - near),
        out_specs=[HBM] * len(outs),
        scratch_shapes=[
            x if isinstance(x, in_smem) else pltpu.VMEM(x.shape, x.dtype) for x in inside
        ]
        + [pltpu.SemaphoreType.DMA((n,)) for n in sems],
        compiler_params=pltpu.CompilerParams(vmem_limit_bytes=grant * 2**20),
        cost_estimate=pl.CostEstimate(flops=int(flops), bytes_accessed=moved, transcendentals=0),
    )(*args)


def swap(value, axis, k):
    return lax.ppermute(value, axis, [(i, i ^ k) for i in range(lax.axis_size(axis))])


def with_kernels(features, targets, coefficients, momentum, block_index, pivot_index, core):
    rows, owners = lax.axis_size("rows"), lax.axis_size("pts")
    points, width = features.shape
    block = block_index.shape[1]
    rank = pivot_index.shape[1]
    outputs = coefficients.shape[1]
    count = block // rows
    cap = 3 * count // owners
    devices = rows * owners
    own = outputs // devices
    deep = 2 * own * UPDATES
    half = rows // 2
    wide = like(coefficients.shape, f32)

    (packed,) = call(
        functools.partial(pack_kernel, count, cap, owners),
        [like((UPDATES * cap, width))],
        [block_index, features, like((UPDATES * cap, width))],
        block_index,
        features,
        sems=(2,),
    )
    came = {k: swap(packed, "pts", k) for k in reversed(range(1, owners))}
    kept = [
        like((UPDATES, outputs, points)),
        like((UPDATES, outputs, count), f32),
        like((8, 128), i32),
    ]
    given = [block_index, coefficients, momentum, targets]
    coef, offset, row_starts = call(
        functools.partial(prepare_kernel, count, owners),
        kept,
        given + kept,
        *given,
        sems=(4, 1 + 2 * UPDATES),
    )
    feats = like((UPDATES, width, count))
    inside_starts = pltpu.SMEM(row_starts.shape, i32)
    (mine,) = call(
        compact_kernel,
        [feats],
        [
            like((owners, *packed.shape)),
            inside_starts,
            like((UPDATES, count + cap, width), f32),
            feats,
        ],
        packed,
        *[came[k] for k in range(1, owners)],
        row_starts,
        sems=(owners + 1,),
        grant=61,
    )
    beside, across = swap(mine, "rows", 1), swap(mine, "rows", 2)
    pieces = like((devices, deep, count // 2))
    (pieces,) = call(
        sums_kernel,
        [pieces],
        [feats, features, coef, offset, like((points, count)), pieces],
        mine,
        features,
        coef,
        offset,
        sems=(4,),
        flops=2.0 * UPDATES * points * count * (2 * width + outputs),
    )
    pieces, later_index = lax.optimization_barrier((pieces, block_index))
    kept = [like((UPDATES * rows, count), i32), like((8, 128), i32), like((UPDATES, rank), i32)]
    ids, starts, chosen = call(
        functools.partial(order_kernel, count, points, owners),
        kept,
        [block_index, pivot_index, *kept],
        later_index,
        pivot_index,
        sems=(3,),
    )
    pieces, across, ids = lax.optimization_barrier((pieces, across, ids))
    summed = lax.all_to_all(pieces, ("rows", "pts"), 0, 0, tiled=True)
    kept = [like((UPDATES, rank, block)), like((rows, block, count))]
    factor, cross = call(
        factors_kernel,
        kept,
        [
            like((rows, *feats.shape)),
            ids,
            chosen,
            kept[0],
            like((rows, rows, count, count)),
        ],
        mine,
        beside,
        across,
        swap(across, "rows", 1),
        ids,
        chosen,
        sems=(rows * rows + 2,),
        grant=61,
        flops=2.0 * width * block * (UPDATES * rank + block),
    )
    pieces = like((owners, deep, half * cap))
    (steps,) = call(
        functools.partial(chain_kernel, cap, owners),
        [pieces],
        [summed, factor, core, cross, inside_starts, pieces],
        summed,
        factor,
        core,
        cross,
        starts,
        sems=(2 * UPDATES + 2 + rows,),
        grant=61,
    )
    steps, later_index = lax.optimization_barrier((steps, block_index))
    (slots,) = call(
        functools.partial(slots_kernel, count, points, cap),
        [like((UPDATES, rows * cap), i32)],
        [block_index, like((UPDATES, rows * cap), i32)],
        later_index,
        sems=(1,),
    )
    got = lax.all_to_all(steps, "pts", 0, 0, tiled=True)
    got, slots = lax.optimization_barrier((got, slots))
    beside, across = swap(got, "rows", 1), swap(got, "rows", 2)
    parts = points // CHUNK
    return call(
        finish_kernel,
        [wide] * 2,
        [
            like((devices, deep, half * cap)),
            slots,
            wide,
            wide,
            like((UPDATES, rows * cap, outputs)),
            wide,
            wide,
        ],
        got,
        beside,
        across,
        swap(across, "rows", 1),
        slots,
        coefficients,
        momentum,
        sems=(1 + rows + 2 * parts, 2 * parts),
        grant=61,
    )


def kernel_tile(left_rows, right_rows):
    inner_prod = mm(left_rows, right_rows, 1, 1)
    left_sq = jnp.sum(jnp.square(left_rows.astype(f32)), axis=1)
    right_sq = jnp.sum(jnp.square(right_rows.astype(f32)), axis=1)
    squared = left_sq[:, None] + right_sq[None, :] - 2.0 * inner_prod
    return jnp.exp(squared * (-3.5 / left_rows.shape[1])).astype(bf16)


def with_operations(features, targets, coefficients, momentum, block_index, pivot_index, core):
    row_count, pts_count = lax.axis_size("rows"), lax.axis_size("pts")
    row_id, pts_id = lax.axis_index("rows"), lax.axis_index("pts")
    points = features.shape[0]
    block = block_index.shape[1]
    outputs = coefficients.shape[1]
    per_row = block // row_count
    per_device = per_row // pts_count
    row_cols = outputs // row_count
    own_cols = row_cols // pts_count
    first = row_id * row_cols
    current, moving, goal = (
        lax.dynamic_slice_in_dim(value, first, row_cols, axis=1).T.astype(f32)
        for value in (coefficients, momentum, targets)
    )
    ids = iota((points, 1), 0) + pts_id * points
    place = [(ids == block_index[u][None, :]).astype(bf16) for u in range(UPDATES)]
    own_rows = []
    for u in range(UPDATES):
        mine = lax.dynamic_slice_in_dim(place[u], row_id * per_row, per_row, axis=1)
        own_rows.append(mm(mine, features, 0, 0).astype(bf16).reshape(pts_count, per_device, -1))
    came = lax.all_to_all(jnp.concatenate(own_rows, axis=1), "pts", 0, 0, tiled=False)
    chunk = jnp.sum(came.astype(f32), axis=0).astype(bf16)
    spread = lax.all_gather(lax.all_gather(chunk, "pts", axis=0), "rows", axis=0)
    spread = spread.reshape(row_count, pts_count, UPDATES, per_device, features.shape[1])
    all_steps = []
    for u in range(UPDATES):
        block_feats = spread[:, :, u].reshape(block, features.shape[1])
        mixed = mixed_of(current, moving)
        high, low = split_two(ridge_term * mixed - goal)
        tile = kernel_tile(features, block_feats)
        partial_value = (
            mm(mixed.astype(bf16), tile, 1, 0) + mm(high, place[u], 1, 0) + mm(low, place[u], 1, 0)
        )
        pieces = partial_value.astype(bf16).reshape(pts_count, own_cols, block)
        summed = lax.all_to_all(pieces, "pts", 0, 0, tiled=False)
        resid = jnp.sum(summed.astype(f32), axis=0)
        at_pivot = (iota((block, 1), 0) == pivot_index[u][None, :]).astype(bf16)
        factor = kernel_tile(block_feats, mm(at_pivot, block_feats, 0, 0).astype(bf16))
        proj = mm(resid.astype(bf16), factor, 1, 0)
        lifted = mm(proj.astype(bf16), core[u], 1, 1).astype(bf16)
        step_bf = (resid - mm(lifted, factor, 1, 1)).astype(bf16)
        steps = lax.all_gather(step_bf, "pts", axis=0, tiled=True)
        change = mm(steps, place[u], 1, 1)
        all_steps.append(change.astype(bf16))
        current, moving = stepped(current, moving, change)
    gathered = lax.all_gather(jnp.stack(all_steps), "rows", axis=1, tiled=True)
    current, moving = coefficients, momentum
    for u in range(UPDATES):
        current, moving = stepped(current, moving, gathered[u].T.astype(f32))
    return (current, moving)


def shards(features, targets, coefficients, momentum, block_index, pivot_index, nystrom_core):
    rows, owners = lax.axis_size("rows"), lax.axis_size("pts")
    count = block_index.shape[1] // rows
    fits = rows == 4 and owners == 8 and coefficients.shape[1] == 8 * rows * owners
    fits = fits and coefficients.shape[0] % CHUNK == 0 and count % CHUNK == 0 and (3 * count // owners) % 64 == 0 and UPDATES * rows == 8
    plan = with_kernels if fits else with_operations
    return plan(
        features, targets, coefficients, momentum, block_index, pivot_index, nystrom_core
    )


def solution(mesh):
    in_specs = (P("pts", None), P("pts", None), P("pts", None), P("pts", None), P(), P(), P())
    out_specs = (P("pts", None), P("pts", None))
    return jax.shard_map(shards, mesh=mesh, in_specs=in_specs, out_specs=out_specs, check_vma=False)
```

```python
import functools
import math

import jax
import jax.numpy as jnp
from jax import lax
from jax.experimental import pallas as pl
from jax.experimental.pallas import tpu as pltpu
from jax.sharding import PartitionSpec as P

UPDATES = 2


alpha_mix = 0.6
beta_keep = 0.9
step_size = 0.2
momentum_gain = 1.5
ridge_term = 1.0

f32 = jnp.float32
bf16 = jnp.bfloat16
i32 = jnp.int32


def mm(a, b, ca, cb):
    return lax.dot_general(a, b, (((ca,), (cb,)), ((), ())), preferred_element_type=f32)


def split_two(value):
    high = value.astype(bf16)
    return high, (value - high.astype(f32)).astype(bf16)


def mixed_of(current, moving):
    return alpha_mix * moving + (1.0 - alpha_mix) * current


mix_per_step = alpha_mix * step_size * momentum_gain + (1.0 - alpha_mix) * step_size


def stepped(current, moving, change):
    mixed = mixed_of(current, moving)
    if change is None:
        return mixed, beta_keep * moving + (1.0 - beta_keep) * mixed
    return (
        mixed - step_size * change,
        beta_keep * moving + (1.0 - beta_keep) * mixed - step_size * momentum_gain * change,
    )


def iota(shape, axis):
    return lax.broadcasted_iota(i32, shape, axis)


def one_hot(chosen):
    return jnp.where(chosen, 1.0, 0.0).astype(bf16)


def before_matrix(n):
    return one_hot(iota((n, n), 0) < iota((n, n), 1))


def owners_of(indices, before, points, owners):
    owner = lax.div(indices, jnp.full_like(indices, points))
    owner_ids = iota((owners, indices.shape[1]), 0)
    marks = jnp.where(owner_ids == owner, 1.0, 0.0)
    earlier = mm(marks.astype(bf16), before, 1, 0)
    rank = jnp.sum(marks * earlier, axis=0, keepdims=True)
    start = jnp.sum(jnp.where(owner < owner_ids, 1.0, 0.0), axis=1, keepdims=True)
    return marks, rank, start


def sorted_places(marks, rank, start):
    return (rank + jnp.sum(marks * start, axis=0, keepdims=True)).astype(i32)


def lane_row(column):
    n = column.shape[0]
    diagonal = iota((n, 128), 0) == iota((n, 128), 1)
    return jnp.sum(jnp.where(diagonal, column, 0.0), axis=0, keepdims=True).astype(i32)


def sorted_points(indices, place):
    count = indices.shape[1]
    return from_digits(mm(two_digits(indices), one_hot(iota((count, count), 0) == place), 1, 1))


def two_digits(row):
    high = lax.shift_right_logical(row, jnp.full_like(row, 7))
    shape = (8, row.shape[1])
    value = jnp.where(iota(shape, 0) == 0, high, lax.bitwise_and(row, jnp.full_like(row, 127)))
    return value.astype(f32).astype(bf16)


def from_digits(digits):
    return (digits[0:1] * 128.0 + digits[1:2]).astype(i32)


def start_all(pairs, sems):
    copies = [pltpu.make_async_copy(a, b, sems.at[n]) for n, (a, b) in enumerate(pairs)]
    for copy in copies:
        copy.start()
    return copies


def wait_all(copies):
    for copy in copies:
        copy.wait()


def group_row(blocks, u, group, count):
    return blocks[u : u + 1, pl.ds(pl.multiple_of(group * count, count), count)]


def pack_kernel(count, cap, owners, blocks_hbm, feats_hbm, out_hbm, blocks, feats, packed, sems):
    row, me = lax.axis_index("rows"), lax.axis_index("pts")
    points = feats.shape[0]
    reads = start_all([(blocks_hbm, blocks), (feats_hbm, feats)], sems)
    before = before_matrix(count)
    reads[0].wait()
    rows = []
    for u in range(UPDATES):
        indices = group_row(blocks, u, row, count)
        local = indices - me * points
        mine = jnp.where((local >= 0) & (local < points), 1.0, 0.0)
        rank = mm(jnp.broadcast_to(mine, (8, count)).astype(bf16), before, 1, 0)[0:1]
        held = (iota((cap, count), 0) == rank.astype(i32)) & (mine > 0.0)
        point = jnp.sum(jnp.where(held, (local + 1).astype(f32), 0.0), axis=1, keepdims=True)
        rows.append(one_hot(iota((cap, points), 1) == point.astype(i32) - 1))
    reads[1].wait()
    for u in range(UPDATES):
        packed[u * cap : (u + 1) * cap, :] = mm(rows[u], feats[...], 1, 0).astype(bf16)
    wait_all(start_all([(packed, out_hbm)], sems))


def prepare_kernel(
    count, owners,
    blocks_hbm, w_hbm, z_hbm, t_hbm, coef_hbm, offset_hbm,
    blocks, w, z, t, coef, offset, sems, out_sems,
):
    row, me = lax.axis_index("rows"), lax.axis_index("pts")
    points, outputs = w.shape
    reads = start_all([(blocks_hbm, blocks), (w_hbm, w), (z_hbm, z), (t_hbm, t)], sems)
    before = before_matrix(count)
    reads[0].wait()
    locals_of = []
    for u in range(UPDATES):
        indices = group_row(blocks, u, row, count)
        marks, rank, start = owners_of(indices, before, points, owners)
        locals_of.append(sorted_points(indices, sorted_places(marks, rank, start)) - me * points)
    writes = []
    wait_all(reads[1:])
    current, moving = w[...], z[...]
    goal = t[...].astype(f32).T
    for u in range(UPDATES):
        mixed = mixed_of(current, moving).T
        high, low = split_two(ridge_term * mixed - goal)
        coef[u] = mixed.astype(bf16)
        place = one_hot(iota((points, count), 0) == locals_of[u])
        offset[u] = mm(high, place, 1, 0) + mm(low, place, 1, 0)
        current, moving = stepped(current, moving, None)
        for a, b in ((coef, coef_hbm), (offset, offset_hbm)):
            writes.append(pltpu.make_async_copy(a.at[u], b.at[u], out_sems.at[len(writes)]))
            writes[-1].start()
    wait_all(writes)


def order_kernel(
    count, points, owners,
    blocks_hbm, pivots_hbm, ids_hbm, starts_hbm, chosen_hbm,
    blocks, pivots, ids, starts, chosen, sems,
):
    wait_all(start_all([(blocks_hbm, blocks), (pivots_hbm, pivots)], sems))
    before = before_matrix(count)
    groups = blocks.shape[1] // count
    for u in range(UPDATES):
        pivot = pivots[u : u + 1, :]
        found = jnp.zeros((8, pivot.shape[1]), f32)
        for g in range(groups):
            n = u * groups + g
            indices = blocks[u : u + 1, g * count : (g + 1) * count]
            marks, rank, start = owners_of(indices, before, points, owners)
            place = sorted_places(marks, rank, start)
            ids[n : n + 1, :] = sorted_points(indices, place)
            starts[n : n + 1, :] = lane_row(start)
            at_pivot = one_hot(iota((count, pivot.shape[1]), 0) + g * count == pivot)
            found += mm(two_digits(place + g * count), at_pivot, 1, 0)
        chosen[u : u + 1, :] = from_digits(found)
    wait_all(start_all([(ids, ids_hbm), (starts, starts_hbm), (chosen, chosen_hbm)], sems))


def slots_kernel(count, points, cap, blocks_hbm, slots_hbm, blocks, slots, sems):
    me = lax.axis_index("pts")
    wait_all(start_all([(blocks_hbm, blocks)], sems))
    before = before_matrix(count)
    groups = blocks.shape[1] // count
    for u in range(UPDATES):
        found = jnp.zeros((8, groups * cap), f32)
        for g in range(groups):
            local = blocks[u : u + 1, g * count : (g + 1) * count] - me * points
            mine = (local >= 0) & (local < points)
            counts = jnp.where(mine, 1.0, 0.0)
            rank = mm(jnp.broadcast_to(counts, (8, count)).astype(bf16), before, 1, 0)[0:1]
            held = jnp.where(mine, rank.astype(i32) + g * cap, -1)
            chosen = one_hot(iota((groups * cap, count), 0) == held)
            found += mm(two_digits(jnp.where(mine, local + 1, 0)), chosen, 1, 1)
        slots[u : u + 1, :] = from_digits(found) - 1
    wait_all(start_all([(slots, slots_hbm)], sems))


def extended(rows, axis, first):
    rest = -0.5 * jnp.sum(jnp.square(rows.astype(f32)), axis=axis, keepdims=True)
    parts = []
    for _ in range(3):
        parts.append(rest.astype(bf16).astype(f32))
        rest = rest - parts[-1]
    parts = parts + [1.0] * 3 if first else [1.0] * 3 + parts
    at = iota(rows.shape, axis)
    extra = jnp.zeros(rows.shape, f32)
    for n, part in enumerate(parts):
        extra = jnp.where(at == n, part, extra)
    return jnp.concatenate([rows.astype(bf16), extra.astype(bf16)], axis=axis)


def exponent(left, right):
    return mm(left, right, 1, 0) * (7.0 / (left.shape[1] // 2) * math.log2(math.e))


CHUNK = 256


def compact_kernel(*refs):
    *came_hbm, starts_hbm, block_hbm, first_hbm, second_hbm, came, starts, wide, block, sems = refs
    row, me = lax.axis_index("rows"), lax.axis_index("pts")
    owners, deep, _ = came.shape
    cap = deep // UPDATES
    groups = starts.shape[0] // UPDATES
    count = block.shape[2]
    pairs = [(a, came.at[k]) for k, a in enumerate(came_hbm)]
    wait_all(start_all([*pairs, (starts_hbm, starts)], sems))
    for u in range(UPDATES):
        for o in range(owners):
            start = starts[u * groups + row, o]
            rows = came[lax.bitwise_xor(me, o), u * cap : (u + 1) * cap, :]
            wide[u, pl.ds(start, cap), :] = rows.astype(f32)
        block[u] = wide[u, 0:count, :].T.astype(bf16)
    pairs = [(block, block_hbm), (block.at[0], first_hbm), (block.at[1], second_hbm)]
    wait_all(start_all(pairs, sems))


def sums_kernel(
    block_hbm, feats_hbm, coef_hbm, offset_hbm, pieces_hbm,
    block, feats, coef, offset, tile, pieces, sems,
):
    outputs = coef.shape[1]
    pairs = [(block_hbm, block), (feats_hbm, feats), (coef_hbm, coef), (offset_hbm, offset)]
    reads = start_all(pairs, sems)
    wait_all(reads[:2])
    left = extended(feats[...], 1, True)
    for u in range(UPDATES):
        right = extended(block[u], 0, False)
        tile[...] = jnp.exp2(exponent(left, right)).astype(bf16)
        if u == 0:
            wait_all(reads[2:])
        total = offset[u] + mm(coef[u], tile[...], 1, 0)
        devices, _, lanes = pieces.shape
        own = outputs // devices
        for d in range(devices):
            part = total[d * own : (d + 1) * own]
            pieces[d, 2 * own * u : 2 * own * (u + 1), :] = jnp.concatenate(
                [part[:, :lanes], part[:, lanes:]], axis=0
            ).astype(bf16)
    wait_all(start_all([(pieces, pieces_hbm)], sems))


def factors_kernel(
    mine_hbm, beside_hbm, a0_hbm, a1_hbm, d0_hbm, d1_hbm, ids_hbm, pivots_hbm, factor_hbm, cross_hbm,
    feats, ids, pivots, factor, cross, sems,
):
    row = lax.axis_index("rows")
    groups, _, width, count = feats.shape
    pairs = [(mine_hbm, feats.at[0]), (beside_hbm, feats.at[1])]
    pairs += [(a0_hbm, feats.at[2, 0]), (a1_hbm, feats.at[2, 1])]
    pairs += [(d0_hbm, feats.at[3, 0]), (d1_hbm, feats.at[3, 1])]
    wait_all(start_all(pairs + [(ids_hbm, ids), (pivots_hbm, pivots)], sems))
    places = [lax.bitwise_xor(row, k) for k in range(groups)]
    rights = [[extended(feats[k, u], 0, False) for k in range(groups)] for u in range(UPDATES)]
    for u in range(UPDATES):
        chosen_feats = jnp.zeros((width, pivots.shape[1]), f32)
        for k in range(groups):
            chosen = iota((count, pivots.shape[1]), 0) + places[k] * count == pivots[u : u + 1, :]
            chosen_feats += mm(feats[k, u], one_hot(chosen), 1, 0)
        left = extended(chosen_feats.T, 1, True)
        for k in range(groups):
            start = pl.multiple_of(places[k] * count, count)
            value = jnp.exp2(exponent(left, rights[u][k]))
            factor[u, :, pl.ds(start, count)] = value.astype(bf16)
    writes = start_all([(factor, factor_hbm)], sems)
    lefts, left_points = [], []
    for k in range(groups):
        lefts.append(extended(feats[k, 0].astype(f32).T, 1, True))
        points = ids[pl.ds(places[k], 1), :].astype(f32)
        left_points.append(jnp.broadcast_to(points, (8, count)).T[:, 0:1])
    left, left_points = jnp.concatenate(lefts, axis=0), jnp.concatenate(left_points, axis=0)
    sent = 1
    for m in range(groups):
        right_points = ids[pl.ds(groups + places[m], 1), :].astype(f32)
        power = exponent(left, rights[1][m])
        power = jnp.where(left_points == right_points, math.log2(1.0 + ridge_term), power)
        cross[m] = jnp.exp2(power).astype(bf16).reshape(groups, count, count)
        for k in range(groups):
            start = pl.multiple_of(places[k] * count, count)
            copy = pltpu.make_async_copy(
                cross.at[m, k], cross_hbm.at[places[m], pl.ds(start, count), :], sems.at[sent]
            )
            copy.start()
            writes.append(copy)
            sent += 1
    wait_all(writes)


def chain_kernel(
    cap, owners,
    summed_hbm, factor_hbm, core_hbm, cross_hbm, starts_hbm, out_hbm,
    summed, factor, core, cross, starts, packed, sems,
):
    groups, _, count = cross.shape
    own = summed.shape[1] // (2 * UPDATES)
    pairs = [(summed_hbm, summed)]
    for u in range(UPDATES):
        pairs += [(factor_hbm.at[u], factor.at[u]), (core_hbm.at[u], core.at[u])]
        if u == 0:
            pairs += [(starts_hbm, starts)]
            pairs += [(cross_hbm.at[g], cross.at[g]) for g in range(groups)]
    reads = start_all(pairs, sems)
    first, *reads = reads
    first.wait()
    step = None
    for u in range(UPDATES):
        sums = []
        for g in range(groups):
            part = summed[g * owners, 2 * own * u : 2 * own * (u + 1), :].astype(f32)
            for o in range(1, owners):
                part += summed[g * owners + o, 2 * own * u : 2 * own * (u + 1), :].astype(f32)
            part = jnp.concatenate([part[:own], part[own:]], axis=1)
            if u:
                reads[3 + g].wait()
                part -= mix_per_step * mm(step, cross[g], 1, 0)
            sums.append(part)
        resid = jnp.concatenate(sums, axis=1)
        wait_all(reads[0:3] if u == 0 else reads[3 + groups :])
        proj = mm(resid.astype(bf16), factor[u], 1, 1)
        lifted = mm(proj.astype(bf16), core[u], 1, 1).astype(bf16)
        step = (resid - mm(lifted, factor[u], 1, 0)).astype(bf16)
        half = groups // 2
        for o in range(owners):
            lanes = []
            for g in range(groups):
                part = step[:, g * count : (g + 1) * count].astype(f32)
                back = lax.rem(count - starts[u * groups + g, o], count)
                lanes.append(pltpu.roll(part, back, 1)[:, :cap])
            packed[o, 2 * own * u : 2 * own * (u + 1), :] = jnp.concatenate(
                [jnp.concatenate(lanes[h * half : (h + 1) * half], axis=1) for h in range(2)], axis=0
            ).astype(bf16)
    wait_all(start_all([(packed, out_hbm)], sems))


def finish_kernel(
    g0_hbm, g1_hbm, g2_hbm, g3_hbm, slots_hbm, w_hbm, z_hbm, w_out, z_out,
    got, slots, w, z, steps, w_new, z_new, sems, out_sems,
):
    row = lax.axis_index("rows")
    points = w.shape[0]
    sources, deep, lanes = got.shape
    own = deep // (2 * UPDATES)
    chunks = range(0, points, CHUNK)
    pairs = [(slots_hbm, slots)]
    for k, g_hbm in enumerate((g0_hbm, g1_hbm, g2_hbm, g3_hbm)):
        size = g_hbm.shape[0]
        first = pl.multiple_of(lax.bitwise_xor(row, k) * size, size)
        pairs.append((g_hbm, got.at[pl.ds(first, size)]))
    for c in chunks:
        part = slice(c, c + CHUNK)
        pairs += [(w_hbm.at[part], w.at[part]), (z_hbm.at[part], z.at[part])]
    reads = start_all(pairs, sems)
    wait_all(reads[:5])
    reads = reads[5:]
    wide = got[...].astype(f32)
    for u in range(UPDATES):
        for h in range(2):
            first = own * (2 * u + h)
            part = wide[:, first : first + own, :].reshape(sources * own, lanes)
            steps[u, h * lanes : (h + 1) * lanes, :] = part.T.astype(bf16)
    changes = []
    for u in range(UPDATES):
        rows = one_hot(iota((points, slots.shape[1]), 0) == slots[u : u + 1, :])
        changes.append(mm(rows, steps[u], 1, 0))
    writes = []
    for n, c in enumerate(chunks):
        part = slice(c, c + CHUNK)
        wait_all(reads[2 * n : 2 * n + 2])
        current, moving = w[part, :], z[part, :]
        for change in changes:
            current, moving = stepped(current, moving, change[part])
        w_new[part, :] = current
        z_new[part, :] = moving
        for m, (a, b) in enumerate(((w_new, w_out), (z_new, z_out))):
            copy = pltpu.make_async_copy(a.at[part], b.at[part], out_sems.at[2 * n + m])
            copy.start()
            writes.append(copy)
    wait_all(writes)


VMEM = pl.BlockSpec(memory_space=pltpu.VMEM)
HBM = pl.BlockSpec(memory_space=pltpu.HBM)
in_smem = type(pltpu.SMEM((1,), i32))


def like(shape, dtype=bf16):
    return jax.ShapeDtypeStruct(shape, dtype)


def call(body, outs, inside, *args, near=0, sems=(), flops=0, grant=62):
    moved = sum(math.prod(o.shape) * o.dtype.itemsize for o in [*outs, *args])
    return pl.pallas_call(
        body,
        out_shape=outs,
        in_specs=[VMEM] * near + [HBM] * (len(args) - near),
        out_specs=[HBM] * len(outs),
        scratch_shapes=[
            x if isinstance(x, in_smem) else pltpu.VMEM(x.shape, x.dtype) for x in inside
        ]
        + [pltpu.SemaphoreType.DMA((n,)) for n in sems],
        compiler_params=pltpu.CompilerParams(vmem_limit_bytes=grant * 2**20),
        cost_estimate=pl.CostEstimate(flops=int(flops), bytes_accessed=moved, transcendentals=0),
    )(*args)


def swap(value, axis, k):
    return lax.ppermute(value, axis, [(i, i ^ k) for i in range(lax.axis_size(axis))])


def with_kernels(features, targets, coefficients, momentum, block_index, pivot_index, core):
    rows, owners = lax.axis_size("rows"), lax.axis_size("pts")
    points, width = features.shape
    block = block_index.shape[1]
    rank = pivot_index.shape[1]
    outputs = coefficients.shape[1]
    count = block // rows
    cap = 3 * count // owners
    devices = rows * owners
    own = outputs // devices
    deep = 2 * own * UPDATES
    half = rows // 2
    wide = like(coefficients.shape, f32)

    (packed,) = call(
        functools.partial(pack_kernel, count, cap, owners),
        [like((UPDATES * cap, width))],
        [block_index, features, like((UPDATES * cap, width))],
        block_index,
        features,
        sems=(2,),
    )
    came = {k: swap(packed, "pts", k) for k in reversed(range(3, owners))}
    kept = [like((UPDATES, outputs, points)), like((UPDATES, outputs, count), f32)]
    given = [block_index, coefficients, momentum, targets]
    coef, offset = call(
        functools.partial(prepare_kernel, count, owners),
        kept,
        given + kept,
        *given,
        sems=(4, 2 * UPDATES),
    )
    again, coef, later_index = lax.optimization_barrier((packed, coef, block_index))
    came.update({k: swap(again, "pts", k) for k in (2, 1)})
    kept = [like((UPDATES * rows, count), i32), like((8, 128), i32), like((UPDATES, rank), i32)]
    ids, starts, chosen = call(
        functools.partial(order_kernel, count, points, owners),
        kept,
        [block_index, pivot_index, *kept],
        later_index,
        pivot_index,
        sems=(3,),
    )
    feats = like((UPDATES, width, count))
    one = like((width, count))
    inside_starts = pltpu.SMEM(starts.shape, i32)
    mine, first, second = call(
        compact_kernel,
        [feats, one, one],
        [
            like((owners, *packed.shape)),
            inside_starts,
            like((UPDATES, count + cap, width), f32),
            feats,
        ],
        packed,
        *[came[k] for k in range(1, owners)],
        starts,
        sems=(owners + 1,),
        grant=61,
    )
    beside, across = swap(mine, "rows", 1), swap(first, "rows", 2)
    across_second = swap(second, "rows", 2)
    pieces = like((devices, deep, count // 2))
    (pieces,) = call(
        sums_kernel,
        [pieces],
        [feats, features, coef, offset, like((points, count)), pieces],
        mine,
        features,
        coef,
        offset,
        sems=(4,),
        flops=2.0 * UPDATES * points * count * (2 * width + outputs),
    )
    pieces, across = lax.optimization_barrier((pieces, across))
    summed = lax.all_to_all(pieces, ("rows", "pts"), 0, 0, tiled=True)
    kept = [like((UPDATES, rank, block)), like((rows, block, count))]
    factor, cross = call(
        factors_kernel,
        kept,
        [
            like((rows, *feats.shape)),
            ids,
            chosen,
            kept[0],
            like((rows, rows, count, count)),
        ],
        mine,
        beside,
        across,
        across_second,
        swap(across, "rows", 1),
        swap(across_second, "rows", 1),
        ids,
        chosen,
        sems=(rows * rows + 2,),
        grant=61,
        flops=2.0 * width * block * (UPDATES * rank + block),
    )
    pieces = like((owners, deep, half * cap))
    (steps,) = call(
        functools.partial(chain_kernel, cap, owners),
        [pieces],
        [summed, factor, core, cross, inside_starts, pieces],
        summed,
        factor,
        core,
        cross,
        starts,
        sems=(2 * UPDATES + 2 + rows,),
        grant=61,
    )
    steps, later_index = lax.optimization_barrier((steps, block_index))
    (slots,) = call(
        functools.partial(slots_kernel, count, points, cap),
        [like((UPDATES, rows * cap), i32)],
        [block_index, like((UPDATES, rows * cap), i32)],
        later_index,
        sems=(1,),
    )
    got = lax.all_to_all(steps, "pts", 0, 0, tiled=True)
    got, slots = lax.optimization_barrier((got, slots))
    beside, across = swap(got, "rows", 1), swap(got, "rows", 2)
    parts = points // CHUNK
    return call(
        finish_kernel,
        [wide] * 2,
        [
            like((devices, deep, half * cap)),
            slots,
            wide,
            wide,
            like((UPDATES, rows * cap, outputs)),
            wide,
            wide,
        ],
        got,
        beside,
        across,
        swap(across, "rows", 1),
        slots,
        coefficients,
        momentum,
        sems=(1 + rows + 2 * parts, 2 * parts),
        grant=61,
    )


def kernel_tile(left_rows, right_rows):
    inner_prod = mm(left_rows, right_rows, 1, 1)
    left_sq = jnp.sum(jnp.square(left_rows.astype(f32)), axis=1)
    right_sq = jnp.sum(jnp.square(right_rows.astype(f32)), axis=1)
    squared = left_sq[:, None] + right_sq[None, :] - 2.0 * inner_prod
    return jnp.exp(squared * (-3.5 / left_rows.shape[1])).astype(bf16)


def with_operations(features, targets, coefficients, momentum, block_index, pivot_index, core):
    row_count, pts_count = lax.axis_size("rows"), lax.axis_size("pts")
    row_id, pts_id = lax.axis_index("rows"), lax.axis_index("pts")
    points = features.shape[0]
    block = block_index.shape[1]
    outputs = coefficients.shape[1]
    per_row = block // row_count
    per_device = per_row // pts_count
    row_cols = outputs // row_count
    own_cols = row_cols // pts_count
    first = row_id * row_cols
    current, moving, goal = (
        lax.dynamic_slice_in_dim(value, first, row_cols, axis=1).T.astype(f32)
        for value in (coefficients, momentum, targets)
    )
    ids = iota((points, 1), 0) + pts_id * points
    place = [(ids == block_index[u][None, :]).astype(bf16) for u in range(UPDATES)]
    own_rows = []
    for u in range(UPDATES):
        mine = lax.dynamic_slice_in_dim(place[u], row_id * per_row, per_row, axis=1)
        own_rows.append(mm(mine, features, 0, 0).astype(bf16).reshape(pts_count, per_device, -1))
    came = lax.all_to_all(jnp.concatenate(own_rows, axis=1), "pts", 0, 0, tiled=False)
    chunk = jnp.sum(came.astype(f32), axis=0).astype(bf16)
    spread = lax.all_gather(lax.all_gather(chunk, "pts", axis=0), "rows", axis=0)
    spread = spread.reshape(row_count, pts_count, UPDATES, per_device, features.shape[1])
    all_steps = []
    for u in range(UPDATES):
        block_feats = spread[:, :, u].reshape(block, features.shape[1])
        mixed = mixed_of(current, moving)
        high, low = split_two(ridge_term * mixed - goal)
        tile = kernel_tile(features, block_feats)
        partial_value = (
            mm(mixed.astype(bf16), tile, 1, 0) + mm(high, place[u], 1, 0) + mm(low, place[u], 1, 0)
        )
        pieces = partial_value.astype(bf16).reshape(pts_count, own_cols, block)
        summed = lax.all_to_all(pieces, "pts", 0, 0, tiled=False)
        resid = jnp.sum(summed.astype(f32), axis=0)
        at_pivot = (iota((block, 1), 0) == pivot_index[u][None, :]).astype(bf16)
        factor = kernel_tile(block_feats, mm(at_pivot, block_feats, 0, 0).astype(bf16))
        proj = mm(resid.astype(bf16), factor, 1, 0)
        lifted = mm(proj.astype(bf16), core[u], 1, 1).astype(bf16)
        step_bf = (resid - mm(lifted, factor, 1, 1)).astype(bf16)
        steps = lax.all_gather(step_bf, "pts", axis=0, tiled=True)
        change = mm(steps, place[u], 1, 1)
        all_steps.append(change.astype(bf16))
        current, moving = stepped(current, moving, change)
    gathered = lax.all_gather(jnp.stack(all_steps), "rows", axis=1, tiled=True)
    current, moving = coefficients, momentum
    for u in range(UPDATES):
        current, moving = stepped(current, moving, gathered[u].T.astype(f32))
    return (current, moving)


def shards(features, targets, coefficients, momentum, block_index, pivot_index, nystrom_core):
    rows, owners = lax.axis_size("rows"), lax.axis_size("pts")
    count = block_index.shape[1] // rows
    fits = rows == 4 and owners == 8 and coefficients.shape[1] == 8 * rows * owners
    fits = fits and coefficients.shape[0] % CHUNK == 0 and count % CHUNK == 0 and (3 * count // owners) % 64 == 0 and UPDATES * rows == 8
    plan = with_kernels if fits else with_operations
    return plan(
        features, targets, coefficients, momentum, block_index, pivot_index, nystrom_core
    )


def solution(mesh):
    in_specs = (P("pts", None), P("pts", None), P("pts", None), P("pts", None), P(), P(), P())
    out_specs = (P("pts", None), P("pts", None))
    return jax.shard_map(shards, mesh=mesh, in_specs=in_specs, out_specs=out_specs, check_vma=False)
```

```python
import functools
import math

import jax
import jax.numpy as jnp
from jax import lax
from jax.experimental import pallas as pl
from jax.experimental.pallas import tpu as pltpu
from jax.sharding import PartitionSpec as P

UPDATES = 2


alpha_mix = 0.6
beta_keep = 0.9
step_size = 0.2
momentum_gain = 1.5
ridge_term = 1.0

f32 = jnp.float32
bf16 = jnp.bfloat16
i32 = jnp.int32


def mm(a, b, ca, cb):
    return lax.dot_general(a, b, (((ca,), (cb,)), ((), ())), preferred_element_type=f32)


def split_two(value):
    high = value.astype(bf16)
    return high, (value - high.astype(f32)).astype(bf16)


def mixed_of(current, moving):
    return alpha_mix * moving + (1.0 - alpha_mix) * current


mix_per_step = alpha_mix * step_size * momentum_gain + (1.0 - alpha_mix) * step_size


def stepped(current, moving, change):
    mixed = mixed_of(current, moving)
    if change is None:
        return mixed, beta_keep * moving + (1.0 - beta_keep) * mixed
    return (
        mixed - step_size * change,
        beta_keep * moving + (1.0 - beta_keep) * mixed - step_size * momentum_gain * change,
    )


def iota(shape, axis):
    return lax.broadcasted_iota(i32, shape, axis)


def one_hot(chosen):
    return jnp.where(chosen, 1.0, 0.0).astype(bf16)


def before_matrix(n):
    return one_hot(iota((n, n), 0) < iota((n, n), 1))


def owners_of(indices, before, points, owners):
    owner = lax.div(indices, jnp.full_like(indices, points))
    owner_ids = iota((owners, indices.shape[1]), 0)
    marks = jnp.where(owner_ids == owner, 1.0, 0.0)
    earlier = mm(marks.astype(bf16), before, 1, 0)
    rank = jnp.sum(marks * earlier, axis=0, keepdims=True)
    start = jnp.sum(jnp.where(owner < owner_ids, 1.0, 0.0), axis=1, keepdims=True)
    return marks, rank, start


def sorted_places(marks, rank, start):
    return (rank + jnp.sum(marks * start, axis=0, keepdims=True)).astype(i32)


def lane_row(column):
    n = column.shape[0]
    diagonal = iota((n, 128), 0) == iota((n, 128), 1)
    return jnp.sum(jnp.where(diagonal, column, 0.0), axis=0, keepdims=True).astype(i32)


def sorted_points(indices, place):
    count = indices.shape[1]
    return from_digits(mm(two_digits(indices), one_hot(iota((count, count), 0) == place), 1, 1))


def two_digits(row):
    high = lax.shift_right_logical(row, jnp.full_like(row, 7))
    shape = (8, row.shape[1])
    value = jnp.where(iota(shape, 0) == 0, high, lax.bitwise_and(row, jnp.full_like(row, 127)))
    return value.astype(f32).astype(bf16)


def from_digits(digits):
    return (digits[0:1] * 128.0 + digits[1:2]).astype(i32)


def start_all(pairs, sems):
    copies = [pltpu.make_async_copy(a, b, sems.at[n]) for n, (a, b) in enumerate(pairs)]
    for copy in copies:
        copy.start()
    return copies


def wait_all(copies):
    for copy in copies:
        copy.wait()


def group_row(blocks, u, group, count):
    return blocks[u : u + 1, pl.ds(pl.multiple_of(group * count, count), count)]


def pack_kernel(count, cap, owners, blocks_hbm, feats_hbm, out_hbm, blocks, feats, packed, sems):
    row, me = lax.axis_index("rows"), lax.axis_index("pts")
    points = feats.shape[0]
    reads = start_all([(blocks_hbm, blocks), (feats_hbm, feats)], sems)
    before = before_matrix(count)
    reads[0].wait()
    rows = []
    for u in range(UPDATES):
        indices = group_row(blocks, u, row, count)
        local = indices - me * points
        mine = jnp.where((local >= 0) & (local < points), 1.0, 0.0)
        rank = mm(jnp.broadcast_to(mine, (8, count)).astype(bf16), before, 1, 0)[0:1]
        held = (iota((cap, count), 0) == rank.astype(i32)) & (mine > 0.0)
        point = jnp.sum(jnp.where(held, (local + 1).astype(f32), 0.0), axis=1, keepdims=True)
        rows.append(one_hot(iota((cap, points), 1) == point.astype(i32) - 1))
    reads[1].wait()
    for u in range(UPDATES):
        packed[u * cap : (u + 1) * cap, :] = mm(rows[u], feats[...], 1, 0).astype(bf16)
    wait_all(start_all([(packed, out_hbm)], sems))


def prepare_kernel(
    count, owners,
    blocks_hbm, w_hbm, z_hbm, t_hbm, coef_hbm, offset_hbm, starts_hbm,
    blocks, w, z, t, coef, offset, starts, sems, out_sems,
):
    row, me = lax.axis_index("rows"), lax.axis_index("pts")
    points, outputs = w.shape
    reads = start_all([(blocks_hbm, blocks), (w_hbm, w), (z_hbm, z), (t_hbm, t)], sems)
    before = before_matrix(count)
    reads[0].wait()
    locals_of = []
    for u in range(UPDATES):
        indices = group_row(blocks, u, row, count)
        marks, rank, start = owners_of(indices, before, points, owners)
        starts[u : u + 1, :] = lane_row(start)
        locals_of.append(sorted_points(indices, sorted_places(marks, rank, start)) - me * points)
    writes = start_all([(starts, starts_hbm)], out_sems)
    wait_all(reads[1:])
    current, moving = w[...], z[...]
    goal = t[...].astype(f32).T
    for u in range(UPDATES):
        mixed = mixed_of(current, moving).T
        high, low = split_two(ridge_term * mixed - goal)
        coef[u] = mixed.astype(bf16)
        place = one_hot(iota((points, count), 0) == locals_of[u])
        offset[u] = mm(high, place, 1, 0) + mm(low, place, 1, 0)
        current, moving = stepped(current, moving, None)
        for a, b in ((coef, coef_hbm), (offset, offset_hbm)):
            writes.append(pltpu.make_async_copy(a.at[u], b.at[u], out_sems.at[len(writes)]))
            writes[-1].start()
    wait_all(writes)


def order_kernel(
    count, points, owners,
    blocks_hbm, pivots_hbm, ids_hbm, starts_hbm, chosen_hbm,
    blocks, pivots, ids, starts, chosen, sems,
):
    wait_all(start_all([(blocks_hbm, blocks), (pivots_hbm, pivots)], sems))
    before = before_matrix(count)
    groups = blocks.shape[1] // count
    for u in range(UPDATES):
        pivot = pivots[u : u + 1, :]
        found = jnp.zeros((8, pivot.shape[1]), f32)
        for g in range(groups):
            n = u * groups + g
            indices = blocks[u : u + 1, g * count : (g + 1) * count]
            marks, rank, start = owners_of(indices, before, points, owners)
            place = sorted_places(marks, rank, start)
            ids[n : n + 1, :] = sorted_points(indices, place)
            starts[n : n + 1, :] = lane_row(start)
            at_pivot = one_hot(iota((count, pivot.shape[1]), 0) + g * count == pivot)
            found += mm(two_digits(place + g * count), at_pivot, 1, 0)
        chosen[u : u + 1, :] = from_digits(found)
    wait_all(start_all([(ids, ids_hbm), (starts, starts_hbm), (chosen, chosen_hbm)], sems))


def slots_kernel(count, points, cap, blocks_hbm, slots_hbm, blocks, slots, sems):
    me = lax.axis_index("pts")
    wait_all(start_all([(blocks_hbm, blocks)], sems))
    before = before_matrix(count)
    groups = blocks.shape[1] // count
    for u in range(UPDATES):
        found = jnp.zeros((8, groups * cap), f32)
        for g in range(groups):
            local = blocks[u : u + 1, g * count : (g + 1) * count] - me * points
            mine = (local >= 0) & (local < points)
            counts = jnp.where(mine, 1.0, 0.0)
            rank = mm(jnp.broadcast_to(counts, (8, count)).astype(bf16), before, 1, 0)[0:1]
            held = jnp.where(mine, rank.astype(i32) + g * cap, -1)
            chosen = one_hot(iota((groups * cap, count), 0) == held)
            found += mm(two_digits(jnp.where(mine, local + 1, 0)), chosen, 1, 1)
        slots[u : u + 1, :] = from_digits(found) - 1
    wait_all(start_all([(slots, slots_hbm)], sems))


def extended(rows, axis, first):
    rest = -0.5 * jnp.sum(jnp.square(rows.astype(f32)), axis=axis, keepdims=True)
    parts = []
    for _ in range(3):
        parts.append(rest.astype(bf16).astype(f32))
        rest = rest - parts[-1]
    parts = parts + [1.0] * 3 if first else [1.0] * 3 + parts
    at = iota(rows.shape, axis)
    extra = jnp.zeros(rows.shape, f32)
    for n, part in enumerate(parts):
        extra = jnp.where(at == n, part, extra)
    return jnp.concatenate([rows.astype(bf16), extra.astype(bf16)], axis=axis)


def exponent(left, right):
    return mm(left, right, 1, 0) * (7.0 / (left.shape[1] // 2) * math.log2(math.e))


CHUNK = 256


def compact_kernel(*refs):
    *came_hbm, starts_hbm, block_hbm, came, starts, wide, block, sems = refs
    me = lax.axis_index("pts")
    owners, deep, _ = came.shape
    cap = deep // UPDATES
    count = block.shape[2]
    pairs = [(a, came.at[k]) for k, a in enumerate(came_hbm)]
    wait_all(start_all([*pairs, (starts_hbm, starts)], sems))
    for u in range(UPDATES):
        for o in range(owners):
            start = starts[u, o]
            rows = came[lax.bitwise_xor(me, o), u * cap : (u + 1) * cap, :]
            wide[u, pl.ds(start, cap), :] = rows.astype(f32)
        block[u] = wide[u, 0:count, :].T.astype(bf16)
    wait_all(start_all([(block, block_hbm)], sems))


def sums_kernel(
    block_hbm, feats_hbm, coef_hbm, offset_hbm, pieces_hbm,
    block, feats, coef, offset, tile, pieces, sems,
):
    outputs = coef.shape[1]
    pairs = [(block_hbm, block), (feats_hbm, feats), (coef_hbm, coef), (offset_hbm, offset)]
    reads = start_all(pairs, sems)
    wait_all(reads[:2])
    left = extended(feats[...], 1, True)
    for u in range(UPDATES):
        right = extended(block[u], 0, False)
        tile[...] = jnp.exp2(exponent(left, right)).astype(bf16)
        if u == 0:
            wait_all(reads[2:])
        total = offset[u] + mm(coef[u], tile[...], 1, 0)
        devices, _, lanes = pieces.shape
        own = outputs // devices
        for d in range(devices):
            part = total[d * own : (d + 1) * own]
            pieces[d, 2 * own * u : 2 * own * (u + 1), :] = jnp.concatenate(
                [part[:, :lanes], part[:, lanes:]], axis=0
            ).astype(bf16)
    wait_all(start_all([(pieces, pieces_hbm)], sems))


def factors_kernel(
    b0_hbm, b1_hbm, b2_hbm, b3_hbm, ids_hbm, pivots_hbm, factor_hbm, cross_hbm,
    feats, ids, pivots, factor, cross, sems,
):
    row = lax.axis_index("rows")
    groups, _, width, count = feats.shape
    pairs = [(b_hbm, feats.at[k]) for k, b_hbm in enumerate((b0_hbm, b1_hbm, b2_hbm, b3_hbm))]
    wait_all(start_all(pairs + [(ids_hbm, ids), (pivots_hbm, pivots)], sems))
    places = [lax.bitwise_xor(row, k) for k in range(groups)]
    rights = [[extended(feats[k, u], 0, False) for k in range(groups)] for u in range(UPDATES)]
    for u in range(UPDATES):
        chosen_feats = jnp.zeros((width, pivots.shape[1]), f32)
        for k in range(groups):
            chosen = iota((count, pivots.shape[1]), 0) + places[k] * count == pivots[u : u + 1, :]
            chosen_feats += mm(feats[k, u], one_hot(chosen), 1, 0)
        left = extended(chosen_feats.T, 1, True)
        for k in range(groups):
            start = pl.multiple_of(places[k] * count, count)
            value = jnp.exp2(exponent(left, rights[u][k]))
            factor[u, :, pl.ds(start, count)] = value.astype(bf16)
    writes = start_all([(factor, factor_hbm)], sems)
    lefts, left_points = [], []
    for k in range(groups):
        lefts.append(extended(feats[k, 0].astype(f32).T, 1, True))
        points = ids[pl.ds(places[k], 1), :].astype(f32)
        left_points.append(jnp.broadcast_to(points, (8, count)).T[:, 0:1])
    left, left_points = jnp.concatenate(lefts, axis=0), jnp.concatenate(left_points, axis=0)
    sent = 1
    for m in range(groups):
        right_points = ids[pl.ds(groups + places[m], 1), :].astype(f32)
        power = exponent(left, rights[1][m])
        power = jnp.where(left_points == right_points, math.log2(1.0 + ridge_term), power)
        cross[m] = jnp.exp2(power).astype(bf16).reshape(groups, count, count)
        for k in range(groups):
            start = pl.multiple_of(places[k] * count, count)
            copy = pltpu.make_async_copy(
                cross.at[m, k], cross_hbm.at[places[m], pl.ds(start, count), :], sems.at[sent]
            )
            copy.start()
            writes.append(copy)
            sent += 1
    wait_all(writes)


def chain_kernel(
    cap, owners,
    summed_hbm, factor_hbm, core_hbm, cross_hbm, starts_hbm, out_hbm,
    summed, factor, core, cross, starts, packed, sems,
):
    groups, _, count = cross.shape
    own = summed.shape[1] // (2 * UPDATES)
    pairs = [(summed_hbm, summed)]
    for u in range(UPDATES):
        pairs += [(factor_hbm.at[u], factor.at[u]), (core_hbm.at[u], core.at[u])]
        if u == 0:
            pairs += [(starts_hbm, starts)]
            pairs += [(cross_hbm.at[g], cross.at[g]) for g in range(groups)]
    reads = start_all(pairs, sems)
    first, *reads = reads
    first.wait()
    step = None
    for u in range(UPDATES):
        sums = []
        for g in range(groups):
            part = summed[g * owners, 2 * own * u : 2 * own * (u + 1), :].astype(f32)
            for o in range(1, owners):
                part += summed[g * owners + o, 2 * own * u : 2 * own * (u + 1), :].astype(f32)
            part = jnp.concatenate([part[:own], part[own:]], axis=1)
            if u:
                reads[3 + g].wait()
                part -= mix_per_step * mm(step, cross[g], 1, 0)
            sums.append(part)
        resid = jnp.concatenate(sums, axis=1)
        wait_all(reads[0:3] if u == 0 else reads[3 + groups :])
        proj = mm(resid.astype(bf16), factor[u], 1, 1)
        lifted = mm(proj.astype(bf16), core[u], 1, 1).astype(bf16)
        step = (resid - mm(lifted, factor[u], 1, 0)).astype(bf16)
        half = groups // 2
        for o in range(owners):
            lanes = []
            for g in range(groups):
                part = step[:, g * count : (g + 1) * count].astype(f32)
                back = lax.rem(count - starts[u * groups + g, o], count)
                lanes.append(pltpu.roll(part, back, 1)[:, :cap])
            packed[o, 2 * own * u : 2 * own * (u + 1), :] = jnp.concatenate(
                [jnp.concatenate(lanes[h * half : (h + 1) * half], axis=1) for h in range(2)], axis=0
            ).astype(bf16)
    wait_all(start_all([(packed, out_hbm)], sems))


def finish_kernel(
    g0_hbm, g1_hbm, g2_hbm, g3_hbm, slots_hbm, w_hbm, z_hbm, w_out, z_out,
    got, slots, w, z, steps, w_new, z_new, sems, out_sems,
):
    row = lax.axis_index("rows")
    points = w.shape[0]
    sources, deep, lanes = got.shape
    own = deep // (2 * UPDATES)
    chunks = range(0, points, CHUNK)
    pairs = [(slots_hbm, slots)]
    for k, g_hbm in enumerate((g0_hbm, g1_hbm, g2_hbm, g3_hbm)):
        size = g_hbm.shape[0]
        first = pl.multiple_of(lax.bitwise_xor(row, k) * size, size)
        pairs.append((g_hbm, got.at[pl.ds(first, size)]))
    for c in chunks:
        part = slice(c, c + CHUNK)
        pairs += [(w_hbm.at[part], w.at[part]), (z_hbm.at[part], z.at[part])]
    reads = start_all(pairs, sems)
    wait_all(reads[:5])
    reads = reads[5:]
    wide = got[...].astype(f32)
    for u in range(UPDATES):
        for h in range(2):
            first = own * (2 * u + h)
            part = wide[:, first : first + own, :].reshape(sources * own, lanes)
            steps[u, h * lanes : (h + 1) * lanes, :] = part.T.astype(bf16)
    changes = []
    for u in range(UPDATES):
        rows = one_hot(iota((points, slots.shape[1]), 0) == slots[u : u + 1, :])
        changes.append(mm(rows, steps[u], 1, 0))
    writes = []
    for n, c in enumerate(chunks):
        part = slice(c, c + CHUNK)
        wait_all(reads[2 * n : 2 * n + 2])
        current, moving = w[part, :], z[part, :]
        for change in changes:
            current, moving = stepped(current, moving, change[part])
        w_new[part, :] = current
        z_new[part, :] = moving
        for m, (a, b) in enumerate(((w_new, w_out), (z_new, z_out))):
            copy = pltpu.make_async_copy(a.at[part], b.at[part], out_sems.at[2 * n + m])
            copy.start()
            writes.append(copy)
    wait_all(writes)


VMEM = pl.BlockSpec(memory_space=pltpu.VMEM)
HBM = pl.BlockSpec(memory_space=pltpu.HBM)
in_smem = type(pltpu.SMEM((1,), i32))


def like(shape, dtype=bf16):
    return jax.ShapeDtypeStruct(shape, dtype)


def call(body, outs, inside, *args, near=0, sems=(), flops=0, grant=62):
    moved = sum(math.prod(o.shape) * o.dtype.itemsize for o in [*outs, *args])
    return pl.pallas_call(
        body,
        out_shape=outs,
        in_specs=[VMEM] * near + [HBM] * (len(args) - near),
        out_specs=[HBM] * len(outs),
        scratch_shapes=[
            x if isinstance(x, in_smem) else pltpu.VMEM(x.shape, x.dtype) for x in inside
        ]
        + [pltpu.SemaphoreType.DMA((n,)) for n in sems],
        compiler_params=pltpu.CompilerParams(vmem_limit_bytes=grant * 2**20),
        cost_estimate=pl.CostEstimate(flops=int(flops), bytes_accessed=moved, transcendentals=0),
    )(*args)


def swap(value, axis, k):
    return lax.ppermute(value, axis, [(i, i ^ k) for i in range(lax.axis_size(axis))])


def with_kernels(features, targets, coefficients, momentum, block_index, pivot_index, core):
    rows, owners = lax.axis_size("rows"), lax.axis_size("pts")
    points, width = features.shape
    block = block_index.shape[1]
    rank = pivot_index.shape[1]
    outputs = coefficients.shape[1]
    count = block // rows
    cap = 3 * count // owners
    devices = rows * owners
    own = outputs // devices
    deep = 2 * own * UPDATES
    half = rows // 2
    wide = like(coefficients.shape, f32)

    (packed,) = call(
        functools.partial(pack_kernel, count, cap, owners),
        [like((UPDATES * cap, width))],
        [block_index, features, like((UPDATES * cap, width))],
        block_index,
        features,
        sems=(2,),
    )
    came = {k: swap(packed, "pts", k) for k in reversed(range(3, owners))}
    kept = [
        like((UPDATES, outputs, points)),
        like((UPDATES, outputs, count), f32),
        like((8, 128), i32),
    ]
    given = [block_index, coefficients, momentum, targets]
    coef, offset, row_starts = call(
        functools.partial(prepare_kernel, count, owners),
        kept,
        given + kept,
        *given,
        sems=(4, 1 + 2 * UPDATES),
    )
    again, row_starts = lax.optimization_barrier((packed, row_starts))
    came.update({k: swap(again, "pts", k) for k in (2, 1)})
    feats = like((UPDATES, width, count))
    inside_starts = pltpu.SMEM(row_starts.shape, i32)
    (mine,) = call(
        compact_kernel,
        [feats],
        [
            like((owners, *packed.shape)),
            inside_starts,
            like((UPDATES, count + cap, width), f32),
            feats,
        ],
        packed,
        *[came[k] for k in range(1, owners)],
        row_starts,
        sems=(owners + 1,),
        grant=60,
    )
    beside, across = swap(mine, "rows", 1), swap(mine, "rows", 2)
    pieces = like((devices, deep, count // 2))
    (pieces,) = call(
        sums_kernel,
        [pieces],
        [feats, features, coef, offset, like((points, count)), pieces],
        mine,
        features,
        coef,
        offset,
        sems=(4,),
        flops=2.0 * UPDATES * points * count * (2 * width + outputs),
    )
    pieces, later_index = lax.optimization_barrier((pieces, block_index))
    kept = [like((UPDATES * rows, count), i32), like((8, 128), i32), like((UPDATES, rank), i32)]
    ids, starts, chosen = call(
        functools.partial(order_kernel, count, points, owners),
        kept,
        [block_index, pivot_index, *kept],
        later_index,
        pivot_index,
        sems=(3,),
    )
    pieces, across, ids = lax.optimization_barrier((pieces, across, ids))
    summed = lax.all_to_all(pieces, ("rows", "pts"), 0, 0, tiled=True)
    kept = [like((UPDATES, rank, block)), like((rows, block, count))]
    factor, cross = call(
        factors_kernel,
        kept,
        [
            like((rows, *feats.shape)),
            ids,
            chosen,
            kept[0],
            like((rows, rows, count, count)),
        ],
        mine,
        beside,
        across,
        swap(across, "rows", 1),
        ids,
        chosen,
        sems=(rows * rows + 2,),
        grant=60,
        flops=2.0 * width * block * (UPDATES * rank + block),
    )
    pieces = like((owners, deep, half * cap))
    (steps,) = call(
        functools.partial(chain_kernel, cap, owners),
        [pieces],
        [summed, factor, core, cross, inside_starts, pieces],
        summed,
        factor,
        core,
        cross,
        starts,
        sems=(2 * UPDATES + 2 + rows,),
        grant=60,
    )
    steps, later_index = lax.optimization_barrier((steps, block_index))
    (slots,) = call(
        functools.partial(slots_kernel, count, points, cap),
        [like((UPDATES, rows * cap), i32)],
        [block_index, like((UPDATES, rows * cap), i32)],
        later_index,
        sems=(1,),
    )
    got = lax.all_to_all(steps, "pts", 0, 0, tiled=True)
    got, slots = lax.optimization_barrier((got, slots))
    beside, across = swap(got, "rows", 1), swap(got, "rows", 2)
    parts = points // CHUNK
    return call(
        finish_kernel,
        [wide] * 2,
        [
            like((devices, deep, half * cap)),
            slots,
            wide,
            wide,
            like((UPDATES, rows * cap, outputs)),
            wide,
            wide,
        ],
        got,
        beside,
        across,
        swap(across, "rows", 1),
        slots,
        coefficients,
        momentum,
        sems=(1 + rows + 2 * parts, 2 * parts),
        grant=60,
    )


def kernel_tile(left_rows, right_rows):
    inner_prod = mm(left_rows, right_rows, 1, 1)
    left_sq = jnp.sum(jnp.square(left_rows.astype(f32)), axis=1)
    right_sq = jnp.sum(jnp.square(right_rows.astype(f32)), axis=1)
    squared = left_sq[:, None] + right_sq[None, :] - 2.0 * inner_prod
    return jnp.exp(squared * (-3.5 / left_rows.shape[1])).astype(bf16)


def with_operations(features, targets, coefficients, momentum, block_index, pivot_index, core):
    row_count, pts_count = lax.axis_size("rows"), lax.axis_size("pts")
    row_id, pts_id = lax.axis_index("rows"), lax.axis_index("pts")
    points = features.shape[0]
    block = block_index.shape[1]
    outputs = coefficients.shape[1]
    per_row = block // row_count
    per_device = per_row // pts_count
    row_cols = outputs // row_count
    own_cols = row_cols // pts_count
    first = row_id * row_cols
    current, moving, goal = (
        lax.dynamic_slice_in_dim(value, first, row_cols, axis=1).T.astype(f32)
        for value in (coefficients, momentum, targets)
    )
    ids = iota((points, 1), 0) + pts_id * points
    place = [(ids == block_index[u][None, :]).astype(bf16) for u in range(UPDATES)]
    own_rows = []
    for u in range(UPDATES):
        mine = lax.dynamic_slice_in_dim(place[u], row_id * per_row, per_row, axis=1)
        own_rows.append(mm(mine, features, 0, 0).astype(bf16).reshape(pts_count, per_device, -1))
    came = lax.all_to_all(jnp.concatenate(own_rows, axis=1), "pts", 0, 0, tiled=False)
    chunk = jnp.sum(came.astype(f32), axis=0).astype(bf16)
    spread = lax.all_gather(lax.all_gather(chunk, "pts", axis=0), "rows", axis=0)
    spread = spread.reshape(row_count, pts_count, UPDATES, per_device, features.shape[1])
    all_steps = []
    for u in range(UPDATES):
        block_feats = spread[:, :, u].reshape(block, features.shape[1])
        mixed = mixed_of(current, moving)
        high, low = split_two(ridge_term * mixed - goal)
        tile = kernel_tile(features, block_feats)
        partial_value = (
            mm(mixed.astype(bf16), tile, 1, 0) + mm(high, place[u], 1, 0) + mm(low, place[u], 1, 0)
        )
        pieces = partial_value.astype(bf16).reshape(pts_count, own_cols, block)
        summed = lax.all_to_all(pieces, "pts", 0, 0, tiled=False)
        resid = jnp.sum(summed.astype(f32), axis=0)
        at_pivot = (iota((block, 1), 0) == pivot_index[u][None, :]).astype(bf16)
        factor = kernel_tile(block_feats, mm(at_pivot, block_feats, 0, 0).astype(bf16))
        proj = mm(resid.astype(bf16), factor, 1, 0)
        lifted = mm(proj.astype(bf16), core[u], 1, 1).astype(bf16)
        step_bf = (resid - mm(lifted, factor, 1, 1)).astype(bf16)
        steps = lax.all_gather(step_bf, "pts", axis=0, tiled=True)
        change = mm(steps, place[u], 1, 1)
        all_steps.append(change.astype(bf16))
        current, moving = stepped(current, moving, change)
    gathered = lax.all_gather(jnp.stack(all_steps), "rows", axis=1, tiled=True)
    current, moving = coefficients, momentum
    for u in range(UPDATES):
        current, moving = stepped(current, moving, gathered[u].T.astype(f32))
    return (current, moving)


def shards(features, targets, coefficients, momentum, block_index, pivot_index, nystrom_core):
    rows, owners = lax.axis_size("rows"), lax.axis_size("pts")
    count = block_index.shape[1] // rows
    fits = rows == 4 and owners == 8 and coefficients.shape[1] == 8 * rows * owners
    fits = fits and coefficients.shape[0] % CHUNK == 0 and count % CHUNK == 0 and (3 * count // owners) % 64 == 0 and UPDATES * rows == 8
    plan = with_kernels if fits else with_operations
    return plan(
        features, targets, coefficients, momentum, block_index, pivot_index, nystrom_core
    )


def solution(mesh):
    in_specs = (P("pts", None), P("pts", None), P("pts", None), P("pts", None), P(), P(), P())
    out_specs = (P("pts", None), P("pts", None))
    return jax.shard_map(shards, mesh=mesh, in_specs=in_specs, out_specs=out_specs, check_vma=False)
```

```python
import functools
import math

import jax
import jax.numpy as jnp
from jax import lax
from jax.experimental import pallas as pl
from jax.experimental.pallas import tpu as pltpu
from jax.sharding import PartitionSpec as P

UPDATES = 2


alpha_mix = 0.6
beta_keep = 0.9
step_size = 0.2
momentum_gain = 1.5
ridge_term = 1.0

f32 = jnp.float32
bf16 = jnp.bfloat16
i32 = jnp.int32


def mm(a, b, ca, cb):
    return lax.dot_general(a, b, (((ca,), (cb,)), ((), ())), preferred_element_type=f32)


def split_two(value):
    high = value.astype(bf16)
    return high, (value - high.astype(f32)).astype(bf16)


def mixed_of(current, moving):
    return alpha_mix * moving + (1.0 - alpha_mix) * current


mix_per_step = alpha_mix * step_size * momentum_gain + (1.0 - alpha_mix) * step_size


def stepped(current, moving, change):
    mixed = mixed_of(current, moving)
    if change is None:
        return mixed, beta_keep * moving + (1.0 - beta_keep) * mixed
    return (
        mixed - step_size * change,
        beta_keep * moving + (1.0 - beta_keep) * mixed - step_size * momentum_gain * change,
    )


def iota(shape, axis):
    return lax.broadcasted_iota(i32, shape, axis)


def one_hot(chosen):
    return jnp.where(chosen, 1.0, 0.0).astype(bf16)


def before_matrix(n):
    return one_hot(iota((n, n), 0) < iota((n, n), 1))


def owners_of(indices, before, points, owners):
    owner = lax.div(indices, jnp.full_like(indices, points))
    owner_ids = iota((owners, indices.shape[1]), 0)
    marks = jnp.where(owner_ids == owner, 1.0, 0.0)
    earlier = mm(marks.astype(bf16), before, 1, 0)
    rank = jnp.sum(marks * earlier, axis=0, keepdims=True)
    start = jnp.sum(jnp.where(owner < owner_ids, 1.0, 0.0), axis=1, keepdims=True)
    return marks, rank, start


def sorted_places(marks, rank, start):
    return (rank + jnp.sum(marks * start, axis=0, keepdims=True)).astype(i32)


def lane_row(column):
    n = column.shape[0]
    diagonal = iota((n, 128), 0) == iota((n, 128), 1)
    return jnp.sum(jnp.where(diagonal, column, 0.0), axis=0, keepdims=True).astype(i32)


def sorted_points(indices, place):
    count = indices.shape[1]
    return from_digits(mm(two_digits(indices), one_hot(iota((count, count), 0) == place), 1, 1))


def two_digits(row):
    high = lax.shift_right_logical(row, jnp.full_like(row, 7))
    shape = (8, row.shape[1])
    value = jnp.where(iota(shape, 0) == 0, high, lax.bitwise_and(row, jnp.full_like(row, 127)))
    return value.astype(f32).astype(bf16)


def from_digits(digits):
    return (digits[0:1] * 128.0 + digits[1:2]).astype(i32)


def start_all(pairs, sems):
    copies = [pltpu.make_async_copy(a, b, sems.at[n]) for n, (a, b) in enumerate(pairs)]
    for copy in copies:
        copy.start()
    return copies


def wait_all(copies):
    for copy in copies:
        copy.wait()


def group_row(blocks, u, group, count):
    return blocks[u : u + 1, pl.ds(pl.multiple_of(group * count, count), count)]


def pack_kernel(count, cap, owners, blocks_hbm, feats_hbm, out_hbm, blocks, feats, packed, sems):
    row, me = lax.axis_index("rows"), lax.axis_index("pts")
    points = feats.shape[0]
    reads = start_all([(blocks_hbm, blocks), (feats_hbm, feats)], sems)
    before = before_matrix(count)
    reads[0].wait()
    rows = []
    for u in range(UPDATES):
        indices = group_row(blocks, u, row, count)
        local = indices - me * points
        mine = jnp.where((local >= 0) & (local < points), 1.0, 0.0)
        rank = mm(jnp.broadcast_to(mine, (8, count)).astype(bf16), before, 1, 0)[0:1]
        held = (iota((cap, count), 0) == rank.astype(i32)) & (mine > 0.0)
        point = jnp.sum(jnp.where(held, (local + 1).astype(f32), 0.0), axis=1, keepdims=True)
        rows.append(one_hot(iota((cap, points), 1) == point.astype(i32) - 1))
    reads[1].wait()
    for u in range(UPDATES):
        packed[u * cap : (u + 1) * cap, :] = mm(rows[u], feats[...], 1, 0).astype(bf16)
    wait_all(start_all([(packed, out_hbm)], sems))


def prepare_kernel(
    count, owners,
    blocks_hbm, w_hbm, z_hbm, t_hbm, coef_hbm, offset_hbm, starts_hbm,
    blocks, w, z, t, coef, offset, starts, sems, out_sems,
):
    row, me = lax.axis_index("rows"), lax.axis_index("pts")
    points, outputs = w.shape
    reads = start_all([(blocks_hbm, blocks), (w_hbm, w), (z_hbm, z), (t_hbm, t)], sems)
    before = before_matrix(count)
    reads[0].wait()
    locals_of = []
    for u in range(UPDATES):
        indices = group_row(blocks, u, row, count)
        marks, rank, start = owners_of(indices, before, points, owners)
        starts[u : u + 1, :] = lane_row(start)
        locals_of.append(sorted_points(indices, sorted_places(marks, rank, start)) - me * points)
    writes = start_all([(starts, starts_hbm)], out_sems)
    wait_all(reads[1:])
    current, moving = w[...], z[...]
    goal = t[...].astype(f32).T
    for u in range(UPDATES):
        mixed = mixed_of(current, moving).T
        high, low = split_two(ridge_term * mixed - goal)
        coef[u] = mixed.astype(bf16)
        place = one_hot(iota((points, count), 0) == locals_of[u])
        offset[u] = mm(high, place, 1, 0) + mm(low, place, 1, 0)
        current, moving = stepped(current, moving, None)
        for a, b in ((coef, coef_hbm), (offset, offset_hbm)):
            writes.append(pltpu.make_async_copy(a.at[u], b.at[u], out_sems.at[len(writes)]))
            writes[-1].start()
    wait_all(writes)


def order_kernel(
    u, count, points, owners,
    blocks_hbm, pivots_hbm, ids_hbm, starts_hbm, chosen_hbm,
    blocks, pivots, ids, starts, chosen, sems,
):
    wait_all(start_all([(blocks_hbm, blocks), (pivots_hbm, pivots)], sems))
    before = before_matrix(count)
    groups = blocks.shape[1] // count
    pivot = pivots[u : u + 1, :]
    found = jnp.zeros((8, pivot.shape[1]), f32)
    for g in range(groups):
        indices = blocks[u : u + 1, g * count : (g + 1) * count]
        marks, rank, start = owners_of(indices, before, points, owners)
        place = sorted_places(marks, rank, start)
        ids[g : g + 1, :] = sorted_points(indices, place)
        starts[g : g + 1, :] = lane_row(start)
        at_pivot = one_hot(iota((count, pivot.shape[1]), 0) + g * count == pivot)
        found += mm(two_digits(place + g * count), at_pivot, 1, 0)
    chosen[0:1, :] = from_digits(found)
    wait_all(start_all([(ids, ids_hbm), (starts, starts_hbm), (chosen, chosen_hbm)], sems))


def slots_kernel(count, points, cap, blocks_hbm, slots_hbm, blocks, slots, sems):
    me = lax.axis_index("pts")
    wait_all(start_all([(blocks_hbm, blocks)], sems))
    before = before_matrix(count)
    groups = blocks.shape[1] // count
    for u in range(UPDATES):
        found = jnp.zeros((8, groups * cap), f32)
        for g in range(groups):
            local = blocks[u : u + 1, g * count : (g + 1) * count] - me * points
            mine = (local >= 0) & (local < points)
            counts = jnp.where(mine, 1.0, 0.0)
            rank = mm(jnp.broadcast_to(counts, (8, count)).astype(bf16), before, 1, 0)[0:1]
            held = jnp.where(mine, rank.astype(i32) + g * cap, -1)
            chosen = one_hot(iota((groups * cap, count), 0) == held)
            found += mm(two_digits(jnp.where(mine, local + 1, 0)), chosen, 1, 1)
        slots[u : u + 1, :] = from_digits(found) - 1
    wait_all(start_all([(slots, slots_hbm)], sems))


def extended(rows, axis, first):
    rest = -0.5 * jnp.sum(jnp.square(rows.astype(f32)), axis=axis, keepdims=True)
    parts = []
    for _ in range(3):
        parts.append(rest.astype(bf16).astype(f32))
        rest = rest - parts[-1]
    parts = parts + [1.0] * 3 if first else [1.0] * 3 + parts
    at = iota(rows.shape, axis)
    extra = jnp.zeros(rows.shape, f32)
    for n, part in enumerate(parts):
        extra = jnp.where(at == n, part, extra)
    return jnp.concatenate([rows.astype(bf16), extra.astype(bf16)], axis=axis)


def exponent(left, right):
    return mm(left, right, 1, 0) * (7.0 / (left.shape[1] // 2) * math.log2(math.e))


CHUNK = 256


def compact_kernel(*refs):
    *came_hbm, starts_hbm, block_hbm, came, starts, wide, block, sems = refs
    me = lax.axis_index("pts")
    owners, deep, _ = came.shape
    cap = deep // UPDATES
    count = block.shape[2]
    pairs = [(a, came.at[k]) for k, a in enumerate(came_hbm)]
    wait_all(start_all([*pairs, (starts_hbm, starts)], sems))
    for u in range(UPDATES):
        for o in range(owners):
            start = starts[u, o]
            rows = came[lax.bitwise_xor(me, o), u * cap : (u + 1) * cap, :]
            wide[u, pl.ds(start, cap), :] = rows.astype(f32)
        block[u] = wide[u, 0:count, :].T.astype(bf16)
    wait_all(start_all([(block, block_hbm)], sems))


def sums_kernel(
    block_hbm, feats_hbm, coef_hbm, offset_hbm, pieces_hbm,
    block, feats, coef, offset, tile, pieces, sems,
):
    outputs = coef.shape[1]
    pairs = [(block_hbm, block), (feats_hbm, feats), (coef_hbm, coef), (offset_hbm, offset)]
    reads = start_all(pairs, sems)
    wait_all(reads[:2])
    left = extended(feats[...], 1, True)
    for u in range(UPDATES):
        right = extended(block[u], 0, False)
        tile[...] = jnp.exp2(exponent(left, right)).astype(bf16)
        if u == 0:
            wait_all(reads[2:])
        total = offset[u] + mm(coef[u], tile[...], 1, 0)
        devices, _, lanes = pieces.shape
        own = outputs // devices
        for d in range(devices):
            part = total[d * own : (d + 1) * own]
            pieces[d, 2 * own * u : 2 * own * (u + 1), :] = jnp.concatenate(
                [part[:, :lanes], part[:, lanes:]], axis=0
            ).astype(bf16)
    wait_all(start_all([(pieces, pieces_hbm)], sems))


def factors_kernel(
    b0_hbm, b1_hbm, b2_hbm, b3_hbm, ids0_hbm, ids1_hbm, pivots0_hbm, pivots1_hbm, factor_hbm, cross_hbm,
    feats, ids, pivots, factor, cross, sems,
):
    row = lax.axis_index("rows")
    groups, _, width, count = feats.shape
    pairs = [(b_hbm, feats.at[k]) for k, b_hbm in enumerate((b0_hbm, b1_hbm, b2_hbm, b3_hbm))]
    pairs += [(ids0_hbm, ids.at[0]), (ids1_hbm, ids.at[1])]
    pairs += [(pivots0_hbm, pivots.at[0]), (pivots1_hbm, pivots.at[1])]
    wait_all(start_all(pairs, sems))
    places = [lax.bitwise_xor(row, k) for k in range(groups)]
    rights = [[extended(feats[k, u], 0, False) for k in range(groups)] for u in range(UPDATES)]
    for u in range(UPDATES):
        chosen_feats = jnp.zeros((width, pivots.shape[2]), f32)
        for k in range(groups):
            chosen = iota((count, pivots.shape[2]), 0) + places[k] * count == pivots[u, 0:1, :]
            chosen_feats += mm(feats[k, u], one_hot(chosen), 1, 0)
        left = extended(chosen_feats.T, 1, True)
        for k in range(groups):
            start = pl.multiple_of(places[k] * count, count)
            value = jnp.exp2(exponent(left, rights[u][k]))
            factor[u, :, pl.ds(start, count)] = value.astype(bf16)
    writes = start_all([(factor, factor_hbm)], sems)
    lefts, left_points = [], []
    for k in range(groups):
        lefts.append(extended(feats[k, 0].astype(f32).T, 1, True))
        points = ids[0, pl.ds(places[k], 1), :].astype(f32)
        left_points.append(jnp.broadcast_to(points, (8, count)).T[:, 0:1])
    left, left_points = jnp.concatenate(lefts, axis=0), jnp.concatenate(left_points, axis=0)
    sent = 1
    for m in range(groups):
        right_points = ids[1, pl.ds(places[m], 1), :].astype(f32)
        power = exponent(left, rights[1][m])
        power = jnp.where(left_points == right_points, math.log2(1.0 + ridge_term), power)
        cross[m] = jnp.exp2(power).astype(bf16).reshape(groups, count, count)
        for k in range(groups):
            start = pl.multiple_of(places[k] * count, count)
            copy = pltpu.make_async_copy(
                cross.at[m, k], cross_hbm.at[places[m], pl.ds(start, count), :], sems.at[sent]
            )
            copy.start()
            writes.append(copy)
            sent += 1
    wait_all(writes)


def chain_kernel(
    cap, owners,
    summed, factor_hbm, core_hbm, cross_hbm, starts0_hbm, starts1_hbm, out_hbm,
    factor, core, cross, starts0, starts1, packed, sems,
):
    groups, _, count = cross.shape
    own = summed.shape[1] // (2 * UPDATES)
    pairs, starts = [], (starts0, starts1)
    for u in range(UPDATES):
        pairs += [(factor_hbm.at[u], factor.at[u]), (core_hbm.at[u], core.at[u])]
        if u == 0:
            pairs += [(starts0_hbm, starts0), (starts1_hbm, starts1)]
            pairs += [(cross_hbm.at[g], cross.at[g]) for g in range(groups)]
    reads = start_all(pairs, sems)
    step = None
    for u in range(UPDATES):
        sums = []
        for g in range(groups):
            part = summed[g * owners, 2 * own * u : 2 * own * (u + 1), :].astype(f32)
            for o in range(1, owners):
                part += summed[g * owners + o, 2 * own * u : 2 * own * (u + 1), :].astype(f32)
            part = jnp.concatenate([part[:own], part[own:]], axis=1)
            if u:
                reads[4 + g].wait()
                part -= mix_per_step * mm(step, cross[g], 1, 0)
            sums.append(part)
        resid = jnp.concatenate(sums, axis=1)
        wait_all(reads[0:4] if u == 0 else reads[4 + groups :])
        proj = mm(resid.astype(bf16), factor[u], 1, 1)
        lifted = mm(proj.astype(bf16), core[u], 1, 1).astype(bf16)
        step = (resid - mm(lifted, factor[u], 1, 0)).astype(bf16)
        half = groups // 2
        for o in range(owners):
            lanes = []
            for g in range(groups):
                part = step[:, g * count : (g + 1) * count].astype(f32)
                back = lax.rem(count - starts[u][g, o], count)
                lanes.append(pltpu.roll(part, back, 1)[:, :cap])
            packed[o, 2 * own * u : 2 * own * (u + 1), :] = jnp.concatenate(
                [jnp.concatenate(lanes[h * half : (h + 1) * half], axis=1) for h in range(2)], axis=0
            ).astype(bf16)
    wait_all(start_all([(packed, out_hbm)], sems))


def finish_kernel(
    g0_hbm, g1_hbm, g2_hbm, g3_hbm, slots_hbm, w_hbm, z_hbm, w_out, z_out,
    got, slots, w, z, steps, w_new, z_new, sems, out_sems,
):
    row = lax.axis_index("rows")
    points = w.shape[0]
    sources, deep, lanes = got.shape
    own = deep // (2 * UPDATES)
    chunks = range(0, points, CHUNK)
    pairs = [(slots_hbm, slots)]
    for k, g_hbm in enumerate((g0_hbm, g1_hbm, g2_hbm, g3_hbm)):
        size = g_hbm.shape[0]
        first = pl.multiple_of(lax.bitwise_xor(row, k) * size, size)
        pairs.append((g_hbm, got.at[pl.ds(first, size)]))
    for c in chunks:
        part = slice(c, c + CHUNK)
        pairs += [(w_hbm.at[part], w.at[part]), (z_hbm.at[part], z.at[part])]
    reads = start_all(pairs, sems)
    wait_all(reads[:5])
    reads = reads[5:]
    wide = got[...].astype(f32)
    for u in range(UPDATES):
        for h in range(2):
            first = own * (2 * u + h)
            part = wide[:, first : first + own, :].reshape(sources * own, lanes)
            steps[u, h * lanes : (h + 1) * lanes, :] = part.T.astype(bf16)
    changes = []
    for u in range(UPDATES):
        rows = one_hot(iota((points, slots.shape[1]), 0) == slots[u : u + 1, :])
        changes.append(mm(rows, steps[u], 1, 0))
    writes = []
    for n, c in enumerate(chunks):
        part = slice(c, c + CHUNK)
        wait_all(reads[2 * n : 2 * n + 2])
        current, moving = w[part, :], z[part, :]
        for change in changes:
            current, moving = stepped(current, moving, change[part])
        w_new[part, :] = current
        z_new[part, :] = moving
        for m, (a, b) in enumerate(((w_new, w_out), (z_new, z_out))):
            copy = pltpu.make_async_copy(a.at[part], b.at[part], out_sems.at[2 * n + m])
            copy.start()
            writes.append(copy)
    wait_all(writes)


VMEM = pl.BlockSpec(memory_space=pltpu.VMEM)
HBM = pl.BlockSpec(memory_space=pltpu.HBM)
in_smem = type(pltpu.SMEM((1,), i32))


def like(shape, dtype=bf16):
    return jax.ShapeDtypeStruct(shape, dtype)


def call(body, outs, inside, *args, near=0, sems=(), flops=0, grant=62):
    moved = sum(math.prod(o.shape) * o.dtype.itemsize for o in [*outs, *args])
    return pl.pallas_call(
        body,
        out_shape=outs,
        in_specs=[VMEM] * near + [HBM] * (len(args) - near),
        out_specs=[HBM] * len(outs),
        scratch_shapes=[
            x if isinstance(x, in_smem) else pltpu.VMEM(x.shape, x.dtype) for x in inside
        ]
        + [pltpu.SemaphoreType.DMA((n,)) for n in sems],
        compiler_params=pltpu.CompilerParams(vmem_limit_bytes=grant * 2**20),
        cost_estimate=pl.CostEstimate(flops=int(flops), bytes_accessed=moved, transcendentals=0),
    )(*args)


def swap(value, axis, k):
    return lax.ppermute(value, axis, [(i, i ^ k) for i in range(lax.axis_size(axis))])


def with_kernels(features, targets, coefficients, momentum, block_index, pivot_index, core):
    rows, owners = lax.axis_size("rows"), lax.axis_size("pts")
    points, width = features.shape
    block = block_index.shape[1]
    rank = pivot_index.shape[1]
    outputs = coefficients.shape[1]
    count = block // rows
    cap = 3 * count // owners
    devices = rows * owners
    own = outputs // devices
    deep = 2 * own * UPDATES
    half = rows // 2
    wide = like(coefficients.shape, f32)

    (packed,) = call(
        functools.partial(pack_kernel, count, cap, owners),
        [like((UPDATES * cap, width))],
        [block_index, features, like((UPDATES * cap, width))],
        block_index,
        features,
        sems=(2,),
    )
    came = {k: swap(packed, "pts", k) for k in reversed(range(3, owners))}
    kept = [
        like((UPDATES, outputs, points)),
        like((UPDATES, outputs, count), f32),
        like((8, 128), i32),
    ]
    given = [block_index, coefficients, momentum, targets]
    coef, offset, row_starts = call(
        functools.partial(prepare_kernel, count, owners),
        kept,
        given + kept,
        *given,
        sems=(4, 1 + 2 * UPDATES),
    )
    again, row_starts, later_index = lax.optimization_barrier((packed, row_starts, block_index))
    came.update({k: swap(again, "pts", k) for k in (2, 1)})

    def ordered(u, indices):
        kept = [like((rows, count), i32), like((8, 128), i32), like((8, rank), i32)]
        return call(
            functools.partial(order_kernel, u, count, points, owners),
            kept,
            [block_index, pivot_index, *kept],
            indices,
            pivot_index,
            sems=(3,),
        )

    ids, starts, chosen = ordered(0, later_index)
    row_starts, ids = lax.optimization_barrier((row_starts, ids))
    feats = like((UPDATES, width, count))
    inside_starts = pltpu.SMEM(row_starts.shape, i32)
    (mine,) = call(
        compact_kernel,
        [feats],
        [
            like((owners, *packed.shape)),
            inside_starts,
            like((UPDATES, count + cap, width), f32),
            feats,
        ],
        packed,
        *[came[k] for k in range(1, owners)],
        row_starts,
        sems=(owners + 1,),
        grant=48,
    )
    beside, across = swap(mine, "rows", 1), swap(mine, "rows", 2)
    pieces = like((devices, deep, count // 2))
    (pieces,) = call(
        sums_kernel,
        [pieces],
        [feats, features, coef, offset, like((points, count)), pieces],
        mine,
        features,
        coef,
        offset,
        sems=(4,),
        flops=2.0 * UPDATES * points * count * (2 * width + outputs),
    )
    pieces, later_index = lax.optimization_barrier((pieces, block_index))
    later_ids, later_starts, later_chosen = ordered(1, later_index)
    pieces, beside, across, later_ids = lax.optimization_barrier(
        (pieces, beside, across, later_ids)
    )
    summed = lax.all_to_all(pieces, ("rows", "pts"), 0, 0, tiled=True)
    kept = [like((UPDATES, rank, block)), like((rows, block, count))]
    factor, cross = call(
        factors_kernel,
        kept,
        [
            like((rows, *feats.shape)),
            like((UPDATES, *ids.shape), i32),
            like((UPDATES, *chosen.shape), i32),
            kept[0],
            like((rows, rows, count, count)),
        ],
        mine,
        beside,
        across,
        swap(across, "rows", 1),
        ids,
        later_ids,
        chosen,
        later_chosen,
        sems=(rows * rows + 2,),
        grant=57,
        flops=2.0 * width * block * (UPDATES * rank + block),
    )
    pieces = like((owners, deep, half * cap))
    (steps,) = call(
        functools.partial(chain_kernel, cap, owners),
        [pieces],
        [factor, core, cross, inside_starts, inside_starts, pieces],
        summed,
        factor,
        core,
        cross,
        starts,
        later_starts,
        near=1,
        sems=(2 * UPDATES + 2 + rows,),
        grant=52,
    )
    steps, later_index = lax.optimization_barrier((steps, block_index))
    (slots,) = call(
        functools.partial(slots_kernel, count, points, cap),
        [like((UPDATES, rows * cap), i32)],
        [block_index, like((UPDATES, rows * cap), i32)],
        later_index,
        sems=(1,),
    )
    got = lax.all_to_all(steps, "pts", 0, 0, tiled=True)
    got, slots = lax.optimization_barrier((got, slots))
    beside, across = swap(got, "rows", 1), swap(got, "rows", 2)
    parts = points // CHUNK
    return call(
        finish_kernel,
        [wide] * 2,
        [
            like((devices, deep, half * cap)),
            slots,
            wide,
            wide,
            like((UPDATES, rows * cap, outputs)),
            wide,
            wide,
        ],
        got,
        beside,
        across,
        swap(across, "rows", 1),
        slots,
        coefficients,
        momentum,
        sems=(1 + rows + 2 * parts, 2 * parts),
        grant=48,
    )


def kernel_tile(left_rows, right_rows):
    inner_prod = mm(left_rows, right_rows, 1, 1)
    left_sq = jnp.sum(jnp.square(left_rows.astype(f32)), axis=1)
    right_sq = jnp.sum(jnp.square(right_rows.astype(f32)), axis=1)
    squared = left_sq[:, None] + right_sq[None, :] - 2.0 * inner_prod
    return jnp.exp(squared * (-3.5 / left_rows.shape[1])).astype(bf16)


def with_operations(features, targets, coefficients, momentum, block_index, pivot_index, core):
    row_count, pts_count = lax.axis_size("rows"), lax.axis_size("pts")
    row_id, pts_id = lax.axis_index("rows"), lax.axis_index("pts")
    points = features.shape[0]
    block = block_index.shape[1]
    outputs = coefficients.shape[1]
    per_row = block // row_count
    per_device = per_row // pts_count
    row_cols = outputs // row_count
    own_cols = row_cols // pts_count
    first = row_id * row_cols
    current, moving, goal = (
        lax.dynamic_slice_in_dim(value, first, row_cols, axis=1).T.astype(f32)
        for value in (coefficients, momentum, targets)
    )
    ids = iota((points, 1), 0) + pts_id * points
    place = [(ids == block_index[u][None, :]).astype(bf16) for u in range(UPDATES)]
    own_rows = []
    for u in range(UPDATES):
        mine = lax.dynamic_slice_in_dim(place[u], row_id * per_row, per_row, axis=1)
        own_rows.append(mm(mine, features, 0, 0).astype(bf16).reshape(pts_count, per_device, -1))
    came = lax.all_to_all(jnp.concatenate(own_rows, axis=1), "pts", 0, 0, tiled=False)
    chunk = jnp.sum(came.astype(f32), axis=0).astype(bf16)
    spread = lax.all_gather(lax.all_gather(chunk, "pts", axis=0), "rows", axis=0)
    spread = spread.reshape(row_count, pts_count, UPDATES, per_device, features.shape[1])
    all_steps = []
    for u in range(UPDATES):
        block_feats = spread[:, :, u].reshape(block, features.shape[1])
        mixed = mixed_of(current, moving)
        high, low = split_two(ridge_term * mixed - goal)
        tile = kernel_tile(features, block_feats)
        partial_value = (
            mm(mixed.astype(bf16), tile, 1, 0) + mm(high, place[u], 1, 0) + mm(low, place[u], 1, 0)
        )
        pieces = partial_value.astype(bf16).reshape(pts_count, own_cols, block)
        summed = lax.all_to_all(pieces, "pts", 0, 0, tiled=False)
        resid = jnp.sum(summed.astype(f32), axis=0)
        at_pivot = (iota((block, 1), 0) == pivot_index[u][None, :]).astype(bf16)
        factor = kernel_tile(block_feats, mm(at_pivot, block_feats, 0, 0).astype(bf16))
        proj = mm(resid.astype(bf16), factor, 1, 0)
        lifted = mm(proj.astype(bf16), core[u], 1, 1).astype(bf16)
        step_bf = (resid - mm(lifted, factor, 1, 1)).astype(bf16)
        steps = lax.all_gather(step_bf, "pts", axis=0, tiled=True)
        change = mm(steps, place[u], 1, 1)
        all_steps.append(change.astype(bf16))
        current, moving = stepped(current, moving, change)
    gathered = lax.all_gather(jnp.stack(all_steps), "rows", axis=1, tiled=True)
    current, moving = coefficients, momentum
    for u in range(UPDATES):
        current, moving = stepped(current, moving, gathered[u].T.astype(f32))
    return (current, moving)


def shards(features, targets, coefficients, momentum, block_index, pivot_index, nystrom_core):
    rows, owners = lax.axis_size("rows"), lax.axis_size("pts")
    count = block_index.shape[1] // rows
    fits = rows == 4 and owners == 8 and coefficients.shape[1] == 8 * rows * owners
    fits = fits and coefficients.shape[0] % CHUNK == 0 and count % CHUNK == 0 and (3 * count // owners) % 64 == 0 and UPDATES * rows == 8
    plan = with_kernels if fits else with_operations
    return plan(
        features, targets, coefficients, momentum, block_index, pivot_index, nystrom_core
    )


def solution(mesh):
    in_specs = (P("pts", None), P("pts", None), P("pts", None), P("pts", None), P(), P(), P())
    out_specs = (P("pts", None), P("pts", None))
    return jax.shard_map(shards, mesh=mesh, in_specs=in_specs, out_specs=out_specs, check_vma=False)
```

```python
import functools
import math

import jax
import jax.numpy as jnp
from jax import lax
from jax.experimental import pallas as pl
from jax.experimental.pallas import tpu as pltpu
from jax.sharding import PartitionSpec as P

UPDATES = 2


alpha_mix = 0.6
beta_keep = 0.9
step_size = 0.2
momentum_gain = 1.5
ridge_term = 1.0

f32 = jnp.float32
bf16 = jnp.bfloat16
i32 = jnp.int32


def mm(a, b, ca, cb):
    return lax.dot_general(a, b, (((ca,), (cb,)), ((), ())), preferred_element_type=f32)


def split_two(value):
    high = value.astype(bf16)
    return high, (value - high.astype(f32)).astype(bf16)


def mixed_of(current, moving):
    return alpha_mix * moving + (1.0 - alpha_mix) * current


mix_per_step = alpha_mix * step_size * momentum_gain + (1.0 - alpha_mix) * step_size


def stepped(current, moving, change):
    mixed = mixed_of(current, moving)
    if change is None:
        return mixed, beta_keep * moving + (1.0 - beta_keep) * mixed
    return (
        mixed - step_size * change,
        beta_keep * moving + (1.0 - beta_keep) * mixed - step_size * momentum_gain * change,
    )


def iota(shape, axis):
    return lax.broadcasted_iota(i32, shape, axis)


def one_hot(chosen):
    return jnp.where(chosen, 1.0, 0.0).astype(bf16)


def before_matrix(n):
    return one_hot(iota((n, n), 0) < iota((n, n), 1))


def owners_of(indices, before, points, owners):
    owner = lax.div(indices, jnp.full_like(indices, points))
    owner_ids = iota((owners, indices.shape[1]), 0)
    marks = jnp.where(owner_ids == owner, 1.0, 0.0)
    earlier = mm(marks.astype(bf16), before, 1, 0)
    rank = jnp.sum(marks * earlier, axis=0, keepdims=True)
    start = jnp.sum(jnp.where(owner < owner_ids, 1.0, 0.0), axis=1, keepdims=True)
    return marks, rank, start


def sorted_places(marks, rank, start):
    return (rank + jnp.sum(marks * start, axis=0, keepdims=True)).astype(i32)


def lane_row(column):
    n = column.shape[0]
    diagonal = iota((n, 128), 0) == iota((n, 128), 1)
    return jnp.sum(jnp.where(diagonal, column, 0.0), axis=0, keepdims=True).astype(i32)


def sorted_points(indices, place):
    count = indices.shape[1]
    return from_digits(mm(two_digits(indices), one_hot(iota((count, count), 0) == place), 1, 1))


def two_digits(row):
    high = lax.shift_right_logical(row, jnp.full_like(row, 7))
    shape = (8, row.shape[1])
    value = jnp.where(iota(shape, 0) == 0, high, lax.bitwise_and(row, jnp.full_like(row, 127)))
    return value.astype(f32).astype(bf16)


def from_digits(digits):
    return (digits[0:1] * 128.0 + digits[1:2]).astype(i32)


def start_all(pairs, sems):
    copies = [pltpu.make_async_copy(a, b, sems.at[n]) for n, (a, b) in enumerate(pairs)]
    for copy in copies:
        copy.start()
    return copies


def wait_all(copies):
    for copy in copies:
        copy.wait()


def group_row(blocks, u, group, count):
    return blocks[u : u + 1, pl.ds(pl.multiple_of(group * count, count), count)]


def pack_kernel(count, cap, owners, blocks_hbm, feats_hbm, out_hbm, blocks, feats, packed, sems):
    row, me = lax.axis_index("rows"), lax.axis_index("pts")
    points = feats.shape[0]
    reads = start_all([(blocks_hbm, blocks), (feats_hbm, feats)], sems)
    before = before_matrix(count)
    reads[0].wait()
    rows = []
    for u in range(UPDATES):
        indices = group_row(blocks, u, row, count)
        local = indices - me * points
        mine = jnp.where((local >= 0) & (local < points), 1.0, 0.0)
        rank = mm(jnp.broadcast_to(mine, (8, count)).astype(bf16), before, 1, 0)[0:1]
        held = (iota((cap, count), 0) == rank.astype(i32)) & (mine > 0.0)
        point = jnp.sum(jnp.where(held, (local + 1).astype(f32), 0.0), axis=1, keepdims=True)
        rows.append(one_hot(iota((cap, points), 1) == point.astype(i32) - 1))
    reads[1].wait()
    for u in range(UPDATES):
        packed[u * cap : (u + 1) * cap, :] = mm(rows[u], feats[...], 1, 0).astype(bf16)
    wait_all(start_all([(packed, out_hbm)], sems))


def prepare_kernel(
    count, owners,
    blocks_hbm, w_hbm, z_hbm, t_hbm, coef_hbm, offset_hbm, starts_hbm,
    blocks, w, z, t, coef, offset, starts, sems, out_sems,
):
    row, me = lax.axis_index("rows"), lax.axis_index("pts")
    points, outputs = w.shape
    reads = start_all([(blocks_hbm, blocks), (w_hbm, w), (z_hbm, z), (t_hbm, t)], sems)
    before = before_matrix(count)
    reads[0].wait()
    locals_of = []
    for u in range(UPDATES):
        indices = group_row(blocks, u, row, count)
        marks, rank, start = owners_of(indices, before, points, owners)
        starts[u : u + 1, :] = lane_row(start)
        locals_of.append(sorted_points(indices, sorted_places(marks, rank, start)) - me * points)
    writes = start_all([(starts, starts_hbm)], out_sems)
    wait_all(reads[1:])
    current, moving = w[...], z[...]
    goal = t[...].astype(f32).T
    for u in range(UPDATES):
        mixed = mixed_of(current, moving).T
        high, low = split_two(ridge_term * mixed - goal)
        coef[u] = mixed.astype(bf16)
        place = one_hot(iota((points, count), 0) == locals_of[u])
        offset[u] = mm(high, place, 1, 0) + mm(low, place, 1, 0)
        current, moving = stepped(current, moving, None)
        for a, b in ((coef, coef_hbm), (offset, offset_hbm)):
            writes.append(pltpu.make_async_copy(a.at[u], b.at[u], out_sems.at[len(writes)]))
            writes[-1].start()
    wait_all(writes)


def order_kernel(
    u, count, points, owners,
    blocks_hbm, pivots_hbm, ids_hbm, starts_hbm, chosen_hbm,
    blocks, pivots, ids, starts, chosen, sems,
):
    wait_all(start_all([(blocks_hbm, blocks), (pivots_hbm, pivots)], sems))
    before = before_matrix(count)
    groups = blocks.shape[1] // count
    pivot = pivots[u : u + 1, :]
    found = jnp.zeros((8, pivot.shape[1]), f32)
    for g in range(groups):
        indices = blocks[u : u + 1, g * count : (g + 1) * count]
        marks, rank, start = owners_of(indices, before, points, owners)
        place = sorted_places(marks, rank, start)
        ids[g : g + 1, :] = sorted_points(indices, place)
        starts[g : g + 1, :] = lane_row(start)
        at_pivot = one_hot(iota((count, pivot.shape[1]), 0) + g * count == pivot)
        found += mm(two_digits(place + g * count), at_pivot, 1, 0)
    chosen[0:1, :] = from_digits(found)
    wait_all(start_all([(ids, ids_hbm), (starts, starts_hbm), (chosen, chosen_hbm)], sems))


def slots_kernel(count, points, cap, blocks_hbm, slots_hbm, blocks, slots, sems):
    me = lax.axis_index("pts")
    wait_all(start_all([(blocks_hbm, blocks)], sems))
    before = before_matrix(count)
    groups = blocks.shape[1] // count
    for u in range(UPDATES):
        found = jnp.zeros((8, groups * cap), f32)
        for g in range(groups):
            local = blocks[u : u + 1, g * count : (g + 1) * count] - me * points
            mine = (local >= 0) & (local < points)
            counts = jnp.where(mine, 1.0, 0.0)
            rank = mm(jnp.broadcast_to(counts, (8, count)).astype(bf16), before, 1, 0)[0:1]
            held = jnp.where(mine, rank.astype(i32) + g * cap, -1)
            chosen = one_hot(iota((groups * cap, count), 0) == held)
            found += mm(two_digits(jnp.where(mine, local + 1, 0)), chosen, 1, 1)
        slots[u : u + 1, :] = from_digits(found) - 1
    wait_all(start_all([(slots, slots_hbm)], sems))


def extended(rows, axis, first):
    rest = -0.5 * jnp.sum(jnp.square(rows.astype(f32)), axis=axis, keepdims=True)
    parts = []
    for _ in range(3):
        parts.append(rest.astype(bf16).astype(f32))
        rest = rest - parts[-1]
    parts = parts + [1.0] * 3 if first else [1.0] * 3 + parts
    at = iota(rows.shape, axis)
    extra = jnp.zeros(rows.shape, f32)
    for n, part in enumerate(parts):
        extra = jnp.where(at == n, part, extra)
    return jnp.concatenate([rows.astype(bf16), extra.astype(bf16)], axis=axis)


def exponent(left, right):
    return mm(left, right, 1, 0) * (7.0 / (left.shape[1] // 2) * math.log2(math.e))


CHUNK = 256


def compact_kernel(*refs):
    *came_hbm, starts_hbm, block_hbm, came, starts, wide, block, sems = refs
    me = lax.axis_index("pts")
    owners, deep, _ = came.shape
    cap = deep // UPDATES
    count = block.shape[2]
    pairs = [(a, came.at[k]) for k, a in enumerate(came_hbm)]
    wait_all(start_all([*pairs, (starts_hbm, starts)], sems))
    for u in range(UPDATES):
        for o in range(owners):
            start = starts[u, o]
            rows = came[lax.bitwise_xor(me, o), u * cap : (u + 1) * cap, :]
            wide[u, pl.ds(start, cap), :] = rows.astype(f32)
        block[u] = wide[u, 0:count, :].T.astype(bf16)
    wait_all(start_all([(block, block_hbm)], sems))


def sums_kernel(
    block_hbm, feats_hbm, coef_hbm, offset_hbm, pieces_hbm,
    block, feats, coef, offset, tile, pieces, sems,
):
    outputs = coef.shape[1]
    pairs = [(block_hbm, block), (feats_hbm, feats), (coef_hbm, coef), (offset_hbm, offset)]
    reads = start_all(pairs, sems)
    wait_all(reads[:2])
    left = extended(feats[...], 1, True)
    for u in range(UPDATES):
        right = extended(block[u], 0, False)
        tile[...] = jnp.exp2(exponent(left, right)).astype(bf16)
        if u == 0:
            wait_all(reads[2:])
        total = offset[u] + mm(coef[u], tile[...], 1, 0)
        devices, _, lanes = pieces.shape
        own = outputs // devices
        for d in range(devices):
            part = total[d * own : (d + 1) * own]
            pieces[d, 2 * own * u : 2 * own * (u + 1), :] = jnp.concatenate(
                [part[:, :lanes], part[:, lanes:]], axis=0
            ).astype(bf16)
    wait_all(start_all([(pieces, pieces_hbm)], sems))


def factors_kernel(
    b0_hbm, b1_hbm, b2_hbm, b3_hbm, ids0_hbm, ids1_hbm, pivots0_hbm, pivots1_hbm, factor_hbm, cross_hbm,
    feats, ids, pivots, factor, cross, sems,
):
    row = lax.axis_index("rows")
    groups, _, width, count = feats.shape
    pairs = [(b_hbm, feats.at[k]) for k, b_hbm in enumerate((b0_hbm, b1_hbm, b2_hbm, b3_hbm))]
    pairs += [(ids0_hbm, ids.at[0]), (ids1_hbm, ids.at[1])]
    pairs += [(pivots0_hbm, pivots.at[0]), (pivots1_hbm, pivots.at[1])]
    wait_all(start_all(pairs, sems))
    places = [lax.bitwise_xor(row, k) for k in range(groups)]
    rights = [[extended(feats[k, u], 0, False) for k in range(groups)] for u in range(UPDATES)]
    for u in range(UPDATES):
        chosen_feats = jnp.zeros((width, pivots.shape[2]), f32)
        for k in range(groups):
            chosen = iota((count, pivots.shape[2]), 0) + places[k] * count == pivots[u, 0:1, :]
            chosen_feats += mm(feats[k, u], one_hot(chosen), 1, 0)
        left = extended(chosen_feats.T, 1, True)
        for k in range(groups):
            start = pl.multiple_of(places[k] * count, count)
            value = jnp.exp2(exponent(left, rights[u][k]))
            factor[u, :, pl.ds(start, count)] = value.astype(bf16)
    writes = start_all([(factor, factor_hbm)], sems)
    lefts, left_points = [], []
    for k in range(groups):
        lefts.append(extended(feats[k, 0].astype(f32).T, 1, True))
        points = ids[0, pl.ds(places[k], 1), :].astype(f32)
        left_points.append(jnp.broadcast_to(points, (8, count)).T[:, 0:1])
    left, left_points = jnp.concatenate(lefts, axis=0), jnp.concatenate(left_points, axis=0)
    sent = 1
    for m in range(groups):
        right_points = ids[1, pl.ds(places[m], 1), :].astype(f32)
        power = exponent(left, rights[1][m])
        power = jnp.where(left_points == right_points, math.log2(1.0 + ridge_term), power)
        cross[m] = jnp.exp2(power).astype(bf16).reshape(groups, count, count)
        for k in range(groups):
            start = pl.multiple_of(places[k] * count, count)
            copy = pltpu.make_async_copy(
                cross.at[m, k], cross_hbm.at[places[m], pl.ds(start, count), :], sems.at[sent]
            )
            copy.start()
            writes.append(copy)
            sent += 1
    wait_all(writes)


def chain_kernel(
    cap, owners,
    summed_hbm, factor_hbm, core_hbm, cross_hbm, starts0_hbm, starts1_hbm, out_hbm,
    summed, factor, core, cross, starts0, starts1, packed, sems,
):
    groups, _, count = cross.shape
    own = summed.shape[1] // (2 * UPDATES)
    pairs, starts = [(summed_hbm, summed)], (starts0, starts1)
    for u in range(UPDATES):
        pairs += [(factor_hbm.at[u], factor.at[u]), (core_hbm.at[u], core.at[u])]
        if u == 0:
            pairs += [(starts0_hbm, starts0), (starts1_hbm, starts1)]
            pairs += [(cross_hbm.at[g], cross.at[g]) for g in range(groups)]
    reads = start_all(pairs, sems)
    first, *reads = reads
    first.wait()
    step = None
    for u in range(UPDATES):
        sums = []
        for g in range(groups):
            part = summed[g * owners, 2 * own * u : 2 * own * (u + 1), :].astype(f32)
            for o in range(1, owners):
                part += summed[g * owners + o, 2 * own * u : 2 * own * (u + 1), :].astype(f32)
            part = jnp.concatenate([part[:own], part[own:]], axis=1)
            if u:
                reads[4 + g].wait()
                part -= mix_per_step * mm(step, cross[g], 1, 0)
            sums.append(part)
        resid = jnp.concatenate(sums, axis=1)
        wait_all(reads[0:4] if u == 0 else reads[4 + groups :])
        proj = mm(resid.astype(bf16), factor[u], 1, 1)
        lifted = mm(proj.astype(bf16), core[u], 1, 1).astype(bf16)
        step = (resid - mm(lifted, factor[u], 1, 0)).astype(bf16)
        half = groups // 2
        for o in range(owners):
            lanes = []
            for g in range(groups):
                part = step[:, g * count : (g + 1) * count].astype(f32)
                back = lax.rem(count - starts[u][g, o], count)
                lanes.append(pltpu.roll(part, back, 1)[:, :cap])
            packed[o, 2 * own * u : 2 * own * (u + 1), :] = jnp.concatenate(
                [jnp.concatenate(lanes[h * half : (h + 1) * half], axis=1) for h in range(2)], axis=0
            ).astype(bf16)
    wait_all(start_all([(packed, out_hbm)], sems))


def finish_kernel(
    g0_hbm, g1_hbm, g2_hbm, g3_hbm, slots_hbm, w_hbm, z_hbm, w_out, z_out,
    got, slots, w, z, steps, w_new, z_new, sems, out_sems,
):
    row = lax.axis_index("rows")
    points = w.shape[0]
    sources, deep, lanes = got.shape
    own = deep // (2 * UPDATES)
    chunks = range(0, points, CHUNK)
    pairs = [(slots_hbm, slots)]
    for k, g_hbm in enumerate((g0_hbm, g1_hbm, g2_hbm, g3_hbm)):
        size = g_hbm.shape[0]
        first = pl.multiple_of(lax.bitwise_xor(row, k) * size, size)
        pairs.append((g_hbm, got.at[pl.ds(first, size)]))
    for c in chunks:
        part = slice(c, c + CHUNK)
        pairs += [(w_hbm.at[part], w.at[part]), (z_hbm.at[part], z.at[part])]
    reads = start_all(pairs, sems)
    wait_all(reads[:5])
    reads = reads[5:]
    wide = got[...].astype(f32)
    for u in range(UPDATES):
        for h in range(2):
            first = own * (2 * u + h)
            part = wide[:, first : first + own, :].reshape(sources * own, lanes)
            steps[u, h * lanes : (h + 1) * lanes, :] = part.T.astype(bf16)
    changes = []
    for u in range(UPDATES):
        rows = one_hot(iota((points, slots.shape[1]), 0) == slots[u : u + 1, :])
        changes.append(mm(rows, steps[u], 1, 0))
    writes = []
    for n, c in enumerate(chunks):
        part = slice(c, c + CHUNK)
        wait_all(reads[2 * n : 2 * n + 2])
        current, moving = w[part, :], z[part, :]
        for change in changes:
            current, moving = stepped(current, moving, change[part])
        w_new[part, :] = current
        z_new[part, :] = moving
        for m, (a, b) in enumerate(((w_new, w_out), (z_new, z_out))):
            copy = pltpu.make_async_copy(a.at[part], b.at[part], out_sems.at[2 * n + m])
            copy.start()
            writes.append(copy)
    wait_all(writes)


VMEM = pl.BlockSpec(memory_space=pltpu.VMEM)
HBM = pl.BlockSpec(memory_space=pltpu.HBM)
in_smem = type(pltpu.SMEM((1,), i32))


def like(shape, dtype=bf16):
    return jax.ShapeDtypeStruct(shape, dtype)


def call(body, outs, inside, *args, near=0, sems=(), flops=0, grant=62):
    moved = sum(math.prod(o.shape) * o.dtype.itemsize for o in [*outs, *args])
    return pl.pallas_call(
        body,
        out_shape=outs,
        in_specs=[VMEM] * near + [HBM] * (len(args) - near),
        out_specs=[HBM] * len(outs),
        scratch_shapes=[
            x if isinstance(x, in_smem) else pltpu.VMEM(x.shape, x.dtype) for x in inside
        ]
        + [pltpu.SemaphoreType.DMA((n,)) for n in sems],
        compiler_params=pltpu.CompilerParams(vmem_limit_bytes=grant * 2**20),
        cost_estimate=pl.CostEstimate(flops=int(flops), bytes_accessed=moved, transcendentals=0),
    )(*args)


def swap(value, axis, k):
    return lax.ppermute(value, axis, [(i, i ^ k) for i in range(lax.axis_size(axis))])


def with_kernels(features, targets, coefficients, momentum, block_index, pivot_index, core):
    rows, owners = lax.axis_size("rows"), lax.axis_size("pts")
    points, width = features.shape
    block = block_index.shape[1]
    rank = pivot_index.shape[1]
    outputs = coefficients.shape[1]
    count = block // rows
    cap = 3 * count // owners
    devices = rows * owners
    own = outputs // devices
    deep = 2 * own * UPDATES
    half = rows // 2
    wide = like(coefficients.shape, f32)

    (packed,) = call(
        functools.partial(pack_kernel, count, cap, owners),
        [like((UPDATES * cap, width))],
        [block_index, features, like((UPDATES * cap, width))],
        block_index,
        features,
        sems=(2,),
    )
    came = {k: swap(packed, "pts", k) for k in (1, 2, *reversed(range(3, owners)))}
    kept = [
        like((UPDATES, outputs, points)),
        like((UPDATES, outputs, count), f32),
        like((8, 128), i32),
    ]
    given = [block_index, coefficients, momentum, targets]
    coef, offset, row_starts = call(
        functools.partial(prepare_kernel, count, owners),
        kept,
        given + kept,
        *given,
        sems=(4, 1 + 2 * UPDATES),
    )
    row_starts, later_index = lax.optimization_barrier((row_starts, block_index))

    def ordered(u, indices):
        kept = [like((rows, count), i32), like((8, 128), i32), like((8, rank), i32)]
        return call(
            functools.partial(order_kernel, u, count, points, owners),
            kept,
            [block_index, pivot_index, *kept],
            indices,
            pivot_index,
            sems=(3,),
        )

    ids, starts, chosen = ordered(0, later_index)
    row_starts, ids = lax.optimization_barrier((row_starts, ids))
    feats = like((UPDATES, width, count))
    inside_starts = pltpu.SMEM(row_starts.shape, i32)
    (mine,) = call(
        compact_kernel,
        [feats],
        [
            like((owners, *packed.shape)),
            inside_starts,
            like((UPDATES, count + cap, width), f32),
            feats,
        ],
        packed,
        *[came[k] for k in range(1, owners)],
        row_starts,
        sems=(owners + 1,),
        grant=60,
    )
    beside, across = swap(mine, "rows", 1), swap(mine, "rows", 2)
    pieces = like((devices, deep, count // 2))
    (pieces,) = call(
        sums_kernel,
        [pieces],
        [feats, features, coef, offset, like((points, count)), pieces],
        mine,
        features,
        coef,
        offset,
        sems=(4,),
        flops=2.0 * UPDATES * points * count * (2 * width + outputs),
    )
    pieces, later_index = lax.optimization_barrier((pieces, block_index))
    later_ids, later_starts, later_chosen = ordered(1, later_index)
    pieces, beside, across, later_ids = lax.optimization_barrier(
        (pieces, beside, across, later_ids)
    )
    summed = lax.all_to_all(pieces, ("rows", "pts"), 0, 0, tiled=True)
    kept = [like((UPDATES, rank, block)), like((rows, block, count))]
    factor, cross = call(
        factors_kernel,
        kept,
        [
            like((rows, *feats.shape)),
            like((UPDATES, *ids.shape), i32),
            like((UPDATES, *chosen.shape), i32),
            kept[0],
            like((rows, rows, count, count)),
        ],
        mine,
        beside,
        across,
        swap(across, "rows", 1),
        ids,
        later_ids,
        chosen,
        later_chosen,
        sems=(rows * rows + 2,),
        grant=60,
        flops=2.0 * width * block * (UPDATES * rank + block),
    )
    pieces = like((owners, deep, half * cap))
    (steps,) = call(
        functools.partial(chain_kernel, cap, owners),
        [pieces],
        [summed, factor, core, cross, inside_starts, inside_starts, pieces],
        summed,
        factor,
        core,
        cross,
        starts,
        later_starts,
        sems=(2 * UPDATES + 3 + rows,),
        grant=60,
    )
    steps, later_index = lax.optimization_barrier((steps, block_index))
    (slots,) = call(
        functools.partial(slots_kernel, count, points, cap),
        [like((UPDATES, rows * cap), i32)],
        [block_index, like((UPDATES, rows * cap), i32)],
        later_index,
        sems=(1,),
    )
    got = lax.all_to_all(steps, "pts", 0, 0, tiled=True)
    got, slots = lax.optimization_barrier((got, slots))
    beside, across = swap(got, "rows", 1), swap(got, "rows", 2)
    parts = points // CHUNK
    return call(
        finish_kernel,
        [wide] * 2,
        [
            like((devices, deep, half * cap)),
            slots,
            wide,
            wide,
            like((UPDATES, rows * cap, outputs)),
            wide,
            wide,
        ],
        got,
        beside,
        across,
        swap(across, "rows", 1),
        slots,
        coefficients,
        momentum,
        sems=(1 + rows + 2 * parts, 2 * parts),
        grant=60,
    )


def kernel_tile(left_rows, right_rows):
    inner_prod = mm(left_rows, right_rows, 1, 1)
    left_sq = jnp.sum(jnp.square(left_rows.astype(f32)), axis=1)
    right_sq = jnp.sum(jnp.square(right_rows.astype(f32)), axis=1)
    squared = left_sq[:, None] + right_sq[None, :] - 2.0 * inner_prod
    return jnp.exp(squared * (-3.5 / left_rows.shape[1])).astype(bf16)


def with_operations(features, targets, coefficients, momentum, block_index, pivot_index, core):
    row_count, pts_count = lax.axis_size("rows"), lax.axis_size("pts")
    row_id, pts_id = lax.axis_index("rows"), lax.axis_index("pts")
    points = features.shape[0]
    block = block_index.shape[1]
    outputs = coefficients.shape[1]
    per_row = block // row_count
    per_device = per_row // pts_count
    row_cols = outputs // row_count
    own_cols = row_cols // pts_count
    first = row_id * row_cols
    current, moving, goal = (
        lax.dynamic_slice_in_dim(value, first, row_cols, axis=1).T.astype(f32)
        for value in (coefficients, momentum, targets)
    )
    ids = iota((points, 1), 0) + pts_id * points
    place = [(ids == block_index[u][None, :]).astype(bf16) for u in range(UPDATES)]
    own_rows = []
    for u in range(UPDATES):
        mine = lax.dynamic_slice_in_dim(place[u], row_id * per_row, per_row, axis=1)
        own_rows.append(mm(mine, features, 0, 0).astype(bf16).reshape(pts_count, per_device, -1))
    came = lax.all_to_all(jnp.concatenate(own_rows, axis=1), "pts", 0, 0, tiled=False)
    chunk = jnp.sum(came.astype(f32), axis=0).astype(bf16)
    spread = lax.all_gather(lax.all_gather(chunk, "pts", axis=0), "rows", axis=0)
    spread = spread.reshape(row_count, pts_count, UPDATES, per_device, features.shape[1])
    all_steps = []
    for u in range(UPDATES):
        block_feats = spread[:, :, u].reshape(block, features.shape[1])
        mixed = mixed_of(current, moving)
        high, low = split_two(ridge_term * mixed - goal)
        tile = kernel_tile(features, block_feats)
        partial_value = (
            mm(mixed.astype(bf16), tile, 1, 0) + mm(high, place[u], 1, 0) + mm(low, place[u], 1, 0)
        )
        pieces = partial_value.astype(bf16).reshape(pts_count, own_cols, block)
        summed = lax.all_to_all(pieces, "pts", 0, 0, tiled=False)
        resid = jnp.sum(summed.astype(f32), axis=0)
        at_pivot = (iota((block, 1), 0) == pivot_index[u][None, :]).astype(bf16)
        factor = kernel_tile(block_feats, mm(at_pivot, block_feats, 0, 0).astype(bf16))
        proj = mm(resid.astype(bf16), factor, 1, 0)
        lifted = mm(proj.astype(bf16), core[u], 1, 1).astype(bf16)
        step_bf = (resid - mm(lifted, factor, 1, 1)).astype(bf16)
        steps = lax.all_gather(step_bf, "pts", axis=0, tiled=True)
        change = mm(steps, place[u], 1, 1)
        all_steps.append(change.astype(bf16))
        current, moving = stepped(current, moving, change)
    gathered = lax.all_gather(jnp.stack(all_steps), "rows", axis=1, tiled=True)
    current, moving = coefficients, momentum
    for u in range(UPDATES):
        current, moving = stepped(current, moving, gathered[u].T.astype(f32))
    return (current, moving)


def shards(features, targets, coefficients, momentum, block_index, pivot_index, nystrom_core):
    rows, owners = lax.axis_size("rows"), lax.axis_size("pts")
    count = block_index.shape[1] // rows
    fits = rows == 4 and owners == 8 and coefficients.shape[1] == 8 * rows * owners
    fits = fits and coefficients.shape[0] % CHUNK == 0 and count % CHUNK == 0 and (3 * count // owners) % 64 == 0 and UPDATES * rows == 8
    plan = with_kernels if fits else with_operations
    return plan(
        features, targets, coefficients, momentum, block_index, pivot_index, nystrom_core
    )


def solution(mesh):
    in_specs = (P("pts", None), P("pts", None), P("pts", None), P("pts", None), P(), P(), P())
    out_specs = (P("pts", None), P("pts", None))
    return jax.shard_map(shards, mesh=mesh, in_specs=in_specs, out_specs=out_specs, check_vma=False)
```

```python
import functools
import math

import jax
import jax.numpy as jnp
from jax import lax
from jax.experimental import pallas as pl
from jax.experimental.pallas import tpu as pltpu
from jax.sharding import PartitionSpec as P

UPDATES = 2


alpha_mix = 0.6
beta_keep = 0.9
step_size = 0.2
momentum_gain = 1.5
ridge_term = 1.0

f32 = jnp.float32
bf16 = jnp.bfloat16
i32 = jnp.int32


def mm(a, b, ca, cb):
    return lax.dot_general(a, b, (((ca,), (cb,)), ((), ())), preferred_element_type=f32)


def split_two(value):
    high = value.astype(bf16)
    return high, (value - high.astype(f32)).astype(bf16)


def mixed_of(current, moving):
    return alpha_mix * moving + (1.0 - alpha_mix) * current


mix_per_step = alpha_mix * step_size * momentum_gain + (1.0 - alpha_mix) * step_size


def stepped(current, moving, change):
    mixed = mixed_of(current, moving)
    if change is None:
        return mixed, beta_keep * moving + (1.0 - beta_keep) * mixed
    return (
        mixed - step_size * change,
        beta_keep * moving + (1.0 - beta_keep) * mixed - step_size * momentum_gain * change,
    )


def iota(shape, axis):
    return lax.broadcasted_iota(i32, shape, axis)


def one_hot(chosen):
    return jnp.where(chosen, 1.0, 0.0).astype(bf16)


def before_matrix(n):
    return one_hot(iota((n, n), 0) < iota((n, n), 1))


def owners_of(indices, before, points, owners):
    owner = lax.div(indices, jnp.full_like(indices, points))
    owner_ids = iota((owners, indices.shape[1]), 0)
    marks = jnp.where(owner_ids == owner, 1.0, 0.0)
    earlier = mm(marks.astype(bf16), before, 1, 0)
    rank = jnp.sum(marks * earlier, axis=0, keepdims=True)
    start = jnp.sum(jnp.where(owner < owner_ids, 1.0, 0.0), axis=1, keepdims=True)
    return marks, rank, start


def sorted_places(marks, rank, start):
    return (rank + jnp.sum(marks * start, axis=0, keepdims=True)).astype(i32)


def lane_row(column):
    n = column.shape[0]
    diagonal = iota((n, 128), 0) == iota((n, 128), 1)
    return jnp.sum(jnp.where(diagonal, column, 0.0), axis=0, keepdims=True).astype(i32)


def sorted_points(indices, place):
    count = indices.shape[1]
    return from_digits(mm(two_digits(indices), one_hot(iota((count, count), 0) == place), 1, 1))


def two_digits(row):
    high = lax.shift_right_logical(row, jnp.full_like(row, 7))
    shape = (8, row.shape[1])
    value = jnp.where(iota(shape, 0) == 0, high, lax.bitwise_and(row, jnp.full_like(row, 127)))
    return value.astype(f32).astype(bf16)


def from_digits(digits):
    return (digits[0:1] * 128.0 + digits[1:2]).astype(i32)


def start_all(pairs, sems):
    copies = [pltpu.make_async_copy(a, b, sems.at[n]) for n, (a, b) in enumerate(pairs)]
    for copy in copies:
        copy.start()
    return copies


def wait_all(copies):
    for copy in copies:
        copy.wait()


def group_row(blocks, u, group, count):
    return blocks[u : u + 1, pl.ds(pl.multiple_of(group * count, count), count)]


def pack_kernel(count, cap, owners, blocks_hbm, feats_hbm, out_hbm, blocks, feats, packed, sems):
    row, me = lax.axis_index("rows"), lax.axis_index("pts")
    points = feats.shape[0]
    reads = start_all([(blocks_hbm, blocks), (feats_hbm, feats)], sems)
    before = before_matrix(count)
    reads[0].wait()
    rows = []
    for u in range(UPDATES):
        indices = group_row(blocks, u, row, count)
        local = indices - me * points
        mine = jnp.where((local >= 0) & (local < points), 1.0, 0.0)
        rank = mm(jnp.broadcast_to(mine, (8, count)).astype(bf16), before, 1, 0)[0:1]
        held = (iota((cap, count), 0) == rank.astype(i32)) & (mine > 0.0)
        point = jnp.sum(jnp.where(held, (local + 1).astype(f32), 0.0), axis=1, keepdims=True)
        rows.append(one_hot(iota((cap, points), 1) == point.astype(i32) - 1))
    reads[1].wait()
    for u in range(UPDATES):
        packed[u * cap : (u + 1) * cap, :] = mm(rows[u], feats[...], 1, 0).astype(bf16)
    wait_all(start_all([(packed, out_hbm)], sems))


def prepare_kernel(
    count, owners,
    blocks_hbm, w_hbm, z_hbm, t_hbm, coef_hbm, offset_hbm, starts_hbm,
    blocks, w, z, t, coef, offset, starts, sems, out_sems,
):
    row, me = lax.axis_index("rows"), lax.axis_index("pts")
    points, outputs = w.shape
    reads = start_all([(blocks_hbm, blocks), (w_hbm, w), (z_hbm, z), (t_hbm, t)], sems)
    before = before_matrix(count)
    reads[0].wait()
    locals_of = []
    for u in range(UPDATES):
        indices = group_row(blocks, u, row, count)
        marks, rank, start = owners_of(indices, before, points, owners)
        starts[u : u + 1, :] = lane_row(start)
        locals_of.append(sorted_points(indices, sorted_places(marks, rank, start)) - me * points)
    writes = start_all([(starts, starts_hbm)], out_sems)
    wait_all(reads[1:])
    current, moving = w[...], z[...]
    goal = t[...].astype(f32).T
    for u in range(UPDATES):
        mixed = mixed_of(current, moving).T
        high, low = split_two(ridge_term * mixed - goal)
        coef[u] = mixed.astype(bf16)
        place = one_hot(iota((points, count), 0) == locals_of[u])
        offset[u] = mm(high, place, 1, 0) + mm(low, place, 1, 0)
        current, moving = stepped(current, moving, None)
        for a, b in ((coef, coef_hbm), (offset, offset_hbm)):
            writes.append(pltpu.make_async_copy(a.at[u], b.at[u], out_sems.at[len(writes)]))
            writes[-1].start()
    wait_all(writes)


def order_kernel(
    u, count, points, owners,
    blocks_hbm, pivots_hbm, ids_hbm, starts_hbm, chosen_hbm,
    blocks, pivots, ids, starts, chosen, sems,
):
    wait_all(start_all([(blocks_hbm, blocks), (pivots_hbm, pivots)], sems))
    before = before_matrix(count)
    groups = blocks.shape[1] // count
    pivot = pivots[u : u + 1, :]
    found = jnp.zeros((8, pivot.shape[1]), f32)
    for g in range(groups):
        indices = blocks[u : u + 1, g * count : (g + 1) * count]
        marks, rank, start = owners_of(indices, before, points, owners)
        place = sorted_places(marks, rank, start)
        ids[g : g + 1, :] = sorted_points(indices, place)
        starts[g : g + 1, :] = lane_row(start)
        at_pivot = one_hot(iota((count, pivot.shape[1]), 0) + g * count == pivot)
        found += mm(two_digits(place + g * count), at_pivot, 1, 0)
    chosen[0:1, :] = from_digits(found)
    wait_all(start_all([(ids, ids_hbm), (starts, starts_hbm), (chosen, chosen_hbm)], sems))


def slots_kernel(count, points, cap, blocks_hbm, slots_hbm, blocks, slots, sems):
    me = lax.axis_index("pts")
    wait_all(start_all([(blocks_hbm, blocks)], sems))
    before = before_matrix(count)
    groups = blocks.shape[1] // count
    for u in range(UPDATES):
        found = jnp.zeros((8, groups * cap), f32)
        for g in range(groups):
            local = blocks[u : u + 1, g * count : (g + 1) * count] - me * points
            mine = (local >= 0) & (local < points)
            counts = jnp.where(mine, 1.0, 0.0)
            rank = mm(jnp.broadcast_to(counts, (8, count)).astype(bf16), before, 1, 0)[0:1]
            held = jnp.where(mine, rank.astype(i32) + g * cap, -1)
            chosen = one_hot(iota((groups * cap, count), 0) == held)
            found += mm(two_digits(jnp.where(mine, local + 1, 0)), chosen, 1, 1)
        slots[u : u + 1, :] = from_digits(found) - 1
    wait_all(start_all([(slots, slots_hbm)], sems))


def extended(rows, axis, first):
    rest = -0.5 * jnp.sum(jnp.square(rows.astype(f32)), axis=axis, keepdims=True)
    parts = []
    for _ in range(3):
        parts.append(rest.astype(bf16).astype(f32))
        rest = rest - parts[-1]
    parts = parts + [1.0] * 3 if first else [1.0] * 3 + parts
    at = iota(rows.shape, axis)
    extra = jnp.zeros(rows.shape, f32)
    for n, part in enumerate(parts):
        extra = jnp.where(at == n, part, extra)
    return jnp.concatenate([rows.astype(bf16), extra.astype(bf16)], axis=axis)


def exponent(left, right):
    return mm(left, right, 1, 0) * (7.0 / (left.shape[1] // 2) * math.log2(math.e))


CHUNK = 256


def compact_kernel(*refs):
    *came_hbm, starts_hbm, block_hbm, came, starts, wide, block, sems = refs
    me = lax.axis_index("pts")
    owners, deep, _ = came.shape
    cap = deep // UPDATES
    count = block.shape[2]
    pairs = [(a, came.at[k]) for k, a in enumerate(came_hbm)]
    wait_all(start_all([*pairs, (starts_hbm, starts)], sems))
    for u in range(UPDATES):
        for o in range(owners):
            start = starts[u, o]
            rows = came[lax.bitwise_xor(me, o), u * cap : (u + 1) * cap, :]
            wide[u, pl.ds(start, cap), :] = rows.astype(f32)
        block[u] = wide[u, 0:count, :].T.astype(bf16)
    wait_all(start_all([(block, block_hbm)], sems))


def sums_kernel(
    block_hbm, feats_hbm, coef_hbm, offset_hbm, pieces_hbm,
    block, feats, coef, offset, tile, pieces, sems,
):
    outputs = coef.shape[1]
    pairs = [(block_hbm, block), (feats_hbm, feats), (coef_hbm, coef), (offset_hbm, offset)]
    reads = start_all(pairs, sems)
    wait_all(reads[:2])
    left = extended(feats[...], 1, True)
    for u in range(UPDATES):
        right = extended(block[u], 0, False)
        tile[...] = jnp.exp2(exponent(left, right)).astype(bf16)
        if u == 0:
            wait_all(reads[2:])
        total = offset[u] + mm(coef[u], tile[...], 1, 0)
        devices, _, lanes = pieces.shape
        own = outputs // devices
        for d in range(devices):
            part = total[d * own : (d + 1) * own]
            pieces[d, 2 * own * u : 2 * own * (u + 1), :] = jnp.concatenate(
                [part[:, :lanes], part[:, lanes:]], axis=0
            ).astype(bf16)
    wait_all(start_all([(pieces, pieces_hbm)], sems))


def factors_kernel(
    b0_hbm, b1_hbm, b2_hbm, b3_hbm, ids0_hbm, ids1_hbm, pivots0_hbm, pivots1_hbm, factor_hbm, cross_hbm,
    feats, ids, pivots, factor, cross, sems,
):
    row = lax.axis_index("rows")
    groups, _, width, count = feats.shape
    pairs = [(b_hbm, feats.at[k]) for k, b_hbm in enumerate((b0_hbm, b1_hbm, b2_hbm, b3_hbm))]
    pairs += [(ids0_hbm, ids.at[0]), (ids1_hbm, ids.at[1])]
    pairs += [(pivots0_hbm, pivots.at[0]), (pivots1_hbm, pivots.at[1])]
    wait_all(start_all(pairs, sems))
    places = [lax.bitwise_xor(row, k) for k in range(groups)]
    rights = [[extended(feats[k, u], 0, False) for k in range(groups)] for u in range(UPDATES)]
    for u in range(UPDATES):
        chosen_feats = jnp.zeros((width, pivots.shape[2]), f32)
        for k in range(groups):
            chosen = iota((count, pivots.shape[2]), 0) + places[k] * count == pivots[u, 0:1, :]
            chosen_feats += mm(feats[k, u], one_hot(chosen), 1, 0)
        left = extended(chosen_feats.T, 1, True)
        for k in range(groups):
            start = pl.multiple_of(places[k] * count, count)
            value = jnp.exp2(exponent(left, rights[u][k]))
            factor[u, :, pl.ds(start, count)] = value.astype(bf16)
    writes = start_all([(factor, factor_hbm)], sems)
    lefts, left_points = [], []
    for k in range(groups):
        lefts.append(extended(feats[k, 0].astype(f32).T, 1, True))
        points = ids[0, pl.ds(places[k], 1), :].astype(f32)
        left_points.append(jnp.broadcast_to(points, (8, count)).T[:, 0:1])
    left, left_points = jnp.concatenate(lefts, axis=0), jnp.concatenate(left_points, axis=0)
    sent = 1
    for m in range(groups):
        right_points = ids[1, pl.ds(places[m], 1), :].astype(f32)
        power = exponent(left, rights[1][m])
        power = jnp.where(left_points == right_points, math.log2(1.0 + ridge_term), power)
        cross[m] = jnp.exp2(power).astype(bf16).reshape(groups, count, count)
        for k in range(groups):
            start = pl.multiple_of(places[k] * count, count)
            copy = pltpu.make_async_copy(
                cross.at[m, k], cross_hbm.at[places[m], pl.ds(start, count), :], sems.at[sent]
            )
            copy.start()
            writes.append(copy)
            sent += 1
    wait_all(writes)


def chain_kernel(
    cap, owners,
    summed_hbm, factor_hbm, core_hbm, cross_hbm, starts0_hbm, starts1_hbm, out_hbm,
    summed, factor, core, cross, starts0, starts1, packed, sems,
):
    groups, _, count = cross.shape
    own = summed.shape[1] // (2 * UPDATES)
    pairs, starts = [(summed_hbm, summed)], (starts0, starts1)
    for u in range(UPDATES):
        pairs += [(factor_hbm.at[u], factor.at[u]), (core_hbm.at[u], core.at[u])]
        if u == 0:
            pairs += [(starts0_hbm, starts0), (starts1_hbm, starts1)]
            pairs += [(cross_hbm.at[g], cross.at[g]) for g in range(groups)]
    reads = start_all(pairs, sems)
    first, *reads = reads
    first.wait()
    step = None
    for u in range(UPDATES):
        sums = []
        for g in range(groups):
            part = summed[g * owners, 2 * own * u : 2 * own * (u + 1), :].astype(f32)
            for o in range(1, owners):
                part += summed[g * owners + o, 2 * own * u : 2 * own * (u + 1), :].astype(f32)
            part = jnp.concatenate([part[:own], part[own:]], axis=1)
            if u:
                reads[4 + g].wait()
                part -= mix_per_step * mm(step, cross[g], 1, 0)
            sums.append(part)
        resid = jnp.concatenate(sums, axis=1)
        wait_all(reads[0:4] if u == 0 else reads[4 + groups :])
        proj = mm(resid.astype(bf16), factor[u], 1, 1)
        lifted = mm(proj.astype(bf16), core[u], 1, 1).astype(bf16)
        step = (resid - mm(lifted, factor[u], 1, 0)).astype(bf16)
        half = groups // 2
        for o in range(owners):
            lanes = []
            for g in range(groups):
                part = step[:, g * count : (g + 1) * count].astype(f32)
                back = lax.rem(count - starts[u][g, o], count)
                lanes.append(pltpu.roll(part, back, 1)[:, :cap])
            packed[o, 2 * own * u : 2 * own * (u + 1), :] = jnp.concatenate(
                [jnp.concatenate(lanes[h * half : (h + 1) * half], axis=1) for h in range(2)], axis=0
            ).astype(bf16)
    wait_all(start_all([(packed, out_hbm)], sems))


def finish_kernel(
    g0_hbm, g1_hbm, g2_hbm, g3_hbm, slots_hbm, w_hbm, z_hbm, w_out, z_out,
    got, slots, w, z, steps, w_new, z_new, sems, out_sems,
):
    row = lax.axis_index("rows")
    points = w.shape[0]
    sources, deep, lanes = got.shape
    own = deep // (2 * UPDATES)
    chunks = range(0, points, CHUNK)
    pairs = [(slots_hbm, slots)]
    for k, g_hbm in enumerate((g0_hbm, g1_hbm, g2_hbm, g3_hbm)):
        size = g_hbm.shape[0]
        first = pl.multiple_of(lax.bitwise_xor(row, k) * size, size)
        pairs.append((g_hbm, got.at[pl.ds(first, size)]))
    for c in chunks:
        part = slice(c, c + CHUNK)
        pairs += [(w_hbm.at[part], w.at[part]), (z_hbm.at[part], z.at[part])]
    reads = start_all(pairs, sems)
    reads[0].wait()
    places = []
    for u in range(UPDATES):
        places.append(one_hot(iota((points, slots.shape[1]), 0) == slots[u : u + 1, :]))
    wait_all(reads[1:5])
    reads = reads[5:]
    wide = got[...].astype(f32)
    for u in range(UPDATES):
        for h in range(2):
            first = own * (2 * u + h)
            part = wide[:, first : first + own, :].reshape(sources * own, lanes)
            steps[u, h * lanes : (h + 1) * lanes, :] = part.T.astype(bf16)
    changes = [mm(places[u], steps[u], 1, 0) for u in range(UPDATES)]
    writes = []
    for n, c in enumerate(chunks):
        part = slice(c, c + CHUNK)
        wait_all(reads[2 * n : 2 * n + 2])
        current, moving = w[part, :], z[part, :]
        for change in changes:
            current, moving = stepped(current, moving, change[part])
        w_new[part, :] = current
        z_new[part, :] = moving
        for m, (a, b) in enumerate(((w_new, w_out), (z_new, z_out))):
            copy = pltpu.make_async_copy(a.at[part], b.at[part], out_sems.at[2 * n + m])
            copy.start()
            writes.append(copy)
    wait_all(writes)


VMEM = pl.BlockSpec(memory_space=pltpu.VMEM)
HBM = pl.BlockSpec(memory_space=pltpu.HBM)
in_smem = type(pltpu.SMEM((1,), i32))


def like(shape, dtype=bf16):
    return jax.ShapeDtypeStruct(shape, dtype)


def call(body, outs, inside, *args, near=0, sems=(), flops=0, grant=62):
    moved = sum(math.prod(o.shape) * o.dtype.itemsize for o in [*outs, *args])
    return pl.pallas_call(
        body,
        out_shape=outs,
        in_specs=[VMEM] * near + [HBM] * (len(args) - near),
        out_specs=[HBM] * len(outs),
        scratch_shapes=[
            x if isinstance(x, in_smem) else pltpu.VMEM(x.shape, x.dtype) for x in inside
        ]
        + [pltpu.SemaphoreType.DMA((n,)) for n in sems],
        compiler_params=pltpu.CompilerParams(vmem_limit_bytes=grant * 2**20),
        cost_estimate=pl.CostEstimate(flops=int(flops), bytes_accessed=moved, transcendentals=0),
    )(*args)


def swap(value, axis, k):
    return lax.ppermute(value, axis, [(i, i ^ k) for i in range(lax.axis_size(axis))])


def with_kernels(features, targets, coefficients, momentum, block_index, pivot_index, core):
    rows, owners = lax.axis_size("rows"), lax.axis_size("pts")
    points, width = features.shape
    block = block_index.shape[1]
    rank = pivot_index.shape[1]
    outputs = coefficients.shape[1]
    count = block // rows
    cap = 3 * count // owners
    devices = rows * owners
    own = outputs // devices
    deep = 2 * own * UPDATES
    half = rows // 2
    wide = like(coefficients.shape, f32)

    (packed,) = call(
        functools.partial(pack_kernel, count, cap, owners),
        [like((UPDATES * cap, width))],
        [block_index, features, like((UPDATES * cap, width))],
        block_index,
        features,
        sems=(2,),
    )
    came = {k: swap(packed, "pts", k) for k in reversed(range(2, owners, 2))}
    came[1] = swap(packed, "pts", 1)
    came[3] = swap(came[2], "pts", 1)
    kept = [
        like((UPDATES, outputs, points)),
        like((UPDATES, outputs, count), f32),
        like((8, 128), i32),
    ]
    given = [block_index, coefficients, momentum, targets]
    coef, offset, row_starts = call(
        functools.partial(prepare_kernel, count, owners),
        kept,
        given + kept,
        *given,
        sems=(4, 1 + 2 * UPDATES),
    )
    came[4], came[6], row_starts, later_index = lax.optimization_barrier(
        (came[4], came[6], row_starts, block_index)
    )
    came[5], came[7] = swap(came[4], "pts", 1), swap(came[6], "pts", 1)

    def ordered(u, indices):
        kept = [like((rows, count), i32), like((8, 128), i32), like((8, rank), i32)]
        return call(
            functools.partial(order_kernel, u, count, points, owners),
            kept,
            [block_index, pivot_index, *kept],
            indices,
            pivot_index,
            sems=(3,),
        )

    ids, starts, chosen = ordered(0, later_index)
    row_starts, ids = lax.optimization_barrier((row_starts, ids))
    feats = like((UPDATES, width, count))
    inside_starts = pltpu.SMEM(row_starts.shape, i32)
    (mine,) = call(
        compact_kernel,
        [feats],
        [
            like((owners, *packed.shape)),
            inside_starts,
            like((UPDATES, count + cap, width), f32),
            feats,
        ],
        packed,
        *[came[k] for k in range(1, owners)],
        row_starts,
        sems=(owners + 1,),
        grant=60,
    )
    beside, across = swap(mine, "rows", 1), swap(mine, "rows", 2)
    pieces = like((devices, deep, count // 2))
    (pieces,) = call(
        sums_kernel,
        [pieces],
        [feats, features, coef, offset, like((points, count)), pieces],
        mine,
        features,
        coef,
        offset,
        sems=(4,),
        flops=2.0 * UPDATES * points * count * (2 * width + outputs),
    )
    pieces, later_index = lax.optimization_barrier((pieces, block_index))
    later_ids, later_starts, later_chosen = ordered(1, later_index)
    pieces, beside, across, later_ids = lax.optimization_barrier(
        (pieces, beside, across, later_ids)
    )
    summed = lax.all_to_all(pieces, ("rows", "pts"), 0, 0, tiled=True)
    kept = [like((UPDATES, rank, block)), like((rows, block, count))]
    factor, cross = call(
        factors_kernel,
        kept,
        [
            like((rows, *feats.shape)),
            like((UPDATES, *ids.shape), i32),
            like((UPDATES, *chosen.shape), i32),
            kept[0],
            like((rows, rows, count, count)),
        ],
        mine,
        beside,
        across,
        swap(across, "rows", 1),
        ids,
        later_ids,
        chosen,
        later_chosen,
        sems=(rows * rows + 2,),
        grant=60,
        flops=2.0 * width * block * (UPDATES * rank + block),
    )
    pieces = like((owners, deep, half * cap))
    (steps,) = call(
        functools.partial(chain_kernel, cap, owners),
        [pieces],
        [summed, factor, core, cross, inside_starts, inside_starts, pieces],
        summed,
        factor,
        core,
        cross,
        starts,
        later_starts,
        sems=(2 * UPDATES + 3 + rows,),
        grant=60,
    )
    steps, later_index = lax.optimization_barrier((steps, block_index))
    (slots,) = call(
        functools.partial(slots_kernel, count, points, cap),
        [like((UPDATES, rows * cap), i32)],
        [block_index, like((UPDATES, rows * cap), i32)],
        later_index,
        sems=(1,),
    )
    got = lax.all_to_all(steps, "pts", 0, 0, tiled=True)
    got, slots = lax.optimization_barrier((got, slots))
    beside, across = swap(got, "rows", 1), swap(got, "rows", 2)
    parts = points // CHUNK
    return call(
        finish_kernel,
        [wide] * 2,
        [
            like((devices, deep, half * cap)),
            slots,
            wide,
            wide,
            like((UPDATES, rows * cap, outputs)),
            wide,
            wide,
        ],
        got,
        beside,
        across,
        swap(across, "rows", 1),
        slots,
        coefficients,
        momentum,
        sems=(1 + rows + 2 * parts, 2 * parts),
        grant=60,
    )


def kernel_tile(left_rows, right_rows):
    inner_prod = mm(left_rows, right_rows, 1, 1)
    left_sq = jnp.sum(jnp.square(left_rows.astype(f32)), axis=1)
    right_sq = jnp.sum(jnp.square(right_rows.astype(f32)), axis=1)
    squared = left_sq[:, None] + right_sq[None, :] - 2.0 * inner_prod
    return jnp.exp(squared * (-3.5 / left_rows.shape[1])).astype(bf16)


def with_operations(features, targets, coefficients, momentum, block_index, pivot_index, core):
    row_count, pts_count = lax.axis_size("rows"), lax.axis_size("pts")
    row_id, pts_id = lax.axis_index("rows"), lax.axis_index("pts")
    points = features.shape[0]
    block = block_index.shape[1]
    outputs = coefficients.shape[1]
    per_row = block // row_count
    per_device = per_row // pts_count
    row_cols = outputs // row_count
    own_cols = row_cols // pts_count
    first = row_id * row_cols
    current, moving, goal = (
        lax.dynamic_slice_in_dim(value, first, row_cols, axis=1).T.astype(f32)
        for value in (coefficients, momentum, targets)
    )
    ids = iota((points, 1), 0) + pts_id * points
    place = [(ids == block_index[u][None, :]).astype(bf16) for u in range(UPDATES)]
    own_rows = []
    for u in range(UPDATES):
        mine = lax.dynamic_slice_in_dim(place[u], row_id * per_row, per_row, axis=1)
        own_rows.append(mm(mine, features, 0, 0).astype(bf16).reshape(pts_count, per_device, -1))
    came = lax.all_to_all(jnp.concatenate(own_rows, axis=1), "pts", 0, 0, tiled=False)
    chunk = jnp.sum(came.astype(f32), axis=0).astype(bf16)
    spread = lax.all_gather(lax.all_gather(chunk, "pts", axis=0), "rows", axis=0)
    spread = spread.reshape(row_count, pts_count, UPDATES, per_device, features.shape[1])
    all_steps = []
    for u in range(UPDATES):
        block_feats = spread[:, :, u].reshape(block, features.shape[1])
        mixed = mixed_of(current, moving)
        high, low = split_two(ridge_term * mixed - goal)
        tile = kernel_tile(features, block_feats)
        partial_value = (
            mm(mixed.astype(bf16), tile, 1, 0) + mm(high, place[u], 1, 0) + mm(low, place[u], 1, 0)
        )
        pieces = partial_value.astype(bf16).reshape(pts_count, own_cols, block)
        summed = lax.all_to_all(pieces, "pts", 0, 0, tiled=False)
        resid = jnp.sum(summed.astype(f32), axis=0)
        at_pivot = (iota((block, 1), 0) == pivot_index[u][None, :]).astype(bf16)
        factor = kernel_tile(block_feats, mm(at_pivot, block_feats, 0, 0).astype(bf16))
        proj = mm(resid.astype(bf16), factor, 1, 0)
        lifted = mm(proj.astype(bf16), core[u], 1, 1).astype(bf16)
        step_bf = (resid - mm(lifted, factor, 1, 1)).astype(bf16)
        steps = lax.all_gather(step_bf, "pts", axis=0, tiled=True)
        change = mm(steps, place[u], 1, 1)
        all_steps.append(change.astype(bf16))
        current, moving = stepped(current, moving, change)
    gathered = lax.all_gather(jnp.stack(all_steps), "rows", axis=1, tiled=True)
    current, moving = coefficients, momentum
    for u in range(UPDATES):
        current, moving = stepped(current, moving, gathered[u].T.astype(f32))
    return (current, moving)


def shards(features, targets, coefficients, momentum, block_index, pivot_index, nystrom_core):
    rows, owners = lax.axis_size("rows"), lax.axis_size("pts")
    count = block_index.shape[1] // rows
    fits = rows == 4 and owners == 8 and coefficients.shape[1] == 8 * rows * owners
    fits = fits and coefficients.shape[0] % CHUNK == 0 and count % CHUNK == 0 and (3 * count // owners) % 64 == 0 and UPDATES * rows == 8
    plan = with_kernels if fits else with_operations
    return plan(
        features, targets, coefficients, momentum, block_index, pivot_index, nystrom_core
    )


def solution(mesh):
    in_specs = (P("pts", None), P("pts", None), P("pts", None), P("pts", None), P(), P(), P())
    out_specs = (P("pts", None), P("pts", None))
    return jax.shard_map(shards, mesh=mesh, in_specs=in_specs, out_specs=out_specs, check_vma=False)
```

```python
import functools
import math

import jax
import jax.numpy as jnp
from jax import lax
from jax.experimental import pallas as pl
from jax.experimental.pallas import tpu as pltpu
from jax.sharding import PartitionSpec as P

UPDATES = 2


alpha_mix = 0.6
beta_keep = 0.9
step_size = 0.2
momentum_gain = 1.5
ridge_term = 1.0

f32 = jnp.float32
bf16 = jnp.bfloat16
i32 = jnp.int32


def mm(a, b, ca, cb):
    return lax.dot_general(a, b, (((ca,), (cb,)), ((), ())), preferred_element_type=f32)


def split_two(value):
    high = value.astype(bf16)
    return high, (value - high.astype(f32)).astype(bf16)


def mixed_of(current, moving):
    return alpha_mix * moving + (1.0 - alpha_mix) * current


mix_per_step = alpha_mix * step_size * momentum_gain + (1.0 - alpha_mix) * step_size


def stepped(current, moving, change):
    mixed = mixed_of(current, moving)
    if change is None:
        return mixed, beta_keep * moving + (1.0 - beta_keep) * mixed
    return (
        mixed - step_size * change,
        beta_keep * moving + (1.0 - beta_keep) * mixed - step_size * momentum_gain * change,
    )


def iota(shape, axis):
    return lax.broadcasted_iota(i32, shape, axis)


def one_hot(chosen):
    return jnp.where(chosen, 1.0, 0.0).astype(bf16)


def before_matrix(n):
    return one_hot(iota((n, n), 0) < iota((n, n), 1))


def owners_of(groups, points, owners):
    owner_ids = iota((owners, groups[0].shape[1]), 0)
    owner = [lax.div(x, jnp.full_like(x, points)) for x in groups]
    marks = [jnp.where(owner_ids == x, 1.0, 0.0) for x in owner]
    every = jnp.concatenate(marks, axis=0).astype(bf16)
    earlier = mm(every, before_matrix(every.shape[1]), 1, 0)
    out = []
    for n, x in enumerate(owner):
        rank = jnp.sum(marks[n] * earlier[n * owners : (n + 1) * owners], axis=0, keepdims=True)
        start = jnp.sum(jnp.where(x < owner_ids, 1.0, 0.0), axis=1, keepdims=True)
        out.append((marks[n], rank, start))
    return out


def sorted_places(marks, rank, start):
    return (rank + jnp.sum(marks * start, axis=0, keepdims=True)).astype(i32)


def lane_row(column):
    n = column.shape[0]
    diagonal = iota((n, 128), 0) == iota((n, 128), 1)
    return jnp.sum(jnp.where(diagonal, column, 0.0), axis=0, keepdims=True).astype(i32)


def two_digits(*rows):
    shape = (8, rows[0].shape[1])
    value = jnp.zeros(shape, i32)
    for n, row in enumerate(rows):
        high = lax.shift_right_logical(row, jnp.full_like(row, 7))
        low = lax.bitwise_and(row, jnp.full_like(row, 127))
        value = jnp.where(iota(shape, 0) == 2 * n, high, value)
        value = jnp.where(iota(shape, 0) == 2 * n + 1, low, value)
    return value.astype(f32).astype(bf16)


def from_digits(digits):
    return (digits[0:1] * 128.0 + digits[1:2]).astype(i32)


def start_all(pairs, sems):
    copies = [pltpu.make_async_copy(a, b, sems.at[n]) for n, (a, b) in enumerate(pairs)]
    for copy in copies:
        copy.start()
    return copies


def wait_all(copies):
    for copy in copies:
        copy.wait()


def group_row(blocks, u, group, count):
    return blocks[u : u + 1, pl.ds(pl.multiple_of(group * count, count), count)]


def pack_kernel(count, cap, owners, blocks_hbm, feats_hbm, out_hbm, blocks, feats, packed, sems):
    row, me = lax.axis_index("rows"), lax.axis_index("pts")
    points = feats.shape[0]
    reads = start_all([(blocks_hbm, blocks), (feats_hbm, feats)], sems)
    before = before_matrix(count)
    reads[0].wait()
    rows = []
    for u in range(UPDATES):
        indices = group_row(blocks, u, row, count)
        local = indices - me * points
        mine = jnp.where((local >= 0) & (local < points), 1.0, 0.0)
        rank = mm(jnp.broadcast_to(mine, (8, count)).astype(bf16), before, 1, 0)[0:1]
        held = (iota((cap, count), 0) == rank.astype(i32)) & (mine > 0.0)
        point = jnp.sum(jnp.where(held, (local + 1).astype(f32), 0.0), axis=1, keepdims=True)
        rows.append(one_hot(iota((cap, points), 1) == point.astype(i32) - 1))
    reads[1].wait()
    for u in range(UPDATES):
        packed[u * cap : (u + 1) * cap, :] = mm(rows[u], feats[...], 1, 0).astype(bf16)
    wait_all(start_all([(packed, out_hbm)], sems))


def prepare_kernel(
    count, owners,
    blocks_hbm, w_hbm, z_hbm, t_hbm, coef_hbm, offset_hbm, starts_hbm,
    blocks, w, z, t, coef, offset, starts, sems, out_sems,
):
    row, me = lax.axis_index("rows"), lax.axis_index("pts")
    points, outputs = w.shape
    reads = start_all([(blocks_hbm, blocks), (w_hbm, w), (z_hbm, z), (t_hbm, t)], sems)
    reads[0].wait()
    groups = [group_row(blocks, u, row, count) for u in range(UPDATES)]
    found, shift = [], []
    for u, (_, rank, start) in enumerate(owners_of(groups, points, owners)):
        starts[u : u + 1, :] = lane_row(start)
        local = groups[u] - me * points
        mine = (local >= 0) & (local < points)
        held = jnp.where(mine, rank.astype(i32), -1)
        chosen = one_hot(iota((count // 2, count), 0) == held)
        digits = two_digits(jnp.where(mine, local + 1, 0))
        found.append(from_digits(mm(digits, chosen, 1, 1)) - 1)
        earlier = jnp.sum(jnp.where(groups[u] < me * points, 1.0, 0.0))
        shift.append(lax.rem(earlier.astype(i32), count))
    writes = start_all([(starts, starts_hbm)], out_sems)
    wait_all(reads[1:])
    current, moving = w[...], z[...]
    goal = t[...].astype(f32).T
    for u in range(UPDATES):
        mixed = mixed_of(current, moving).T
        high, low = split_two(ridge_term * mixed - goal)
        coef[u] = mixed.astype(bf16)
        place = one_hot(iota((points, count // 2), 0) == found[u])
        both = mm(jnp.concatenate([high, low], axis=0), place, 1, 0)
        held = both[:outputs] + both[outputs:]
        held = jnp.concatenate([held, jnp.zeros_like(held)], axis=1)
        offset[u] = pltpu.roll(held, shift[u], 1)
        current, moving = stepped(current, moving, None)
        for a, b in ((coef, coef_hbm), (offset, offset_hbm)):
            writes.append(pltpu.make_async_copy(a.at[u], b.at[u], out_sems.at[len(writes)]))
            writes[-1].start()
    wait_all(writes)


def order_kernel(
    count, points, owners,
    blocks_hbm, ids_hbm, from_hbm, starts_hbm,
    blocks, ids, came_from, starts, sems,
):
    wait_all(start_all([(blocks_hbm, blocks)], sems))
    count_of = blocks.shape[1] // count
    groups = [
        blocks[u : u + 1, g * count : (g + 1) * count]
        for u in range(UPDATES)
        for g in range(count_of)
    ]
    for n, (marks, rank, start) in enumerate(owners_of(groups, points, owners)):
        place = sorted_places(marks, rank, start)
        given = iota((1, count), 1) + (n % count_of) * count
        digits = two_digits(groups[n], given)
        moved = mm(digits, one_hot(iota((count, count), 0) == place), 1, 1)
        ids[n : n + 1, :] = from_digits(moved[0:2])
        came_from[n : n + 1, :] = from_digits(moved[2:4])
        starts[n : n + 1, :] = lane_row(start)
    wait_all(start_all([(ids, ids_hbm), (came_from, from_hbm), (starts, starts_hbm)], sems))


def slots_kernel(count, points, cap, blocks_hbm, slots_hbm, blocks, slots, sems):
    me = lax.axis_index("pts")
    wait_all(start_all([(blocks_hbm, blocks)], sems))
    before = before_matrix(count)
    groups = blocks.shape[1] // count
    for u in range(UPDATES):
        found = jnp.zeros((8, groups * cap), f32)
        for g in range(groups):
            local = blocks[u : u + 1, g * count : (g + 1) * count] - me * points
            mine = (local >= 0) & (local < points)
            counts = jnp.where(mine, 1.0, 0.0)
            rank = mm(jnp.broadcast_to(counts, (8, count)).astype(bf16), before, 1, 0)[0:1]
            held = jnp.where(mine, rank.astype(i32) + g * cap, -1)
            chosen = one_hot(iota((groups * cap, count), 0) == held)
            found += mm(two_digits(jnp.where(mine, local + 1, 0)), chosen, 1, 1)
        slots[u : u + 1, :] = from_digits(found) - 1
    wait_all(start_all([(slots, slots_hbm)], sems))


def extended(rows, axis, first):
    rest = -0.5 * jnp.sum(jnp.square(rows.astype(f32)), axis=axis, keepdims=True)
    parts = []
    for _ in range(3):
        parts.append(rest.astype(bf16).astype(f32))
        rest = rest - parts[-1]
    parts = parts + [1.0] * 3 if first else [1.0] * 3 + parts
    at = iota(rows.shape, axis)
    extra = jnp.zeros(rows.shape, f32)
    for n, part in enumerate(parts):
        extra = jnp.where(at == n, part, extra)
    return jnp.concatenate([rows.astype(bf16), extra.astype(bf16)], axis=axis)


def exponent(left, right):
    return mm(left, right, 1, 0) * (7.0 / (left.shape[1] // 2) * math.log2(math.e))


CHUNK = 256


def compact_kernel(*refs):
    *came_hbm, starts_hbm, block_hbm, came, starts, wide, block, sems = refs
    me = lax.axis_index("pts")
    owners, deep, _ = came.shape
    cap = deep // UPDATES
    count = block.shape[2]
    pairs = [(a, came.at[k]) for k, a in enumerate(came_hbm)]
    wait_all(start_all([*pairs, (starts_hbm, starts)], sems))
    for u in range(UPDATES):
        for o in range(owners):
            start = starts[u, o]
            rows = came[lax.bitwise_xor(me, o), u * cap : (u + 1) * cap, :]
            wide[u, pl.ds(start, cap), :] = rows.astype(f32)
        block[u] = wide[u, 0:count, :].T.astype(bf16)
    wait_all(start_all([(block, block_hbm)], sems))


def sums_kernel(
    block_hbm, feats_hbm, coef_hbm, offset_hbm, pieces_hbm,
    block, feats, coef, offset, tile, pieces, sems,
):
    outputs = coef.shape[1]
    pairs = [(block_hbm, block), (feats_hbm, feats), (coef_hbm, coef), (offset_hbm, offset)]
    reads = start_all(pairs, sems)
    wait_all(reads[:2])
    left = extended(feats[...], 1, True)
    for u in range(UPDATES):
        right = extended(block[u], 0, False)
        tile[...] = jnp.exp2(exponent(left, right)).astype(bf16)
        if u == 0:
            wait_all(reads[2:])
        total = offset[u] + mm(coef[u], tile[...], 1, 0)
        devices, _, lanes = pieces.shape
        own = outputs // devices
        for d in range(devices):
            part = total[d * own : (d + 1) * own]
            pieces[d, 2 * own * u : 2 * own * (u + 1), :] = jnp.concatenate(
                [part[:, :lanes], part[:, lanes:]], axis=0
            ).astype(bf16)
    wait_all(start_all([(pieces, pieces_hbm)], sems))


def factors_kernel(
    b0_hbm, b1_hbm, b2_hbm, b3_hbm, ids_hbm, from_hbm, pivots_hbm, factor_hbm, cross_hbm,
    feats, ids, came_from, pivots, factor, cross, sems,
):
    row = lax.axis_index("rows")
    groups, _, width, count = feats.shape
    pairs = [(b_hbm, feats.at[k]) for k, b_hbm in enumerate((b0_hbm, b1_hbm, b2_hbm, b3_hbm))]
    pairs += [(ids_hbm, ids), (from_hbm, came_from), (pivots_hbm, pivots)]
    wait_all(start_all(pairs, sems))
    places = [lax.bitwise_xor(row, k) for k in range(groups)]
    rights = [[extended(feats[k, u], 0, False) for k in range(groups)] for u in range(UPDATES)]
    given = [[feats[k, u].astype(f32).T for k in range(groups)] for u in range(UPDATES)]
    for u in range(UPDATES):
        wanted = pivots[u : u + 1, :].astype(f32)
        wanted = jnp.broadcast_to(wanted, (8, wanted.shape[1])).T[:, 0:1]
        chosen_feats = jnp.zeros((pivots.shape[1], width), f32)
        for k in range(groups):
            here = came_from[pl.ds(u * groups + places[k], 1), :].astype(f32)
            chosen_feats += mm(one_hot(wanted == here), given[u][k].astype(bf16), 1, 0)
        left = extended(chosen_feats, 1, True)
        for k in range(groups):
            start = pl.multiple_of(places[k] * count, count)
            value = jnp.exp2(exponent(left, rights[u][k]))
            factor[u, :, pl.ds(start, count)] = value.astype(bf16)
    writes = start_all([(factor, factor_hbm)], sems)
    lefts, left_points = [], []
    for k in range(groups):
        lefts.append(extended(given[0][k], 1, True))
        points = ids[pl.ds(places[k], 1), :].astype(f32)
        left_points.append(jnp.broadcast_to(points, (8, count)).T[:, 0:1])
    left, left_points = jnp.concatenate(lefts, axis=0), jnp.concatenate(left_points, axis=0)
    sent = 1
    for m in range(groups):
        right_points = ids[pl.ds(groups + places[m], 1), :].astype(f32)
        power = exponent(left, rights[1][m])
        power = jnp.where(left_points == right_points, math.log2(1.0 + ridge_term), power)
        cross[m] = jnp.exp2(power).astype(bf16).reshape(groups, count, count)
        for k in range(groups):
            start = pl.multiple_of(places[k] * count, count)
            copy = pltpu.make_async_copy(
                cross.at[m, k], cross_hbm.at[places[m], pl.ds(start, count), :], sems.at[sent]
            )
            copy.start()
            writes.append(copy)
            sent += 1
    wait_all(writes)


def chain_kernel(
    cap, owners,
    summed_hbm, factor_hbm, core_hbm, cross_hbm, starts_hbm, out_hbm,
    summed, factor, core, cross, starts, packed, sems,
):
    groups, _, count = cross.shape
    own = summed.shape[1] // (2 * UPDATES)
    pairs = [(summed_hbm, summed)]
    for u in range(UPDATES):
        pairs += [(factor_hbm.at[u], factor.at[u]), (core_hbm.at[u], core.at[u])]
        if u == 0:
            pairs += [(starts_hbm, starts)]
            pairs += [(cross_hbm.at[g], cross.at[g]) for g in range(groups)]
    reads = start_all(pairs, sems)
    first, *reads = reads
    first.wait()
    step = None
    for u in range(UPDATES):
        sums = []
        for g in range(groups):
            part = summed[g * owners, 2 * own * u : 2 * own * (u + 1), :].astype(f32)
            for o in range(1, owners):
                part += summed[g * owners + o, 2 * own * u : 2 * own * (u + 1), :].astype(f32)
            part = jnp.concatenate([part[:own], part[own:]], axis=1)
            if u:
                reads[3 + g].wait()
                part -= mix_per_step * mm(step, cross[g], 1, 0)
            sums.append(part)
        resid = jnp.concatenate(sums, axis=1)
        wait_all(reads[0:3] if u == 0 else reads[3 + groups :])
        proj = mm(resid.astype(bf16), factor[u], 1, 1)
        lifted = mm(proj.astype(bf16), core[u], 1, 1).astype(bf16)
        step = (resid - mm(lifted, factor[u], 1, 0)).astype(bf16)
        half = groups // 2
        for o in range(owners):
            lanes = []
            for g in range(groups):
                part = step[:, g * count : (g + 1) * count].astype(f32)
                back = lax.rem(count - starts[u * groups + g, o], count)
                lanes.append(pltpu.roll(part, back, 1)[:, :cap])
            packed[o, 2 * own * u : 2 * own * (u + 1), :] = jnp.concatenate(
                [jnp.concatenate(lanes[h * half : (h + 1) * half], axis=1) for h in range(2)], axis=0
            ).astype(bf16)
    wait_all(start_all([(packed, out_hbm)], sems))


def finish_kernel(
    g0_hbm, g1_hbm, g2_hbm, g3_hbm, slots_hbm, w_hbm, z_hbm, w_out, z_out,
    got, slots, w, z, steps, w_new, z_new, sems, out_sems,
):
    row = lax.axis_index("rows")
    points = w.shape[0]
    sources, deep, lanes = got.shape
    own = deep // (2 * UPDATES)
    chunks = range(0, points, CHUNK)
    pairs = [(slots_hbm, slots)]
    for k, g_hbm in enumerate((g0_hbm, g1_hbm, g2_hbm, g3_hbm)):
        size = g_hbm.shape[0]
        first = pl.multiple_of(lax.bitwise_xor(row, k) * size, size)
        pairs.append((g_hbm, got.at[pl.ds(first, size)]))
    for c in chunks:
        part = slice(c, c + CHUNK)
        pairs += [(w_hbm.at[part], w.at[part]), (z_hbm.at[part], z.at[part])]
    reads = start_all(pairs, sems)
    wait_all(reads[:5])
    reads = reads[5:]
    wide = got[...].astype(f32)
    for u in range(UPDATES):
        for h in range(2):
            first = own * (2 * u + h)
            part = wide[:, first : first + own, :].reshape(sources * own, lanes)
            steps[u, h * lanes : (h + 1) * lanes, :] = part.T.astype(bf16)
    changes = []
    for u in range(UPDATES):
        rows = one_hot(iota((points, slots.shape[1]), 0) == slots[u : u + 1, :])
        changes.append(mm(rows, steps[u], 1, 0))
    writes = []
    for n, c in enumerate(chunks):
        part = slice(c, c + CHUNK)
        wait_all(reads[2 * n : 2 * n + 2])
        current, moving = w[part, :], z[part, :]
        for change in changes:
            current, moving = stepped(current, moving, change[part])
        w_new[part, :] = current
        z_new[part, :] = moving
        for m, (a, b) in enumerate(((w_new, w_out), (z_new, z_out))):
            copy = pltpu.make_async_copy(a.at[part], b.at[part], out_sems.at[2 * n + m])
            copy.start()
            writes.append(copy)
    wait_all(writes)


VMEM = pl.BlockSpec(memory_space=pltpu.VMEM)
HBM = pl.BlockSpec(memory_space=pltpu.HBM)
in_smem = type(pltpu.SMEM((1,), i32))


def like(shape, dtype=bf16):
    return jax.ShapeDtypeStruct(shape, dtype)


def call(body, outs, inside, *args, near=0, sems=(), flops=0, grant=62):
    moved = sum(math.prod(o.shape) * o.dtype.itemsize for o in [*outs, *args])
    return pl.pallas_call(
        body,
        out_shape=outs,
        in_specs=[VMEM] * near + [HBM] * (len(args) - near),
        out_specs=[HBM] * len(outs),
        scratch_shapes=[
            x if isinstance(x, in_smem) else pltpu.VMEM(x.shape, x.dtype) for x in inside
        ]
        + [pltpu.SemaphoreType.DMA((n,)) for n in sems],
        compiler_params=pltpu.CompilerParams(vmem_limit_bytes=grant * 2**20),
        cost_estimate=pl.CostEstimate(flops=int(flops), bytes_accessed=moved, transcendentals=0),
    )(*args)


def swap(value, axis, k):
    return lax.ppermute(value, axis, [(i, i ^ k) for i in range(lax.axis_size(axis))])


def with_kernels(features, targets, coefficients, momentum, block_index, pivot_index, core):
    rows, owners = lax.axis_size("rows"), lax.axis_size("pts")
    points, width = features.shape
    block = block_index.shape[1]
    rank = pivot_index.shape[1]
    outputs = coefficients.shape[1]
    count = block // rows
    cap = 3 * count // owners
    devices = rows * owners
    own = outputs // devices
    deep = 2 * own * UPDATES
    half = rows // 2
    wide = like(coefficients.shape, f32)

    (packed,) = call(
        functools.partial(pack_kernel, count, cap, owners),
        [like((UPDATES * cap, width))],
        [block_index, features, like((UPDATES * cap, width))],
        block_index,
        features,
        sems=(2,),
    )
    came = {k: swap(packed, "pts", k) for k in reversed(range(2, owners, 2))}
    came[1] = swap(packed, "pts", 1)
    came[3] = swap(came[2], "pts", 1)
    kept = [
        like((UPDATES, outputs, points)),
        like((UPDATES, outputs, count), f32),
        like((8, 128), i32),
    ]
    given = [block_index, coefficients, momentum, targets]
    coef, offset, row_starts = call(
        functools.partial(prepare_kernel, count, owners),
        kept,
        given + kept,
        *given,
        sems=(4, 1 + 2 * UPDATES),
    )
    came[4], came[6], row_starts, later_index = lax.optimization_barrier(
        (came[4], came[6], row_starts, block_index)
    )
    came[5], came[7] = swap(came[4], "pts", 1), swap(came[6], "pts", 1)

    kept = [like((UPDATES * rows, count), i32)] * 2 + [like((8, 128), i32)]
    ids, came_from, starts = call(
        functools.partial(order_kernel, count, points, owners),
        kept,
        [block_index, *kept],
        later_index,
        sems=(3,),
    )
    row_starts, ids = lax.optimization_barrier((row_starts, ids))
    feats = like((UPDATES, width, count))
    inside_starts = pltpu.SMEM(row_starts.shape, i32)
    (mine,) = call(
        compact_kernel,
        [feats],
        [
            like((owners, *packed.shape)),
            inside_starts,
            like((UPDATES, count + cap, width), f32),
            feats,
        ],
        packed,
        *[came[k] for k in range(1, owners)],
        row_starts,
        sems=(owners + 1,),
        grant=60,
    )
    beside, across = swap(mine, "rows", 1), swap(mine, "rows", 2)
    pieces = like((devices, deep, count // 2))
    (pieces,) = call(
        sums_kernel,
        [pieces],
        [feats, features, coef, offset, like((points, count)), pieces],
        mine,
        features,
        coef,
        offset,
        sems=(4,),
        flops=2.0 * UPDATES * points * count * (2 * width + outputs),
    )
    pieces, beside, across = lax.optimization_barrier((pieces, beside, across))
    summed = lax.all_to_all(pieces, ("rows", "pts"), 0, 0, tiled=True)
    kept = [like((UPDATES, rank, block)), like((rows, block, count))]
    factor, cross = call(
        factors_kernel,
        kept,
        [
            like((rows, *feats.shape)),
            ids,
            came_from,
            pivot_index,
            kept[0],
            like((rows, rows, count, count)),
        ],
        mine,
        beside,
        across,
        swap(across, "rows", 1),
        ids,
        came_from,
        pivot_index,
        sems=(rows * rows + 2,),
        grant=60,
        flops=2.0 * width * block * (UPDATES * rank + block),
    )
    pieces = like((owners, deep, half * cap))
    (steps,) = call(
        functools.partial(chain_kernel, cap, owners),
        [pieces],
        [summed, factor, core, cross, inside_starts, pieces],
        summed,
        factor,
        core,
        cross,
        starts,
        sems=(2 * UPDATES + 3 + rows,),
        grant=60,
    )
    steps, later_index = lax.optimization_barrier((steps, block_index))
    (slots,) = call(
        functools.partial(slots_kernel, count, points, cap),
        [like((UPDATES, rows * cap), i32)],
        [block_index, like((UPDATES, rows * cap), i32)],
        later_index,
        sems=(1,),
    )
    got = lax.all_to_all(steps, "pts", 0, 0, tiled=True)
    got, slots = lax.optimization_barrier((got, slots))
    beside, across = swap(got, "rows", 1), swap(got, "rows", 2)
    parts = points // CHUNK
    return call(
        finish_kernel,
        [wide] * 2,
        [
            like((devices, deep, half * cap)),
            slots,
            wide,
            wide,
            like((UPDATES, rows * cap, outputs)),
            wide,
            wide,
        ],
        got,
        beside,
        across,
        swap(across, "rows", 1),
        slots,
        coefficients,
        momentum,
        sems=(1 + rows + 2 * parts, 2 * parts),
        grant=60,
    )


def kernel_tile(left_rows, right_rows):
    inner_prod = mm(left_rows, right_rows, 1, 1)
    left_sq = jnp.sum(jnp.square(left_rows.astype(f32)), axis=1)
    right_sq = jnp.sum(jnp.square(right_rows.astype(f32)), axis=1)
    squared = left_sq[:, None] + right_sq[None, :] - 2.0 * inner_prod
    return jnp.exp(squared * (-3.5 / left_rows.shape[1])).astype(bf16)


def with_operations(features, targets, coefficients, momentum, block_index, pivot_index, core):
    row_count, pts_count = lax.axis_size("rows"), lax.axis_size("pts")
    row_id, pts_id = lax.axis_index("rows"), lax.axis_index("pts")
    points = features.shape[0]
    block = block_index.shape[1]
    outputs = coefficients.shape[1]
    per_row = block // row_count
    per_device = per_row // pts_count
    row_cols = outputs // row_count
    own_cols = row_cols // pts_count
    first = row_id * row_cols
    current, moving, goal = (
        lax.dynamic_slice_in_dim(value, first, row_cols, axis=1).T.astype(f32)
        for value in (coefficients, momentum, targets)
    )
    ids = iota((points, 1), 0) + pts_id * points
    place = [(ids == block_index[u][None, :]).astype(bf16) for u in range(UPDATES)]
    own_rows = []
    for u in range(UPDATES):
        mine = lax.dynamic_slice_in_dim(place[u], row_id * per_row, per_row, axis=1)
        own_rows.append(mm(mine, features, 0, 0).astype(bf16).reshape(pts_count, per_device, -1))
    came = lax.all_to_all(jnp.concatenate(own_rows, axis=1), "pts", 0, 0, tiled=False)
    chunk = jnp.sum(came.astype(f32), axis=0).astype(bf16)
    spread = lax.all_gather(lax.all_gather(chunk, "pts", axis=0), "rows", axis=0)
    spread = spread.reshape(row_count, pts_count, UPDATES, per_device, features.shape[1])
    all_steps = []
    for u in range(UPDATES):
        block_feats = spread[:, :, u].reshape(block, features.shape[1])
        mixed = mixed_of(current, moving)
        high, low = split_two(ridge_term * mixed - goal)
        tile = kernel_tile(features, block_feats)
        partial_value = (
            mm(mixed.astype(bf16), tile, 1, 0) + mm(high, place[u], 1, 0) + mm(low, place[u], 1, 0)
        )
        pieces = partial_value.astype(bf16).reshape(pts_count, own_cols, block)
        summed = lax.all_to_all(pieces, "pts", 0, 0, tiled=False)
        resid = jnp.sum(summed.astype(f32), axis=0)
        at_pivot = (iota((block, 1), 0) == pivot_index[u][None, :]).astype(bf16)
        factor = kernel_tile(block_feats, mm(at_pivot, block_feats, 0, 0).astype(bf16))
        proj = mm(resid.astype(bf16), factor, 1, 0)
        lifted = mm(proj.astype(bf16), core[u], 1, 1).astype(bf16)
        step_bf = (resid - mm(lifted, factor, 1, 1)).astype(bf16)
        steps = lax.all_gather(step_bf, "pts", axis=0, tiled=True)
        change = mm(steps, place[u], 1, 1)
        all_steps.append(change.astype(bf16))
        current, moving = stepped(current, moving, change)
    gathered = lax.all_gather(jnp.stack(all_steps), "rows", axis=1, tiled=True)
    current, moving = coefficients, momentum
    for u in range(UPDATES):
        current, moving = stepped(current, moving, gathered[u].T.astype(f32))
    return (current, moving)


def shards(features, targets, coefficients, momentum, block_index, pivot_index, nystrom_core):
    rows, owners = lax.axis_size("rows"), lax.axis_size("pts")
    count = block_index.shape[1] // rows
    fits = rows == 4 and owners == 8 and coefficients.shape[1] == 8 * rows * owners
    fits = fits and 6 * count <= count * owners and coefficients.shape[0] % CHUNK == 0 and count % CHUNK == 0 and (3 * count // owners) % 64 == 0 and UPDATES * rows == 8
    plan = with_kernels if fits else with_operations
    return plan(
        features, targets, coefficients, momentum, block_index, pivot_index, nystrom_core
    )


def solution(mesh):
    in_specs = (P("pts", None), P("pts", None), P("pts", None), P("pts", None), P(), P(), P())
    out_specs = (P("pts", None), P("pts", None))
    return jax.shard_map(shards, mesh=mesh, in_specs=in_specs, out_specs=out_specs, check_vma=False)
```

```python
import functools
import math

import jax
import jax.numpy as jnp
from jax import lax
from jax.experimental import pallas as pl
from jax.experimental.pallas import tpu as pltpu
from jax.sharding import PartitionSpec as P

UPDATES = 2


alpha_mix = 0.6
beta_keep = 0.9
step_size = 0.2
momentum_gain = 1.5
ridge_term = 1.0

f32 = jnp.float32
bf16 = jnp.bfloat16
i32 = jnp.int32


def mm(a, b, ca, cb):
    return lax.dot_general(a, b, (((ca,), (cb,)), ((), ())), preferred_element_type=f32)


def split_two(value):
    high = value.astype(bf16)
    return high, (value - high.astype(f32)).astype(bf16)


def mixed_of(current, moving):
    return alpha_mix * moving + (1.0 - alpha_mix) * current


mix_per_step = alpha_mix * step_size * momentum_gain + (1.0 - alpha_mix) * step_size


def stepped(current, moving, change):
    mixed = mixed_of(current, moving)
    if change is None:
        return mixed, beta_keep * moving + (1.0 - beta_keep) * mixed
    return (
        mixed - step_size * change,
        beta_keep * moving + (1.0 - beta_keep) * mixed - step_size * momentum_gain * change,
    )


def iota(shape, axis):
    return lax.broadcasted_iota(i32, shape, axis)


def one_hot(chosen):
    return jnp.where(chosen, 1.0, 0.0).astype(bf16)


def before_matrix(n):
    return one_hot(iota((n, n), 0) < iota((n, n), 1))


def owners_of(groups, points, owners):
    owner_ids = iota((owners, groups[0].shape[1]), 0)
    owner = [lax.div(x, jnp.full_like(x, points)) for x in groups]
    marks = [jnp.where(owner_ids == x, 1.0, 0.0) for x in owner]
    every = jnp.concatenate(marks, axis=0).astype(bf16)
    earlier = mm(every, before_matrix(every.shape[1]), 1, 0)
    out = []
    for n, x in enumerate(owner):
        rank = jnp.sum(marks[n] * earlier[n * owners : (n + 1) * owners], axis=0, keepdims=True)
        start = jnp.sum(jnp.where(x < owner_ids, 1.0, 0.0), axis=1, keepdims=True)
        out.append((marks[n], rank, start))
    return out


def sorted_places(marks, rank, start):
    return (rank + jnp.sum(marks * start, axis=0, keepdims=True)).astype(i32)


def lane_row(column):
    n = column.shape[0]
    diagonal = iota((n, 128), 0) == iota((n, 128), 1)
    return jnp.sum(jnp.where(diagonal, column, 0.0), axis=0, keepdims=True).astype(i32)


def two_digits(*rows):
    shape = (8, rows[0].shape[1])
    value = jnp.zeros(shape, i32)
    for n, row in enumerate(rows):
        high = lax.shift_right_logical(row, jnp.full_like(row, 7))
        low = lax.bitwise_and(row, jnp.full_like(row, 127))
        value = jnp.where(iota(shape, 0) == 2 * n, high, value)
        value = jnp.where(iota(shape, 0) == 2 * n + 1, low, value)
    return value.astype(f32).astype(bf16)


def from_digits(digits):
    return (digits[0:1] * 128.0 + digits[1:2]).astype(i32)


def start_all(pairs, sems):
    copies = [pltpu.make_async_copy(a, b, sems.at[n]) for n, (a, b) in enumerate(pairs)]
    for copy in copies:
        copy.start()
    return copies


def wait_all(copies):
    for copy in copies:
        copy.wait()


def group_row(blocks, u, group, count):
    return blocks[u : u + 1, pl.ds(pl.multiple_of(group * count, count), count)]


def pack_kernel(count, cap, owners, blocks_hbm, feats_hbm, out_hbm, blocks, feats, packed, sems):
    row, me = lax.axis_index("rows"), lax.axis_index("pts")
    points = feats.shape[0]
    reads = start_all([(blocks_hbm, blocks), (feats_hbm, feats)], sems)
    before = before_matrix(count)
    reads[0].wait()
    rows = []
    for u in range(UPDATES):
        indices = group_row(blocks, u, row, count)
        local = indices - me * points
        mine = jnp.where((local >= 0) & (local < points), 1.0, 0.0)
        rank = mm(jnp.broadcast_to(mine, (8, count)).astype(bf16), before, 1, 0)[0:1]
        held = (iota((cap, count), 0) == rank.astype(i32)) & (mine > 0.0)
        point = jnp.sum(jnp.where(held, (local + 1).astype(f32), 0.0), axis=1, keepdims=True)
        rows.append(one_hot(iota((cap, points), 1) == point.astype(i32) - 1))
    reads[1].wait()
    for u in range(UPDATES):
        packed[u * cap : (u + 1) * cap, :] = mm(rows[u], feats[...], 1, 0).astype(bf16)
    wait_all(start_all([(packed, out_hbm)], sems))


def prepare_kernel(
    count, owners,
    blocks_hbm, w_hbm, z_hbm, t_hbm, coef_hbm, offset_hbm, starts_hbm,
    blocks, w, z, t, coef, offset, starts, sems, out_sems,
):
    row, me = lax.axis_index("rows"), lax.axis_index("pts")
    points, outputs = w.shape
    reads = start_all([(blocks_hbm, blocks), (w_hbm, w), (z_hbm, z), (t_hbm, t)], sems)
    reads[0].wait()
    groups = [group_row(blocks, u, row, count) for u in range(UPDATES)]
    found, shift = [], []
    for u, (_, rank, start) in enumerate(owners_of(groups, points, owners)):
        starts[u : u + 1, :] = lane_row(start)
        local = groups[u] - me * points
        mine = (local >= 0) & (local < points)
        held = jnp.where(mine, rank.astype(i32), -1)
        chosen = one_hot(iota((count // 2, count), 0) == held)
        digits = two_digits(jnp.where(mine, local + 1, 0))
        found.append(from_digits(mm(digits, chosen, 1, 1)) - 1)
        earlier = jnp.sum(jnp.where(groups[u] < me * points, 1.0, 0.0))
        shift.append(lax.rem(earlier.astype(i32), count))
    writes = start_all([(starts, starts_hbm)], out_sems)
    wait_all(reads[1:])
    current, moving = w[...], z[...]
    goal = t[...].astype(f32).T
    for u in range(UPDATES):
        mixed = mixed_of(current, moving).T
        high, low = split_two(ridge_term * mixed - goal)
        coef[u] = mixed.astype(bf16)
        place = one_hot(iota((points, count // 2), 0) == found[u])
        both = mm(jnp.concatenate([high, low], axis=0), place, 1, 0)
        held = both[:outputs] + both[outputs:]
        held = jnp.concatenate([held, jnp.zeros_like(held)], axis=1)
        offset[u] = pltpu.roll(held, shift[u], 1)
        current, moving = stepped(current, moving, None)
        for a, b in ((coef, coef_hbm), (offset, offset_hbm)):
            writes.append(pltpu.make_async_copy(a.at[u], b.at[u], out_sems.at[len(writes)]))
            writes[-1].start()
    wait_all(writes)


def order_kernel(
    count, points, owners,
    blocks_hbm, ids_hbm, from_hbm, starts_hbm,
    blocks, ids, came_from, starts, sems,
):
    wait_all(start_all([(blocks_hbm, blocks)], sems))
    count_of = blocks.shape[1] // count
    groups = [
        blocks[u : u + 1, g * count : (g + 1) * count]
        for u in range(UPDATES)
        for g in range(count_of)
    ]
    for n, (marks, rank, start) in enumerate(owners_of(groups, points, owners)):
        place = sorted_places(marks, rank, start)
        given = iota((1, count), 1) + (n % count_of) * count
        digits = two_digits(groups[n], given)
        moved = mm(digits, one_hot(iota((count, count), 0) == place), 1, 1)
        ids[n : n + 1, :] = from_digits(moved[0:2])
        came_from[n : n + 1, :] = from_digits(moved[2:4])
        starts[n : n + 1, :] = lane_row(start)
    wait_all(start_all([(ids, ids_hbm), (came_from, from_hbm), (starts, starts_hbm)], sems))


def slots_kernel(count, points, cap, blocks_hbm, slots_hbm, blocks, slots, sems):
    me = lax.axis_index("pts")
    wait_all(start_all([(blocks_hbm, blocks)], sems))
    before = before_matrix(count)
    groups = blocks.shape[1] // count
    for u in range(UPDATES):
        found = jnp.zeros((8, groups * cap), f32)
        for g in range(groups):
            local = blocks[u : u + 1, g * count : (g + 1) * count] - me * points
            mine = (local >= 0) & (local < points)
            counts = jnp.where(mine, 1.0, 0.0)
            rank = mm(jnp.broadcast_to(counts, (8, count)).astype(bf16), before, 1, 0)[0:1]
            held = jnp.where(mine, rank.astype(i32) + g * cap, -1)
            chosen = one_hot(iota((groups * cap, count), 0) == held)
            found += mm(two_digits(jnp.where(mine, local + 1, 0)), chosen, 1, 1)
        slots[u : u + 1, :] = from_digits(found) - 1
    wait_all(start_all([(slots, slots_hbm)], sems))


def extended(rows, axis, first):
    rest = -0.5 * jnp.sum(jnp.square(rows.astype(f32)), axis=axis, keepdims=True)
    parts = []
    for _ in range(3):
        parts.append(rest.astype(bf16).astype(f32))
        rest = rest - parts[-1]
    parts = parts + [1.0] * 3 if first else [1.0] * 3 + parts
    at = iota(rows.shape, axis)
    extra = jnp.zeros(rows.shape, f32)
    for n, part in enumerate(parts):
        extra = jnp.where(at == n, part, extra)
    return jnp.concatenate([rows.astype(bf16), extra.astype(bf16)], axis=axis)


def exponent(left, right):
    return mm(left, right, 1, 0) * (7.0 / (left.shape[1] // 2))


CHUNK = 256


def compact_kernel(*refs):
    *came_hbm, starts_hbm, block_hbm, came, starts, wide, block, sems = refs
    me = lax.axis_index("pts")
    owners, deep, _ = came.shape
    cap = deep // UPDATES
    count = block.shape[2]
    pairs = [(a, came.at[k]) for k, a in enumerate(came_hbm)]
    wait_all(start_all([*pairs, (starts_hbm, starts)], sems))
    for u in range(UPDATES):
        for o in range(owners):
            start = starts[u, o]
            rows = came[lax.bitwise_xor(me, o), u * cap : (u + 1) * cap, :]
            wide[u, pl.ds(start, cap), :] = rows.astype(f32)
        block[u] = wide[u, 0:count, :].T.astype(bf16)
    wait_all(start_all([(block, block_hbm)], sems))


def sums_kernel(
    block_hbm, feats_hbm, coef_hbm, offset_hbm, pieces_hbm,
    block, feats, coef, offset, tile, pieces, sems,
):
    outputs = coef.shape[1]
    pairs = [(block_hbm, block), (feats_hbm, feats), (coef_hbm, coef), (offset_hbm, offset)]
    reads = start_all(pairs, sems)
    wait_all(reads[:2])
    left = extended(feats[...], 1, True)
    for u in range(UPDATES):
        right = extended(block[u], 0, False)
        tile[...] = jnp.exp(exponent(left, right)).astype(bf16)
        if u == 0:
            wait_all(reads[2:])
        total = offset[u] + mm(coef[u], tile[...], 1, 0)
        devices, _, lanes = pieces.shape
        own = outputs // devices
        for d in range(devices):
            part = total[d * own : (d + 1) * own]
            pieces[d, 2 * own * u : 2 * own * (u + 1), :] = jnp.concatenate(
                [part[:, :lanes], part[:, lanes:]], axis=0
            ).astype(bf16)
    wait_all(start_all([(pieces, pieces_hbm)], sems))


def factors_kernel(
    b0_hbm, b1_hbm, b2_hbm, b3_hbm, ids_hbm, from_hbm, pivots_hbm, factor_hbm, cross_hbm,
    feats, ids, came_from, pivots, factor, cross, sems,
):
    row = lax.axis_index("rows")
    groups, _, width, count = feats.shape
    pairs = [(b_hbm, feats.at[k]) for k, b_hbm in enumerate((b0_hbm, b1_hbm, b2_hbm, b3_hbm))]
    pairs += [(ids_hbm, ids), (from_hbm, came_from), (pivots_hbm, pivots)]
    wait_all(start_all(pairs, sems))
    places = [lax.bitwise_xor(row, k) for k in range(groups)]
    rights = [[extended(feats[k, u], 0, False) for k in range(groups)] for u in range(UPDATES)]
    given = [[feats[k, u].astype(f32).T for k in range(groups)] for u in range(UPDATES)]
    for u in range(UPDATES):
        wanted = pivots[u : u + 1, :].astype(f32)
        wanted = jnp.broadcast_to(wanted, (8, wanted.shape[1])).T[:, 0:1]
        chosen_feats = jnp.zeros((pivots.shape[1], width), f32)
        for k in range(groups):
            here = came_from[pl.ds(u * groups + places[k], 1), :].astype(f32)
            chosen_feats += mm(one_hot(wanted == here), given[u][k].astype(bf16), 1, 0)
        left = extended(chosen_feats, 1, True)
        for k in range(groups):
            start = pl.multiple_of(places[k] * count, count)
            value = jnp.exp(exponent(left, rights[u][k]))
            factor[u, :, pl.ds(start, count)] = value.astype(bf16)
    writes = start_all([(factor, factor_hbm)], sems)
    lefts, left_points = [], []
    for k in range(groups):
        lefts.append(extended(given[0][k], 1, True))
        points = ids[pl.ds(places[k], 1), :].astype(f32)
        left_points.append(jnp.broadcast_to(points, (8, count)).T[:, 0:1])
    left, left_points = jnp.concatenate(lefts, axis=0), jnp.concatenate(left_points, axis=0)
    sent = 1
    for m in range(groups):
        right_points = ids[pl.ds(groups + places[m], 1), :].astype(f32)
        power = exponent(left, rights[1][m])
        power = jnp.where(left_points == right_points, math.log(1.0 + ridge_term), power)
        cross[m] = jnp.exp(power).astype(bf16).reshape(groups, count, count)
        for k in range(groups):
            start = pl.multiple_of(places[k] * count, count)
            copy = pltpu.make_async_copy(
                cross.at[m, k], cross_hbm.at[places[m], pl.ds(start, count), :], sems.at[sent]
            )
            copy.start()
            writes.append(copy)
            sent += 1
    wait_all(writes)


def chain_kernel(
    cap, owners,
    summed_hbm, factor_hbm, core_hbm, cross_hbm, starts_hbm, out_hbm,
    summed, factor, core, cross, starts, packed, sems,
):
    groups, _, count = cross.shape
    own = summed.shape[1] // (2 * UPDATES)
    pairs = [(summed_hbm, summed)]
    for u in range(UPDATES):
        pairs += [(factor_hbm.at[u], factor.at[u]), (core_hbm.at[u], core.at[u])]
        if u == 0:
            pairs += [(starts_hbm, starts)]
            pairs += [(cross_hbm.at[g], cross.at[g]) for g in range(groups)]
    reads = start_all(pairs, sems)
    first, *reads = reads
    first.wait()
    step = None
    for u in range(UPDATES):
        sums = []
        for g in range(groups):
            part = summed[g * owners, 2 * own * u : 2 * own * (u + 1), :].astype(f32)
            for o in range(1, owners):
                part += summed[g * owners + o, 2 * own * u : 2 * own * (u + 1), :].astype(f32)
            part = jnp.concatenate([part[:own], part[own:]], axis=1)
            if u:
                reads[3 + g].wait()
                part -= mix_per_step * mm(step, cross[g], 1, 0)
            sums.append(part)
        resid = jnp.concatenate(sums, axis=1)
        wait_all(reads[0:3] if u == 0 else reads[3 + groups :])
        proj = mm(resid.astype(bf16), factor[u], 1, 1)
        lifted = mm(proj.astype(bf16), core[u], 1, 1).astype(bf16)
        step = (resid - mm(lifted, factor[u], 1, 0)).astype(bf16)
        half = groups // 2
        for o in range(owners):
            lanes = []
            for g in range(groups):
                part = step[:, g * count : (g + 1) * count].astype(f32)
                back = lax.rem(count - starts[u * groups + g, o], count)
                lanes.append(pltpu.roll(part, back, 1)[:, :cap])
            packed[o, 2 * own * u : 2 * own * (u + 1), :] = jnp.concatenate(
                [jnp.concatenate(lanes[h * half : (h + 1) * half], axis=1) for h in range(2)], axis=0
            ).astype(bf16)
    wait_all(start_all([(packed, out_hbm)], sems))


def finish_kernel(
    g0_hbm, g1_hbm, g2_hbm, g3_hbm, slots_hbm, w_hbm, z_hbm, w_out, z_out,
    got, slots, w, z, steps, w_new, z_new, sems, out_sems,
):
    row = lax.axis_index("rows")
    points = w.shape[0]
    sources, deep, lanes = got.shape
    own = deep // (2 * UPDATES)
    chunks = range(0, points, CHUNK)
    pairs = [(slots_hbm, slots)]
    for k, g_hbm in enumerate((g0_hbm, g1_hbm, g2_hbm, g3_hbm)):
        size = g_hbm.shape[0]
        first = pl.multiple_of(lax.bitwise_xor(row, k) * size, size)
        pairs.append((g_hbm, got.at[pl.ds(first, size)]))
    for c in chunks:
        part = slice(c, c + CHUNK)
        pairs += [(w_hbm.at[part], w.at[part]), (z_hbm.at[part], z.at[part])]
    reads = start_all(pairs, sems)
    wait_all(reads[:5])
    reads = reads[5:]
    wide = got[...].astype(f32)
    for u in range(UPDATES):
        for h in range(2):
            first = own * (2 * u + h)
            part = wide[:, first : first + own, :].reshape(sources * own, lanes)
            steps[u, h * lanes : (h + 1) * lanes, :] = part.T.astype(bf16)
    changes = []
    for u in range(UPDATES):
        rows = one_hot(iota((points, slots.shape[1]), 0) == slots[u : u + 1, :])
        changes.append(mm(rows, steps[u], 1, 0))
    writes = []
    for n, c in enumerate(chunks):
        part = slice(c, c + CHUNK)
        wait_all(reads[2 * n : 2 * n + 2])
        current, moving = w[part, :], z[part, :]
        for change in changes:
            current, moving = stepped(current, moving, change[part])
        w_new[part, :] = current
        z_new[part, :] = moving
        for m, (a, b) in enumerate(((w_new, w_out), (z_new, z_out))):
            copy = pltpu.make_async_copy(a.at[part], b.at[part], out_sems.at[2 * n + m])
            copy.start()
            writes.append(copy)
    wait_all(writes)


VMEM = pl.BlockSpec(memory_space=pltpu.VMEM)
HBM = pl.BlockSpec(memory_space=pltpu.HBM)
in_smem = type(pltpu.SMEM((1,), i32))


def like(shape, dtype=bf16):
    return jax.ShapeDtypeStruct(shape, dtype)


def call(body, outs, inside, *args, near=0, sems=(), flops=0, grant=62):
    moved = sum(math.prod(o.shape) * o.dtype.itemsize for o in [*outs, *args])
    return pl.pallas_call(
        body,
        out_shape=outs,
        in_specs=[VMEM] * near + [HBM] * (len(args) - near),
        out_specs=[HBM] * len(outs),
        scratch_shapes=[
            x if isinstance(x, in_smem) else pltpu.VMEM(x.shape, x.dtype) for x in inside
        ]
        + [pltpu.SemaphoreType.DMA((n,)) for n in sems],
        compiler_params=pltpu.CompilerParams(vmem_limit_bytes=grant * 2**20),
        cost_estimate=pl.CostEstimate(flops=int(flops), bytes_accessed=moved, transcendentals=0),
    )(*args)


def swap(value, axis, k):
    return lax.ppermute(value, axis, [(i, i ^ k) for i in range(lax.axis_size(axis))])


def with_kernels(features, targets, coefficients, momentum, block_index, pivot_index, core):
    rows, owners = lax.axis_size("rows"), lax.axis_size("pts")
    points, width = features.shape
    block = block_index.shape[1]
    rank = pivot_index.shape[1]
    outputs = coefficients.shape[1]
    count = block // rows
    cap = 3 * count // owners
    devices = rows * owners
    own = outputs // devices
    deep = 2 * own * UPDATES
    half = rows // 2
    wide = like(coefficients.shape, f32)

    (packed,) = call(
        functools.partial(pack_kernel, count, cap, owners),
        [like((UPDATES * cap, width))],
        [block_index, features, like((UPDATES * cap, width))],
        block_index,
        features,
        sems=(2,),
    )
    came = {k: swap(packed, "pts", k) for k in reversed(range(2, owners, 2))}
    came[1] = swap(packed, "pts", 1)
    came[2], first_index = lax.optimization_barrier((came[2], block_index))
    came[3] = swap(came[2], "pts", 1)
    kept = [
        like((UPDATES, outputs, points)),
        like((UPDATES, outputs, count), f32),
        like((8, 128), i32),
    ]
    given = [first_index, coefficients, momentum, targets]
    coef, offset, row_starts = call(
        functools.partial(prepare_kernel, count, owners),
        kept,
        given + kept,
        *given,
        sems=(4, 1 + 2 * UPDATES),
    )
    came[4], came[6], row_starts, later_index = lax.optimization_barrier(
        (came[4], came[6], row_starts, block_index)
    )
    came[5], came[7] = swap(came[4], "pts", 1), swap(came[6], "pts", 1)

    kept = [like((UPDATES * rows, count), i32)] * 2 + [like((8, 128), i32)]
    ids, came_from, starts = call(
        functools.partial(order_kernel, count, points, owners),
        kept,
        [block_index, *kept],
        later_index,
        sems=(3,),
    )
    row_starts, ids = lax.optimization_barrier((row_starts, ids))
    feats = like((UPDATES, width, count))
    inside_starts = pltpu.SMEM(row_starts.shape, i32)
    (mine,) = call(
        compact_kernel,
        [feats],
        [
            like((owners, *packed.shape)),
            inside_starts,
            like((UPDATES, count + cap, width), f32),
            feats,
        ],
        packed,
        *[came[k] for k in range(1, owners)],
        row_starts,
        sems=(owners + 1,),
        grant=60,
    )
    beside, across = swap(mine, "rows", 1), swap(mine, "rows", 2)
    pieces = like((devices, deep, count // 2))
    (pieces,) = call(
        sums_kernel,
        [pieces],
        [feats, features, coef, offset, like((points, count)), pieces],
        mine,
        features,
        coef,
        offset,
        sems=(4,),
        flops=2.0 * UPDATES * points * count * (2 * width + outputs),
    )
    pieces, beside, across = lax.optimization_barrier((pieces, beside, across))
    summed = lax.all_to_all(pieces, ("rows", "pts"), 0, 0, tiled=True)
    kept = [like((UPDATES, rank, block)), like((rows, block, count))]
    factor, cross = call(
        factors_kernel,
        kept,
        [
            like((rows, *feats.shape)),
            ids,
            came_from,
            pivot_index,
            kept[0],
            like((rows, rows, count, count)),
        ],
        mine,
        beside,
        across,
        swap(across, "rows", 1),
        ids,
        came_from,
        pivot_index,
        sems=(rows * rows + 2,),
        grant=60,
        flops=2.0 * width * block * (UPDATES * rank + block),
    )
    pieces = like((owners, deep, half * cap))
    (steps,) = call(
        functools.partial(chain_kernel, cap, owners),
        [pieces],
        [summed, factor, core, cross, inside_starts, pieces],
        summed,
        factor,
        core,
        cross,
        starts,
        sems=(2 * UPDATES + 3 + rows,),
        grant=60,
    )
    steps, later_index = lax.optimization_barrier((steps, block_index))
    (slots,) = call(
        functools.partial(slots_kernel, count, points, cap),
        [like((UPDATES, rows * cap), i32)],
        [block_index, like((UPDATES, rows * cap), i32)],
        later_index,
        sems=(1,),
    )
    got = lax.all_to_all(steps, "pts", 0, 0, tiled=True)
    got, slots = lax.optimization_barrier((got, slots))
    beside, across = swap(got, "rows", 1), swap(got, "rows", 2)
    parts = points // CHUNK
    return call(
        finish_kernel,
        [wide] * 2,
        [
            like((devices, deep, half * cap)),
            slots,
            wide,
            wide,
            like((UPDATES, rows * cap, outputs)),
            wide,
            wide,
        ],
        got,
        beside,
        across,
        swap(across, "rows", 1),
        slots,
        coefficients,
        momentum,
        sems=(1 + rows + 2 * parts, 2 * parts),
        grant=60,
    )


def kernel_tile(left_rows, right_rows):
    inner_prod = mm(left_rows, right_rows, 1, 1)
    left_sq = jnp.sum(jnp.square(left_rows.astype(f32)), axis=1)
    right_sq = jnp.sum(jnp.square(right_rows.astype(f32)), axis=1)
    squared = left_sq[:, None] + right_sq[None, :] - 2.0 * inner_prod
    return jnp.exp(squared * (-3.5 / left_rows.shape[1])).astype(bf16)


def with_operations(features, targets, coefficients, momentum, block_index, pivot_index, core):
    row_count, pts_count = lax.axis_size("rows"), lax.axis_size("pts")
    row_id, pts_id = lax.axis_index("rows"), lax.axis_index("pts")
    points = features.shape[0]
    block = block_index.shape[1]
    outputs = coefficients.shape[1]
    per_row = block // row_count
    per_device = per_row // pts_count
    row_cols = outputs // row_count
    own_cols = row_cols // pts_count
    first = row_id * row_cols
    current, moving, goal = (
        lax.dynamic_slice_in_dim(value, first, row_cols, axis=1).T.astype(f32)
        for value in (coefficients, momentum, targets)
    )
    ids = iota((points, 1), 0) + pts_id * points
    place = [(ids == block_index[u][None, :]).astype(bf16) for u in range(UPDATES)]
    own_rows = []
    for u in range(UPDATES):
        mine = lax.dynamic_slice_in_dim(place[u], row_id * per_row, per_row, axis=1)
        own_rows.append(mm(mine, features, 0, 0).astype(bf16).reshape(pts_count, per_device, -1))
    came = lax.all_to_all(jnp.concatenate(own_rows, axis=1), "pts", 0, 0, tiled=False)
    chunk = jnp.sum(came.astype(f32), axis=0).astype(bf16)
    spread = lax.all_gather(lax.all_gather(chunk, "pts", axis=0), "rows", axis=0)
    spread = spread.reshape(row_count, pts_count, UPDATES, per_device, features.shape[1])
    all_steps = []
    for u in range(UPDATES):
        block_feats = spread[:, :, u].reshape(block, features.shape[1])
        mixed = mixed_of(current, moving)
        high, low = split_two(ridge_term * mixed - goal)
        tile = kernel_tile(features, block_feats)
        partial_value = (
            mm(mixed.astype(bf16), tile, 1, 0) + mm(high, place[u], 1, 0) + mm(low, place[u], 1, 0)
        )
        pieces = partial_value.astype(bf16).reshape(pts_count, own_cols, block)
        summed = lax.all_to_all(pieces, "pts", 0, 0, tiled=False)
        resid = jnp.sum(summed.astype(f32), axis=0)
        at_pivot = (iota((block, 1), 0) == pivot_index[u][None, :]).astype(bf16)
        factor = kernel_tile(block_feats, mm(at_pivot, block_feats, 0, 0).astype(bf16))
        proj = mm(resid.astype(bf16), factor, 1, 0)
        lifted = mm(proj.astype(bf16), core[u], 1, 1).astype(bf16)
        step_bf = (resid - mm(lifted, factor, 1, 1)).astype(bf16)
        steps = lax.all_gather(step_bf, "pts", axis=0, tiled=True)
        change = mm(steps, place[u], 1, 1)
        all_steps.append(change.astype(bf16))
        current, moving = stepped(current, moving, change)
    gathered = lax.all_gather(jnp.stack(all_steps), "rows", axis=1, tiled=True)
    current, moving = coefficients, momentum
    for u in range(UPDATES):
        current, moving = stepped(current, moving, gathered[u].T.astype(f32))
    return (current, moving)


def shards(features, targets, coefficients, momentum, block_index, pivot_index, nystrom_core):
    rows, owners = lax.axis_size("rows"), lax.axis_size("pts")
    count = block_index.shape[1] // rows
    fits = rows == 4 and owners == 8 and coefficients.shape[1] == 8 * rows * owners
    fits = fits and 6 * count <= count * owners and coefficients.shape[0] % CHUNK == 0 and count % CHUNK == 0 and (3 * count // owners) % 64 == 0 and UPDATES * rows == 8
    plan = with_kernels if fits else with_operations
    return plan(
        features, targets, coefficients, momentum, block_index, pivot_index, nystrom_core
    )


def solution(mesh):
    in_specs = (P("pts", None), P("pts", None), P("pts", None), P("pts", None), P(), P(), P())
    out_specs = (P("pts", None), P("pts", None))
    return jax.shard_map(shards, mesh=mesh, in_specs=in_specs, out_specs=out_specs, check_vma=False)
```

```python
import functools
import math

import jax
import jax.numpy as jnp
from jax import lax
from jax.experimental import pallas as pl
from jax.experimental.pallas import tpu as pltpu
from jax.sharding import PartitionSpec as P

UPDATES = 2


alpha_mix = 0.6
beta_keep = 0.9
step_size = 0.2
momentum_gain = 1.5
ridge_term = 1.0

f32 = jnp.float32
bf16 = jnp.bfloat16
i32 = jnp.int32


def mm(a, b, ca, cb):
    return lax.dot_general(a, b, (((ca,), (cb,)), ((), ())), preferred_element_type=f32)


def split_two(value):
    high = value.astype(bf16)
    return high, (value - high.astype(f32)).astype(bf16)


def mixed_of(current, moving):
    return alpha_mix * moving + (1.0 - alpha_mix) * current


mix_per_step = alpha_mix * step_size * momentum_gain + (1.0 - alpha_mix) * step_size


def stepped(current, moving, change):
    mixed = mixed_of(current, moving)
    if change is None:
        return mixed, beta_keep * moving + (1.0 - beta_keep) * mixed
    return (
        mixed - step_size * change,
        beta_keep * moving + (1.0 - beta_keep) * mixed - step_size * momentum_gain * change,
    )


def iota(shape, axis):
    return lax.broadcasted_iota(i32, shape, axis)


def one_hot(chosen):
    return jnp.where(chosen, 1.0, 0.0).astype(bf16)


def before_matrix(n):
    return one_hot(iota((n, n), 0) < iota((n, n), 1))


def owners_of(groups, points, owners):
    owner_ids = iota((owners, groups[0].shape[1]), 0)
    owner = [lax.div(x, jnp.full_like(x, points)) for x in groups]
    marks = [jnp.where(owner_ids == x, 1.0, 0.0) for x in owner]
    every = jnp.concatenate(marks, axis=0).astype(bf16)
    earlier = mm(every, before_matrix(every.shape[1]), 1, 0)
    out = []
    for n, x in enumerate(owner):
        rank = jnp.sum(marks[n] * earlier[n * owners : (n + 1) * owners], axis=0, keepdims=True)
        start = jnp.sum(jnp.where(x < owner_ids, 1.0, 0.0), axis=1, keepdims=True)
        out.append((marks[n], rank, start))
    return out


def sorted_places(marks, rank, start):
    return (rank + jnp.sum(marks * start, axis=0, keepdims=True)).astype(i32)


def lane_row(column):
    n = column.shape[0]
    diagonal = iota((n, 128), 0) == iota((n, 128), 1)
    return jnp.sum(jnp.where(diagonal, column, 0.0), axis=0, keepdims=True).astype(i32)


def two_digits(*rows):
    shape = (8, rows[0].shape[1])
    value = jnp.zeros(shape, i32)
    for n, row in enumerate(rows):
        high = lax.shift_right_logical(row, jnp.full_like(row, 7))
        low = lax.bitwise_and(row, jnp.full_like(row, 127))
        value = jnp.where(iota(shape, 0) == 2 * n, high, value)
        value = jnp.where(iota(shape, 0) == 2 * n + 1, low, value)
    return value.astype(f32).astype(bf16)


def from_digits(digits):
    return (digits[0:1] * 128.0 + digits[1:2]).astype(i32)


def start_all(pairs, sems):
    copies = [pltpu.make_async_copy(a, b, sems.at[n]) for n, (a, b) in enumerate(pairs)]
    for copy in copies:
        copy.start()
    return copies


def wait_all(copies):
    for copy in copies:
        copy.wait()


def group_row(blocks, u, group, count):
    return blocks[u : u + 1, pl.ds(pl.multiple_of(group * count, count), count)]


def pack_kernel(count, cap, owners, blocks_hbm, feats_hbm, out_hbm, blocks, feats, packed, sems):
    row, me = lax.axis_index("rows"), lax.axis_index("pts")
    points = feats.shape[0]
    reads = start_all([(blocks_hbm, blocks), (feats_hbm, feats)], sems)
    before = before_matrix(count)
    reads[0].wait()
    rows = []
    for u in range(UPDATES):
        indices = group_row(blocks, u, row, count)
        local = indices - me * points
        mine = jnp.where((local >= 0) & (local < points), 1.0, 0.0)
        rank = mm(jnp.broadcast_to(mine, (8, count)).astype(bf16), before, 1, 0)[0:1]
        held = (iota((cap, count), 0) == rank.astype(i32)) & (mine > 0.0)
        point = jnp.sum(jnp.where(held, (local + 1).astype(f32), 0.0), axis=1, keepdims=True)
        rows.append(one_hot(iota((cap, points), 1) == point.astype(i32) - 1))
    reads[1].wait()
    for u in range(UPDATES):
        packed[u * cap : (u + 1) * cap, :] = mm(rows[u], feats[...], 1, 0).astype(bf16)
    wait_all(start_all([(packed, out_hbm)], sems))


def prepare_kernel(
    count, owners,
    blocks_hbm, w_hbm, z_hbm, t_hbm, coef_hbm, offset_hbm, starts_hbm,
    blocks, w, z, t, coef, offset, starts, sems, out_sems,
):
    row, me = lax.axis_index("rows"), lax.axis_index("pts")
    points, outputs = w.shape
    reads = start_all([(blocks_hbm, blocks), (w_hbm, w), (z_hbm, z), (t_hbm, t)], sems)
    reads[0].wait()
    groups = [group_row(blocks, u, row, count) for u in range(UPDATES)]
    found, shift = [], []
    for u, (_, rank, start) in enumerate(owners_of(groups, points, owners)):
        starts[u : u + 1, :] = lane_row(start)
        local = groups[u] - me * points
        mine = (local >= 0) & (local < points)
        held = jnp.where(mine, rank.astype(i32), -1)
        chosen = one_hot(iota((count // 2, count), 0) == held)
        digits = two_digits(jnp.where(mine, local + 1, 0))
        found.append(from_digits(mm(digits, chosen, 1, 1)) - 1)
        earlier = jnp.sum(jnp.where(groups[u] < me * points, 1.0, 0.0))
        shift.append(lax.rem(earlier.astype(i32), count))
    writes = start_all([(starts, starts_hbm)], out_sems)
    wait_all(reads[1:])
    current, moving = w[...], z[...]
    goal = t[...].astype(f32).T
    for u in range(UPDATES):
        mixed = mixed_of(current, moving).T
        high, low = split_two(ridge_term * mixed - goal)
        coef[u] = mixed.astype(bf16)
        place = one_hot(iota((points, count // 2), 0) == found[u])
        both = mm(jnp.concatenate([high, low], axis=0), place, 1, 0)
        held = both[:outputs] + both[outputs:]
        held = jnp.concatenate([held, jnp.zeros_like(held)], axis=1)
        offset[u] = pltpu.roll(held, shift[u], 1)
        current, moving = stepped(current, moving, None)
        for a, b in ((coef, coef_hbm), (offset, offset_hbm)):
            writes.append(pltpu.make_async_copy(a.at[u], b.at[u], out_sems.at[len(writes)]))
            writes[-1].start()
    wait_all(writes)


def order_kernel(
    count, points, owners,
    blocks_hbm, ids_hbm, from_hbm, starts_hbm,
    blocks, ids, came_from, starts, sems,
):
    wait_all(start_all([(blocks_hbm, blocks)], sems))
    count_of = blocks.shape[1] // count
    groups = [
        blocks[u : u + 1, g * count : (g + 1) * count]
        for u in range(UPDATES)
        for g in range(count_of)
    ]
    for n, (marks, rank, start) in enumerate(owners_of(groups, points, owners)):
        place = sorted_places(marks, rank, start)
        given = iota((1, count), 1) + (n % count_of) * count
        digits = two_digits(groups[n], given)
        moved = mm(digits, one_hot(iota((count, count), 0) == place), 1, 1)
        ids[n : n + 1, :] = from_digits(moved[0:2])
        came_from[n : n + 1, :] = from_digits(moved[2:4])
        starts[n : n + 1, :] = lane_row(start)
    wait_all(start_all([(ids, ids_hbm), (came_from, from_hbm), (starts, starts_hbm)], sems))


def slots_kernel(count, points, cap, blocks_hbm, slots_hbm, blocks, slots, sems):
    me = lax.axis_index("pts")
    wait_all(start_all([(blocks_hbm, blocks)], sems))
    before = before_matrix(count)
    groups = blocks.shape[1] // count
    for u in range(UPDATES):
        found = jnp.zeros((8, groups * cap), f32)
        for g in range(groups):
            local = blocks[u : u + 1, g * count : (g + 1) * count] - me * points
            mine = (local >= 0) & (local < points)
            counts = jnp.where(mine, 1.0, 0.0)
            rank = mm(jnp.broadcast_to(counts, (8, count)).astype(bf16), before, 1, 0)[0:1]
            held = jnp.where(mine, rank.astype(i32) + g * cap, -1)
            chosen = one_hot(iota((groups * cap, count), 0) == held)
            found += mm(two_digits(jnp.where(mine, local + 1, 0)), chosen, 1, 1)
        slots[u : u + 1, :] = from_digits(found) - 1
    wait_all(start_all([(slots, slots_hbm)], sems))


def column_of(row):
    return jnp.broadcast_to(row.astype(f32), (8, row.shape[1])).T[:, 0:1]


def extended(rows, axis, first):
    rest = -0.5 * jnp.sum(jnp.square(rows.astype(f32)), axis=axis, keepdims=True)
    parts = []
    for _ in range(3):
        parts.append(rest.astype(bf16).astype(f32))
        rest = rest - parts[-1]
    parts = parts + [1.0] * 3 if first else [1.0] * 3 + parts
    at = iota(rows.shape, axis)
    extra = jnp.zeros(rows.shape, f32)
    for n, part in enumerate(parts):
        extra = jnp.where(at == n, part, extra)
    return jnp.concatenate([rows.astype(bf16), extra.astype(bf16)], axis=axis)


def exponent(left, right):
    return mm(left, right, 1, 0) * (7.0 / (left.shape[1] // 2) * math.log2(math.e))


CHUNK = 256


def compact_kernel(*refs):
    *came_hbm, starts_hbm, block_hbm, came, starts, wide, block, sems = refs
    me = lax.axis_index("pts")
    owners, deep, _ = came.shape
    cap = deep // UPDATES
    count = block.shape[2]
    pairs = [(a, came.at[k]) for k, a in enumerate(came_hbm)]
    wait_all(start_all([*pairs, (starts_hbm, starts)], sems))
    for u in range(UPDATES):
        for o in range(owners):
            start = starts[u, o]
            rows = came[lax.bitwise_xor(me, o), u * cap : (u + 1) * cap, :]
            wide[u, pl.ds(start, cap), :] = rows.astype(f32)
        block[u] = wide[u, 0:count, :].T.astype(bf16)
    wait_all(start_all([(block, block_hbm)], sems))


def sums_kernel(
    block_hbm, feats_hbm, coef_hbm, offset_hbm, pieces_hbm,
    block, feats, coef, offset, tile, pieces, sems,
):
    outputs = coef.shape[1]
    pairs = [(block_hbm, block), (feats_hbm, feats), (coef_hbm, coef), (offset_hbm, offset)]
    reads = start_all(pairs, sems)
    wait_all(reads[:2])
    left = extended(feats[...], 1, True)
    for u in range(UPDATES):
        right = extended(block[u], 0, False)
        tile[...] = jnp.exp2(exponent(left, right)).astype(bf16)
        if u == 0:
            wait_all(reads[2:])
        total = offset[u] + mm(coef[u], tile[...], 1, 0)
        devices, _, lanes = pieces.shape
        own = outputs // devices
        for d in range(devices):
            part = total[d * own : (d + 1) * own]
            pieces[d, 2 * own * u : 2 * own * (u + 1), :] = jnp.concatenate(
                [part[:, :lanes], part[:, lanes:]], axis=0
            ).astype(bf16)
    wait_all(start_all([(pieces, pieces_hbm)], sems))


def factors_kernel(
    b0_hbm, b1_hbm, b2_hbm, b3_hbm, ids_hbm, from_hbm, pivots_hbm, factor_hbm, cross_hbm,
    feats, ids, came_from, pivots, factor, cross, sems,
):
    row = lax.axis_index("rows")
    groups, _, width, count = feats.shape
    pairs = [(b_hbm, feats.at[k]) for k, b_hbm in enumerate((b0_hbm, b1_hbm, b2_hbm, b3_hbm))]
    pairs += [(ids_hbm, ids), (from_hbm, came_from), (pivots_hbm, pivots)]
    wait_all(start_all(pairs, sems))
    places = [lax.bitwise_xor(row, k) for k in range(groups)]
    rights = [[extended(feats[k, u], 0, False) for k in range(groups)] for u in range(UPDATES)]
    for u in range(UPDATES):
        wanted = pivots[u : u + 1, :].astype(f32)
        chosen_feats = jnp.zeros((width, wanted.shape[1]), f32)
        for k in range(groups):
            here = column_of(came_from[pl.ds(u * groups + places[k], 1), :])
            chosen_feats += mm(feats[k, u], one_hot(here == wanted), 1, 0)
        left = extended(chosen_feats.T, 1, True)
        for k in range(groups):
            start = pl.multiple_of(places[k] * count, count)
            value = jnp.exp2(exponent(left, rights[u][k]))
            factor[u, :, pl.ds(start, count)] = value.astype(bf16)
    writes = start_all([(factor, factor_hbm)], sems)
    lefts, left_points = [], []
    for k in range(groups):
        lefts.append(extended(feats[k, 0].astype(f32).T, 1, True))
        left_points.append(column_of(ids[pl.ds(places[k], 1), :]))
    left, left_points = jnp.concatenate(lefts, axis=0), jnp.concatenate(left_points, axis=0)
    sent = 1
    for m in range(groups):
        right_points = ids[pl.ds(groups + places[m], 1), :].astype(f32)
        power = exponent(left, rights[1][m])
        power = jnp.where(left_points == right_points, math.log2(1.0 + ridge_term), power)
        cross[m] = jnp.exp2(power).astype(bf16).reshape(groups, count, count)
        for k in range(groups):
            start = pl.multiple_of(places[k] * count, count)
            copy = pltpu.make_async_copy(
                cross.at[m, k], cross_hbm.at[places[m], pl.ds(start, count), :], sems.at[sent]
            )
            copy.start()
            writes.append(copy)
            sent += 1
    wait_all(writes)


def chain_kernel(
    cap, owners,
    summed_hbm, factor_hbm, core_hbm, cross_hbm, starts_hbm, out_hbm,
    summed, factor, core, cross, starts, packed, sems,
):
    groups, _, count = cross.shape
    own = summed.shape[1] // (2 * UPDATES)
    pairs = [(summed_hbm, summed)]
    for u in range(UPDATES):
        pairs += [(factor_hbm.at[u], factor.at[u]), (core_hbm.at[u], core.at[u])]
        if u == 0:
            pairs += [(starts_hbm, starts)]
            pairs += [(cross_hbm.at[g], cross.at[g]) for g in range(groups)]
    reads = start_all(pairs, sems)
    first, *reads = reads
    first.wait()
    step = None
    for u in range(UPDATES):
        sums = []
        for g in range(groups):
            part = summed[g * owners, 2 * own * u : 2 * own * (u + 1), :].astype(f32)
            for o in range(1, owners):
                part += summed[g * owners + o, 2 * own * u : 2 * own * (u + 1), :].astype(f32)
            part = jnp.concatenate([part[:own], part[own:]], axis=1)
            if u:
                reads[3 + g].wait()
                part -= mix_per_step * mm(step, cross[g], 1, 0)
            sums.append(part)
        resid = jnp.concatenate(sums, axis=1)
        wait_all(reads[0:3] if u == 0 else reads[3 + groups :])
        proj = mm(resid.astype(bf16), factor[u], 1, 1)
        lifted = mm(proj.astype(bf16), core[u], 1, 1).astype(bf16)
        step = (resid - mm(lifted, factor[u], 1, 0)).astype(bf16)
        half = groups // 2
        for o in range(owners):
            lanes = []
            for g in range(groups):
                part = step[:, g * count : (g + 1) * count].astype(f32)
                back = lax.rem(count - starts[u * groups + g, o], count)
                lanes.append(pltpu.roll(part, back, 1)[:, :cap])
            packed[o, 2 * own * u : 2 * own * (u + 1), :] = jnp.concatenate(
                [jnp.concatenate(lanes[h * half : (h + 1) * half], axis=1) for h in range(2)], axis=0
            ).astype(bf16)
    wait_all(start_all([(packed, out_hbm)], sems))


def finish_kernel(
    g0_hbm, g1_hbm, g2_hbm, g3_hbm, slots_hbm, w_hbm, z_hbm, w_out, z_out,
    got, slots, w, z, steps, w_new, z_new, sems, out_sems,
):
    row = lax.axis_index("rows")
    points = w.shape[0]
    sources, deep, lanes = got.shape
    own = deep // (2 * UPDATES)
    chunks = range(0, points, CHUNK)
    pairs = [(slots_hbm, slots)]
    for k, g_hbm in enumerate((g0_hbm, g1_hbm, g2_hbm, g3_hbm)):
        size = g_hbm.shape[0]
        first = pl.multiple_of(lax.bitwise_xor(row, k) * size, size)
        pairs.append((g_hbm, got.at[pl.ds(first, size)]))
    for c in chunks:
        part = slice(c, c + CHUNK)
        pairs += [(w_hbm.at[part], w.at[part]), (z_hbm.at[part], z.at[part])]
    reads = start_all(pairs, sems)
    wait_all(reads[:5])
    reads = reads[5:]
    wide = got[...].astype(f32)
    for u in range(UPDATES):
        for h in range(2):
            first = own * (2 * u + h)
            part = wide[:, first : first + own, :].reshape(sources * own, lanes)
            steps[u, h * lanes : (h + 1) * lanes, :] = part.T.astype(bf16)
    changes = []
    for u in range(UPDATES):
        rows = one_hot(iota((points, slots.shape[1]), 0) == slots[u : u + 1, :])
        changes.append(mm(rows, steps[u], 1, 0))
    writes = []
    for n, c in enumerate(chunks):
        part = slice(c, c + CHUNK)
        wait_all(reads[2 * n : 2 * n + 2])
        current, moving = w[part, :], z[part, :]
        for change in changes:
            current, moving = stepped(current, moving, change[part])
        w_new[part, :] = current
        z_new[part, :] = moving
        for m, (a, b) in enumerate(((w_new, w_out), (z_new, z_out))):
            copy = pltpu.make_async_copy(a.at[part], b.at[part], out_sems.at[2 * n + m])
            copy.start()
            writes.append(copy)
    wait_all(writes)


VMEM = pl.BlockSpec(memory_space=pltpu.VMEM)
HBM = pl.BlockSpec(memory_space=pltpu.HBM)
in_smem = type(pltpu.SMEM((1,), i32))


def like(shape, dtype=bf16):
    return jax.ShapeDtypeStruct(shape, dtype)


def call(body, outs, inside, *args, near=0, sems=(), flops=0, grant=63.9):
    moved = sum(math.prod(o.shape) * o.dtype.itemsize for o in [*outs, *args])
    return pl.pallas_call(
        body,
        out_shape=outs,
        in_specs=[VMEM] * near + [HBM] * (len(args) - near),
        out_specs=[HBM] * len(outs),
        scratch_shapes=[
            x if isinstance(x, in_smem) else pltpu.VMEM(x.shape, x.dtype) for x in inside
        ]
        + [pltpu.SemaphoreType.DMA((n,)) for n in sems],
        compiler_params=pltpu.CompilerParams(vmem_limit_bytes=int(grant * 2**20)),
        cost_estimate=pl.CostEstimate(flops=int(flops), bytes_accessed=moved, transcendentals=0),
    )(*args)


def swap(value, axis, k):
    return lax.ppermute(value, axis, [(i, i ^ k) for i in range(lax.axis_size(axis))])


def with_kernels(features, targets, coefficients, momentum, block_index, pivot_index, core):
    rows, owners = lax.axis_size("rows"), lax.axis_size("pts")
    points, width = features.shape
    block = block_index.shape[1]
    rank = pivot_index.shape[1]
    outputs = coefficients.shape[1]
    count = block // rows
    cap = 3 * count // owners
    devices = rows * owners
    own = outputs // devices
    deep = 2 * own * UPDATES
    half = rows // 2
    wide = like(coefficients.shape, f32)

    (packed,) = call(
        functools.partial(pack_kernel, count, cap, owners),
        [like((UPDATES * cap, width))],
        [block_index, features, like((UPDATES * cap, width))],
        block_index,
        features,
        sems=(2,),
    )
    came = {k: swap(packed, "pts", k) for k in reversed(range(2, owners, 2))}
    came[1] = swap(packed, "pts", 1)
    came[3] = swap(came[2], "pts", 1)
    kept = [
        like((UPDATES, outputs, points)),
        like((UPDATES, outputs, count), f32),
        like((8, 128), i32),
    ]
    given = [block_index, coefficients, momentum, targets]
    coef, offset, row_starts = call(
        functools.partial(prepare_kernel, count, owners),
        kept,
        given + kept,
        *given,
        sems=(4, 1 + 2 * UPDATES),
    )
    came[4], came[6], row_starts, later_index = lax.optimization_barrier(
        (came[4], came[6], row_starts, block_index)
    )
    came[5], came[7] = swap(came[4], "pts", 1), swap(came[6], "pts", 1)

    kept = [like((UPDATES * rows, count), i32)] * 2 + [like((8, 128), i32)]
    ids, came_from, starts = call(
        functools.partial(order_kernel, count, points, owners),
        kept,
        [block_index, *kept],
        later_index,
        sems=(3,),
    )
    row_starts, ids = lax.optimization_barrier((row_starts, ids))
    feats = like((UPDATES, width, count))
    inside_starts = pltpu.SMEM(row_starts.shape, i32)
    (mine,) = call(
        compact_kernel,
        [feats],
        [
            like((owners, *packed.shape)),
            inside_starts,
            like((UPDATES, count + cap, width), f32),
            feats,
        ],
        packed,
        *[came[k] for k in range(1, owners)],
        row_starts,
        sems=(owners + 1,),
    )
    beside, across = swap(mine, "rows", 1), swap(mine, "rows", 2)
    pieces = like((devices, deep, count // 2))
    (pieces,) = call(
        sums_kernel,
        [pieces],
        [feats, features, coef, offset, like((points, count)), pieces],
        mine,
        features,
        coef,
        offset,
        sems=(4,),
        flops=2.0 * UPDATES * points * count * (2 * width + outputs),
    )
    pieces, beside, across = lax.optimization_barrier((pieces, beside, across))
    summed = lax.all_to_all(pieces, ("rows", "pts"), 0, 0, tiled=True)
    kept = [like((UPDATES, rank, block)), like((rows, block, count))]
    factor, cross = call(
        factors_kernel,
        kept,
        [
            like((rows, *feats.shape)),
            ids,
            came_from,
            pivot_index,
            kept[0],
            like((rows, rows, count, count)),
        ],
        mine,
        beside,
        across,
        swap(across, "rows", 1),
        ids,
        came_from,
        pivot_index,
        sems=(rows * rows + 2,),
        flops=2.0 * width * block * (UPDATES * rank + block),
    )
    pieces = like((owners, deep, half * cap))
    (steps,) = call(
        functools.partial(chain_kernel, cap, owners),
        [pieces],
        [summed, factor, core, cross, inside_starts, pieces],
        summed,
        factor,
        core,
        cross,
        starts,
        sems=(2 * UPDATES + 3 + rows,),
    )
    steps, later_index = lax.optimization_barrier((steps, block_index))
    (slots,) = call(
        functools.partial(slots_kernel, count, points, cap),
        [like((UPDATES, rows * cap), i32)],
        [block_index, like((UPDATES, rows * cap), i32)],
        later_index,
        sems=(1,),
    )
    got = lax.all_to_all(steps, "pts", 0, 0, tiled=True)
    got, slots = lax.optimization_barrier((got, slots))
    beside, across = swap(got, "rows", 1), swap(got, "rows", 2)
    parts = points // CHUNK
    return call(
        finish_kernel,
        [wide] * 2,
        [
            like((devices, deep, half * cap)),
            slots,
            wide,
            wide,
            like((UPDATES, rows * cap, outputs)),
            wide,
            wide,
        ],
        got,
        beside,
        across,
        swap(across, "rows", 1),
        slots,
        coefficients,
        momentum,
        sems=(1 + rows + 2 * parts, 2 * parts),
    )


def kernel_tile(left_rows, right_rows):
    inner_prod = mm(left_rows, right_rows, 1, 1)
    left_sq = jnp.sum(jnp.square(left_rows.astype(f32)), axis=1)
    right_sq = jnp.sum(jnp.square(right_rows.astype(f32)), axis=1)
    squared = left_sq[:, None] + right_sq[None, :] - 2.0 * inner_prod
    return jnp.exp(squared * (-3.5 / left_rows.shape[1])).astype(bf16)


def with_operations(features, targets, coefficients, momentum, block_index, pivot_index, core):
    row_count, pts_count = lax.axis_size("rows"), lax.axis_size("pts")
    row_id, pts_id = lax.axis_index("rows"), lax.axis_index("pts")
    points = features.shape[0]
    block = block_index.shape[1]
    outputs = coefficients.shape[1]
    per_row = block // row_count
    per_device = per_row // pts_count
    row_cols = outputs // row_count
    own_cols = row_cols // pts_count
    first = row_id * row_cols
    current, moving, goal = (
        lax.dynamic_slice_in_dim(value, first, row_cols, axis=1).T.astype(f32)
        for value in (coefficients, momentum, targets)
    )
    ids = iota((points, 1), 0) + pts_id * points
    place = [(ids == block_index[u][None, :]).astype(bf16) for u in range(UPDATES)]
    own_rows = []
    for u in range(UPDATES):
        mine = lax.dynamic_slice_in_dim(place[u], row_id * per_row, per_row, axis=1)
        own_rows.append(mm(mine, features, 0, 0).astype(bf16).reshape(pts_count, per_device, -1))
    came = lax.all_to_all(jnp.concatenate(own_rows, axis=1), "pts", 0, 0, tiled=False)
    chunk = jnp.sum(came.astype(f32), axis=0).astype(bf16)
    spread = lax.all_gather(lax.all_gather(chunk, "pts", axis=0), "rows", axis=0)
    spread = spread.reshape(row_count, pts_count, UPDATES, per_device, features.shape[1])
    all_steps = []
    for u in range(UPDATES):
        block_feats = spread[:, :, u].reshape(block, features.shape[1])
        mixed = mixed_of(current, moving)
        high, low = split_two(ridge_term * mixed - goal)
        tile = kernel_tile(features, block_feats)
        partial_value = (
            mm(mixed.astype(bf16), tile, 1, 0) + mm(high, place[u], 1, 0) + mm(low, place[u], 1, 0)
        )
        pieces = partial_value.astype(bf16).reshape(pts_count, own_cols, block)
        summed = lax.all_to_all(pieces, "pts", 0, 0, tiled=False)
        resid = jnp.sum(summed.astype(f32), axis=0)
        at_pivot = (iota((block, 1), 0) == pivot_index[u][None, :]).astype(bf16)
        factor = kernel_tile(block_feats, mm(at_pivot, block_feats, 0, 0).astype(bf16))
        proj = mm(resid.astype(bf16), factor, 1, 0)
        lifted = mm(proj.astype(bf16), core[u], 1, 1).astype(bf16)
        step_bf = (resid - mm(lifted, factor, 1, 1)).astype(bf16)
        steps = lax.all_gather(step_bf, "pts", axis=0, tiled=True)
        change = mm(steps, place[u], 1, 1)
        all_steps.append(change.astype(bf16))
        current, moving = stepped(current, moving, change)
    gathered = lax.all_gather(jnp.stack(all_steps), "rows", axis=1, tiled=True)
    current, moving = coefficients, momentum
    for u in range(UPDATES):
        current, moving = stepped(current, moving, gathered[u].T.astype(f32))
    return (current, moving)


def shards(features, targets, coefficients, momentum, block_index, pivot_index, nystrom_core):
    rows, owners = lax.axis_size("rows"), lax.axis_size("pts")
    count = block_index.shape[1] // rows
    fits = rows == 4 and owners == 8 and coefficients.shape[1] == 8 * rows * owners
    fits = fits and 6 * count <= count * owners and coefficients.shape[0] % CHUNK == 0 and count % CHUNK == 0 and (3 * count // owners) % 64 == 0 and UPDATES * rows == 8
    plan = with_kernels if fits else with_operations
    return plan(
        features, targets, coefficients, momentum, block_index, pivot_index, nystrom_core
    )


def solution(mesh):
    in_specs = (P("pts", None), P("pts", None), P("pts", None), P("pts", None), P(), P(), P())
    out_specs = (P("pts", None), P("pts", None))
    return jax.shard_map(shards, mesh=mesh, in_specs=in_specs, out_specs=out_specs, check_vma=False)
```

```python
import functools
import math

import jax
import jax.numpy as jnp
from jax import lax
from jax.experimental import pallas as pl
from jax.experimental.pallas import tpu as pltpu
from jax.sharding import PartitionSpec as P

UPDATES = 2


alpha_mix = 0.6
beta_keep = 0.9
step_size = 0.2
momentum_gain = 1.5
ridge_term = 1.0

f32 = jnp.float32
bf16 = jnp.bfloat16
i32 = jnp.int32


def mm(a, b, ca, cb):
    return lax.dot_general(a, b, (((ca,), (cb,)), ((), ())), preferred_element_type=f32)


def split_two(value):
    high = value.astype(bf16)
    return high, (value - high.astype(f32)).astype(bf16)


def mixed_of(current, moving):
    return alpha_mix * moving + (1.0 - alpha_mix) * current


mix_per_step = alpha_mix * step_size * momentum_gain + (1.0 - alpha_mix) * step_size


def stepped(current, moving, change):
    mixed = mixed_of(current, moving)
    if change is None:
        return mixed, beta_keep * moving + (1.0 - beta_keep) * mixed
    return (
        mixed - step_size * change,
        beta_keep * moving + (1.0 - beta_keep) * mixed - step_size * momentum_gain * change,
    )


def iota(shape, axis):
    return lax.broadcasted_iota(i32, shape, axis)


def one_hot(chosen):
    return jnp.where(chosen, 1.0, 0.0).astype(bf16)


def before_matrix(n):
    return one_hot(iota((n, n), 0) < iota((n, n), 1))


def owners_of(groups, points, owners):
    owner_ids = iota((owners, groups[0].shape[1]), 0)
    owner = [lax.div(x, jnp.full_like(x, points)) for x in groups]
    marks = [jnp.where(owner_ids == x, 1.0, 0.0) for x in owner]
    every = jnp.concatenate(marks, axis=0).astype(bf16)
    earlier = mm(every, before_matrix(every.shape[1]), 1, 0)
    out = []
    for n, x in enumerate(owner):
        rank = jnp.sum(marks[n] * earlier[n * owners : (n + 1) * owners], axis=0, keepdims=True)
        start = jnp.sum(jnp.where(x < owner_ids, 1.0, 0.0), axis=1, keepdims=True)
        out.append((marks[n], rank, start))
    return out


def sorted_places(marks, rank, start):
    return (rank + jnp.sum(marks * start, axis=0, keepdims=True)).astype(i32)


def lane_row(column):
    n = column.shape[0]
    diagonal = iota((n, 128), 0) == iota((n, 128), 1)
    return jnp.sum(jnp.where(diagonal, column, 0.0), axis=0, keepdims=True).astype(i32)


def two_digits(*rows):
    shape = (8, rows[0].shape[1])
    value = jnp.zeros(shape, i32)
    for n, row in enumerate(rows):
        high = lax.shift_right_logical(row, jnp.full_like(row, 7))
        low = lax.bitwise_and(row, jnp.full_like(row, 127))
        value = jnp.where(iota(shape, 0) == 2 * n, high, value)
        value = jnp.where(iota(shape, 0) == 2 * n + 1, low, value)
    return value.astype(f32).astype(bf16)


def from_digits(digits):
    return (digits[0:1] * 128.0 + digits[1:2]).astype(i32)


def start_all(pairs, sems):
    copies = [pltpu.make_async_copy(a, b, sems.at[n]) for n, (a, b) in enumerate(pairs)]
    for copy in copies:
        copy.start()
    return copies


def wait_all(copies):
    for copy in copies:
        copy.wait()


def group_row(blocks, u, group, count):
    return blocks[u : u + 1, pl.ds(pl.multiple_of(group * count, count), count)]


def pack_kernel(count, cap, owners, blocks_hbm, feats_hbm, out_hbm, blocks, feats, packed, sems):
    row, me = lax.axis_index("rows"), lax.axis_index("pts")
    points = feats.shape[0]
    reads = start_all([(blocks_hbm, blocks), (feats_hbm, feats)], sems)
    before = before_matrix(count)
    reads[0].wait()
    rows = []
    for u in range(UPDATES):
        indices = group_row(blocks, u, row, count)
        local = indices - me * points
        mine = jnp.where((local >= 0) & (local < points), 1.0, 0.0)
        rank = mm(jnp.broadcast_to(mine, (8, count)).astype(bf16), before, 1, 0)[0:1]
        held = (iota((cap, count), 0) == rank.astype(i32)) & (mine > 0.0)
        point = jnp.sum(jnp.where(held, (local + 1).astype(f32), 0.0), axis=1, keepdims=True)
        rows.append(one_hot(iota((cap, points), 1) == point.astype(i32) - 1))
    reads[1].wait()
    for u in range(UPDATES):
        packed[u * cap : (u + 1) * cap, :] = mm(rows[u], feats[...], 1, 0).astype(bf16)
    wait_all(start_all([(packed, out_hbm)], sems))


def prepare_kernel(
    count, owners,
    blocks_hbm, w_hbm, z_hbm, t_hbm, coef_hbm, offset_hbm, starts_hbm,
    blocks, w, z, t, coef, offset, starts, sems, out_sems,
):
    row, me = lax.axis_index("rows"), lax.axis_index("pts")
    points, outputs = w.shape
    reads = start_all([(blocks_hbm, blocks), (w_hbm, w), (z_hbm, z), (t_hbm, t)], sems)
    reads[0].wait()
    groups = [group_row(blocks, u, row, count) for u in range(UPDATES)]
    found, shift = [], []
    for u, (_, rank, start) in enumerate(owners_of(groups, points, owners)):
        starts[u : u + 1, :] = lane_row(start)
        local = groups[u] - me * points
        mine = (local >= 0) & (local < points)
        held = jnp.where(mine, rank.astype(i32), -1)
        chosen = one_hot(iota((count // 2, count), 0) == held)
        digits = two_digits(jnp.where(mine, local + 1, 0))
        found.append(from_digits(mm(digits, chosen, 1, 1)) - 1)
        earlier = jnp.sum(jnp.where(groups[u] < me * points, 1.0, 0.0))
        shift.append(lax.rem(earlier.astype(i32), count))
    writes = start_all([(starts, starts_hbm)], out_sems)
    wait_all(reads[1:])
    current, moving = w[...], z[...]
    goal = t[...].astype(f32).T
    for u in range(UPDATES):
        mixed = mixed_of(current, moving).T
        high, low = split_two(ridge_term * mixed - goal)
        coef[u] = mixed.astype(bf16)
        place = one_hot(iota((points, count // 2), 0) == found[u])
        both = mm(jnp.concatenate([high, low], axis=0), place, 1, 0)
        held = both[:outputs] + both[outputs:]
        held = jnp.concatenate([held, jnp.zeros_like(held)], axis=1)
        offset[u] = pltpu.roll(held, shift[u], 1)
        current, moving = stepped(current, moving, None)
        for a, b in ((coef, coef_hbm), (offset, offset_hbm)):
            writes.append(pltpu.make_async_copy(a.at[u], b.at[u], out_sems.at[len(writes)]))
            writes[-1].start()
    wait_all(writes)


def order_kernel(
    count, points, owners,
    blocks_hbm, ids_hbm, from_hbm, starts_hbm,
    blocks, ids, came_from, starts, sems,
):
    wait_all(start_all([(blocks_hbm, blocks)], sems))
    count_of = blocks.shape[1] // count
    groups = [
        blocks[u : u + 1, g * count : (g + 1) * count]
        for u in range(UPDATES)
        for g in range(count_of)
    ]
    for n, (marks, rank, start) in enumerate(owners_of(groups, points, owners)):
        place = sorted_places(marks, rank, start)
        given = iota((1, count), 1) + (n % count_of) * count
        digits = two_digits(groups[n], given)
        moved = mm(digits, one_hot(iota((count, count), 0) == place), 1, 1)
        ids[n : n + 1, :] = from_digits(moved[0:2])
        came_from[n : n + 1, :] = from_digits(moved[2:4])
        starts[n : n + 1, :] = lane_row(start)
    wait_all(start_all([(ids, ids_hbm), (came_from, from_hbm), (starts, starts_hbm)], sems))


def slots_kernel(count, points, cap, blocks_hbm, slots_hbm, blocks, slots, sems):
    me = lax.axis_index("pts")
    wait_all(start_all([(blocks_hbm, blocks)], sems))
    before = before_matrix(count)
    groups = blocks.shape[1] // count
    for u in range(UPDATES):
        found = jnp.zeros((8, groups * cap), f32)
        for g in range(groups):
            local = blocks[u : u + 1, g * count : (g + 1) * count] - me * points
            mine = (local >= 0) & (local < points)
            counts = jnp.where(mine, 1.0, 0.0)
            rank = mm(jnp.broadcast_to(counts, (8, count)).astype(bf16), before, 1, 0)[0:1]
            held = jnp.where(mine, rank.astype(i32) + g * cap, -1)
            chosen = one_hot(iota((groups * cap, count), 0) == held)
            found += mm(two_digits(jnp.where(mine, local + 1, 0)), chosen, 1, 1)
        slots[u : u + 1, :] = from_digits(found) - 1
    wait_all(start_all([(slots, slots_hbm)], sems))


def column_of(row):
    return jnp.broadcast_to(row.astype(f32), (8, row.shape[1])).T[:, 0:1]


def extended(rows, axis, first):
    rest = -0.5 * jnp.sum(jnp.square(rows.astype(f32)), axis=axis, keepdims=True)
    parts = []
    for _ in range(3):
        parts.append(rest.astype(bf16).astype(f32))
        rest = rest - parts[-1]
    parts = parts + [1.0] * 3 if first else [1.0] * 3 + parts
    at = iota(rows.shape, axis)
    extra = jnp.zeros(rows.shape, f32)
    for n, part in enumerate(parts):
        extra = jnp.where(at == n, part, extra)
    return jnp.concatenate([rows.astype(bf16), extra.astype(bf16)], axis=axis)


def exponent(left, right):
    return mm(left, right, 1, 0) * (7.0 / (left.shape[1] // 2) * math.log2(math.e))


CHUNK = 256


def compact_kernel(*refs):
    *came_hbm, starts_hbm, block_hbm, came, starts, wide, block, sems = refs
    me = lax.axis_index("pts")
    owners, deep, _ = came.shape
    cap = deep // UPDATES
    count = block.shape[2]
    pairs = [(a, came.at[k]) for k, a in enumerate(came_hbm)]
    wait_all(start_all([*pairs, (starts_hbm, starts)], sems))
    for u in range(UPDATES):
        for o in range(owners):
            start = starts[u, o]
            rows = came[lax.bitwise_xor(me, o), u * cap : (u + 1) * cap, :]
            wide[u, pl.ds(start, cap), :] = rows.astype(f32)
        block[u] = wide[u, 0:count, :].T.astype(bf16)
    wait_all(start_all([(block, block_hbm)], sems))


def sums_kernel(
    block_hbm, feats_hbm, coef_hbm, offset_hbm, pieces_hbm,
    block, feats, coef, offset, tile, pieces, sems,
):
    outputs = coef.shape[1]
    pairs = [(block_hbm, block), (feats_hbm, feats), (coef_hbm, coef), (offset_hbm, offset)]
    reads = start_all(pairs, sems)
    wait_all(reads[:2])
    left = extended(feats[...], 1, True)
    for u in range(UPDATES):
        right = extended(block[u], 0, False)
        tile[...] = jnp.exp2(exponent(left, right)).astype(bf16)
        if u == 0:
            wait_all(reads[2:])
        total = offset[u] + mm(coef[u], tile[...], 1, 0)
        devices, _, lanes = pieces.shape
        own = outputs // devices
        for d in range(devices):
            part = total[d * own : (d + 1) * own]
            pieces[d, 2 * own * u : 2 * own * (u + 1), :] = jnp.concatenate(
                [part[:, :lanes], part[:, lanes:]], axis=0
            ).astype(bf16)
    wait_all(start_all([(pieces, pieces_hbm)], sems))


def factors_kernel(
    b0_hbm, b1_hbm, b2_hbm, b3_hbm, ids_hbm, from_hbm, pivots_hbm, factor_hbm, cross_hbm,
    feats, ids, came_from, pivots, factor, cross, sems,
):
    row = lax.axis_index("rows")
    groups, _, width, count = feats.shape
    pairs = [(b_hbm, feats.at[k]) for k, b_hbm in enumerate((b0_hbm, b1_hbm, b2_hbm, b3_hbm))]
    pairs += [(ids_hbm, ids), (from_hbm, came_from), (pivots_hbm, pivots)]
    wait_all(start_all(pairs, sems))
    places = [lax.bitwise_xor(row, k) for k in range(groups)]
    rights = [[extended(feats[k, u], 0, False) for k in range(groups)] for u in range(UPDATES)]
    for u in range(UPDATES):
        wanted = pivots[u : u + 1, :].astype(f32)
        chosen_feats = jnp.zeros((width, wanted.shape[1]), f32)
        for k in range(groups):
            here = column_of(came_from[pl.ds(u * groups + places[k], 1), :])
            chosen_feats += mm(feats[k, u], one_hot(here == wanted), 1, 0)
        left = extended(chosen_feats.T, 1, True)
        for k in range(groups):
            start = pl.multiple_of(places[k] * count, count)
            value = jnp.exp2(exponent(left, rights[u][k]))
            factor[u, :, pl.ds(start, count)] = value.astype(bf16)
    writes = start_all([(factor, factor_hbm)], sems)
    lefts, left_points = [], []
    for k in range(groups):
        lefts.append(extended(feats[k, 0].astype(f32).T, 1, True))
        left_points.append(column_of(ids[pl.ds(places[k], 1), :]))
    left, left_points = jnp.concatenate(lefts, axis=0), jnp.concatenate(left_points, axis=0)
    sent = 1
    for m in range(groups):
        right_points = ids[pl.ds(groups + places[m], 1), :].astype(f32)
        power = exponent(left, rights[1][m])
        power = jnp.where(left_points == right_points, math.log2(1.0 + ridge_term), power)
        cross[m] = jnp.exp2(power).astype(bf16).reshape(groups, count, count)
        for k in range(groups):
            start = pl.multiple_of(places[k] * count, count)
            copy = pltpu.make_async_copy(
                cross.at[m, k], cross_hbm.at[places[m], pl.ds(start, count), :], sems.at[sent]
            )
            copy.start()
            writes.append(copy)
            sent += 1
    wait_all(writes)


def chain_kernel(
    cap, owners,
    summed_hbm, factor_hbm, core_hbm, cross_hbm, starts_hbm, out_hbm,
    summed, factor, core, cross, starts, packed, sems,
):
    groups, _, count = cross.shape
    own = summed.shape[1] // (2 * UPDATES)
    pairs = [(summed_hbm, summed)]
    for u in range(UPDATES):
        pairs += [(factor_hbm.at[u], factor.at[u]), (core_hbm.at[u], core.at[u])]
        if u == 0:
            pairs += [(starts_hbm, starts)]
            pairs += [(cross_hbm.at[g], cross.at[g]) for g in range(groups)]
    reads = start_all(pairs, sems)
    first, *reads = reads
    first.wait()
    step = None
    for u in range(UPDATES):
        sums = []
        for g in range(groups):
            part = summed[g * owners, 2 * own * u : 2 * own * (u + 1), :].astype(f32)
            for o in range(1, owners):
                part += summed[g * owners + o, 2 * own * u : 2 * own * (u + 1), :].astype(f32)
            part = jnp.concatenate([part[:own], part[own:]], axis=1)
            if u:
                reads[3 + g].wait()
                part -= mix_per_step * mm(step, cross[g], 1, 0)
            sums.append(part)
        resid = jnp.concatenate(sums, axis=1)
        wait_all(reads[0:3] if u == 0 else reads[3 + groups :])
        proj = mm(resid.astype(bf16), factor[u], 1, 1)
        lifted = mm(proj.astype(bf16), core[u], 1, 1).astype(bf16)
        step = (resid - mm(lifted, factor[u], 1, 0)).astype(bf16)
        half = groups // 2
        for o in range(owners):
            lanes = []
            for g in range(groups):
                part = step[:, g * count : (g + 1) * count].astype(f32)
                back = lax.rem(count - starts[u * groups + g, o], count)
                lanes.append(pltpu.roll(part, back, 1)[:, :cap])
            packed[o, 2 * own * u : 2 * own * (u + 1), :] = jnp.concatenate(
                [jnp.concatenate(lanes[h * half : (h + 1) * half], axis=1) for h in range(2)], axis=0
            ).astype(bf16)
    wait_all(start_all([(packed, out_hbm)], sems))


def finish_kernel(
    g0_hbm, g1_hbm, g2_hbm, g3_hbm, slots_hbm, w_hbm, z_hbm, w_out, z_out,
    got, slots, w, z, steps, w_new, z_new, sems, out_sems,
):
    row = lax.axis_index("rows")
    points = w.shape[0]
    sources, deep, lanes = got.shape
    own = deep // (2 * UPDATES)
    chunks = range(0, points, CHUNK)
    pairs = [(slots_hbm, slots)]
    for k, g_hbm in enumerate((g0_hbm, g1_hbm, g2_hbm, g3_hbm)):
        size = g_hbm.shape[0]
        first = pl.multiple_of(lax.bitwise_xor(row, k) * size, size)
        pairs.append((g_hbm, got.at[pl.ds(first, size)]))
    for c in chunks:
        part = slice(c, c + CHUNK)
        pairs += [(w_hbm.at[part], w.at[part]), (z_hbm.at[part], z.at[part])]
    reads = start_all(pairs, sems)
    wait_all(reads[:5])
    reads = reads[5:]
    wide = got[...].astype(f32)
    for u in range(UPDATES):
        for h in range(2):
            first = own * (2 * u + h)
            part = wide[:, first : first + own, :].reshape(sources * own, lanes)
            steps[u, h * lanes : (h + 1) * lanes, :] = part.T.astype(bf16)
    changes = []
    for u in range(UPDATES):
        rows = one_hot(iota((points, slots.shape[1]), 0) == slots[u : u + 1, :])
        changes.append(mm(rows, steps[u], 1, 0))
    writes = []
    for n, c in enumerate(chunks):
        part = slice(c, c + CHUNK)
        wait_all(reads[2 * n : 2 * n + 2])
        current, moving = w[part, :], z[part, :]
        for change in changes:
            current, moving = stepped(current, moving, change[part])
        w_new[part, :] = current
        z_new[part, :] = moving
        for m, (a, b) in enumerate(((w_new, w_out), (z_new, z_out))):
            copy = pltpu.make_async_copy(a.at[part], b.at[part], out_sems.at[2 * n + m])
            copy.start()
            writes.append(copy)
    wait_all(writes)


VMEM = pl.BlockSpec(memory_space=pltpu.VMEM)
HBM = pl.BlockSpec(memory_space=pltpu.HBM)
in_smem = type(pltpu.SMEM((1,), i32))


def like(shape, dtype=bf16):
    return jax.ShapeDtypeStruct(shape, dtype)


def call(body, outs, inside, *args, near=0, sems=(), flops=0, grant=63.9):
    moved = sum(math.prod(o.shape) * o.dtype.itemsize for o in [*outs, *args])
    return pl.pallas_call(
        body,
        out_shape=outs,
        in_specs=[VMEM] * near + [HBM] * (len(args) - near),
        out_specs=[HBM] * len(outs),
        scratch_shapes=[
            x if isinstance(x, in_smem) else pltpu.VMEM(x.shape, x.dtype) for x in inside
        ]
        + [pltpu.SemaphoreType.DMA((n,)) for n in sems],
        compiler_params=pltpu.CompilerParams(vmem_limit_bytes=int(grant * 2**20)),
        cost_estimate=pl.CostEstimate(flops=int(flops), bytes_accessed=moved, transcendentals=0),
    )(*args)


def swap(value, axis, k):
    return lax.ppermute(value, axis, [(i, i ^ k) for i in range(lax.axis_size(axis))])


def with_kernels(features, targets, coefficients, momentum, block_index, pivot_index, core):
    rows, owners = lax.axis_size("rows"), lax.axis_size("pts")
    points, width = features.shape
    block = block_index.shape[1]
    rank = pivot_index.shape[1]
    outputs = coefficients.shape[1]
    count = block // rows
    cap = 3 * count // owners
    devices = rows * owners
    own = outputs // devices
    deep = 2 * own * UPDATES
    half = rows // 2
    wide = like(coefficients.shape, f32)

    (packed,) = call(
        functools.partial(pack_kernel, count, cap, owners),
        [like((UPDATES * cap, width))],
        [block_index, features, like((UPDATES * cap, width))],
        block_index,
        features,
        sems=(2,),
    )
    came = {k: swap(packed, "pts", k) for k in (6, 5, 4, 2, 1)}
    kept = [
        like((UPDATES, outputs, points)),
        like((UPDATES, outputs, count), f32),
        like((8, 128), i32),
    ]
    given = [block_index, coefficients, momentum, targets]
    coef, offset, row_starts = call(
        functools.partial(prepare_kernel, count, owners),
        kept,
        given + kept,
        *given,
        sems=(4, 1 + 2 * UPDATES),
    )
    came[2], came[6], row_starts = lax.optimization_barrier((came[2], came[6], row_starts))
    came[3], came[7] = swap(came[2], "pts", 1), swap(came[6], "pts", 1)
    feats = like((UPDATES, width, count))
    inside_starts = pltpu.SMEM(row_starts.shape, i32)
    (mine,) = call(
        compact_kernel,
        [feats],
        [
            like((owners, *packed.shape)),
            inside_starts,
            like((UPDATES, count + cap, width), f32),
            feats,
        ],
        packed,
        *[came[k] for k in range(1, owners)],
        row_starts,
        sems=(owners + 1,),
    )
    beside, across = swap(mine, "rows", 1), swap(mine, "rows", 2)
    pieces = like((devices, deep, count // 2))
    (pieces,) = call(
        sums_kernel,
        [pieces],
        [feats, features, coef, offset, like((points, count)), pieces],
        mine,
        features,
        coef,
        offset,
        sems=(4,),
        flops=2.0 * UPDATES * points * count * (2 * width + outputs),
    )
    pieces, later_index = lax.optimization_barrier((pieces, block_index))
    kept = [like((UPDATES * rows, count), i32)] * 2 + [like((8, 128), i32)]
    ids, came_from, starts = call(
        functools.partial(order_kernel, count, points, owners),
        kept,
        [block_index, *kept],
        later_index,
        sems=(3,),
    )
    pieces, beside, across, ids = lax.optimization_barrier((pieces, beside, across, ids))
    summed = lax.all_to_all(pieces, ("rows", "pts"), 0, 0, tiled=True)
    kept = [like((UPDATES, rank, block)), like((rows, block, count))]
    factor, cross = call(
        factors_kernel,
        kept,
        [
            like((rows, *feats.shape)),
            ids,
            came_from,
            pivot_index,
            kept[0],
            like((rows, rows, count, count)),
        ],
        mine,
        beside,
        across,
        swap(across, "rows", 1),
        ids,
        came_from,
        pivot_index,
        sems=(rows * rows + 2,),
        flops=2.0 * width * block * (UPDATES * rank + block),
    )
    pieces = like((owners, deep, half * cap))
    (steps,) = call(
        functools.partial(chain_kernel, cap, owners),
        [pieces],
        [summed, factor, core, cross, inside_starts, pieces],
        summed,
        factor,
        core,
        cross,
        starts,
        sems=(2 * UPDATES + 3 + rows,),
    )
    got = lax.all_to_all(steps, "pts", 0, 0, tiled=True)
    got, later_index = lax.optimization_barrier((got, block_index))
    beside, across = swap(got, "rows", 1), swap(got, "rows", 2)
    (slots,) = call(
        functools.partial(slots_kernel, count, points, cap),
        [like((UPDATES, rows * cap), i32)],
        [block_index, like((UPDATES, rows * cap), i32)],
        later_index,
        sems=(1,),
    )
    across, slots = lax.optimization_barrier((across, slots))
    parts = points // CHUNK
    return call(
        finish_kernel,
        [wide] * 2,
        [
            like((devices, deep, half * cap)),
            slots,
            wide,
            wide,
            like((UPDATES, rows * cap, outputs)),
            wide,
            wide,
        ],
        got,
        beside,
        across,
        swap(across, "rows", 1),
        slots,
        coefficients,
        momentum,
        sems=(1 + rows + 2 * parts, 2 * parts),
    )


def kernel_tile(left_rows, right_rows):
    inner_prod = mm(left_rows, right_rows, 1, 1)
    left_sq = jnp.sum(jnp.square(left_rows.astype(f32)), axis=1)
    right_sq = jnp.sum(jnp.square(right_rows.astype(f32)), axis=1)
    squared = left_sq[:, None] + right_sq[None, :] - 2.0 * inner_prod
    return jnp.exp(squared * (-3.5 / left_rows.shape[1])).astype(bf16)


def with_operations(features, targets, coefficients, momentum, block_index, pivot_index, core):
    row_count, pts_count = lax.axis_size("rows"), lax.axis_size("pts")
    row_id, pts_id = lax.axis_index("rows"), lax.axis_index("pts")
    points = features.shape[0]
    block = block_index.shape[1]
    outputs = coefficients.shape[1]
    per_row = block // row_count
    per_device = per_row // pts_count
    row_cols = outputs // row_count
    own_cols = row_cols // pts_count
    first = row_id * row_cols
    current, moving, goal = (
        lax.dynamic_slice_in_dim(value, first, row_cols, axis=1).T.astype(f32)
        for value in (coefficients, momentum, targets)
    )
    ids = iota((points, 1), 0) + pts_id * points
    place = [(ids == block_index[u][None, :]).astype(bf16) for u in range(UPDATES)]
    own_rows = []
    for u in range(UPDATES):
        mine = lax.dynamic_slice_in_dim(place[u], row_id * per_row, per_row, axis=1)
        own_rows.append(mm(mine, features, 0, 0).astype(bf16).reshape(pts_count, per_device, -1))
    came = lax.all_to_all(jnp.concatenate(own_rows, axis=1), "pts", 0, 0, tiled=False)
    chunk = jnp.sum(came.astype(f32), axis=0).astype(bf16)
    spread = lax.all_gather(lax.all_gather(chunk, "pts", axis=0), "rows", axis=0)
    spread = spread.reshape(row_count, pts_count, UPDATES, per_device, features.shape[1])
    all_steps = []
    for u in range(UPDATES):
        block_feats = spread[:, :, u].reshape(block, features.shape[1])
        mixed = mixed_of(current, moving)
        high, low = split_two(ridge_term * mixed - goal)
        tile = kernel_tile(features, block_feats)
        partial_value = (
            mm(mixed.astype(bf16), tile, 1, 0) + mm(high, place[u], 1, 0) + mm(low, place[u], 1, 0)
        )
        pieces = partial_value.astype(bf16).reshape(pts_count, own_cols, block)
        summed = lax.all_to_all(pieces, "pts", 0, 0, tiled=False)
        resid = jnp.sum(summed.astype(f32), axis=0)
        at_pivot = (iota((block, 1), 0) == pivot_index[u][None, :]).astype(bf16)
        factor = kernel_tile(block_feats, mm(at_pivot, block_feats, 0, 0).astype(bf16))
        proj = mm(resid.astype(bf16), factor, 1, 0)
        lifted = mm(proj.astype(bf16), core[u], 1, 1).astype(bf16)
        step_bf = (resid - mm(lifted, factor, 1, 1)).astype(bf16)
        steps = lax.all_gather(step_bf, "pts", axis=0, tiled=True)
        change = mm(steps, place[u], 1, 1)
        all_steps.append(change.astype(bf16))
        current, moving = stepped(current, moving, change)
    gathered = lax.all_gather(jnp.stack(all_steps), "rows", axis=1, tiled=True)
    current, moving = coefficients, momentum
    for u in range(UPDATES):
        current, moving = stepped(current, moving, gathered[u].T.astype(f32))
    return (current, moving)


def shards(features, targets, coefficients, momentum, block_index, pivot_index, nystrom_core):
    rows, owners = lax.axis_size("rows"), lax.axis_size("pts")
    count = block_index.shape[1] // rows
    fits = rows == 4 and owners == 8 and coefficients.shape[1] == 8 * rows * owners
    fits = fits and 6 * count <= count * owners and coefficients.shape[0] % CHUNK == 0 and count % CHUNK == 0 and (3 * count // owners) % 64 == 0 and UPDATES * rows == 8
    plan = with_kernels if fits else with_operations
    return plan(
        features, targets, coefficients, momentum, block_index, pivot_index, nystrom_core
    )


def solution(mesh):
    in_specs = (P("pts", None), P("pts", None), P("pts", None), P("pts", None), P(), P(), P())
    out_specs = (P("pts", None), P("pts", None))
    return jax.shard_map(shards, mesh=mesh, in_specs=in_specs, out_specs=out_specs, check_vma=False)
```

```python
import functools
import math

import jax
import jax.numpy as jnp
from jax import lax
from jax.experimental import pallas as pl
from jax.experimental.pallas import tpu as pltpu
from jax.sharding import PartitionSpec as P

UPDATES = 2


alpha_mix = 0.6
beta_keep = 0.9
step_size = 0.2
momentum_gain = 1.5
ridge_term = 1.0

f32 = jnp.float32
bf16 = jnp.bfloat16
i32 = jnp.int32


def mm(a, b, ca, cb):
    return lax.dot_general(a, b, (((ca,), (cb,)), ((), ())), preferred_element_type=f32)


def split_two(value):
    high = value.astype(bf16)
    return high, (value - high.astype(f32)).astype(bf16)


def mixed_of(current, moving):
    return alpha_mix * moving + (1.0 - alpha_mix) * current


mix_per_step = alpha_mix * step_size * momentum_gain + (1.0 - alpha_mix) * step_size


def stepped(current, moving, change):
    mixed = mixed_of(current, moving)
    if change is None:
        return mixed, beta_keep * moving + (1.0 - beta_keep) * mixed
    return (
        mixed - step_size * change,
        beta_keep * moving + (1.0 - beta_keep) * mixed - step_size * momentum_gain * change,
    )


def iota(shape, axis):
    return lax.broadcasted_iota(i32, shape, axis)


def one_hot(chosen):
    return jnp.where(chosen, 1.0, 0.0).astype(bf16)


def before_matrix(n):
    return one_hot(iota((n, n), 0) < iota((n, n), 1))


def owners_of(groups, points, owners):
    owner_ids = iota((owners, groups[0].shape[1]), 0)
    owner = [lax.div(x, jnp.full_like(x, points)) for x in groups]
    marks = [jnp.where(owner_ids == x, 1.0, 0.0) for x in owner]
    every = jnp.concatenate(marks, axis=0).astype(bf16)
    earlier = mm(every, before_matrix(every.shape[1]), 1, 0)
    out = []
    for n, x in enumerate(owner):
        rank = jnp.sum(marks[n] * earlier[n * owners : (n + 1) * owners], axis=0, keepdims=True)
        start = jnp.sum(jnp.where(x < owner_ids, 1.0, 0.0), axis=1, keepdims=True)
        out.append((marks[n], rank, start))
    return out


def sorted_places(marks, rank, start):
    return (rank + jnp.sum(marks * start, axis=0, keepdims=True)).astype(i32)


def lane_row(column):
    n = column.shape[0]
    diagonal = iota((n, 128), 0) == iota((n, 128), 1)
    return jnp.sum(jnp.where(diagonal, column, 0.0), axis=0, keepdims=True).astype(i32)


def two_digits(*rows):
    shape = (8, rows[0].shape[1])
    value = jnp.zeros(shape, i32)
    for n, row in enumerate(rows):
        high = lax.shift_right_logical(row, jnp.full_like(row, 7))
        low = lax.bitwise_and(row, jnp.full_like(row, 127))
        value = jnp.where(iota(shape, 0) == 2 * n, high, value)
        value = jnp.where(iota(shape, 0) == 2 * n + 1, low, value)
    return value.astype(f32).astype(bf16)


def from_digits(digits):
    return (digits[0:1] * 128.0 + digits[1:2]).astype(i32)


def start_all(pairs, sems):
    copies = [pltpu.make_async_copy(a, b, sems.at[n]) for n, (a, b) in enumerate(pairs)]
    for copy in copies:
        copy.start()
    return copies


def wait_all(copies):
    for copy in copies:
        copy.wait()


def group_row(blocks, u, group, count):
    return blocks[u : u + 1, pl.ds(pl.multiple_of(group * count, count), count)]


def pack_kernel(count, cap, owners, blocks_hbm, feats_hbm, out_hbm, blocks, feats, packed, sems):
    row, me = lax.axis_index("rows"), lax.axis_index("pts")
    points = feats.shape[0]
    reads = start_all([(blocks_hbm, blocks), (feats_hbm, feats)], sems)
    before = before_matrix(count)
    reads[0].wait()
    rows = []
    for u in range(UPDATES):
        indices = group_row(blocks, u, row, count)
        local = indices - me * points
        mine = jnp.where((local >= 0) & (local < points), 1.0, 0.0)
        rank = mm(jnp.broadcast_to(mine, (8, count)).astype(bf16), before, 1, 0)[0:1]
        held = (iota((cap, count), 0) == rank.astype(i32)) & (mine > 0.0)
        point = jnp.sum(jnp.where(held, (local + 1).astype(f32), 0.0), axis=1, keepdims=True)
        rows.append(one_hot(iota((cap, points), 1) == point.astype(i32) - 1))
    reads[1].wait()
    for u in range(UPDATES):
        packed[u * cap : (u + 1) * cap, :] = mm(rows[u], feats[...], 1, 0).astype(bf16)
    wait_all(start_all([(packed, out_hbm)], sems))


def prepare_kernel(
    count, owners,
    blocks_hbm, w_hbm, z_hbm, t_hbm, coef_hbm, offset_hbm, starts_hbm,
    blocks, w, z, t, coef, offset, starts, sems, out_sems,
):
    row, me = lax.axis_index("rows"), lax.axis_index("pts")
    points, outputs = w.shape
    reads = start_all([(blocks_hbm, blocks), (w_hbm, w), (z_hbm, z), (t_hbm, t)], sems)
    reads[0].wait()
    groups = [group_row(blocks, u, row, count) for u in range(UPDATES)]
    found, shift = [], []
    for u, (_, rank, start) in enumerate(owners_of(groups, points, owners)):
        starts[u : u + 1, :] = lane_row(start)
        local = groups[u] - me * points
        mine = (local >= 0) & (local < points)
        held = jnp.where(mine, rank.astype(i32), -1)
        chosen = one_hot(iota((count // 2, count), 0) == held)
        digits = two_digits(jnp.where(mine, local + 1, 0))
        found.append(from_digits(mm(digits, chosen, 1, 1)) - 1)
        earlier = jnp.sum(jnp.where(groups[u] < me * points, 1.0, 0.0))
        shift.append(lax.rem(earlier.astype(i32), count))
    writes = start_all([(starts, starts_hbm)], out_sems)
    wait_all(reads[1:])
    current, moving = w[...], z[...]
    goal = t[...].astype(f32).T
    for u in range(UPDATES):
        mixed = mixed_of(current, moving).T
        high, low = split_two(ridge_term * mixed - goal)
        coef[u] = mixed.astype(bf16)
        place = one_hot(iota((points, count // 2), 0) == found[u])
        both = mm(jnp.concatenate([high, low], axis=0), place, 1, 0)
        held = both[:outputs] + both[outputs:]
        held = jnp.concatenate([held, jnp.zeros_like(held)], axis=1)
        offset[u] = pltpu.roll(held, shift[u], 1)
        current, moving = stepped(current, moving, None)
        for a, b in ((coef, coef_hbm), (offset, offset_hbm)):
            writes.append(pltpu.make_async_copy(a.at[u], b.at[u], out_sems.at[len(writes)]))
            writes[-1].start()
    wait_all(writes)


def order_kernel(
    count, points, owners,
    blocks_hbm, ids_hbm, from_hbm, starts_hbm,
    blocks, ids, came_from, starts, sems,
):
    wait_all(start_all([(blocks_hbm, blocks)], sems))
    count_of = blocks.shape[1] // count
    groups = [
        blocks[u : u + 1, g * count : (g + 1) * count]
        for u in range(UPDATES)
        for g in range(count_of)
    ]
    for n, (marks, rank, start) in enumerate(owners_of(groups, points, owners)):
        place = sorted_places(marks, rank, start)
        given = iota((1, count), 1) + (n % count_of) * count
        digits = two_digits(groups[n], given)
        moved = mm(digits, one_hot(iota((count, count), 0) == place), 1, 1)
        ids[n : n + 1, :] = from_digits(moved[0:2])
        came_from[n : n + 1, :] = from_digits(moved[2:4])
        starts[n : n + 1, :] = lane_row(start)
    wait_all(start_all([(ids, ids_hbm), (came_from, from_hbm), (starts, starts_hbm)], sems))


def slots_kernel(count, points, cap, blocks_hbm, slots_hbm, blocks, slots, sems):
    me = lax.axis_index("pts")
    wait_all(start_all([(blocks_hbm, blocks)], sems))
    before = before_matrix(count)
    groups = blocks.shape[1] // count
    for u in range(UPDATES):
        found = jnp.zeros((8, groups * cap), f32)
        for g in range(groups):
            local = blocks[u : u + 1, g * count : (g + 1) * count] - me * points
            mine = (local >= 0) & (local < points)
            counts = jnp.where(mine, 1.0, 0.0)
            rank = mm(jnp.broadcast_to(counts, (8, count)).astype(bf16), before, 1, 0)[0:1]
            held = jnp.where(mine, rank.astype(i32) + g * cap, -1)
            chosen = one_hot(iota((groups * cap, count), 0) == held)
            found += mm(two_digits(jnp.where(mine, local + 1, 0)), chosen, 1, 1)
        slots[u : u + 1, :] = from_digits(found) - 1
    wait_all(start_all([(slots, slots_hbm)], sems))


def column_of(row):
    return jnp.broadcast_to(row.astype(f32), (8, row.shape[1])).T[:, 0:1]


def extended(rows, axis, first):
    rest = -0.5 * jnp.sum(jnp.square(rows.astype(f32)), axis=axis, keepdims=True)
    parts = []
    for _ in range(3):
        parts.append(rest.astype(bf16).astype(f32))
        rest = rest - parts[-1]
    parts = parts + [1.0] * 3 if first else [1.0] * 3 + parts
    at = iota(rows.shape, axis)
    extra = jnp.zeros(rows.shape, f32)
    for n, part in enumerate(parts):
        extra = jnp.where(at == n, part, extra)
    return jnp.concatenate([rows.astype(bf16), extra.astype(bf16)], axis=axis)


def exponent(left, right):
    return mm(left, right, 1, 0) * (7.0 / (left.shape[1] // 2) * math.log2(math.e))


CHUNK = 256


def compact_kernel(*refs):
    *came_hbm, starts_hbm, block_hbm, came, starts, wide, block, sems = refs
    me = lax.axis_index("pts")
    owners, deep, _ = came.shape
    cap = deep // UPDATES
    count = block.shape[2]
    pairs = [(a, came.at[k]) for k, a in enumerate(came_hbm)]
    wait_all(start_all([*pairs, (starts_hbm, starts)], sems))
    for u in range(UPDATES):
        for o in range(owners):
            start = starts[u, o]
            rows = came[lax.bitwise_xor(me, o), u * cap : (u + 1) * cap, :]
            wide[u, pl.ds(start, cap), :] = rows.astype(f32)
        block[u] = wide[u, 0:count, :].T.astype(bf16)
    wait_all(start_all([(block, block_hbm)], sems))


def sums_kernel(
    block_hbm, feats_hbm, coef_hbm, offset_hbm, pieces_hbm,
    block, feats, coef, offset, tile, pieces, sems,
):
    outputs = coef.shape[1]
    pairs = [(block_hbm, block), (feats_hbm, feats), (coef_hbm, coef), (offset_hbm, offset)]
    reads = start_all(pairs, sems)
    wait_all(reads[:2])
    left = extended(feats[...], 1, True)
    for u in range(UPDATES):
        right = extended(block[u], 0, False)
        tile[...] = jnp.exp2(exponent(left, right)).astype(bf16)
        if u == 0:
            wait_all(reads[2:])
        total = offset[u] + mm(coef[u], tile[...], 1, 0)
        devices, _, lanes = pieces.shape
        own = outputs // devices
        for d in range(devices):
            part = total[d * own : (d + 1) * own]
            pieces[d, 2 * own * u : 2 * own * (u + 1), :] = jnp.concatenate(
                [part[:, :lanes], part[:, lanes:]], axis=0
            ).astype(bf16)
    wait_all(start_all([(pieces, pieces_hbm)], sems))


def factors_kernel(
    b0_hbm, b1_hbm, b2_hbm, b3_hbm, ids_hbm, from_hbm, pivots_hbm, factor_hbm, cross_hbm,
    feats, ids, came_from, pivots, factor, cross, sems,
):
    row = lax.axis_index("rows")
    groups, _, width, count = feats.shape
    pairs = [(b_hbm, feats.at[k]) for k, b_hbm in enumerate((b0_hbm, b1_hbm, b2_hbm, b3_hbm))]
    pairs += [(ids_hbm, ids), (from_hbm, came_from), (pivots_hbm, pivots)]
    wait_all(start_all(pairs, sems))
    places = [lax.bitwise_xor(row, k) for k in range(groups)]
    rights = [[extended(feats[k, u], 0, False) for k in range(groups)] for u in range(UPDATES)]
    for u in range(UPDATES):
        wanted = pivots[u : u + 1, :].astype(f32)
        chosen_feats = jnp.zeros((width, wanted.shape[1]), f32)
        for k in range(groups):
            here = column_of(came_from[pl.ds(u * groups + places[k], 1), :])
            chosen_feats += mm(feats[k, u], one_hot(here == wanted), 1, 0)
        left = extended(chosen_feats.T, 1, True)
        for k in range(groups):
            start = pl.multiple_of(places[k] * count, count)
            value = jnp.exp2(exponent(left, rights[u][k]))
            factor[u, :, pl.ds(start, count)] = value.astype(bf16)
    writes = start_all([(factor, factor_hbm)], sems)
    lefts, left_points = [], []
    for k in range(groups):
        lefts.append(extended(feats[k, 0].astype(f32).T, 1, True))
        left_points.append(column_of(ids[pl.ds(places[k], 1), :]))
    left, left_points = jnp.concatenate(lefts, axis=0), jnp.concatenate(left_points, axis=0)
    sent = 1
    for m in range(groups):
        right_points = ids[pl.ds(groups + places[m], 1), :].astype(f32)
        power = exponent(left, rights[1][m])
        power = jnp.where(left_points == right_points, math.log2(1.0 + ridge_term), power)
        cross[m] = jnp.exp2(power).astype(bf16).reshape(groups, count, count)
        for k in range(groups):
            start = pl.multiple_of(places[k] * count, count)
            copy = pltpu.make_async_copy(
                cross.at[m, k], cross_hbm.at[places[m], pl.ds(start, count), :], sems.at[sent]
            )
            copy.start()
            writes.append(copy)
            sent += 1
    wait_all(writes)


def chain_kernel(
    cap, owners,
    summed_hbm, factor_hbm, core_hbm, cross_hbm, starts_hbm, out_hbm,
    summed, factor, core, cross, starts, packed, sems,
):
    groups, _, count = cross.shape
    own = summed.shape[1] // (2 * UPDATES)
    pairs = [(summed_hbm, summed)]
    for u in range(UPDATES):
        pairs += [(factor_hbm.at[u], factor.at[u]), (core_hbm.at[u], core.at[u])]
        if u == 0:
            pairs += [(starts_hbm, starts)]
            pairs += [(cross_hbm.at[g], cross.at[g]) for g in range(groups)]
    reads = start_all(pairs, sems)
    first, *reads = reads
    first.wait()
    step = None
    for u in range(UPDATES):
        sums = []
        for g in range(groups):
            part = summed[g * owners, 2 * own * u : 2 * own * (u + 1), :].astype(f32)
            for o in range(1, owners):
                part += summed[g * owners + o, 2 * own * u : 2 * own * (u + 1), :].astype(f32)
            part = jnp.concatenate([part[:own], part[own:]], axis=1)
            if u:
                reads[3 + g].wait()
                part -= mix_per_step * mm(step, cross[g], 1, 0)
            sums.append(part)
        resid = jnp.concatenate(sums, axis=1)
        wait_all(reads[0:3] if u == 0 else reads[3 + groups :])
        proj = mm(resid.astype(bf16), factor[u], 1, 1)
        lifted = mm(proj.astype(bf16), core[u], 1, 1).astype(bf16)
        step = (resid - mm(lifted, factor[u], 1, 0)).astype(bf16)
        half = groups // 2
        for o in range(owners):
            lanes = []
            for g in range(groups):
                part = step[:, g * count : (g + 1) * count].astype(f32)
                back = lax.rem(count - starts[u * groups + g, o], count)
                lanes.append(pltpu.roll(part, back, 1)[:, :cap])
            packed[o, 2 * own * u : 2 * own * (u + 1), :] = jnp.concatenate(
                [jnp.concatenate(lanes[h * half : (h + 1) * half], axis=1) for h in range(2)], axis=0
            ).astype(bf16)
    wait_all(start_all([(packed, out_hbm)], sems))


def finish_kernel(
    g0_hbm, g1_hbm, g2_hbm, g3_hbm, slots_hbm, w_hbm, z_hbm, w_out, z_out,
    got, slots, w, z, steps, w_new, z_new, sems, out_sems,
):
    row = lax.axis_index("rows")
    points = w.shape[0]
    sources, deep, lanes = got.shape
    own = deep // (2 * UPDATES)
    chunks = range(0, points, CHUNK)
    pairs = [(slots_hbm, slots)]
    for k, g_hbm in enumerate((g0_hbm, g1_hbm, g2_hbm, g3_hbm)):
        size = g_hbm.shape[0]
        first = pl.multiple_of(lax.bitwise_xor(row, k) * size, size)
        pairs.append((g_hbm, got.at[pl.ds(first, size)]))
    for c in chunks:
        part = slice(c, c + CHUNK)
        pairs += [(w_hbm.at[part], w.at[part]), (z_hbm.at[part], z.at[part])]
    reads = start_all(pairs, sems)
    wait_all(reads[:5])
    reads = reads[5:]
    wide = got[...].astype(f32)
    for u in range(UPDATES):
        for h in range(2):
            first = own * (2 * u + h)
            part = wide[:, first : first + own, :].reshape(sources * own, lanes)
            steps[u, h * lanes : (h + 1) * lanes, :] = part.T.astype(bf16)
    changes = []
    for u in range(UPDATES):
        rows = one_hot(iota((points, slots.shape[1]), 0) == slots[u : u + 1, :])
        changes.append(mm(rows, steps[u], 1, 0))
    writes = []
    for n, c in enumerate(chunks):
        part = slice(c, c + CHUNK)
        wait_all(reads[2 * n : 2 * n + 2])
        current, moving = w[part, :], z[part, :]
        for change in changes:
            current, moving = stepped(current, moving, change[part])
        w_new[part, :] = current
        z_new[part, :] = moving
        for m, (a, b) in enumerate(((w_new, w_out), (z_new, z_out))):
            copy = pltpu.make_async_copy(a.at[part], b.at[part], out_sems.at[2 * n + m])
            copy.start()
            writes.append(copy)
    wait_all(writes)


VMEM = pl.BlockSpec(memory_space=pltpu.VMEM)
HBM = pl.BlockSpec(memory_space=pltpu.HBM)
in_smem = type(pltpu.SMEM((1,), i32))


def like(shape, dtype=bf16):
    return jax.ShapeDtypeStruct(shape, dtype)


def call(body, outs, inside, *args, near=0, sems=(), flops=0, grant=63.9):
    moved = sum(math.prod(o.shape) * o.dtype.itemsize for o in [*outs, *args])
    return pl.pallas_call(
        body,
        out_shape=outs,
        in_specs=[VMEM] * near + [HBM] * (len(args) - near),
        out_specs=[HBM] * len(outs),
        scratch_shapes=[
            x if isinstance(x, in_smem) else pltpu.VMEM(x.shape, x.dtype) for x in inside
        ]
        + [pltpu.SemaphoreType.DMA((n,)) for n in sems],
        compiler_params=pltpu.CompilerParams(vmem_limit_bytes=int(grant * 2**20)),
        cost_estimate=pl.CostEstimate(flops=int(flops), bytes_accessed=moved, transcendentals=0),
    )(*args)


def swap(value, axis, k):
    return lax.ppermute(value, axis, [(i, i ^ k) for i in range(lax.axis_size(axis))])


def with_kernels(features, targets, coefficients, momentum, block_index, pivot_index, core):
    rows, owners = lax.axis_size("rows"), lax.axis_size("pts")
    points, width = features.shape
    block = block_index.shape[1]
    rank = pivot_index.shape[1]
    outputs = coefficients.shape[1]
    count = block // rows
    cap = 3 * count // owners
    devices = rows * owners
    own = outputs // devices
    deep = 2 * own * UPDATES
    half = rows // 2
    wide = like(coefficients.shape, f32)

    (packed,) = call(
        functools.partial(pack_kernel, count, cap, owners),
        [like((UPDATES * cap, width))],
        [block_index, features, like((UPDATES * cap, width))],
        block_index,
        features,
        sems=(2,),
    )
    came = {k: swap(packed, "pts", k) for k in (6, 5, 4, 2, 1)}
    came[2], came[6], first_index = lax.optimization_barrier((came[2], came[6], block_index))
    came[3], came[7] = swap(came[2], "pts", 1), swap(came[6], "pts", 1)
    kept = [
        like((UPDATES, outputs, points)),
        like((UPDATES, outputs, count), f32),
        like((8, 128), i32),
    ]
    given = [first_index, coefficients, momentum, targets]
    coef, offset, row_starts = call(
        functools.partial(prepare_kernel, count, owners),
        kept,
        given + kept,
        *given,
        sems=(4, 1 + 2 * UPDATES),
    )
    feats = like((UPDATES, width, count))
    inside_starts = pltpu.SMEM(row_starts.shape, i32)
    (mine,) = call(
        compact_kernel,
        [feats],
        [
            like((owners, *packed.shape)),
            inside_starts,
            like((UPDATES, count + cap, width), f32),
            feats,
        ],
        packed,
        *[came[k] for k in range(1, owners)],
        row_starts,
        sems=(owners + 1,),
    )
    beside, across = swap(mine, "rows", 1), swap(mine, "rows", 2)
    pieces = like((devices, deep, count // 2))
    (pieces,) = call(
        sums_kernel,
        [pieces],
        [feats, features, coef, offset, like((points, count)), pieces],
        mine,
        features,
        coef,
        offset,
        sems=(4,),
        flops=2.0 * UPDATES * points * count * (2 * width + outputs),
    )
    pieces, later_index = lax.optimization_barrier((pieces, block_index))
    kept = [like((UPDATES * rows, count), i32)] * 2 + [like((8, 128), i32)]
    ids, came_from, starts = call(
        functools.partial(order_kernel, count, points, owners),
        kept,
        [block_index, *kept],
        later_index,
        sems=(3,),
    )
    pieces, beside, across, ids = lax.optimization_barrier((pieces, beside, across, ids))
    summed = lax.all_to_all(pieces, ("rows", "pts"), 0, 0, tiled=True)
    kept = [like((UPDATES, rank, block)), like((rows, block, count))]
    factor, cross = call(
        factors_kernel,
        kept,
        [
            like((rows, *feats.shape)),
            ids,
            came_from,
            pivot_index,
            kept[0],
            like((rows, rows, count, count)),
        ],
        mine,
        beside,
        across,
        swap(across, "rows", 1),
        ids,
        came_from,
        pivot_index,
        sems=(rows * rows + 2,),
        flops=2.0 * width * block * (UPDATES * rank + block),
    )
    pieces = like((owners, deep, half * cap))
    (steps,) = call(
        functools.partial(chain_kernel, cap, owners),
        [pieces],
        [summed, factor, core, cross, inside_starts, pieces],
        summed,
        factor,
        core,
        cross,
        starts,
        sems=(2 * UPDATES + 3 + rows,),
    )
    got = lax.all_to_all(steps, "pts", 0, 0, tiled=True)
    got, later_index = lax.optimization_barrier((got, block_index))
    beside, across = swap(got, "rows", 1), swap(got, "rows", 2)
    (slots,) = call(
        functools.partial(slots_kernel, count, points, cap),
        [like((UPDATES, rows * cap), i32)],
        [block_index, like((UPDATES, rows * cap), i32)],
        later_index,
        sems=(1,),
    )
    across, slots = lax.optimization_barrier((across, slots))
    parts = points // CHUNK
    return call(
        finish_kernel,
        [wide] * 2,
        [
            like((devices, deep, half * cap)),
            slots,
            wide,
            wide,
            like((UPDATES, rows * cap, outputs)),
            wide,
            wide,
        ],
        got,
        beside,
        across,
        swap(across, "rows", 1),
        slots,
        coefficients,
        momentum,
        sems=(1 + rows + 2 * parts, 2 * parts),
    )


def kernel_tile(left_rows, right_rows):
    inner_prod = mm(left_rows, right_rows, 1, 1)
    left_sq = jnp.sum(jnp.square(left_rows.astype(f32)), axis=1)
    right_sq = jnp.sum(jnp.square(right_rows.astype(f32)), axis=1)
    squared = left_sq[:, None] + right_sq[None, :] - 2.0 * inner_prod
    return jnp.exp(squared * (-3.5 / left_rows.shape[1])).astype(bf16)


def with_operations(features, targets, coefficients, momentum, block_index, pivot_index, core):
    row_count, pts_count = lax.axis_size("rows"), lax.axis_size("pts")
    row_id, pts_id = lax.axis_index("rows"), lax.axis_index("pts")
    points = features.shape[0]
    block = block_index.shape[1]
    outputs = coefficients.shape[1]
    per_row = block // row_count
    per_device = per_row // pts_count
    row_cols = outputs // row_count
    own_cols = row_cols // pts_count
    first = row_id * row_cols
    current, moving, goal = (
        lax.dynamic_slice_in_dim(value, first, row_cols, axis=1).T.astype(f32)
        for value in (coefficients, momentum, targets)
    )
    ids = iota((points, 1), 0) + pts_id * points
    place = [(ids == block_index[u][None, :]).astype(bf16) for u in range(UPDATES)]
    own_rows = []
    for u in range(UPDATES):
        mine = lax.dynamic_slice_in_dim(place[u], row_id * per_row, per_row, axis=1)
        own_rows.append(mm(mine, features, 0, 0).astype(bf16).reshape(pts_count, per_device, -1))
    came = lax.all_to_all(jnp.concatenate(own_rows, axis=1), "pts", 0, 0, tiled=False)
    chunk = jnp.sum(came.astype(f32), axis=0).astype(bf16)
    spread = lax.all_gather(lax.all_gather(chunk, "pts", axis=0), "rows", axis=0)
    spread = spread.reshape(row_count, pts_count, UPDATES, per_device, features.shape[1])
    all_steps = []
    for u in range(UPDATES):
        block_feats = spread[:, :, u].reshape(block, features.shape[1])
        mixed = mixed_of(current, moving)
        high, low = split_two(ridge_term * mixed - goal)
        tile = kernel_tile(features, block_feats)
        partial_value = (
            mm(mixed.astype(bf16), tile, 1, 0) + mm(high, place[u], 1, 0) + mm(low, place[u], 1, 0)
        )
        pieces = partial_value.astype(bf16).reshape(pts_count, own_cols, block)
        summed = lax.all_to_all(pieces, "pts", 0, 0, tiled=False)
        resid = jnp.sum(summed.astype(f32), axis=0)
        at_pivot = (iota((block, 1), 0) == pivot_index[u][None, :]).astype(bf16)
        factor = kernel_tile(block_feats, mm(at_pivot, block_feats, 0, 0).astype(bf16))
        proj = mm(resid.astype(bf16), factor, 1, 0)
        lifted = mm(proj.astype(bf16), core[u], 1, 1).astype(bf16)
        step_bf = (resid - mm(lifted, factor, 1, 1)).astype(bf16)
        steps = lax.all_gather(step_bf, "pts", axis=0, tiled=True)
        change = mm(steps, place[u], 1, 1)
        all_steps.append(change.astype(bf16))
        current, moving = stepped(current, moving, change)
    gathered = lax.all_gather(jnp.stack(all_steps), "rows", axis=1, tiled=True)
    current, moving = coefficients, momentum
    for u in range(UPDATES):
        current, moving = stepped(current, moving, gathered[u].T.astype(f32))
    return (current, moving)


def shards(features, targets, coefficients, momentum, block_index, pivot_index, nystrom_core):
    rows, owners = lax.axis_size("rows"), lax.axis_size("pts")
    count = block_index.shape[1] // rows
    fits = rows == 4 and owners == 8 and coefficients.shape[1] == 8 * rows * owners
    fits = fits and 6 * count <= count * owners and coefficients.shape[0] % CHUNK == 0 and count % CHUNK == 0 and (3 * count // owners) % 64 == 0 and UPDATES * rows == 8
    plan = with_kernels if fits else with_operations
    return plan(
        features, targets, coefficients, momentum, block_index, pivot_index, nystrom_core
    )


def solution(mesh):
    in_specs = (P("pts", None), P("pts", None), P("pts", None), P("pts", None), P(), P(), P())
    out_specs = (P("pts", None), P("pts", None))
    return jax.shard_map(shards, mesh=mesh, in_specs=in_specs, out_specs=out_specs, check_vma=False)
```

```python
import functools
import math

import jax
import jax.numpy as jnp
from jax import lax
from jax.experimental import pallas as pl
from jax.experimental.pallas import tpu as pltpu
from jax.sharding import PartitionSpec as P

UPDATES = 2


alpha_mix = 0.6
beta_keep = 0.9
step_size = 0.2
momentum_gain = 1.5
ridge_term = 1.0

f32 = jnp.float32
bf16 = jnp.bfloat16
i32 = jnp.int32


def mm(a, b, ca, cb):
    return lax.dot_general(a, b, (((ca,), (cb,)), ((), ())), preferred_element_type=f32)


def split_two(value):
    high = value.astype(bf16)
    return high, (value - high.astype(f32)).astype(bf16)


def mixed_of(current, moving):
    return alpha_mix * moving + (1.0 - alpha_mix) * current


mix_per_step = alpha_mix * step_size * momentum_gain + (1.0 - alpha_mix) * step_size


def stepped(current, moving, change):
    mixed = mixed_of(current, moving)
    if change is None:
        return mixed, beta_keep * moving + (1.0 - beta_keep) * mixed
    return (
        mixed - step_size * change,
        beta_keep * moving + (1.0 - beta_keep) * mixed - step_size * momentum_gain * change,
    )


def iota(shape, axis):
    return lax.broadcasted_iota(i32, shape, axis)


def one_hot(chosen):
    return jnp.where(chosen, 1.0, 0.0).astype(bf16)


def before_matrix(n):
    return one_hot(iota((n, n), 0) < iota((n, n), 1))


def owners_of(groups, points, owners):
    owner_ids = iota((owners, groups[0].shape[1]), 0)
    owner = [lax.div(x, jnp.full_like(x, points)) for x in groups]
    marks = [jnp.where(owner_ids == x, 1.0, 0.0) for x in owner]
    every = jnp.concatenate(marks, axis=0).astype(bf16)
    earlier = mm(every, before_matrix(every.shape[1]), 1, 0)
    out = []
    for n, x in enumerate(owner):
        rank = jnp.sum(marks[n] * earlier[n * owners : (n + 1) * owners], axis=0, keepdims=True)
        start = jnp.sum(jnp.where(x < owner_ids, 1.0, 0.0), axis=1, keepdims=True)
        out.append((marks[n], rank, start))
    return out


def sorted_places(marks, rank, start):
    return (rank + jnp.sum(marks * start, axis=0, keepdims=True)).astype(i32)


def lane_row(column):
    n = column.shape[0]
    diagonal = iota((n, 128), 0) == iota((n, 128), 1)
    return jnp.sum(jnp.where(diagonal, column, 0.0), axis=0, keepdims=True).astype(i32)


def two_digits(*rows):
    shape = (8, rows[0].shape[1])
    value = jnp.zeros(shape, i32)
    for n, row in enumerate(rows):
        high = lax.shift_right_logical(row, jnp.full_like(row, 7))
        low = lax.bitwise_and(row, jnp.full_like(row, 127))
        value = jnp.where(iota(shape, 0) == 2 * n, high, value)
        value = jnp.where(iota(shape, 0) == 2 * n + 1, low, value)
    return value.astype(f32).astype(bf16)


def from_digits(digits):
    return (digits[0:1] * 128.0 + digits[1:2]).astype(i32)


def start_all(pairs, sems):
    copies = [pltpu.make_async_copy(a, b, sems.at[n]) for n, (a, b) in enumerate(pairs)]
    for copy in copies:
        copy.start()
    return copies


def wait_all(copies):
    for copy in copies:
        copy.wait()


def group_row(blocks, u, group, count):
    return blocks[u : u + 1, pl.ds(pl.multiple_of(group * count, count), count)]


def pack_kernel(count, cap, owners, blocks_hbm, feats_hbm, out_hbm, blocks, feats, packed, sems):
    row, me = lax.axis_index("rows"), lax.axis_index("pts")
    points = feats.shape[0]
    reads = start_all([(blocks_hbm, blocks), (feats_hbm, feats)], sems)
    before = before_matrix(count)
    reads[0].wait()
    rows = []
    for u in range(UPDATES):
        indices = group_row(blocks, u, row, count)
        local = indices - me * points
        mine = jnp.where((local >= 0) & (local < points), 1.0, 0.0)
        rank = mm(jnp.broadcast_to(mine, (8, count)).astype(bf16), before, 1, 0)[0:1]
        held = (iota((cap, count), 0) == rank.astype(i32)) & (mine > 0.0)
        point = jnp.sum(jnp.where(held, (local + 1).astype(f32), 0.0), axis=1, keepdims=True)
        rows.append(one_hot(iota((cap, points), 1) == point.astype(i32) - 1))
    reads[1].wait()
    for u in range(UPDATES):
        packed[u * cap : (u + 1) * cap, :] = mm(rows[u], feats[...], 1, 0).astype(bf16)
    wait_all(start_all([(packed, out_hbm)], sems))


def prepare_kernel(
    count, owners,
    blocks_hbm, w_hbm, z_hbm, t_hbm, coef_hbm, offset_hbm, starts_hbm,
    blocks, w, z, t, coef, offset, starts, sems, out_sems,
):
    row, me = lax.axis_index("rows"), lax.axis_index("pts")
    points, outputs = w.shape
    reads = start_all([(blocks_hbm, blocks), (w_hbm, w), (z_hbm, z), (t_hbm, t)], sems)
    reads[0].wait()
    groups = [group_row(blocks, u, row, count) for u in range(UPDATES)]
    found, shift = [], []
    for u, (_, rank, start) in enumerate(owners_of(groups, points, owners)):
        starts[u : u + 1, :] = lane_row(start)
        local = groups[u] - me * points
        mine = (local >= 0) & (local < points)
        held = jnp.where(mine, rank.astype(i32), -1)
        chosen = one_hot(iota((count // 2, count), 0) == held)
        digits = two_digits(jnp.where(mine, local + 1, 0))
        found.append(from_digits(mm(digits, chosen, 1, 1)) - 1)
        earlier = jnp.sum(jnp.where(groups[u] < me * points, 1.0, 0.0))
        shift.append(lax.rem(earlier.astype(i32), count))
    writes = start_all([(starts, starts_hbm)], out_sems)
    wait_all(reads[1:])
    current, moving = w[...], z[...]
    goal = t[...].astype(f32).T
    for u in range(UPDATES):
        mixed = mixed_of(current, moving).T
        high, low = split_two(ridge_term * mixed - goal)
        coef[u] = mixed.astype(bf16)
        place = one_hot(iota((points, count // 2), 0) == found[u])
        both = mm(jnp.concatenate([high, low], axis=0), place, 1, 0)
        held = both[:outputs] + both[outputs:]
        held = jnp.concatenate([held, jnp.zeros_like(held)], axis=1)
        offset[u] = pltpu.roll(held, shift[u], 1)
        current, moving = stepped(current, moving, None)
        for a, b in ((coef, coef_hbm), (offset, offset_hbm)):
            writes.append(pltpu.make_async_copy(a.at[u], b.at[u], out_sems.at[len(writes)]))
            writes[-1].start()
    wait_all(writes)


def put_in_order(count, points, owners, blocks, ids, came_from, starts):
    count_of = blocks.shape[1] // count
    groups = [
        blocks[u : u + 1, g * count : (g + 1) * count]
        for u in range(UPDATES)
        for g in range(count_of)
    ]
    for n, (marks, rank, start) in enumerate(owners_of(groups, points, owners)):
        place = sorted_places(marks, rank, start)
        given = iota((1, count), 1) + (n % count_of) * count
        digits = two_digits(groups[n], given)
        moved = mm(digits, one_hot(iota((count, count), 0) == place), 1, 1)
        ids[n : n + 1, :] = from_digits(moved[0:2])
        came_from[n : n + 1, :] = from_digits(moved[2:4])
        starts[n : n + 1, :] = lane_row(start)


def slots_kernel(count, points, cap, blocks_hbm, slots_hbm, blocks, slots, sems):
    me = lax.axis_index("pts")
    wait_all(start_all([(blocks_hbm, blocks)], sems))
    before = before_matrix(count)
    groups = blocks.shape[1] // count
    for u in range(UPDATES):
        found = jnp.zeros((8, groups * cap), f32)
        for g in range(groups):
            local = blocks[u : u + 1, g * count : (g + 1) * count] - me * points
            mine = (local >= 0) & (local < points)
            counts = jnp.where(mine, 1.0, 0.0)
            rank = mm(jnp.broadcast_to(counts, (8, count)).astype(bf16), before, 1, 0)[0:1]
            held = jnp.where(mine, rank.astype(i32) + g * cap, -1)
            chosen = one_hot(iota((groups * cap, count), 0) == held)
            found += mm(two_digits(jnp.where(mine, local + 1, 0)), chosen, 1, 1)
        slots[u : u + 1, :] = from_digits(found) - 1
    wait_all(start_all([(slots, slots_hbm)], sems))


def column_of(row):
    return jnp.broadcast_to(row.astype(f32), (8, row.shape[1])).T[:, 0:1]


def extended(rows, axis, first):
    rest = -0.5 * jnp.sum(jnp.square(rows.astype(f32)), axis=axis, keepdims=True)
    parts = []
    for _ in range(3):
        parts.append(rest.astype(bf16).astype(f32))
        rest = rest - parts[-1]
    parts = parts + [1.0] * 3 if first else [1.0] * 3 + parts
    at = iota(rows.shape, axis)
    extra = jnp.zeros(rows.shape, f32)
    for n, part in enumerate(parts):
        extra = jnp.where(at == n, part, extra)
    return jnp.concatenate([rows.astype(bf16), extra.astype(bf16)], axis=axis)


def exponent(left, right):
    return mm(left, right, 1, 0) * (7.0 / (left.shape[1] // 2) * math.log2(math.e))


CHUNK = 256


def compact_kernel(*refs):
    *came_hbm, starts_hbm, block_hbm, came, starts, wide, block, sems = refs
    me = lax.axis_index("pts")
    owners, deep, _ = came.shape
    cap = deep // UPDATES
    count = block.shape[2]
    pairs = [(a, came.at[k]) for k, a in enumerate(came_hbm)]
    wait_all(start_all([*pairs, (starts_hbm, starts)], sems))
    for u in range(UPDATES):
        for o in range(owners):
            start = starts[u, o]
            rows = came[lax.bitwise_xor(me, o), u * cap : (u + 1) * cap, :]
            wide[u, pl.ds(start, cap), :] = rows.astype(f32)
        block[u] = wide[u, 0:count, :].T.astype(bf16)
    wait_all(start_all([(block, block_hbm)], sems))


def sums_kernel(
    owners,
    block_hbm, feats_hbm, blocks_hbm, coef_hbm, offset_hbm,
    pieces_hbm, ids_hbm, from_hbm, starts_hbm,
    block, feats, blocks, coef, offset, tile, pieces, ids, came_from, starts, sems, out_sems,
):
    outputs = coef.shape[1]
    pairs = [(block_hbm, block), (feats_hbm, feats), (blocks_hbm, blocks)]
    reads = start_all([*pairs, (coef_hbm, coef), (offset_hbm, offset)], sems)
    wait_all(reads[:3])
    put_in_order(block.shape[2], feats.shape[0], owners, blocks, ids, came_from, starts)
    pairs = [(ids, ids_hbm), (came_from, from_hbm), (starts, starts_hbm)]
    writes = start_all(pairs, out_sems)
    left = extended(feats[...], 1, True)
    for u in range(UPDATES):
        right = extended(block[u], 0, False)
        tile[...] = jnp.exp2(exponent(left, right)).astype(bf16)
        if u == 0:
            wait_all(reads[3:])
        total = offset[u] + mm(coef[u], tile[...], 1, 0)
        devices, _, lanes = pieces.shape
        own = outputs // devices
        for d in range(devices):
            part = total[d * own : (d + 1) * own]
            pieces[d, 2 * own * u : 2 * own * (u + 1), :] = jnp.concatenate(
                [part[:, :lanes], part[:, lanes:]], axis=0
            ).astype(bf16)
    wait_all(writes + start_all([(pieces, pieces_hbm)], sems))


def factors_kernel(
    b0_hbm, b1_hbm, b2_hbm, b3_hbm, ids_hbm, from_hbm, pivots_hbm, factor_hbm, cross_hbm,
    feats, ids, came_from, pivots, factor, cross, sems,
):
    row = lax.axis_index("rows")
    groups, _, width, count = feats.shape
    pairs = [(b_hbm, feats.at[k]) for k, b_hbm in enumerate((b0_hbm, b1_hbm, b2_hbm, b3_hbm))]
    pairs += [(ids_hbm, ids), (from_hbm, came_from), (pivots_hbm, pivots)]
    wait_all(start_all(pairs, sems))
    places = [lax.bitwise_xor(row, k) for k in range(groups)]
    rights = [[extended(feats[k, u], 0, False) for k in range(groups)] for u in range(UPDATES)]
    for u in range(UPDATES):
        wanted = pivots[u : u + 1, :].astype(f32)
        chosen_feats = jnp.zeros((width, wanted.shape[1]), f32)
        for k in range(groups):
            here = column_of(came_from[pl.ds(u * groups + places[k], 1), :])
            chosen_feats += mm(feats[k, u], one_hot(here == wanted), 1, 0)
        left = extended(chosen_feats.T, 1, True)
        for k in range(groups):
            start = pl.multiple_of(places[k] * count, count)
            value = jnp.exp2(exponent(left, rights[u][k]))
            factor[u, :, pl.ds(start, count)] = value.astype(bf16)
    writes = start_all([(factor, factor_hbm)], sems)
    lefts, left_points = [], []
    for k in range(groups):
        lefts.append(extended(feats[k, 0].astype(f32).T, 1, True))
        left_points.append(column_of(ids[pl.ds(places[k], 1), :]))
    left, left_points = jnp.concatenate(lefts, axis=0), jnp.concatenate(left_points, axis=0)
    sent = 1
    for m in range(groups):
        right_points = ids[pl.ds(groups + places[m], 1), :].astype(f32)
        power = exponent(left, rights[1][m])
        power = jnp.where(left_points == right_points, math.log2(1.0 + ridge_term), power)
        cross[m] = jnp.exp2(power).astype(bf16).reshape(groups, count, count)
        for k in range(groups):
            start = pl.multiple_of(places[k] * count, count)
            copy = pltpu.make_async_copy(
                cross.at[m, k], cross_hbm.at[places[m], pl.ds(start, count), :], sems.at[sent]
            )
            copy.start()
            writes.append(copy)
            sent += 1
    wait_all(writes)


def chain_kernel(
    cap, owners,
    summed_hbm, factor_hbm, core_hbm, cross_hbm, starts_hbm, out_hbm,
    summed, factor, core, cross, starts, packed, sems,
):
    groups, _, count = cross.shape
    own = summed.shape[1] // (2 * UPDATES)
    pairs = [(summed_hbm, summed)]
    for u in range(UPDATES):
        pairs += [(factor_hbm.at[u], factor.at[u]), (core_hbm.at[u], core.at[u])]
        if u == 0:
            pairs += [(starts_hbm, starts)]
            pairs += [(cross_hbm.at[g], cross.at[g]) for g in range(groups)]
    reads = start_all(pairs, sems)
    first, *reads = reads
    first.wait()
    step = None
    for u in range(UPDATES):
        sums = []
        for g in range(groups):
            part = summed[g * owners, 2 * own * u : 2 * own * (u + 1), :].astype(f32)
            for o in range(1, owners):
                part += summed[g * owners + o, 2 * own * u : 2 * own * (u + 1), :].astype(f32)
            part = jnp.concatenate([part[:own], part[own:]], axis=1)
            if u:
                reads[3 + g].wait()
                part -= mix_per_step * mm(step, cross[g], 1, 0)
            sums.append(part)
        resid = jnp.concatenate(sums, axis=1)
        wait_all(reads[0:3] if u == 0 else reads[3 + groups :])
        proj = mm(resid.astype(bf16), factor[u], 1, 1)
        lifted = mm(proj.astype(bf16), core[u], 1, 1).astype(bf16)
        step = (resid - mm(lifted, factor[u], 1, 0)).astype(bf16)
        half = groups // 2
        for o in range(owners):
            lanes = []
            for g in range(groups):
                part = step[:, g * count : (g + 1) * count].astype(f32)
                back = lax.rem(count - starts[u * groups + g, o], count)
                lanes.append(pltpu.roll(part, back, 1)[:, :cap])
            packed[o, 2 * own * u : 2 * own * (u + 1), :] = jnp.concatenate(
                [jnp.concatenate(lanes[h * half : (h + 1) * half], axis=1) for h in range(2)], axis=0
            ).astype(bf16)
    wait_all(start_all([(packed, out_hbm)], sems))


def finish_kernel(
    g0_hbm, g1_hbm, g2_hbm, g3_hbm, slots_hbm, w_hbm, z_hbm, w_out, z_out,
    got, slots, w, z, steps, w_new, z_new, sems, out_sems,
):
    row = lax.axis_index("rows")
    points = w.shape[0]
    sources, deep, lanes = got.shape
    own = deep // (2 * UPDATES)
    chunks = range(0, points, CHUNK)
    pairs = [(slots_hbm, slots)]
    for k, g_hbm in enumerate((g0_hbm, g1_hbm, g2_hbm, g3_hbm)):
        size = g_hbm.shape[0]
        first = pl.multiple_of(lax.bitwise_xor(row, k) * size, size)
        pairs.append((g_hbm, got.at[pl.ds(first, size)]))
    for c in chunks:
        part = slice(c, c + CHUNK)
        pairs += [(w_hbm.at[part], w.at[part]), (z_hbm.at[part], z.at[part])]
    reads = start_all(pairs, sems)
    wait_all(reads[:5])
    reads = reads[5:]
    wide = got[...].astype(f32)
    for u in range(UPDATES):
        for h in range(2):
            first = own * (2 * u + h)
            part = wide[:, first : first + own, :].reshape(sources * own, lanes)
            steps[u, h * lanes : (h + 1) * lanes, :] = part.T.astype(bf16)
    changes = []
    for u in range(UPDATES):
        rows = one_hot(iota((points, slots.shape[1]), 0) == slots[u : u + 1, :])
        changes.append(mm(rows, steps[u], 1, 0))
    writes = []
    for n, c in enumerate(chunks):
        part = slice(c, c + CHUNK)
        wait_all(reads[2 * n : 2 * n + 2])
        current, moving = w[part, :], z[part, :]
        for change in changes:
            current, moving = stepped(current, moving, change[part])
        w_new[part, :] = current
        z_new[part, :] = moving
        for m, (a, b) in enumerate(((w_new, w_out), (z_new, z_out))):
            copy = pltpu.make_async_copy(a.at[part], b.at[part], out_sems.at[2 * n + m])
            copy.start()
            writes.append(copy)
    wait_all(writes)


VMEM = pl.BlockSpec(memory_space=pltpu.VMEM)
HBM = pl.BlockSpec(memory_space=pltpu.HBM)
in_smem = type(pltpu.SMEM((1,), i32))


def like(shape, dtype=bf16):
    return jax.ShapeDtypeStruct(shape, dtype)


def call(body, outs, inside, *args, near=0, sems=(), flops=0, grant=63.9):
    moved = sum(math.prod(o.shape) * o.dtype.itemsize for o in [*outs, *args])
    return pl.pallas_call(
        body,
        out_shape=outs,
        in_specs=[VMEM] * near + [HBM] * (len(args) - near),
        out_specs=[HBM] * len(outs),
        scratch_shapes=[
            x if isinstance(x, in_smem) else pltpu.VMEM(x.shape, x.dtype) for x in inside
        ]
        + [pltpu.SemaphoreType.DMA((n,)) for n in sems],
        compiler_params=pltpu.CompilerParams(vmem_limit_bytes=int(grant * 2**20)),
        cost_estimate=pl.CostEstimate(flops=int(flops), bytes_accessed=moved, transcendentals=0),
    )(*args)


def swap(value, axis, k):
    return lax.ppermute(value, axis, [(i, i ^ k) for i in range(lax.axis_size(axis))])


def with_kernels(features, targets, coefficients, momentum, block_index, pivot_index, core):
    rows, owners = lax.axis_size("rows"), lax.axis_size("pts")
    points, width = features.shape
    block = block_index.shape[1]
    rank = pivot_index.shape[1]
    outputs = coefficients.shape[1]
    count = block // rows
    cap = 3 * count // owners
    devices = rows * owners
    own = outputs // devices
    deep = 2 * own * UPDATES
    half = rows // 2
    wide = like(coefficients.shape, f32)

    (packed,) = call(
        functools.partial(pack_kernel, count, cap, owners),
        [like((UPDATES * cap, width))],
        [block_index, features, like((UPDATES * cap, width))],
        block_index,
        features,
        sems=(2,),
    )
    came = {k: swap(packed, "pts", k) for k in (6, 5, 4, 2, 1)}
    came[2], came[6], first_index = lax.optimization_barrier((came[2], came[6], block_index))
    came[3], came[7] = swap(came[2], "pts", 1), swap(came[6], "pts", 1)
    kept = [
        like((UPDATES, outputs, points)),
        like((UPDATES, outputs, count), f32),
        like((8, 128), i32),
    ]
    given = [first_index, coefficients, momentum, targets]
    coef, offset, row_starts = call(
        functools.partial(prepare_kernel, count, owners),
        kept,
        given + kept,
        *given,
        sems=(4, 1 + 2 * UPDATES),
    )
    feats = like((UPDATES, width, count))
    inside_starts = pltpu.SMEM(row_starts.shape, i32)
    (mine,) = call(
        compact_kernel,
        [feats],
        [
            like((owners, *packed.shape)),
            inside_starts,
            like((UPDATES, count + cap, width), f32),
            feats,
        ],
        packed,
        *[came[k] for k in range(1, owners)],
        row_starts,
        sems=(owners + 1,),
    )
    beside, across = swap(mine, "rows", 1), swap(mine, "rows", 2)
    kept = [
        like((devices, deep, count // 2)),
        like((UPDATES * rows, count), i32),
        like((UPDATES * rows, count), i32),
        like((8, 128), i32),
    ]
    given = [mine, features, block_index, coef, offset]
    pieces, ids, came_from, starts = call(
        functools.partial(sums_kernel, owners),
        kept,
        [*given, like((points, count)), *kept],
        *given,
        sems=(5, 3),
        flops=2.0 * UPDATES * points * count * (2 * width + outputs),
    )
    pieces, beside, across = lax.optimization_barrier((pieces, beside, across))
    summed = lax.all_to_all(pieces, ("rows", "pts"), 0, 0, tiled=True)
    kept = [like((UPDATES, rank, block)), like((rows, block, count))]
    factor, cross = call(
        factors_kernel,
        kept,
        [
            like((rows, *feats.shape)),
            ids,
            came_from,
            pivot_index,
            kept[0],
            like((rows, rows, count, count)),
        ],
        mine,
        beside,
        across,
        swap(across, "rows", 1),
        ids,
        came_from,
        pivot_index,
        sems=(rows * rows + 2,),
        flops=2.0 * width * block * (UPDATES * rank + block),
    )
    pieces = like((owners, deep, half * cap))
    (steps,) = call(
        functools.partial(chain_kernel, cap, owners),
        [pieces],
        [summed, factor, core, cross, inside_starts, pieces],
        summed,
        factor,
        core,
        cross,
        starts,
        sems=(2 * UPDATES + 3 + rows,),
    )
    got = lax.all_to_all(steps, "pts", 0, 0, tiled=True)
    got, later_index = lax.optimization_barrier((got, block_index))
    beside, across = swap(got, "rows", 1), swap(got, "rows", 2)
    (slots,) = call(
        functools.partial(slots_kernel, count, points, cap),
        [like((UPDATES, rows * cap), i32)],
        [block_index, like((UPDATES, rows * cap), i32)],
        later_index,
        sems=(1,),
    )
    across, slots = lax.optimization_barrier((across, slots))
    parts = points // CHUNK
    return call(
        finish_kernel,
        [wide] * 2,
        [
            like((devices, deep, half * cap)),
            slots,
            wide,
            wide,
            like((UPDATES, rows * cap, outputs)),
            wide,
            wide,
        ],
        got,
        beside,
        across,
        swap(across, "rows", 1),
        slots,
        coefficients,
        momentum,
        sems=(1 + rows + 2 * parts, 2 * parts),
    )


def kernel_tile(left_rows, right_rows):
    inner_prod = mm(left_rows, right_rows, 1, 1)
    left_sq = jnp.sum(jnp.square(left_rows.astype(f32)), axis=1)
    right_sq = jnp.sum(jnp.square(right_rows.astype(f32)), axis=1)
    squared = left_sq[:, None] + right_sq[None, :] - 2.0 * inner_prod
    return jnp.exp(squared * (-3.5 / left_rows.shape[1])).astype(bf16)


def with_operations(features, targets, coefficients, momentum, block_index, pivot_index, core):
    row_count, pts_count = lax.axis_size("rows"), lax.axis_size("pts")
    row_id, pts_id = lax.axis_index("rows"), lax.axis_index("pts")
    points = features.shape[0]
    block = block_index.shape[1]
    outputs = coefficients.shape[1]
    per_row = block // row_count
    per_device = per_row // pts_count
    row_cols = outputs // row_count
    own_cols = row_cols // pts_count
    first = row_id * row_cols
    current, moving, goal = (
        lax.dynamic_slice_in_dim(value, first, row_cols, axis=1).T.astype(f32)
        for value in (coefficients, momentum, targets)
    )
    ids = iota((points, 1), 0) + pts_id * points
    place = [(ids == block_index[u][None, :]).astype(bf16) for u in range(UPDATES)]
    own_rows = []
    for u in range(UPDATES):
        mine = lax.dynamic_slice_in_dim(place[u], row_id * per_row, per_row, axis=1)
        own_rows.append(mm(mine, features, 0, 0).astype(bf16).reshape(pts_count, per_device, -1))
    came = lax.all_to_all(jnp.concatenate(own_rows, axis=1), "pts", 0, 0, tiled=False)
    chunk = jnp.sum(came.astype(f32), axis=0).astype(bf16)
    spread = lax.all_gather(lax.all_gather(chunk, "pts", axis=0), "rows", axis=0)
    spread = spread.reshape(row_count, pts_count, UPDATES, per_device, features.shape[1])
    all_steps = []
    for u in range(UPDATES):
        block_feats = spread[:, :, u].reshape(block, features.shape[1])
        mixed = mixed_of(current, moving)
        high, low = split_two(ridge_term * mixed - goal)
        tile = kernel_tile(features, block_feats)
        partial_value = (
            mm(mixed.astype(bf16), tile, 1, 0) + mm(high, place[u], 1, 0) + mm(low, place[u], 1, 0)
        )
        pieces = partial_value.astype(bf16).reshape(pts_count, own_cols, block)
        summed = lax.all_to_all(pieces, "pts", 0, 0, tiled=False)
        resid = jnp.sum(summed.astype(f32), axis=0)
        at_pivot = (iota((block, 1), 0) == pivot_index[u][None, :]).astype(bf16)
        factor = kernel_tile(block_feats, mm(at_pivot, block_feats, 0, 0).astype(bf16))
        proj = mm(resid.astype(bf16), factor, 1, 0)
        lifted = mm(proj.astype(bf16), core[u], 1, 1).astype(bf16)
        step_bf = (resid - mm(lifted, factor, 1, 1)).astype(bf16)
        steps = lax.all_gather(step_bf, "pts", axis=0, tiled=True)
        change = mm(steps, place[u], 1, 1)
        all_steps.append(change.astype(bf16))
        current, moving = stepped(current, moving, change)
    gathered = lax.all_gather(jnp.stack(all_steps), "rows", axis=1, tiled=True)
    current, moving = coefficients, momentum
    for u in range(UPDATES):
        current, moving = stepped(current, moving, gathered[u].T.astype(f32))
    return (current, moving)


def shards(features, targets, coefficients, momentum, block_index, pivot_index, nystrom_core):
    rows, owners = lax.axis_size("rows"), lax.axis_size("pts")
    count = block_index.shape[1] // rows
    fits = rows == 4 and owners == 8 and coefficients.shape[1] == 8 * rows * owners
    fits = fits and 6 * count <= count * owners and coefficients.shape[0] % CHUNK == 0 and count % CHUNK == 0 and (3 * count // owners) % 64 == 0 and UPDATES * rows == 8
    plan = with_kernels if fits else with_operations
    return plan(
        features, targets, coefficients, momentum, block_index, pivot_index, nystrom_core
    )


def solution(mesh):
    in_specs = (P("pts", None), P("pts", None), P("pts", None), P("pts", None), P(), P(), P())
    out_specs = (P("pts", None), P("pts", None))
    return jax.shard_map(shards, mesh=mesh, in_specs=in_specs, out_specs=out_specs, check_vma=False)
```

```python
import functools
import math

import jax
import jax.numpy as jnp
from jax import lax
from jax.experimental import pallas as pl
from jax.experimental.pallas import tpu as pltpu
from jax.sharding import PartitionSpec as P

UPDATES = 2


alpha_mix = 0.6
beta_keep = 0.9
step_size = 0.2
momentum_gain = 1.5
ridge_term = 1.0

f32 = jnp.float32
bf16 = jnp.bfloat16
i32 = jnp.int32


def mm(a, b, ca, cb):
    return lax.dot_general(a, b, (((ca,), (cb,)), ((), ())), preferred_element_type=f32)


def split_two(value):
    high = value.astype(bf16)
    return high, (value - high.astype(f32)).astype(bf16)


def mixed_of(current, moving):
    return alpha_mix * moving + (1.0 - alpha_mix) * current


mix_per_step = alpha_mix * step_size * momentum_gain + (1.0 - alpha_mix) * step_size


def stepped(current, moving, change):
    mixed = mixed_of(current, moving)
    if change is None:
        return mixed, beta_keep * moving + (1.0 - beta_keep) * mixed
    return (
        mixed - step_size * change,
        beta_keep * moving + (1.0 - beta_keep) * mixed - step_size * momentum_gain * change,
    )


def iota(shape, axis):
    return lax.broadcasted_iota(i32, shape, axis)


def one_hot(chosen):
    return jnp.where(chosen, 1.0, 0.0).astype(bf16)


def before_matrix(n):
    return one_hot(iota((n, n), 0) < iota((n, n), 1))


def owners_of(groups, points, owners):
    owner_ids = iota((owners, groups[0].shape[1]), 0)
    owner = [lax.div(x, jnp.full_like(x, points)) for x in groups]
    marks = [jnp.where(owner_ids == x, 1.0, 0.0) for x in owner]
    every = jnp.concatenate(marks, axis=0).astype(bf16)
    earlier = mm(every, before_matrix(every.shape[1]), 1, 0)
    out = []
    for n, x in enumerate(owner):
        rank = jnp.sum(marks[n] * earlier[n * owners : (n + 1) * owners], axis=0, keepdims=True)
        start = jnp.sum(jnp.where(x < owner_ids, 1.0, 0.0), axis=1, keepdims=True)
        out.append((marks[n], rank, start))
    return out


def sorted_places(marks, rank, start):
    return (rank + jnp.sum(marks * start, axis=0, keepdims=True)).astype(i32)


def lane_row(column):
    n = column.shape[0]
    diagonal = iota((n, 128), 0) == iota((n, 128), 1)
    return jnp.sum(jnp.where(diagonal, column, 0.0), axis=0, keepdims=True).astype(i32)


def two_digits(*rows):
    shape = (8, rows[0].shape[1])
    value = jnp.zeros(shape, i32)
    for n, row in enumerate(rows):
        high = lax.shift_right_logical(row, jnp.full_like(row, 7))
        low = lax.bitwise_and(row, jnp.full_like(row, 127))
        value = jnp.where(iota(shape, 0) == 2 * n, high, value)
        value = jnp.where(iota(shape, 0) == 2 * n + 1, low, value)
    return value.astype(f32).astype(bf16)


def from_digits(digits):
    return (digits[0:1] * 128.0 + digits[1:2]).astype(i32)


def start_all(pairs, sems):
    copies = [pltpu.make_async_copy(a, b, sems.at[n]) for n, (a, b) in enumerate(pairs)]
    for copy in copies:
        copy.start()
    return copies


def wait_all(copies):
    for copy in copies:
        copy.wait()


def group_row(blocks, u, group, count):
    return blocks[u : u + 1, pl.ds(pl.multiple_of(group * count, count), count)]


def pack_kernel(count, cap, owners, blocks_hbm, feats_hbm, out_hbm, blocks, feats, packed, sems):
    row, me = lax.axis_index("rows"), lax.axis_index("pts")
    points = feats.shape[0]
    reads = start_all([(blocks_hbm, blocks), (feats_hbm, feats)], sems)
    before = before_matrix(count)
    reads[0].wait()
    rows = []
    for u in range(UPDATES):
        indices = group_row(blocks, u, row, count)
        local = indices - me * points
        mine = jnp.where((local >= 0) & (local < points), 1.0, 0.0)
        rank = mm(jnp.broadcast_to(mine, (8, count)).astype(bf16), before, 1, 0)[0:1]
        held = (iota((cap, count), 0) == rank.astype(i32)) & (mine > 0.0)
        point = jnp.sum(jnp.where(held, (local + 1).astype(f32), 0.0), axis=1, keepdims=True)
        rows.append(one_hot(iota((cap, points), 1) == point.astype(i32) - 1))
    reads[1].wait()
    for u in range(UPDATES):
        packed[u * cap : (u + 1) * cap, :] = mm(rows[u], feats[...], 1, 0).astype(bf16)
    wait_all(start_all([(packed, out_hbm)], sems))


def prepare_kernel(
    count, owners,
    blocks_hbm, w_hbm, z_hbm, t_hbm, coef_hbm, offset_hbm, starts_hbm,
    blocks, w, z, t, coef, offset, starts, sems, out_sems,
):
    row, me = lax.axis_index("rows"), lax.axis_index("pts")
    points, outputs = w.shape
    reads = start_all([(blocks_hbm, blocks), (w_hbm, w), (z_hbm, z), (t_hbm, t)], sems)
    reads[0].wait()
    groups = [group_row(blocks, u, row, count) for u in range(UPDATES)]
    found, shift = [], []
    for u, (_, rank, start) in enumerate(owners_of(groups, points, owners)):
        starts[u : u + 1, :] = lane_row(start)
        local = groups[u] - me * points
        mine = (local >= 0) & (local < points)
        held = jnp.where(mine, rank.astype(i32), -1)
        chosen = one_hot(iota((count // 2, count), 0) == held)
        digits = two_digits(jnp.where(mine, local + 1, 0))
        found.append(from_digits(mm(digits, chosen, 1, 1)) - 1)
        earlier = jnp.sum(jnp.where(groups[u] < me * points, 1.0, 0.0))
        shift.append(lax.rem(earlier.astype(i32), count))
    writes = start_all([(starts, starts_hbm)], out_sems)
    wait_all(reads[1:])
    current, moving = w[...], z[...]
    goal = t[...].astype(f32).T
    for u in range(UPDATES):
        mixed = mixed_of(current, moving).T
        high, low = split_two(ridge_term * mixed - goal)
        coef[u] = mixed.astype(bf16)
        place = one_hot(iota((points, count // 2), 0) == found[u])
        both = mm(jnp.concatenate([high, low], axis=0), place, 1, 0)
        held = both[:outputs] + both[outputs:]
        held = jnp.concatenate([held, jnp.zeros_like(held)], axis=1)
        offset[u] = pltpu.roll(held, shift[u], 1)
        current, moving = stepped(current, moving, None)
        for a, b in ((coef, coef_hbm), (offset, offset_hbm)):
            writes.append(pltpu.make_async_copy(a.at[u], b.at[u], out_sems.at[len(writes)]))
            writes[-1].start()
    wait_all(writes)


def put_in_order(count, points, owners, blocks, ids, came_from, starts):
    count_of = blocks.shape[1] // count
    groups = [
        blocks[u : u + 1, g * count : (g + 1) * count]
        for u in range(UPDATES)
        for g in range(count_of)
    ]
    for n, (marks, rank, start) in enumerate(owners_of(groups, points, owners)):
        place = sorted_places(marks, rank, start)
        given = iota((1, count), 1) + (n % count_of) * count
        digits = two_digits(groups[n], given)
        moved = mm(digits, one_hot(iota((count, count), 0) == place), 1, 1)
        ids[n : n + 1, :] = from_digits(moved[0:2])
        came_from[n : n + 1, :] = from_digits(moved[2:4])
        starts[n : n + 1, :] = lane_row(start)


def slots_kernel(count, points, cap, blocks_hbm, slots_hbm, blocks, slots, sems):
    me = lax.axis_index("pts")
    wait_all(start_all([(blocks_hbm, blocks)], sems))
    before = before_matrix(count)
    groups = blocks.shape[1] // count
    for u in range(UPDATES):
        found = jnp.zeros((8, groups * cap), f32)
        for g in range(groups):
            local = blocks[u : u + 1, g * count : (g + 1) * count] - me * points
            mine = (local >= 0) & (local < points)
            counts = jnp.where(mine, 1.0, 0.0)
            rank = mm(jnp.broadcast_to(counts, (8, count)).astype(bf16), before, 1, 0)[0:1]
            held = jnp.where(mine, rank.astype(i32) + g * cap, -1)
            chosen = one_hot(iota((groups * cap, count), 0) == held)
            found += mm(two_digits(jnp.where(mine, local + 1, 0)), chosen, 1, 1)
        slots[u : u + 1, :] = from_digits(found) - 1
    wait_all(start_all([(slots, slots_hbm)], sems))


def column_of(row):
    return jnp.broadcast_to(row.astype(f32), (8, row.shape[1])).T[:, 0:1]


def extended(rows, axis, first):
    rest = -0.5 * jnp.sum(jnp.square(rows.astype(f32)), axis=axis, keepdims=True)
    parts = []
    for _ in range(3):
        parts.append(rest.astype(bf16).astype(f32))
        rest = rest - parts[-1]
    parts = parts + [1.0] * 3 if first else [1.0] * 3 + parts
    at = iota(rows.shape, axis)
    extra = jnp.zeros(rows.shape, f32)
    for n, part in enumerate(parts):
        extra = jnp.where(at == n, part, extra)
    return jnp.concatenate([rows.astype(bf16), extra.astype(bf16)], axis=axis)


def exponent(left, right):
    return mm(left, right, 1, 0) * (7.0 / (left.shape[1] // 2) * math.log2(math.e))


CHUNK = 256


def compact_kernel(*refs):
    *came_hbm, starts_hbm, block_hbm, came, starts, wide, block, sems, out_sems = refs
    me = lax.axis_index("pts")
    owners, deep, _ = came.shape
    cap = deep // UPDATES
    count = block.shape[2]
    pairs = [(a, came.at[k]) for k, a in enumerate(came_hbm)]
    wait_all(start_all([*pairs, (starts_hbm, starts)], sems))
    writes = []
    for u in range(UPDATES):
        for o in range(owners):
            start = starts[u, o]
            rows = came[lax.bitwise_xor(me, o), u * cap : (u + 1) * cap, :]
            wide[u, pl.ds(start, cap), :] = rows.astype(f32)
        block[u] = wide[u, 0:count, :].T.astype(bf16)
        writes += start_all([(block.at[u], block_hbm.at[u])], out_sems.at[u : u + 1])
    wait_all(writes)


def sums_kernel(
    owners,
    block_hbm, feats_hbm, blocks_hbm, coef_hbm, offset_hbm,
    pieces_hbm, ids_hbm, from_hbm, starts_hbm,
    block, feats, blocks, coef, offset, tile, pieces, ids, came_from, starts, sems, out_sems,
):
    outputs = coef.shape[1]
    pairs = [(block_hbm, block), (feats_hbm, feats), (blocks_hbm, blocks)]
    reads = start_all([*pairs, (coef_hbm, coef), (offset_hbm, offset)], sems)
    wait_all(reads[:3])
    put_in_order(block.shape[2], feats.shape[0], owners, blocks, ids, came_from, starts)
    pairs = [(ids, ids_hbm), (came_from, from_hbm), (starts, starts_hbm)]
    writes = start_all(pairs, out_sems)
    left = extended(feats[...], 1, True)
    for u in range(UPDATES):
        right = extended(block[u], 0, False)
        tile[...] = jnp.exp2(exponent(left, right)).astype(bf16)
        if u == 0:
            wait_all(reads[3:])
        total = offset[u] + mm(coef[u], tile[...], 1, 0)
        devices, _, lanes = pieces.shape
        own = outputs // devices
        for d in range(devices):
            part = total[d * own : (d + 1) * own]
            pieces[d, 2 * own * u : 2 * own * (u + 1), :] = jnp.concatenate(
                [part[:, :lanes], part[:, lanes:]], axis=0
            ).astype(bf16)
    wait_all(writes + start_all([(pieces, pieces_hbm)], sems))


def factors_kernel(
    b0_hbm, b1_hbm, b2_hbm, b3_hbm, ids_hbm, from_hbm, pivots_hbm, factor_hbm, cross_hbm,
    feats, ids, came_from, pivots, factor, cross, sems,
):
    row = lax.axis_index("rows")
    groups, _, width, count = feats.shape
    pairs = [(b_hbm, feats.at[k]) for k, b_hbm in enumerate((b0_hbm, b1_hbm, b2_hbm, b3_hbm))]
    pairs += [(ids_hbm, ids), (from_hbm, came_from), (pivots_hbm, pivots)]
    wait_all(start_all(pairs, sems))
    places = [lax.bitwise_xor(row, k) for k in range(groups)]
    rights = [[extended(feats[k, u], 0, False) for k in range(groups)] for u in range(UPDATES)]
    for u in range(UPDATES):
        wanted = pivots[u : u + 1, :].astype(f32)
        chosen_feats = jnp.zeros((width, wanted.shape[1]), f32)
        for k in range(groups):
            here = column_of(came_from[pl.ds(u * groups + places[k], 1), :])
            chosen_feats += mm(feats[k, u], one_hot(here == wanted), 1, 0)
        left = extended(chosen_feats.T, 1, True)
        for k in range(groups):
            start = pl.multiple_of(places[k] * count, count)
            value = jnp.exp2(exponent(left, rights[u][k]))
            factor[u, :, pl.ds(start, count)] = value.astype(bf16)
    writes = start_all([(factor, factor_hbm)], sems)
    lefts, left_points = [], []
    for k in range(groups):
        lefts.append(extended(feats[k, 0].astype(f32).T, 1, True))
        left_points.append(column_of(ids[pl.ds(places[k], 1), :]))
    left, left_points = jnp.concatenate(lefts, axis=0), jnp.concatenate(left_points, axis=0)
    sent = 1
    for m in range(groups):
        right_points = ids[pl.ds(groups + places[m], 1), :].astype(f32)
        power = exponent(left, rights[1][m])
        power = jnp.where(left_points == right_points, math.log2(1.0 + ridge_term), power)
        cross[m] = jnp.exp2(power).astype(bf16).reshape(groups, count, count)
        for k in range(groups):
            start = pl.multiple_of(places[k] * count, count)
            copy = pltpu.make_async_copy(
                cross.at[m, k], cross_hbm.at[places[m], pl.ds(start, count), :], sems.at[sent]
            )
            copy.start()
            writes.append(copy)
            sent += 1
    wait_all(writes)


def chain_kernel(
    cap, owners,
    summed_hbm, factor_hbm, core_hbm, cross_hbm, starts_hbm, out_hbm,
    summed, factor, core, cross, starts, packed, sems,
):
    groups, _, count = cross.shape
    own = summed.shape[1] // (2 * UPDATES)
    pairs = [(summed_hbm, summed)]
    for u in range(UPDATES):
        pairs += [(factor_hbm.at[u], factor.at[u]), (core_hbm.at[u], core.at[u])]
        if u == 0:
            pairs += [(starts_hbm, starts)]
            pairs += [(cross_hbm.at[g], cross.at[g]) for g in range(groups)]
    reads = start_all(pairs, sems)
    first, *reads = reads
    first.wait()
    step = None
    for u in range(UPDATES):
        sums = []
        for g in range(groups):
            part = summed[g * owners, 2 * own * u : 2 * own * (u + 1), :].astype(f32)
            for o in range(1, owners):
                part += summed[g * owners + o, 2 * own * u : 2 * own * (u + 1), :].astype(f32)
            part = jnp.concatenate([part[:own], part[own:]], axis=1)
            if u:
                reads[3 + g].wait()
                part -= mix_per_step * mm(step, cross[g], 1, 0)
            sums.append(part)
        resid = jnp.concatenate(sums, axis=1)
        wait_all(reads[0:3] if u == 0 else reads[3 + groups :])
        proj = mm(resid.astype(bf16), factor[u], 1, 1)
        lifted = mm(proj.astype(bf16), core[u], 1, 1).astype(bf16)
        step = (resid - mm(lifted, factor[u], 1, 0)).astype(bf16)
        half = groups // 2
        for o in range(owners):
            lanes = []
            for g in range(groups):
                part = step[:, g * count : (g + 1) * count].astype(f32)
                back = lax.rem(count - starts[u * groups + g, o], count)
                lanes.append(pltpu.roll(part, back, 1)[:, :cap])
            packed[o, 2 * own * u : 2 * own * (u + 1), :] = jnp.concatenate(
                [jnp.concatenate(lanes[h * half : (h + 1) * half], axis=1) for h in range(2)], axis=0
            ).astype(bf16)
    wait_all(start_all([(packed, out_hbm)], sems))


def finish_kernel(
    g0_hbm, g1_hbm, g2_hbm, g3_hbm, slots_hbm, w_hbm, z_hbm, w_out, z_out,
    got, slots, w, z, steps, w_new, z_new, sems, out_sems,
):
    row = lax.axis_index("rows")
    points = w.shape[0]
    sources, deep, lanes = got.shape
    own = deep // (2 * UPDATES)
    chunks = range(0, points, CHUNK)
    pairs = [(slots_hbm, slots)]
    for k, g_hbm in enumerate((g0_hbm, g1_hbm, g2_hbm, g3_hbm)):
        size = g_hbm.shape[0]
        first = pl.multiple_of(lax.bitwise_xor(row, k) * size, size)
        pairs.append((g_hbm, got.at[pl.ds(first, size)]))
    for c in chunks:
        part = slice(c, c + CHUNK)
        pairs += [(w_hbm.at[part], w.at[part]), (z_hbm.at[part], z.at[part])]
    reads = start_all(pairs, sems)
    wait_all(reads[:5])
    reads = reads[5:]
    wide = got[...].astype(f32)
    for u in range(UPDATES):
        for h in range(2):
            first = own * (2 * u + h)
            part = wide[:, first : first + own, :].reshape(sources * own, lanes)
            steps[u, :, h * lanes : (h + 1) * lanes] = part.astype(bf16)
    changes = []
    for u in range(UPDATES):
        rows = one_hot(iota((points, slots.shape[1]), 0) == slots[u : u + 1, :])
        changes.append(mm(rows, steps[u], 1, 1))
    writes = []
    for n, c in enumerate(chunks):
        part = slice(c, c + CHUNK)
        wait_all(reads[2 * n : 2 * n + 2])
        current, moving = w[part, :], z[part, :]
        for change in changes:
            current, moving = stepped(current, moving, change[part])
        w_new[part, :] = current
        z_new[part, :] = moving
        for m, (a, b) in enumerate(((w_new, w_out), (z_new, z_out))):
            copy = pltpu.make_async_copy(a.at[part], b.at[part], out_sems.at[2 * n + m])
            copy.start()
            writes.append(copy)
    wait_all(writes)


VMEM = pl.BlockSpec(memory_space=pltpu.VMEM)
HBM = pl.BlockSpec(memory_space=pltpu.HBM)
in_smem = type(pltpu.SMEM((1,), i32))


def like(shape, dtype=bf16):
    return jax.ShapeDtypeStruct(shape, dtype)


def call(body, outs, inside, *args, near=0, sems=(), flops=0, grant=63.9):
    moved = sum(math.prod(o.shape) * o.dtype.itemsize for o in [*outs, *args])
    return pl.pallas_call(
        body,
        out_shape=outs,
        in_specs=[VMEM] * near + [HBM] * (len(args) - near),
        out_specs=[HBM] * len(outs),
        scratch_shapes=[
            x if isinstance(x, in_smem) else pltpu.VMEM(x.shape, x.dtype) for x in inside
        ]
        + [pltpu.SemaphoreType.DMA((n,)) for n in sems],
        compiler_params=pltpu.CompilerParams(vmem_limit_bytes=int(grant * 2**20)),
        cost_estimate=pl.CostEstimate(flops=int(flops), bytes_accessed=moved, transcendentals=0),
    )(*args)


def swap(value, axis, k):
    return lax.ppermute(value, axis, [(i, i ^ k) for i in range(lax.axis_size(axis))])


def with_kernels(features, targets, coefficients, momentum, block_index, pivot_index, core):
    rows, owners = lax.axis_size("rows"), lax.axis_size("pts")
    points, width = features.shape
    block = block_index.shape[1]
    rank = pivot_index.shape[1]
    outputs = coefficients.shape[1]
    count = block // rows
    cap = 3 * count // owners
    devices = rows * owners
    own = outputs // devices
    deep = 2 * own * UPDATES
    half = rows // 2
    wide = like(coefficients.shape, f32)

    (packed,) = call(
        functools.partial(pack_kernel, count, cap, owners),
        [like((UPDATES * cap, width))],
        [block_index, features, like((UPDATES * cap, width))],
        block_index,
        features,
        sems=(2,),
    )
    came = {k: swap(packed, "pts", k) for k in (6, 5, 4, 2, 1)}
    came[2], came[6], first_index = lax.optimization_barrier((came[2], came[6], block_index))
    came[3], came[7] = swap(came[2], "pts", 1), swap(came[6], "pts", 1)
    kept = [
        like((UPDATES, outputs, points)),
        like((UPDATES, outputs, count), f32),
        like((8, 128), i32),
    ]
    given = [first_index, coefficients, momentum, targets]
    coef, offset, row_starts = call(
        functools.partial(prepare_kernel, count, owners),
        kept,
        given + kept,
        *given,
        sems=(4, 1 + 2 * UPDATES),
    )
    feats = like((UPDATES, width, count))
    inside_starts = pltpu.SMEM(row_starts.shape, i32)
    (mine,) = call(
        compact_kernel,
        [feats],
        [
            like((owners, *packed.shape)),
            inside_starts,
            like((UPDATES, count + cap, width), f32),
            feats,
        ],
        packed,
        *[came[k] for k in range(1, owners)],
        row_starts,
        sems=(owners + 1, UPDATES),
    )
    beside, across = swap(mine, "rows", 1), swap(mine, "rows", 2)
    kept = [
        like((devices, deep, count // 2)),
        like((UPDATES * rows, count), i32),
        like((UPDATES * rows, count), i32),
        like((8, 128), i32),
    ]
    given = [mine, features, block_index, coef, offset]
    pieces, ids, came_from, starts = call(
        functools.partial(sums_kernel, owners),
        kept,
        [*given, like((points, count)), *kept],
        *given,
        sems=(5, 3),
        flops=2.0 * UPDATES * points * count * (2 * width + outputs),
    )
    pieces, beside, across = lax.optimization_barrier((pieces, beside, across))
    summed = lax.all_to_all(pieces, ("rows", "pts"), 0, 0, tiled=True)
    kept = [like((UPDATES, rank, block)), like((rows, block, count))]
    factor, cross = call(
        factors_kernel,
        kept,
        [
            like((rows, *feats.shape)),
            ids,
            came_from,
            pivot_index,
            kept[0],
            like((rows, rows, count, count)),
        ],
        mine,
        beside,
        across,
        swap(across, "rows", 1),
        ids,
        came_from,
        pivot_index,
        sems=(rows * rows + 2,),
        flops=2.0 * width * block * (UPDATES * rank + block),
    )
    pieces = like((owners, deep, half * cap))
    (steps,) = call(
        functools.partial(chain_kernel, cap, owners),
        [pieces],
        [summed, factor, core, cross, inside_starts, pieces],
        summed,
        factor,
        core,
        cross,
        starts,
        sems=(2 * UPDATES + 3 + rows,),
    )
    got = lax.all_to_all(steps, "pts", 0, 0, tiled=True)
    got, later_index = lax.optimization_barrier((got, block_index))
    beside, across = swap(got, "rows", 1), swap(got, "rows", 2)
    (slots,) = call(
        functools.partial(slots_kernel, count, points, cap),
        [like((UPDATES, rows * cap), i32)],
        [block_index, like((UPDATES, rows * cap), i32)],
        later_index,
        sems=(1,),
    )
    across, slots = lax.optimization_barrier((across, slots))
    parts = points // CHUNK
    return call(
        finish_kernel,
        [wide] * 2,
        [
            like((devices, deep, half * cap)),
            slots,
            wide,
            wide,
            like((UPDATES, outputs, rows * cap)),
            wide,
            wide,
        ],
        got,
        beside,
        across,
        swap(across, "rows", 1),
        slots,
        coefficients,
        momentum,
        sems=(1 + rows + 2 * parts, 2 * parts),
    )


def kernel_tile(left_rows, right_rows):
    inner_prod = mm(left_rows, right_rows, 1, 1)
    left_sq = jnp.sum(jnp.square(left_rows.astype(f32)), axis=1)
    right_sq = jnp.sum(jnp.square(right_rows.astype(f32)), axis=1)
    squared = left_sq[:, None] + right_sq[None, :] - 2.0 * inner_prod
    return jnp.exp(squared * (-3.5 / left_rows.shape[1])).astype(bf16)


def with_operations(features, targets, coefficients, momentum, block_index, pivot_index, core):
    row_count, pts_count = lax.axis_size("rows"), lax.axis_size("pts")
    row_id, pts_id = lax.axis_index("rows"), lax.axis_index("pts")
    points = features.shape[0]
    block = block_index.shape[1]
    outputs = coefficients.shape[1]
    per_row = block // row_count
    per_device = per_row // pts_count
    row_cols = outputs // row_count
    own_cols = row_cols // pts_count
    first = row_id * row_cols
    current, moving, goal = (
        lax.dynamic_slice_in_dim(value, first, row_cols, axis=1).T.astype(f32)
        for value in (coefficients, momentum, targets)
    )
    ids = iota((points, 1), 0) + pts_id * points
    place = [(ids == block_index[u][None, :]).astype(bf16) for u in range(UPDATES)]
    own_rows = []
    for u in range(UPDATES):
        mine = lax.dynamic_slice_in_dim(place[u], row_id * per_row, per_row, axis=1)
        own_rows.append(mm(mine, features, 0, 0).astype(bf16).reshape(pts_count, per_device, -1))
    came = lax.all_to_all(jnp.concatenate(own_rows, axis=1), "pts", 0, 0, tiled=False)
    chunk = jnp.sum(came.astype(f32), axis=0).astype(bf16)
    spread = lax.all_gather(lax.all_gather(chunk, "pts", axis=0), "rows", axis=0)
    spread = spread.reshape(row_count, pts_count, UPDATES, per_device, features.shape[1])
    all_steps = []
    for u in range(UPDATES):
        block_feats = spread[:, :, u].reshape(block, features.shape[1])
        mixed = mixed_of(current, moving)
        high, low = split_two(ridge_term * mixed - goal)
        tile = kernel_tile(features, block_feats)
        partial_value = (
            mm(mixed.astype(bf16), tile, 1, 0) + mm(high, place[u], 1, 0) + mm(low, place[u], 1, 0)
        )
        pieces = partial_value.astype(bf16).reshape(pts_count, own_cols, block)
        summed = lax.all_to_all(pieces, "pts", 0, 0, tiled=False)
        resid = jnp.sum(summed.astype(f32), axis=0)
        at_pivot = (iota((block, 1), 0) == pivot_index[u][None, :]).astype(bf16)
        factor = kernel_tile(block_feats, mm(at_pivot, block_feats, 0, 0).astype(bf16))
        proj = mm(resid.astype(bf16), factor, 1, 0)
        lifted = mm(proj.astype(bf16), core[u], 1, 1).astype(bf16)
        step_bf = (resid - mm(lifted, factor, 1, 1)).astype(bf16)
        steps = lax.all_gather(step_bf, "pts", axis=0, tiled=True)
        change = mm(steps, place[u], 1, 1)
        all_steps.append(change.astype(bf16))
        current, moving = stepped(current, moving, change)
    gathered = lax.all_gather(jnp.stack(all_steps), "rows", axis=1, tiled=True)
    current, moving = coefficients, momentum
    for u in range(UPDATES):
        current, moving = stepped(current, moving, gathered[u].T.astype(f32))
    return (current, moving)


def shards(features, targets, coefficients, momentum, block_index, pivot_index, nystrom_core):
    rows, owners = lax.axis_size("rows"), lax.axis_size("pts")
    count = block_index.shape[1] // rows
    fits = rows == 4 and owners == 8 and coefficients.shape[1] == 8 * rows * owners
    fits = fits and 6 * count <= count * owners and coefficients.shape[0] % CHUNK == 0 and count % CHUNK == 0 and (3 * count // owners) % 64 == 0 and UPDATES * rows == 8
    plan = with_kernels if fits else with_operations
    return plan(
        features, targets, coefficients, momentum, block_index, pivot_index, nystrom_core
    )


def solution(mesh):
    in_specs = (P("pts", None), P("pts", None), P("pts", None), P("pts", None), P(), P(), P())
    out_specs = (P("pts", None), P("pts", None))
    return jax.shard_map(shards, mesh=mesh, in_specs=in_specs, out_specs=out_specs, check_vma=False)
```

```python
import functools
import math

import jax
import jax.numpy as jnp
from jax import lax
from jax.experimental import pallas as pl
from jax.experimental.pallas import tpu as pltpu
from jax.sharding import PartitionSpec as P

UPDATES = 2


alpha_mix = 0.6
beta_keep = 0.9
step_size = 0.2
momentum_gain = 1.5
ridge_term = 1.0

f32 = jnp.float32
bf16 = jnp.bfloat16
i32 = jnp.int32


def mm(a, b, ca, cb):
    return lax.dot_general(a, b, (((ca,), (cb,)), ((), ())), preferred_element_type=f32)


def split_two(value):
    high = value.astype(bf16)
    return high, (value - high.astype(f32)).astype(bf16)


def mixed_of(current, moving):
    return alpha_mix * moving + (1.0 - alpha_mix) * current


mix_per_step = alpha_mix * step_size * momentum_gain + (1.0 - alpha_mix) * step_size


def stepped(current, moving, change):
    mixed = mixed_of(current, moving)
    if change is None:
        return mixed, beta_keep * moving + (1.0 - beta_keep) * mixed
    return (
        mixed - step_size * change,
        beta_keep * moving + (1.0 - beta_keep) * mixed - step_size * momentum_gain * change,
    )


def iota(shape, axis):
    return lax.broadcasted_iota(i32, shape, axis)


def one_hot(chosen):
    return jnp.where(chosen, 1.0, 0.0).astype(bf16)


def before_matrix(n):
    return one_hot(iota((n, n), 0) < iota((n, n), 1))


def owners_of(groups, points, owners):
    owner_ids = iota((owners, groups[0].shape[1]), 0)
    owner = [lax.div(x, jnp.full_like(x, points)) for x in groups]
    marks = [jnp.where(owner_ids == x, 1.0, 0.0) for x in owner]
    every = jnp.concatenate(marks, axis=0).astype(bf16)
    earlier = mm(every, before_matrix(every.shape[1]), 1, 0)
    out = []
    for n, x in enumerate(owner):
        rank = jnp.sum(marks[n] * earlier[n * owners : (n + 1) * owners], axis=0, keepdims=True)
        start = jnp.sum(jnp.where(x < owner_ids, 1.0, 0.0), axis=1, keepdims=True)
        out.append((marks[n], rank, start))
    return out


def sorted_places(marks, rank, start):
    return (rank + jnp.sum(marks * start, axis=0, keepdims=True)).astype(i32)


def lane_row(column):
    n = column.shape[0]
    diagonal = iota((n, 128), 0) == iota((n, 128), 1)
    return jnp.sum(jnp.where(diagonal, column, 0.0), axis=0, keepdims=True).astype(i32)


def two_digits(*rows):
    shape = (8, rows[0].shape[1])
    value = jnp.zeros(shape, i32)
    for n, row in enumerate(rows):
        high = lax.shift_right_logical(row, jnp.full_like(row, 7))
        low = lax.bitwise_and(row, jnp.full_like(row, 127))
        value = jnp.where(iota(shape, 0) == 2 * n, high, value)
        value = jnp.where(iota(shape, 0) == 2 * n + 1, low, value)
    return value.astype(f32).astype(bf16)


def from_digits(digits):
    return (digits[0:1] * 128.0 + digits[1:2]).astype(i32)


def start_all(pairs, sems):
    copies = [pltpu.make_async_copy(a, b, sems.at[n]) for n, (a, b) in enumerate(pairs)]
    for copy in copies:
        copy.start()
    return copies


def wait_all(copies):
    for copy in copies:
        copy.wait()


def group_row(blocks, u, group, count):
    return blocks[u : u + 1, pl.ds(pl.multiple_of(group * count, count), count)]


def pack_kernel(count, cap, owners, blocks_hbm, feats_hbm, out_hbm, blocks, feats, packed, sems):
    row, me = lax.axis_index("rows"), lax.axis_index("pts")
    points = feats.shape[0]
    reads = start_all([(blocks_hbm, blocks), (feats_hbm, feats)], sems)
    before = before_matrix(count)
    reads[0].wait()
    rows = []
    for u in range(UPDATES):
        indices = group_row(blocks, u, row, count)
        local = indices - me * points
        mine = jnp.where((local >= 0) & (local < points), 1.0, 0.0)
        rank = mm(jnp.broadcast_to(mine, (8, count)).astype(bf16), before, 1, 0)[0:1]
        held = (iota((cap, count), 0) == rank.astype(i32)) & (mine > 0.0)
        point = jnp.sum(jnp.where(held, (local + 1).astype(f32), 0.0), axis=1, keepdims=True)
        rows.append(one_hot(iota((cap, points), 1) == point.astype(i32) - 1))
    reads[1].wait()
    for u in range(UPDATES):
        packed[u * cap : (u + 1) * cap, :] = mm(rows[u], feats[...], 1, 0).astype(bf16)
    wait_all(start_all([(packed, out_hbm)], sems))


def prepare_kernel(
    count, owners,
    blocks_hbm, w_hbm, z_hbm, t_hbm, coef_hbm, offset_hbm, starts_hbm,
    blocks, w, z, t, coef, offset, starts, sems, out_sems,
):
    row, me = lax.axis_index("rows"), lax.axis_index("pts")
    points, outputs = w.shape
    reads = start_all([(blocks_hbm, blocks), (w_hbm, w), (z_hbm, z), (t_hbm, t)], sems)
    reads[0].wait()
    groups = [group_row(blocks, u, row, count) for u in range(UPDATES)]
    found, shift = [], []
    for u, (_, rank, start) in enumerate(owners_of(groups, points, owners)):
        starts[u : u + 1, :] = lane_row(start)
        local = groups[u] - me * points
        mine = (local >= 0) & (local < points)
        held = jnp.where(mine, rank.astype(i32), -1)
        chosen = one_hot(iota((count // 2, count), 0) == held)
        digits = two_digits(jnp.where(mine, local + 1, 0))
        found.append(from_digits(mm(digits, chosen, 1, 1)) - 1)
        earlier = jnp.sum(jnp.where(groups[u] < me * points, 1.0, 0.0))
        shift.append(lax.rem(earlier.astype(i32), count))
    writes = start_all([(starts, starts_hbm)], out_sems)
    wait_all(reads[1:])
    current, moving = w[...], z[...]
    goal = t[...].astype(f32).T
    for u in range(UPDATES):
        mixed = mixed_of(current, moving).T
        high, low = split_two(ridge_term * mixed - goal)
        coef[u] = mixed.astype(bf16)
        place = one_hot(iota((points, count // 2), 0) == found[u])
        both = mm(jnp.concatenate([high, low], axis=0), place, 1, 0)
        held = both[:outputs] + both[outputs:]
        held = jnp.concatenate([held, jnp.zeros_like(held)], axis=1)
        offset[u] = pltpu.roll(held, shift[u], 1)
        current, moving = stepped(current, moving, None)
        for a, b in ((coef, coef_hbm), (offset, offset_hbm)):
            writes.append(pltpu.make_async_copy(a.at[u], b.at[u], out_sems.at[len(writes)]))
            writes[-1].start()
    wait_all(writes)


def put_in_order(count, points, owners, blocks, ids, came_from, starts):
    count_of = blocks.shape[1] // count
    groups = [
        blocks[u : u + 1, g * count : (g + 1) * count]
        for u in range(UPDATES)
        for g in range(count_of)
    ]
    for n, (marks, rank, start) in enumerate(owners_of(groups, points, owners)):
        place = sorted_places(marks, rank, start)
        given = iota((1, count), 1) + (n % count_of) * count
        digits = two_digits(groups[n], given)
        moved = mm(digits, one_hot(iota((count, count), 0) == place), 1, 1)
        ids[n : n + 1, :] = from_digits(moved[0:2])
        came_from[n : n + 1, :] = from_digits(moved[2:4])
        starts[n : n + 1, :] = lane_row(start)


def slots_kernel(count, points, cap, blocks_hbm, slots_hbm, blocks, slots, sems):
    me = lax.axis_index("pts")
    wait_all(start_all([(blocks_hbm, blocks)], sems))
    before = before_matrix(count)
    groups = blocks.shape[1] // count
    for u in range(UPDATES):
        found = jnp.zeros((8, groups * cap), f32)
        for g in range(groups):
            local = blocks[u : u + 1, g * count : (g + 1) * count] - me * points
            mine = (local >= 0) & (local < points)
            counts = jnp.where(mine, 1.0, 0.0)
            rank = mm(jnp.broadcast_to(counts, (8, count)).astype(bf16), before, 1, 0)[0:1]
            held = jnp.where(mine, rank.astype(i32) + g * cap, -1)
            chosen = one_hot(iota((groups * cap, count), 0) == held)
            found += mm(two_digits(jnp.where(mine, local + 1, 0)), chosen, 1, 1)
        slots[u : u + 1, :] = from_digits(found) - 1
    wait_all(start_all([(slots, slots_hbm)], sems))


def column_of(row):
    return jnp.broadcast_to(row.astype(f32), (8, row.shape[1])).T[:, 0:1]


def extended(rows, axis, first):
    rest = -0.5 * jnp.sum(jnp.square(rows.astype(f32)), axis=axis, keepdims=True)
    parts = []
    for _ in range(3):
        parts.append(rest.astype(bf16).astype(f32))
        rest = rest - parts[-1]
    parts = parts + [1.0] * 3 if first else [1.0] * 3 + parts
    at = iota(rows.shape, axis)
    extra = jnp.zeros(rows.shape, f32)
    for n, part in enumerate(parts):
        extra = jnp.where(at == n, part, extra)
    return jnp.concatenate([rows.astype(bf16), extra.astype(bf16)], axis=axis)


def exponent(left, right):
    return mm(left, right, 1, 0) * (7.0 / (left.shape[1] // 2) * math.log2(math.e))


CHUNK = 256


def compact_kernel(*refs):
    *came_hbm, starts_hbm, block_hbm, came, starts, wide, block, sems = refs
    me = lax.axis_index("pts")
    owners, deep, _ = came.shape
    cap = deep // UPDATES
    count = block.shape[2]
    pairs = [(a, came.at[k]) for k, a in enumerate(came_hbm)]
    wait_all(start_all([*pairs, (starts_hbm, starts)], sems))
    for u in range(UPDATES):
        for o in range(owners):
            start = starts[u, o]
            rows = came[lax.bitwise_xor(me, o), u * cap : (u + 1) * cap, :]
            wide[u, pl.ds(start, cap), :] = rows.astype(f32)
        block[u] = wide[u, 0:count, :].T.astype(bf16)
    wait_all(start_all([(block, block_hbm)], sems))


def sums_kernel(
    owners,
    block_hbm, feats_hbm, blocks_hbm, coef_hbm, offset_hbm,
    pieces_hbm, ids_hbm, from_hbm, starts_hbm,
    block, feats, blocks, coef, offset, tile, pieces, ids, came_from, starts, sems, out_sems,
):
    outputs = coef.shape[1]
    pairs = [(block_hbm, block), (feats_hbm, feats), (blocks_hbm, blocks)]
    reads = start_all([*pairs, (coef_hbm, coef), (offset_hbm, offset)], sems)
    wait_all(reads[:3])
    put_in_order(block.shape[2], feats.shape[0], owners, blocks, ids, came_from, starts)
    pairs = [(ids, ids_hbm), (came_from, from_hbm), (starts, starts_hbm)]
    writes = start_all(pairs, out_sems)
    left = extended(feats[...], 1, True)
    for u in range(UPDATES):
        right = extended(block[u], 0, False)
        tile[...] = jnp.exp2(exponent(left, right)).astype(bf16)
        if u == 0:
            wait_all(reads[3:])
        total = offset[u] + mm(coef[u], tile[...], 1, 0)
        devices, _, lanes = pieces.shape
        own = outputs // devices
        for d in range(devices):
            part = total[d * own : (d + 1) * own]
            place = d % owners * (devices // owners) + d // owners
            pieces[place, 2 * own * u : 2 * own * (u + 1), :] = jnp.concatenate(
                [part[:, :lanes], part[:, lanes:]], axis=0
            ).astype(bf16)
    wait_all(writes + start_all([(pieces, pieces_hbm)], sems))


def factors_kernel(
    b0_hbm, b1_hbm, b2_hbm, b3_hbm, ids_hbm, from_hbm, pivots_hbm, factor_hbm, cross_hbm,
    feats, ids, came_from, pivots, factor, cross, sems,
):
    row = lax.axis_index("rows")
    groups, _, width, count = feats.shape
    pairs = [(b_hbm, feats.at[k]) for k, b_hbm in enumerate((b0_hbm, b1_hbm, b2_hbm, b3_hbm))]
    pairs += [(ids_hbm, ids), (from_hbm, came_from), (pivots_hbm, pivots)]
    wait_all(start_all(pairs, sems))
    places = [lax.bitwise_xor(row, k) for k in range(groups)]
    rights = [[extended(feats[k, u], 0, False) for k in range(groups)] for u in range(UPDATES)]
    for u in range(UPDATES):
        wanted = pivots[u : u + 1, :].astype(f32)
        chosen_feats = jnp.zeros((width, wanted.shape[1]), f32)
        for k in range(groups):
            here = column_of(came_from[pl.ds(u * groups + places[k], 1), :])
            chosen_feats += mm(feats[k, u], one_hot(here == wanted), 1, 0)
        left = extended(chosen_feats.T, 1, True)
        for k in range(groups):
            start = pl.multiple_of(places[k] * count, count)
            value = jnp.exp2(exponent(left, rights[u][k]))
            factor[u, :, pl.ds(start, count)] = value.astype(bf16)
    writes = start_all([(factor, factor_hbm)], sems)
    lefts, left_points = [], []
    for k in range(groups):
        lefts.append(extended(feats[k, 0].astype(f32).T, 1, True))
        left_points.append(column_of(ids[pl.ds(places[k], 1), :]))
    left, left_points = jnp.concatenate(lefts, axis=0), jnp.concatenate(left_points, axis=0)
    sent = 1
    for m in range(groups):
        right_points = ids[pl.ds(groups + places[m], 1), :].astype(f32)
        power = exponent(left, rights[1][m])
        power = jnp.where(left_points == right_points, math.log2(1.0 + ridge_term), power)
        cross[m] = jnp.exp2(power).astype(bf16).reshape(groups, count, count)
        for k in range(groups):
            start = pl.multiple_of(places[k] * count, count)
            copy = pltpu.make_async_copy(
                cross.at[m, k], cross_hbm.at[places[m], pl.ds(start, count), :], sems.at[sent]
            )
            copy.start()
            writes.append(copy)
            sent += 1
    wait_all(writes)


def chain_kernel(
    cap, owners,
    summed_hbm, factor_hbm, core_hbm, cross_hbm, starts_hbm, out_hbm,
    summed, factor, core, cross, starts, packed, sems,
):
    groups, _, count = cross.shape
    own = summed.shape[1] // (2 * UPDATES)
    pairs = [(summed_hbm, summed)]
    for u in range(UPDATES):
        pairs += [(factor_hbm.at[u], factor.at[u]), (core_hbm.at[u], core.at[u])]
        if u == 0:
            pairs += [(starts_hbm, starts)]
            pairs += [(cross_hbm.at[g], cross.at[g]) for g in range(groups)]
    reads = start_all(pairs, sems)
    first, *reads = reads
    first.wait()
    step = None
    for u in range(UPDATES):
        sums = []
        for g in range(groups):
            part = summed[g, 2 * own * u : 2 * own * (u + 1), :].astype(f32)
            for o in range(1, owners):
                part += summed[o * groups + g, 2 * own * u : 2 * own * (u + 1), :].astype(f32)
            part = jnp.concatenate([part[:own], part[own:]], axis=1)
            if u:
                reads[3 + g].wait()
                part -= mix_per_step * mm(step, cross[g], 1, 0)
            sums.append(part)
        resid = jnp.concatenate(sums, axis=1)
        wait_all(reads[0:3] if u == 0 else reads[3 + groups :])
        proj = mm(resid.astype(bf16), factor[u], 1, 1)
        lifted = mm(proj.astype(bf16), core[u], 1, 1).astype(bf16)
        step = (resid - mm(lifted, factor[u], 1, 0)).astype(bf16)
        half = groups // 2
        for o in range(owners):
            lanes = []
            for g in range(groups):
                part = step[:, g * count : (g + 1) * count].astype(f32)
                back = lax.rem(count - starts[u * groups + g, o], count)
                lanes.append(pltpu.roll(part, back, 1)[:, :cap])
            packed[o, 2 * own * u : 2 * own * (u + 1), :] = jnp.concatenate(
                [jnp.concatenate(lanes[h * half : (h + 1) * half], axis=1) for h in range(2)], axis=0
            ).astype(bf16)
    wait_all(start_all([(packed, out_hbm)], sems))


def finish_kernel(
    g0_hbm, g1_hbm, g2_hbm, g3_hbm, slots_hbm, w_hbm, z_hbm, w_out, z_out,
    got, slots, w, z, steps, w_new, z_new, sems, out_sems,
):
    row = lax.axis_index("rows")
    points = w.shape[0]
    sources, deep, lanes = got.shape
    own = deep // (2 * UPDATES)
    chunks = range(0, points, CHUNK)
    pairs = [(slots_hbm, slots)]
    for k, g_hbm in enumerate((g0_hbm, g1_hbm, g2_hbm, g3_hbm)):
        size = g_hbm.shape[0]
        first = pl.multiple_of(lax.bitwise_xor(row, k) * size, size)
        pairs.append((g_hbm, got.at[pl.ds(first, size)]))
    for c in chunks:
        part = slice(c, c + CHUNK)
        pairs += [(w_hbm.at[part], w.at[part]), (z_hbm.at[part], z.at[part])]
    reads = start_all(pairs, sems)
    wait_all(reads[:5])
    reads = reads[5:]
    wide = got[...].astype(f32)
    for u in range(UPDATES):
        for h in range(2):
            first = own * (2 * u + h)
            part = wide[:, first : first + own, :].reshape(sources * own, lanes)
            steps[u, h * lanes : (h + 1) * lanes, :] = part.T.astype(bf16)
    changes = []
    for u in range(UPDATES):
        rows = one_hot(iota((points, slots.shape[1]), 0) == slots[u : u + 1, :])
        changes.append(mm(rows, steps[u], 1, 0))
    writes = []
    for n, c in enumerate(chunks):
        part = slice(c, c + CHUNK)
        wait_all(reads[2 * n : 2 * n + 2])
        current, moving = w[part, :], z[part, :]
        for change in changes:
            current, moving = stepped(current, moving, change[part])
        w_new[part, :] = current
        z_new[part, :] = moving
        for m, (a, b) in enumerate(((w_new, w_out), (z_new, z_out))):
            copy = pltpu.make_async_copy(a.at[part], b.at[part], out_sems.at[2 * n + m])
            copy.start()
            writes.append(copy)
    wait_all(writes)


VMEM = pl.BlockSpec(memory_space=pltpu.VMEM)
HBM = pl.BlockSpec(memory_space=pltpu.HBM)
in_smem = type(pltpu.SMEM((1,), i32))


def like(shape, dtype=bf16):
    return jax.ShapeDtypeStruct(shape, dtype)


def call(body, outs, inside, *args, near=0, sems=(), flops=0, grant=63.9):
    moved = sum(math.prod(o.shape) * o.dtype.itemsize for o in [*outs, *args])
    return pl.pallas_call(
        body,
        out_shape=outs,
        in_specs=[VMEM] * near + [HBM] * (len(args) - near),
        out_specs=[HBM] * len(outs),
        scratch_shapes=[
            x if isinstance(x, in_smem) else pltpu.VMEM(x.shape, x.dtype) for x in inside
        ]
        + [pltpu.SemaphoreType.DMA((n,)) for n in sems],
        compiler_params=pltpu.CompilerParams(vmem_limit_bytes=int(grant * 2**20)),
        cost_estimate=pl.CostEstimate(flops=int(flops), bytes_accessed=moved, transcendentals=0),
    )(*args)


def swap(value, axis, k):
    return lax.ppermute(value, axis, [(i, i ^ k) for i in range(lax.axis_size(axis))])


def with_kernels(features, targets, coefficients, momentum, block_index, pivot_index, core):
    rows, owners = lax.axis_size("rows"), lax.axis_size("pts")
    points, width = features.shape
    block = block_index.shape[1]
    rank = pivot_index.shape[1]
    outputs = coefficients.shape[1]
    count = block // rows
    cap = 3 * count // owners
    devices = rows * owners
    own = outputs // devices
    deep = 2 * own * UPDATES
    half = rows // 2
    wide = like(coefficients.shape, f32)

    (packed,) = call(
        functools.partial(pack_kernel, count, cap, owners),
        [like((UPDATES * cap, width))],
        [block_index, features, like((UPDATES * cap, width))],
        block_index,
        features,
        sems=(2,),
    )
    came = {k: swap(packed, "pts", k) for k in (6, 5, 4, 2, 1)}
    came[2], came[6], first_index = lax.optimization_barrier((came[2], came[6], block_index))
    came[3], came[7] = swap(came[2], "pts", 1), swap(came[6], "pts", 1)
    kept = [
        like((UPDATES, outputs, points)),
        like((UPDATES, outputs, count), f32),
        like((8, 128), i32),
    ]
    given = [first_index, coefficients, momentum, targets]
    coef, offset, row_starts = call(
        functools.partial(prepare_kernel, count, owners),
        kept,
        given + kept,
        *given,
        sems=(4, 1 + 2 * UPDATES),
    )
    feats = like((UPDATES, width, count))
    inside_starts = pltpu.SMEM(row_starts.shape, i32)
    (mine,) = call(
        compact_kernel,
        [feats],
        [
            like((owners, *packed.shape)),
            inside_starts,
            like((UPDATES, count + cap, width), f32),
            feats,
        ],
        packed,
        *[came[k] for k in range(1, owners)],
        row_starts,
        sems=(owners + 1,),
    )
    beside, across = swap(mine, "rows", 1), swap(mine, "rows", 2)
    kept = [
        like((devices, deep, count // 2)),
        like((UPDATES * rows, count), i32),
        like((UPDATES * rows, count), i32),
        like((8, 128), i32),
    ]
    given = [mine, features, block_index, coef, offset]
    pieces, ids, came_from, starts = call(
        functools.partial(sums_kernel, owners),
        kept,
        [*given, like((points, count)), *kept],
        *given,
        sems=(5, 3),
        flops=2.0 * UPDATES * points * count * (2 * width + outputs),
    )
    pieces, beside, across = lax.optimization_barrier((pieces, beside, across))
    summed = lax.all_to_all(pieces, ("pts", "rows"), 0, 0, tiled=True)
    kept = [like((UPDATES, rank, block)), like((rows, block, count))]
    factor, cross = call(
        factors_kernel,
        kept,
        [
            like((rows, *feats.shape)),
            ids,
            came_from,
            pivot_index,
            kept[0],
            like((rows, rows, count, count)),
        ],
        mine,
        beside,
        across,
        swap(across, "rows", 1),
        ids,
        came_from,
        pivot_index,
        sems=(rows * rows + 2,),
        flops=2.0 * width * block * (UPDATES * rank + block),
    )
    pieces = like((owners, deep, half * cap))
    (steps,) = call(
        functools.partial(chain_kernel, cap, owners),
        [pieces],
        [summed, factor, core, cross, inside_starts, pieces],
        summed,
        factor,
        core,
        cross,
        starts,
        sems=(2 * UPDATES + 3 + rows,),
    )
    got = lax.all_to_all(steps, "pts", 0, 0, tiled=True)
    got, later_index = lax.optimization_barrier((got, block_index))
    beside, across = swap(got, "rows", 1), swap(got, "rows", 2)
    (slots,) = call(
        functools.partial(slots_kernel, count, points, cap),
        [like((UPDATES, rows * cap), i32)],
        [block_index, like((UPDATES, rows * cap), i32)],
        later_index,
        sems=(1,),
    )
    across, slots = lax.optimization_barrier((across, slots))
    parts = points // CHUNK
    return call(
        finish_kernel,
        [wide] * 2,
        [
            like((devices, deep, half * cap)),
            slots,
            wide,
            wide,
            like((UPDATES, rows * cap, outputs)),
            wide,
            wide,
        ],
        got,
        beside,
        across,
        swap(across, "rows", 1),
        slots,
        coefficients,
        momentum,
        sems=(1 + rows + 2 * parts, 2 * parts),
    )


def kernel_tile(left_rows, right_rows):
    inner_prod = mm(left_rows, right_rows, 1, 1)
    left_sq = jnp.sum(jnp.square(left_rows.astype(f32)), axis=1)
    right_sq = jnp.sum(jnp.square(right_rows.astype(f32)), axis=1)
    squared = left_sq[:, None] + right_sq[None, :] - 2.0 * inner_prod
    return jnp.exp(squared * (-3.5 / left_rows.shape[1])).astype(bf16)


def with_operations(features, targets, coefficients, momentum, block_index, pivot_index, core):
    row_count, pts_count = lax.axis_size("rows"), lax.axis_size("pts")
    row_id, pts_id = lax.axis_index("rows"), lax.axis_index("pts")
    points = features.shape[0]
    block = block_index.shape[1]
    outputs = coefficients.shape[1]
    per_row = block // row_count
    per_device = per_row // pts_count
    row_cols = outputs // row_count
    own_cols = row_cols // pts_count
    first = row_id * row_cols
    current, moving, goal = (
        lax.dynamic_slice_in_dim(value, first, row_cols, axis=1).T.astype(f32)
        for value in (coefficients, momentum, targets)
    )
    ids = iota((points, 1), 0) + pts_id * points
    place = [(ids == block_index[u][None, :]).astype(bf16) for u in range(UPDATES)]
    own_rows = []
    for u in range(UPDATES):
        mine = lax.dynamic_slice_in_dim(place[u], row_id * per_row, per_row, axis=1)
        own_rows.append(mm(mine, features, 0, 0).astype(bf16).reshape(pts_count, per_device, -1))
    came = lax.all_to_all(jnp.concatenate(own_rows, axis=1), "pts", 0, 0, tiled=False)
    chunk = jnp.sum(came.astype(f32), axis=0).astype(bf16)
    spread = lax.all_gather(lax.all_gather(chunk, "pts", axis=0), "rows", axis=0)
    spread = spread.reshape(row_count, pts_count, UPDATES, per_device, features.shape[1])
    all_steps = []
    for u in range(UPDATES):
        block_feats = spread[:, :, u].reshape(block, features.shape[1])
        mixed = mixed_of(current, moving)
        high, low = split_two(ridge_term * mixed - goal)
        tile = kernel_tile(features, block_feats)
        partial_value = (
            mm(mixed.astype(bf16), tile, 1, 0) + mm(high, place[u], 1, 0) + mm(low, place[u], 1, 0)
        )
        pieces = partial_value.astype(bf16).reshape(pts_count, own_cols, block)
        summed = lax.all_to_all(pieces, "pts", 0, 0, tiled=False)
        resid = jnp.sum(summed.astype(f32), axis=0)
        at_pivot = (iota((block, 1), 0) == pivot_index[u][None, :]).astype(bf16)
        factor = kernel_tile(block_feats, mm(at_pivot, block_feats, 0, 0).astype(bf16))
        proj = mm(resid.astype(bf16), factor, 1, 0)
        lifted = mm(proj.astype(bf16), core[u], 1, 1).astype(bf16)
        step_bf = (resid - mm(lifted, factor, 1, 1)).astype(bf16)
        steps = lax.all_gather(step_bf, "pts", axis=0, tiled=True)
        change = mm(steps, place[u], 1, 1)
        all_steps.append(change.astype(bf16))
        current, moving = stepped(current, moving, change)
    gathered = lax.all_gather(jnp.stack(all_steps), "rows", axis=1, tiled=True)
    current, moving = coefficients, momentum
    for u in range(UPDATES):
        current, moving = stepped(current, moving, gathered[u].T.astype(f32))
    return (current, moving)


def shards(features, targets, coefficients, momentum, block_index, pivot_index, nystrom_core):
    rows, owners = lax.axis_size("rows"), lax.axis_size("pts")
    count = block_index.shape[1] // rows
    fits = rows == 4 and owners == 8 and coefficients.shape[1] == 8 * rows * owners
    fits = fits and 6 * count <= count * owners and coefficients.shape[0] % CHUNK == 0 and count % CHUNK == 0 and (3 * count // owners) % 64 == 0 and UPDATES * rows == 8
    plan = with_kernels if fits else with_operations
    return plan(
        features, targets, coefficients, momentum, block_index, pivot_index, nystrom_core
    )


def solution(mesh):
    in_specs = (P("pts", None), P("pts", None), P("pts", None), P("pts", None), P(), P(), P())
    out_specs = (P("pts", None), P("pts", None))
    return jax.shard_map(shards, mesh=mesh, in_specs=in_specs, out_specs=out_specs, check_vma=False)
```
